32 devices in a mesh: dp: 8 (over z, core), tensor: 4 (over y, x).
Axes of the slice: x: 2, y: 2, z: 4, core: 2. Of those that a mesh axis runs over, the one named last changes fastest.
Arguments:
- layer_input: bfloat16 [16, 1024, 1024], P('dp', 'tensor'), may hold values from -6 to 6
- memory: bfloat16 [16, 1024, 1024], P('dp', 'tensor'), may hold values from -6 to 6
- grad_out: bfloat16 [16, 1024, 1024], P('dp', 'tensor'), may hold values from -6 to 6
- target_segments: int32 [16, 1024], P('dp'), may hold values from 0 to 15, as said below
- source_segments: int32 [16, 1024], P('dp'), may hold values from 0 to 15, as said below
- self_gain: float32 [1024], replicated, may hold values from 0.5 to 1.5
- self_shift: float32 [1024], replicated, may hold values from -1.75 to 1.75
- query_weight: bfloat16 [1024, 1024], P(None, 'tensor'), may hold values from -0.1875 to 0.1875
- query_bias: float32 [1024], P('tensor'), may hold values from -1.75 to 1.75
- key_weight: bfloat16 [1024, 1024], P(None, 'tensor'), may hold values from -0.1875 to 0.1875
- value_weight: bfloat16 [1024, 1024], P(None, 'tensor'), may hold values from -0.1875 to 0.1875
- value_bias: float32 [1024], P('tensor'), may hold values from -1.75 to 1.75
- attend_weight: bfloat16 [1024, 1024], P('tensor'), may hold values from -0.5 to 0.5
- attend_bias: float32 [1024], replicated, may hold values from -1.75 to 1.75
- cross_gain: float32 [1024], replicated, may hold values from 0.5 to 1.5
- cross_shift: float32 [1024], replicated, may hold values from -1.75 to 1.75
- cross_query: bfloat16 [1024, 1024], P(None, 'tensor'), may hold values from -0.1875 to 0.1875
- cross_query_bias: float32 [1024], P('tensor'), may hold values from -1.75 to 1.75
- cross_key: bfloat16 [1024, 1024], P(None, 'tensor'), may hold values from -0.1875 to 0.1875
- cross_value: bfloat16 [1024, 1024], P(None, 'tensor'), may hold values from -0.1875 to 0.1875
- cross_value_bias: float32 [1024], P('tensor'), may hold values from -1.75 to 1.75
- cross_attend: bfloat16 [1024, 1024], P('tensor'), may hold values from -0.5 to 0.5
- cross_attend_bias: float32 [1024], replicated, may hold values from -1.75 to 1.75
- feed_gain: float32 [1024], replicated, may hold values from 0.5 to 1.5
- feed_shift: float32 [1024], replicated, may hold values from -1.75 to 1.75
- inner_weight: bfloat16 [1024, 4096], P(None, 'tensor'), may hold values from -0.1875 to 0.1875
- inner_bias: float32 [4096], P('tensor'), may hold values from -1.75 to 1.75
- outer_weight: bfloat16 [4096, 1024], P('tensor'), may hold values from -0.125 to 0.125
- outer_bias: float32 [1024], replicated, may hold values from -1.75 to 1.75
Outputs:
- block_out: bfloat16 [16, 1024, 1024], P('dp', 'tensor')
- input_grad: float32 [16, 1024, 1024], P('dp', 'tensor')
- memory_grad: float32 [16, 1024, 1024], P('dp', 'tensor')
- grad_self_gain: float32 [1024], replicated
- grad_self_shift: float32 [1024], replicated
- grad_query_weight: float32 [1024, 1024], P(None, 'tensor')
- grad_query_bias: float32 [1024], P('tensor')
- grad_key_weight: float32 [1024, 1024], P(None, 'tensor')
- grad_value_weight: float32 [1024, 1024], P(None, 'tensor')
- grad_value_bias: float32 [1024], P('tensor')
- grad_attend_weight: float32 [1024, 1024], P('tensor')
- grad_attend_bias: float32 [1024], replicated
- grad_cross_gain: float32 [1024], replicated
- grad_cross_shift: float32 [1024], replicated
- grad_cross_query: float32 [1024, 1024], P(None, 'tensor')
- grad_cross_query_bias: float32 [1024], P('tensor')
- grad_cross_key: float32 [1024, 1024], P(None, 'tensor')
- grad_cross_value: float32 [1024, 1024], P(None, 'tensor')
- grad_cross_value_bias: float32 [1024], P('tensor')
- grad_cross_attend: float32 [1024, 1024], P('tensor')
- grad_cross_attend_bias: float32 [1024], replicated
- grad_feed_gain: float32 [1024], replicated
- grad_feed_shift: float32 [1024], replicated
- grad_inner_weight: float32 [1024, 4096], P(None, 'tensor')
- grad_inner_bias: float32 [4096], P('tensor')
- grad_outer_weight: float32 [4096, 1024], P('tensor')
- grad_outer_bias: float32 [1024], replicated
The draws below stay inside these ranges and needn't reach their ends.
Inputs may be any that keep to these rules, and one draw needn't show every extreme that they name: `target_segments`: in each row the ids never fall, start at 0 and every id from 0 to 15 appears. `source_segments`: in each row the ids never fall, start at 0 and every id from 0 to 15 appears, so each target pair has memory tokens of the same id in its row.
All inputs are finite; a program needn't handle non-finite values.
Results may differ from the reference program's by a relative error of at most 0.02.
Values may be sent and summed in bfloat16 or wider, within the bound.
A program may use at most 192 MiB of HBM per device.

```python
import jax
import jax.numpy as jnp
from jax import lax

D = 1024
H = 16
HD = 64
FF = 4096
LEN = 1024
SRC = 1024
PAIRS = 16
ROWS = 16


def segment_table(key, row_count, seq_length, pair_count):

    def one_row(row_key):
        shuffled = jax.random.permutation(row_key, seq_length - 1) + 1
        boundary = jnp.sort(shuffled[:pair_count - 1])
        places = jnp.arange(seq_length)
        return jnp.sum((places[:, None] >= boundary[None, :]).astype(jnp.int32), axis=1).astype(jnp.int32)
    return jax.vmap(one_row)(jax.random.split(key, row_count))


def draw_target_segments(key, part):
    return segment_table(jax.random.fold_in(key, 11), ROWS, LEN, PAIRS)


def draw_source_segments(key, part):
    return segment_table(jax.random.fold_in(key, 23), ROWS, SRC, PAIRS)


def shard_levels(key, shape, cuts, least, largest):
    def one(axis_at, blocks):
        heights = jax.random.uniform(jax.random.fold_in(jax.random.fold_in(key, 6), axis_at), (blocks,), jnp.float32, least / len(cuts), largest / len(cuts))
        return jnp.repeat(jnp.exp(heights), shape[axis_at] // blocks).reshape((-1,) + (1,) * (len(shape) - axis_at - 1))

    loudness = one(*cuts[0])
    for cut in cuts[1:]:
        loudness = loudness * one(*cut)
    return loudness


def bell_draw(key, dims, width, limit, cuts=(), kind=jnp.bfloat16):
    factor_of = shard_levels(key, dims, cuts, -0.22, 0.18) if cuts else 1.0
    entries = jax.random.normal(key, dims, jnp.float32) * width * factor_of
    return jnp.minimum(jnp.maximum(entries, -limit), limit).astype(kind)


def setup_inputs(seed: int = 0) -> dict:
    splits = jax.random.split(jax.random.key(seed), 30)
    layer_input = bell_draw(splits[0], (ROWS, LEN, D), 1.0, 6.0, ((0, 8), (1, 4)))
    memory = bell_draw(splits[1], (ROWS, SRC, D), 1.0, 6.0, ((0, 8), (1, 4)))
    grad_out = bell_draw(splits[2], (ROWS, LEN, D), 1.0, 6.0, ((0, 8), (1, 4)))
    target_segments = draw_target_segments(jax.random.fold_in(splits[29], 71), 0)
    source_segments = draw_source_segments(jax.random.fold_in(splits[29], 71), 0)
    self_gain = jnp.clip(1.0 + 0.1 * jax.random.normal(splits[5], (D,), jnp.float32), 0.5, 1.5)
    self_shift = bell_draw(splits[6], (D,), 0.3, 1.75, (), jnp.float32)
    query_weight = bell_draw(splits[7], (D, H * HD), D ** -0.5, 0.1875, ((1, 4),))
    query_bias = bell_draw(splits[8], (H * HD,), 0.3, 1.75, ((0, 4),), jnp.float32)
    key_weight = bell_draw(splits[9], (D, H * HD), D ** -0.5, 0.1875, ((1, 4),))
    value_weight = bell_draw(splits[10], (D, H * HD), D ** -0.5, 0.1875, ((1, 4),))
    value_bias = bell_draw(splits[11], (H * HD,), 0.3, 1.75, ((0, 4),), jnp.float32)
    attend_weight = bell_draw(splits[12], (H * HD, D), (H * HD // 8) ** -0.5, 0.5, ((0, 4),))
    attend_bias = bell_draw(splits[13], (D,), 0.3, 1.75, (), jnp.float32)
    cross_gain = jnp.clip(1.0 + 0.1 * jax.random.normal(splits[14], (D,), jnp.float32), 0.5, 1.5)
    cross_shift = bell_draw(splits[15], (D,), 0.3, 1.75, (), jnp.float32)
    cross_query = bell_draw(splits[16], (D, H * HD), D ** -0.5, 0.1875, ((1, 4),))
    cross_query_bias = bell_draw(splits[17], (H * HD,), 0.3, 1.75, ((0, 4),), jnp.float32)
    cross_key = bell_draw(splits[18], (D, H * HD), D ** -0.5, 0.1875, ((1, 4),))
    cross_value = bell_draw(splits[19], (D, H * HD), D ** -0.5, 0.1875, ((1, 4),))
    cross_value_bias = bell_draw(splits[20], (H * HD,), 0.3, 1.75, ((0, 4),), jnp.float32)
    cross_attend = bell_draw(splits[21], (H * HD, D), (H * HD // 8) ** -0.5, 0.5, ((0, 4),))
    cross_attend_bias = bell_draw(splits[22], (D,), 0.3, 1.75, (), jnp.float32)
    feed_gain = jnp.clip(1.0 + 0.1 * jax.random.normal(splits[23], (D,), jnp.float32), 0.5, 1.5)
    feed_shift = bell_draw(splits[24], (D,), 0.3, 1.75, (), jnp.float32)
    inner_weight = bell_draw(splits[25], (D, FF), D ** -0.5, 0.1875, ((1, 4),))
    inner_bias = bell_draw(splits[26], (FF,), 0.3, 1.75, ((0, 4),), jnp.float32)
    outer_weight = bell_draw(splits[27], (FF, D), (FF // 2) ** -0.5, 0.125, ((0, 4),))
    outer_bias = bell_draw(splits[28], (D,), 0.3, 1.75, (), jnp.float32)
    return dict(layer_input=layer_input, memory=memory, grad_out=grad_out, target_segments=target_segments, source_segments=source_segments, self_gain=self_gain, self_shift=self_shift, query_weight=query_weight, query_bias=query_bias, key_weight=key_weight, value_weight=value_weight, value_bias=value_bias, attend_weight=attend_weight, attend_bias=attend_bias, cross_gain=cross_gain, cross_shift=cross_shift, cross_query=cross_query, cross_query_bias=cross_query_bias, cross_key=cross_key, cross_value=cross_value, cross_value_bias=cross_value_bias, cross_attend=cross_attend, cross_attend_bias=cross_attend_bias, feed_gain=feed_gain, feed_shift=feed_shift, inner_weight=inner_weight, inner_bias=inner_bias, outer_weight=outer_weight, outer_bias=outer_bias)


EPSILON = 1e-05
MASKED = -1000000000.0

@jax.custom_vjp
def low(v):
    return lax.optimization_barrier(v.astype(jnp.bfloat16)).astype(jnp.float32)

@jax.custom_vjp
def low_back(v):
    return v

def low_keep(v):
    return (low(v), None)

def low_pass(kept, grad):
    return (grad,)

def back_keep(v):
    return (v, None)

def back_low(kept, grad):
    return (low(grad),)
low.defvjp(low_keep, low_pass)
low_back.defvjp(back_keep, back_low)

def dense(rows_in, weight):
    return jnp.einsum('rtd,dc->rtc', rows_in, weight, precision=lax.Precision.HIGHEST)

def layer_norm(values, gain, shift):
    average = lax.optimization_barrier(jnp.mean(values, axis=-1, keepdims=True))
    center = values - average
    variance = lax.optimization_barrier(jnp.mean(center * center, axis=-1, keepdims=True))
    return center * lax.rsqrt(variance + EPSILON) * gain + shift

def attention(query, keys, values, query_ids, key_ids, causal):
    score_scale = float(HD) ** (-0.5)

    def one_row(inputs):
        query_row, key_row, value_row, query_seg, key_seg = inputs
        query_heads = query_row.reshape(query_row.shape[0], H, HD)
        key_heads = key_row.reshape(key_row.shape[0], H, HD)
        value_heads = value_row.reshape(value_row.shape[0], H, HD)
        raw_scores = jnp.einsum('qhd,khd->hqk', query_heads, key_heads, precision=lax.Precision.HIGHEST) * score_scale
        scores = low_back(raw_scores)
        allowed = query_seg.astype(jnp.int32)[:, None] == key_seg.astype(jnp.int32)[None, :]
        if causal:
            query_place = jnp.arange(query_row.shape[0], dtype=jnp.int32)
            key_place = jnp.arange(key_row.shape[0], dtype=jnp.int32)
            allowed = allowed & (key_place[None, :] <= query_place[:, None])
        scores = jnp.where(allowed[None], scores, jnp.full(scores.shape, MASKED, scores.dtype))
        row_max = lax.optimization_barrier(jnp.max(scores, axis=-1, keepdims=True))
        expo_scores = jnp.exp(scores - row_max)
        softmax_out = expo_scores / lax.optimization_barrier(jnp.sum(expo_scores, axis=-1, keepdims=True))
        attended = jnp.einsum('hqk,khd->qhd', low(softmax_out), value_heads, precision=lax.Precision.HIGHEST)
        return attended.reshape(query_row.shape)
    return lax.map(jax.checkpoint(one_row), (query, keys, values, query_ids, key_ids))

def forward(inputs, memory_in, target_ids, source_ids, weights):
    self_gain, self_shift, query_weight, query_bias, key_weight, value_weight, value_bias, attend_weight, attend_bias, cross_gain, cross_shift, cross_query, cross_query_bias, cross_key, cross_value, cross_value_bias, cross_attend, cross_attend_bias, feed_gain, feed_shift, inner_weight, inner_bias, outer_weight, outer_bias = weights
    normed1 = low(layer_norm(inputs, self_gain, self_shift))
    query1 = low_back(low(dense(normed1, query_weight) + query_bias))
    keys1 = low_back(low(dense(normed1, key_weight)))
    values1 = low_back(low(dense(normed1, value_weight) + value_bias))
    attended1 = low_back(low(attention(query1, keys1, values1, target_ids, target_ids, True)))
    hidden1 = inputs + low_back(dense(attended1, attend_weight)) + attend_bias
    normed2 = low(layer_norm(hidden1, cross_gain, cross_shift))
    query2 = low_back(low(dense(normed2, cross_query) + cross_query_bias))
    keys2 = low_back(low(dense(memory_in, cross_key)))
    values2 = low_back(low(dense(memory_in, cross_value) + cross_value_bias))
    attended2 = low_back(low(attention(query2, keys2, values2, target_ids, source_ids, False)))
    hidden2 = hidden1 + low_back(dense(attended2, cross_attend)) + cross_attend_bias
    normed3 = low(layer_norm(hidden2, feed_gain, feed_shift))
    pre_active = low_back(dense(normed3, inner_weight) + inner_bias)
    active = low(jax.nn.silu(pre_active))
    return hidden2 + low_back(dense(active, outer_weight)) + outer_bias

def reference(layer_input, memory, grad_out, target_segments, source_segments, self_gain, self_shift, query_weight, query_bias, key_weight, value_weight, value_bias, attend_weight, attend_bias, cross_gain, cross_shift, cross_query, cross_query_bias, cross_key, cross_value, cross_value_bias, cross_attend, cross_attend_bias, feed_gain, feed_shift, inner_weight, inner_bias, outer_weight, outer_bias):
    params = tuple((item.astype(jnp.float32) for item in (self_gain, self_shift, query_weight, query_bias, key_weight, value_weight, value_bias, attend_weight, attend_bias, cross_gain, cross_shift, cross_query, cross_query_bias, cross_key, cross_value, cross_value_bias, cross_attend, cross_attend_bias, feed_gain, feed_shift, inner_weight, inner_bias, outer_weight, outer_bias)))
    target_ids = target_segments.astype(jnp.int32)
    source_ids = source_segments.astype(jnp.int32)

    def run_layer(inputs, memory_in, *weights):
        return forward(inputs, memory_in, target_ids, source_ids, weights)
    result, pull_back = jax.vjp(run_layer, layer_input.astype(jnp.float32), memory.astype(jnp.float32), *params)
    grads = pull_back(grad_out.astype(jnp.float32))
    return (result.astype(jnp.bfloat16), grads[0], grads[1], grads[2], grads[3], grads[4], grads[5], grads[6], grads[7], grads[8], grads[9], grads[10], grads[11], grads[12], grads[13], grads[14], grads[15], grads[16], grads[17], grads[18], grads[19], grads[20], grads[21], grads[22], grads[23], grads[24], grads[25])
```

```python
import jax
import jax.numpy as jnp
from jax import lax
from jax.experimental import pallas as pl
from jax.experimental.pallas import tpu as pltpu
from jax.sharding import PartitionSpec as P

HD = 64
MASKED = -1000000000.0
QUERIES = 128
KEYS = 256
NT = (((1,), (1,)), ((), ()))
TN = (((0,), (0,)), ((), ()))
NN = (((1,), (0,)), ((), ()))


def dot(a, b, dims):
    return lax.dot_general(a, b, dims, preferred_element_type=jnp.float32)


def both_heads(block):
    first = lax.broadcasted_iota(jnp.int32, block.shape, 1) < HD
    zero = jnp.zeros_like(block)
    return jnp.concatenate([jnp.where(first, block, zero), jnp.where(first, zero, block)], axis=0)


def key_span(bounds, place, count, step):
    start = bounds[0, place] + step * KEYS
    at = pl.multiple_of(jnp.minimum(start, count - KEYS), 16)
    return start, at


def allowed_keys(low_ref, high_ref, start, at):
    key_place = at + lax.broadcasted_iota(jnp.int32, (KEYS, 1), 0)
    least = jnp.maximum(low_ref[...], start)
    seen = (key_place >= least) & (key_place < high_ref[...])
    return jnp.concatenate([seen, seen], axis=1)


def attend_kernel(bounds, low_ref, high_ref, q_ref, k_ref, v_ref, out_ref, sums_ref, acc, top, total):
    pairs = q_ref.shape[1] // 128
    count = k_ref.shape[0]
    place = pl.program_id(0)
    acc[...] = jnp.zeros_like(acc)
    total[...] = jnp.zeros_like(total)
    top[...] = jnp.full_like(top, -1e30)
    queries = [both_heads(q_ref[:, p * 128:(p + 1) * 128] * jnp.bfloat16(HD ** -0.5)) for p in range(pairs)]

    def step(j, _):
        start, at = key_span(bounds, place, count, j)
        seen = allowed_keys(low_ref, high_ref, start, at)
        for p in range(pairs):
            keys = k_ref[pl.ds(at, KEYS), p * 128:(p + 1) * 128]
            values = v_ref[pl.ds(at, KEYS), p * 128:(p + 1) * 128]
            scores = jnp.where(seen, dot(keys, queries[p], NT), MASKED)
            before = top[p:p + 1]
            now = jnp.maximum(before, jnp.max(scores, axis=0, keepdims=True))
            weight = jnp.exp(scores - now)
            keep = jnp.exp(before - now)
            top[p:p + 1] = now
            total[p:p + 1] = total[p:p + 1] * keep + jnp.sum(weight, axis=0, keepdims=True)
            acc[p] = acc[p] * keep + dot(values, weight.astype(jnp.bfloat16), TN)
        return 0

    lax.fori_loop(0, bounds[1, place], step, 0)
    for p in range(pairs):
        sums = total[p:p + 1]
        mixed = acc[p] / sums
        joined = jnp.concatenate([mixed[:HD, :QUERIES], mixed[HD:, QUERIES:]], axis=0)
        out_ref[:, p * 128:(p + 1) * 128] = joined.T.astype(jnp.bfloat16)
        sums_ref[p:p + 1] = top[p:p + 1] + jnp.log(sums)


def attend(q, k, v, bounds, low, high):
    count, width = q.shape
    source = k.shape[0]
    pairs = width // 128
    whole = lambda i, b: (0, 0)
    return pl.pallas_call(
        attend_kernel,
        grid_spec=pltpu.PrefetchScalarGridSpec(
            num_scalar_prefetch=1,
            grid=(count // QUERIES,),
            in_specs=[
                pl.BlockSpec((1, QUERIES), lambda i, b: (0, i)),
                pl.BlockSpec((1, QUERIES), lambda i, b: (0, i)),
                pl.BlockSpec((QUERIES, width), lambda i, b: (i, 0)),
                pl.BlockSpec((source, width), whole),
                pl.BlockSpec((source, width), whole),
            ],
            out_specs=[
                pl.BlockSpec((QUERIES, width), lambda i, b: (i, 0)),
                pl.BlockSpec((None, pairs, 2 * QUERIES), lambda i, b: (i, 0, 0)),
            ],
            scratch_shapes=[
                pltpu.VMEM((pairs, 128, 2 * QUERIES), jnp.float32),
                pltpu.VMEM((pairs, 2 * QUERIES), jnp.float32),
                pltpu.VMEM((pairs, 2 * QUERIES), jnp.float32),
            ],
        ),
        out_shape=[
            jax.ShapeDtypeStruct((count, width), jnp.bfloat16),
            jax.ShapeDtypeStruct((count // QUERIES, pairs, 2 * QUERIES), jnp.float32),
        ],
        compiler_params=pltpu.CompilerParams(vmem_limit_bytes=32 << 20),
        cost_estimate=pl.CostEstimate(flops=4 * count * 400 * width, bytes_accessed=8 * count * width, transcendentals=0),
        name="attend",
    )(bounds, low, high, q, k, v)


def attend_back_kernel(
    bounds, low_ref, high_ref, q_ref, grad_ref, out_ref, sums_ref, k_ref, v_ref,
    dq_ref, dk_ref, dv_ref, acc, acc_k, acc_v,
):
    pairs = q_ref.shape[1] // 128
    count = k_ref.shape[0]
    place = pl.program_id(0)

    @pl.when(place == 0)
    def _():
        acc_k[...] = jnp.zeros_like(acc_k)
        acc_v[...] = jnp.zeros_like(acc_v)

    acc[...] = jnp.zeros_like(acc)
    queries, grads, fixes = [], [], []
    ones = jnp.ones((8, 128), jnp.bfloat16)
    for p in range(pairs):
        cut = slice(p * 128, (p + 1) * 128)
        queries.append(both_heads(q_ref[:, cut] * jnp.bfloat16(HD ** -0.5)))
        grad = both_heads(grad_ref[:, cut])
        grads.append(grad)
        out = out_ref[:, cut].astype(jnp.float32)
        product = grad.astype(jnp.float32) * jnp.concatenate([out, out], axis=0)
        coarse = product.astype(jnp.bfloat16)
        fine = (product - coarse.astype(jnp.float32)).astype(jnp.bfloat16)
        fixes.append((dot(ones, coarse, NT) + dot(ones, fine, NT))[:1])

    def step(j, _):
        start, at = key_span(bounds, place, count, j)
        seen = allowed_keys(low_ref, high_ref, start, at)
        rows = pl.ds(at, KEYS)
        for p in range(pairs):
            cut = slice(p * 128, (p + 1) * 128)
            keys = k_ref[rows, cut]
            values = v_ref[rows, cut]
            scores = dot(keys, queries[p], NT)
            prob = jnp.exp(jnp.where(seen, scores - sums_ref[p:p + 1], MASKED))
            dprob = dot(values, grads[p], NT)
            dscore = (prob * (dprob - fixes[p])).astype(jnp.bfloat16)
            acc_v[rows, cut] += dot(prob.astype(jnp.bfloat16), grads[p], NN)
            acc_k[rows, cut] += dot(dscore, queries[p], NN)
            acc[p] += dot(keys, dscore, TN)
        return 0

    lax.fori_loop(0, bounds[1, place], step, 0)
    for p in range(pairs):
        mixed = acc[p] * (HD ** -0.5)
        joined = jnp.concatenate([mixed[:HD, :QUERIES], mixed[HD:, QUERIES:]], axis=0)
        dq_ref[:, p * 128:(p + 1) * 128] = joined.T.astype(jnp.bfloat16)

    @pl.when(place == pl.num_programs(0) - 1)
    def _():
        dk_ref[...] = acc_k[...].astype(jnp.bfloat16)
        dv_ref[...] = acc_v[...].astype(jnp.bfloat16)


def attend_back(q, k, v, grad, out, sums, bounds, low, high):
    count, width = q.shape
    source = k.shape[0]
    pairs = width // 128
    whole = lambda i, b: (0, 0)
    rows = lambda i, b: (i, 0)
    return pl.pallas_call(
        attend_back_kernel,
        grid_spec=pltpu.PrefetchScalarGridSpec(
            num_scalar_prefetch=1,
            grid=(count // QUERIES,),
            in_specs=[
                pl.BlockSpec((1, QUERIES), lambda i, b: (0, i)),
                pl.BlockSpec((1, QUERIES), lambda i, b: (0, i)),
                pl.BlockSpec((QUERIES, width), rows),
                pl.BlockSpec((QUERIES, width), rows),
                pl.BlockSpec((QUERIES, width), rows),
                pl.BlockSpec((None, pairs, 2 * QUERIES), lambda i, b: (i, 0, 0)),
                pl.BlockSpec((source, width), whole),
                pl.BlockSpec((source, width), whole),
            ],
            out_specs=[
                pl.BlockSpec((QUERIES, width), rows),
                pl.BlockSpec((source, width), whole),
                pl.BlockSpec((source, width), whole),
            ],
            scratch_shapes=[
                pltpu.VMEM((pairs, 128, 2 * QUERIES), jnp.float32),
                pltpu.VMEM((source, width), jnp.float32),
                pltpu.VMEM((source, width), jnp.float32),
            ],
        ),
        out_shape=[
            jax.ShapeDtypeStruct((count, width), jnp.bfloat16),
            jax.ShapeDtypeStruct((source, width), jnp.bfloat16),
            jax.ShapeDtypeStruct((source, width), jnp.bfloat16),
        ],
        compiler_params=pltpu.CompilerParams(vmem_limit_bytes=40 << 20),
        cost_estimate=pl.CostEstimate(flops=10 * count * 400 * width, bytes_accessed=16 * count * width, transcendentals=0),
        name="attend_back",
    )(bounds, low, high, q, grad, out, sums, k, v)


def reach(query_ids, key_ids, causal):
    count = query_ids.shape[0]
    low = jnp.sum((key_ids[None, :] < query_ids[:, None]).astype(jnp.int32), axis=1)
    if causal:
        high = jnp.arange(count, dtype=jnp.int32) + 1
    else:
        high = jnp.sum((key_ids[None, :] <= query_ids[:, None]).astype(jnp.int32), axis=1)
    first = low[::QUERIES] // 16 * 16
    steps = (high[QUERIES - 1::QUERIES] - first + KEYS - 1) // KEYS
    return jnp.stack([first, steps]), low[None], high[None]


EPSILON = 1e-05
BF = jnp.bfloat16
F32 = jnp.float32


class Links:
    def __init__(self, mesh):
        self.dp = mesh.shape["dp"]
        self.tensor = mesh.shape["tensor"]
        self.planes = self.dp // 2

    def enter(self):
        place = lax.axis_index("dp")
        self.core = place % 2
        self.plane = place // 2
        self.chip = lax.axis_index("tensor")

    def move(self, value, target):
        pairs = []
        for place in range(self.dp):
            for chip in range(self.tensor):
                to = target(place // 2, place % 2, chip)
                if to is not None:
                    pairs.append((place * self.tensor + chip, (to[0] * 2 + to[1]) * self.tensor + to[2]))
        return lax.ppermute(value, ("dp", "tensor"), pairs)

    def other_core(self, value):
        return self.move(value, lambda plane, core, chip: (plane, 1 - core, chip))

    def across(self, value, step):
        return self.move(value, lambda plane, core, chip: (plane, core, chip ^ step))

    def plane_pair(self, value, step):
        return self.move(value, lambda plane, core, chip: (plane ^ step, core, chip))

    def slot(self, value, which):
        def target(plane, core, chip):
            step = 3 if which == 3 else which if plane % 2 == 0 else 3 - which
            return (plane, core, chip ^ step)

        return self.move(value, target)

    def gather_weight(self, own):
        first = self.slot(own, 1)
        diagonal = self.slot(first, 2)
        second = self.plane_pair(first, 1)
        return [own, first, second, diagonal]

    def plane_sum(self, parts, first):
        second = 3 - first
        near = self.slot(parts[first], first)
        passed = self.slot(parts[3], first)
        middle = (parts[second].astype(F32) + passed.astype(F32)).astype(BF)
        far = self.slot(middle, second)
        return parts[0].astype(F32) + near.astype(F32) + far.astype(F32)

    def line_sum(self, total):
        if self.planes % 4:
            low = total.astype(BF)
            step = 1
            while step < self.planes:
                low = (low.astype(F32) + self.plane_pair(low, step).astype(F32)).astype(BF)
                step *= 2
            return low
        inward = {0: 1, 3: 2}
        outward = {1: 0, 2: 3}
        middle = {1: 2, 2: 1}

        def along(table):
            def target(plane, core, chip):
                to = table.get(plane % 4)
                return None if to is None else (plane - plane % 4 + to, core, chip)

            return target

        low = (total + self.move(total.astype(BF), along(inward)).astype(F32)).astype(BF)
        low = (low.astype(F32) + self.move(low, along(middle)).astype(F32)).astype(BF)
        step = 4
        while step < self.planes:
            low = (low.astype(F32) + self.plane_pair(low, step).astype(F32)).astype(BF)
            step *= 2
        back = self.move(low, along(outward))
        inner = (self.plane % 4 == 1) | (self.plane % 4 == 2)
        return jnp.where(inner, low, back)

    def weight_total(self, parts, first):
        return self.line_sum(self.plane_sum(parts, first))

    def halves(self, mine, axis):
        theirs = self.other_core(mine)
        return jnp.where(
            self.core == 0,
            jnp.concatenate([mine, theirs], axis=axis),
            jnp.concatenate([theirs, mine], axis=axis),
        )

    def take_half(self, value, axis, which):
        size = value.shape[axis] // 2
        return lax.dynamic_slice_in_dim(value, which * size, size, axis)

    def swap_parts(self, parts):
        got = [lax.dynamic_index_in_dim(parts, self.chip, 0, keepdims=False)]
        for step in range(1, self.tensor):
            got.append(self.across(lax.dynamic_index_in_dim(parts, self.chip ^ step, 0, keepdims=False), step))
        got = jnp.stack(got)
        return jnp.stack(
            [lax.dynamic_index_in_dim(got, self.chip ^ at, 0, keepdims=False) for at in range(self.tensor)]
        )

    def to_row(self, value):
        keep = self.take_half(value, 1, self.core)
        theirs = self.other_core(self.take_half(value, 1, 1 - self.core))
        rows = jnp.where(self.core == 0, jnp.concatenate([keep, theirs]), jnp.concatenate([theirs, keep]))
        mine = self.swap_parts(rows)
        both = self.halves(mine[:, None], 1)
        return both.reshape(-1, value.shape[-1])

    def half_row(self, row):
        cut = row.reshape(self.tensor, 2, -1, row.shape[-1])
        return lax.dynamic_index_in_dim(cut, self.core, 1, keepdims=False)

    def other_half_row(self, row):
        cut = row.reshape(self.tensor, 2, -1, row.shape[-1])
        return lax.dynamic_index_in_dim(cut, 1 - self.core, 1, keepdims=False)

    def from_row(self, mine):
        rows = self.swap_parts(mine)
        keep = self.take_half(rows, 0, self.core)
        theirs = self.other_core(self.take_half(rows, 0, 1 - self.core))
        return jnp.where(
            self.core == 0,
            jnp.concatenate([keep, theirs], axis=1),
            jnp.concatenate([theirs, keep], axis=1),
        )

    def pair_sum(self, partial):
        low = lax.optimization_barrier(partial.astype(BF))
        return low.astype(F32) + self.other_core(low).astype(F32)

    def pair_sum_half(self, partial):
        low = lax.optimization_barrier(partial.astype(BF))
        return self.half_row(low).astype(F32) + self.other_core(self.other_half_row(low)).astype(F32)

    def chip_sum(self, value):
        for step in (1, 2):
            value = value + self.across(value, step)
        step = 1
        while step < self.planes:
            value = value + self.plane_pair(value, step)
            step *= 2
        return value

    def quarter_sum(self, parts):
        total = parts[0]
        for which in (1, 2, 3):
            total = total + self.slot(parts[which], which)
        step = 1
        while step < self.planes:
            total = total + self.plane_pair(total, step)
            step *= 2
        return total


def norm_stats(values):
    average = jnp.mean(values, axis=-1, keepdims=True)
    center = values - average
    inverse = lax.rsqrt(jnp.mean(center * center, axis=-1, keepdims=True) + EPSILON)
    return center * inverse, inverse


def norm_forward(values, gain, shift):
    unit, _ = norm_stats(values)
    return (unit * gain + shift).astype(BF)


def norm_backward(grad_in, values, gain):
    unit, inverse = norm_stats(values)
    scaled = grad_in * gain
    first_mean = jnp.mean(scaled, axis=-1, keepdims=True)
    second_mean = jnp.mean(scaled * unit, axis=-1, keepdims=True)
    grad_values = inverse * (scaled - first_mean - unit * second_mean)
    return grad_values, jnp.sum(grad_in * unit, axis=0), jnp.sum(grad_in, axis=0)


def cat(parts, axis):
    return jnp.concatenate(parts, axis=axis)


def cut_slots(value, axis):
    return jnp.split(value, 4, axis=axis)


def solution(mesh):
    if mesh.shape["tensor"] != 4:
        return general_solution(mesh)
    links = Links(mesh)

    def local(
        layer_input, memory, grad_out, target_segments, source_segments,
        self_gain, self_shift, query_weight, query_bias, key_weight, value_weight, value_bias,
        attend_weight, attend_bias,
        cross_gain, cross_shift, cross_query, cross_query_bias, cross_key, cross_value, cross_value_bias,
        cross_attend, cross_attend_bias,
        feed_gain, feed_shift, inner_weight, inner_bias, outer_weight, outer_bias,
    ):
        links.enter()
        core, chip = links.core, links.chip
        columns = lambda w: links.take_half(w, 1, core)
        rows = lambda w: links.take_half(w, 0, core)

        ids = jnp.stack([target_segments, source_segments], axis=1)
        their_ids = links.other_core(ids)
        row_ids = jnp.where(core == 0, cat([ids, their_ids], 0), cat([their_ids, ids], 0))
        row_ids = lax.dynamic_index_in_dim(row_ids, chip, 0, keepdims=False)
        target_ids, source_ids = row_ids[0], row_ids[1]
        reach_self = reach(target_ids, target_ids, True)
        reach_cross = reach(target_ids, source_ids, False)

        biases = cat([rows(b) for b in (query_bias, value_bias, cross_query_bias, cross_value_bias, inner_bias)], 0)
        bias_slots = [biases] + [links.slot(biases, which) for which in (1, 2, 3)]

        def bias_of(at, size):
            return cat([b[at:at + size] for b in bias_slots], 0)

        head = columns(query_weight).shape[1]
        unit = columns(inner_weight).shape[1]
        bq, bv, bcq, bcv = (bias_of(i * head, head) for i in range(4))
        bi = bias_of(4 * head, unit)

        inputs = links.to_row(layer_input).astype(F32)
        wqkv = links.gather_weight(cat([columns(query_weight), columns(key_weight), columns(value_weight)], 1))
        wo = links.gather_weight(rows(attend_weight))
        mem = links.to_row(memory)
        wckv = links.gather_weight(cat([columns(cross_key), columns(cross_value)], 1))
        wcq = links.gather_weight(columns(cross_query))
        wco = links.gather_weight(rows(cross_attend))
        grad_top_low = links.to_row(grad_out)
        wi = links.gather_weight(columns(inner_weight))
        wu = links.gather_weight(rows(outer_weight))

        wq = cat([w[:, :head] for w in wqkv], 1)
        wk = cat([w[:, head:2 * head] for w in wqkv], 1)
        wv = cat([w[:, 2 * head:] for w in wqkv], 1)
        wo = cat(wo, 0)
        wck = cat([w[:, :head] for w in wckv], 1)
        wcv = cat([w[:, head:] for w in wckv], 1)
        wcq = cat(wcq, 1)
        wco = cat(wco, 0)

        n1 = norm_forward(inputs, self_gain, self_shift)
        q1 = (dot(n1, wq, NN) + bq).astype(BF)
        k1 = dot(n1, wk, NN).astype(BF)
        v1 = (dot(n1, wv, NN) + bv).astype(BF)
        att1, sums1 = attend(q1, k1, v1, *reach_self)
        hidden1 = inputs + links.pair_sum(dot(att1, wo, NN)) + attend_bias

        k2 = dot(mem, wck, NN).astype(BF)
        v2 = (dot(mem, wcv, NN) + bcv).astype(BF)
        n2 = norm_forward(hidden1, cross_gain, cross_shift)
        q2 = (dot(n2, wcq, NN) + bcq).astype(BF)
        att2, sums2 = attend(q2, k2, v2, *reach_cross)
        hidden2 = hidden1 + links.pair_sum(dot(att2, wco, NN)) + cross_attend_bias

        n3 = norm_forward(hidden2, feed_gain, feed_shift)
        active, slope = [], []
        for s in range(4):
            pre = dot(n3, wi[s], NN) + bi[s * unit:(s + 1) * unit]
            sigmoid = jax.nn.sigmoid(pre)
            active.append((pre * sigmoid).astype(BF))
            slope.append((sigmoid * (1.0 + pre * (1.0 - sigmoid))).astype(BF))

        grad_top = grad_top_low.astype(F32)
        g_outer = [dot(active[s], grad_top_low, TN).astype(BF) for s in range(4)]
        grad_inner = [
            (dot(grad_top_low, wu[s], NT) * slope[s].astype(F32)).astype(BF) for s in range(4)
        ]
        g_inner = [dot(n3, grad_inner[s], TN).astype(BF) for s in range(4)]
        grad_norm3 = sum(dot(grad_inner[s], wi[s], NT) for s in range(4))
        grad_from3, g_feed_gain, g_feed_shift = norm_backward(links.pair_sum(grad_norm3), hidden2, feed_gain)
        grad_hidden2 = grad_top + grad_from3
        g_outer_bias = jnp.sum(grad_top, axis=0)
        t_outer = links.weight_total(g_outer, 1)
        t_inner = links.weight_total(g_inner, 2)

        out_part = sum(dot(active[s], wu[s], NN) for s in range(4))
        out_half = links.half_row(hidden2) + links.pair_sum_half(out_part) + outer_bias
        block_out = links.from_row(out_half.astype(BF))

        gh2 = grad_hidden2.astype(BF)
        grad_att2 = dot(gh2, wco, NT).astype(BF)
        dq2, dk2, dv2 = attend_back(q2, k2, v2, grad_att2, att2, sums2, *reach_cross)
        t_co = links.weight_total(cut_slots(dot(att2, gh2, TN).astype(BF), 0), 1)
        t_cq = links.weight_total(cut_slots(dot(n2, dq2, TN).astype(BF), 1), 2)
        t_ck = links.weight_total(cut_slots(dot(mem, dk2, TN).astype(BF), 1), 1)
        t_cv = links.weight_total(cut_slots(dot(mem, dv2, TN).astype(BF), 1), 2)
        grad_norm2 = dot(dq2, wcq, NT)
        grad_from2, g_cross_gain, g_cross_shift = norm_backward(links.pair_sum(grad_norm2), hidden1, cross_gain)
        grad_hidden1 = grad_hidden2 + grad_from2
        g_cross_attend_bias = jnp.sum(grad_hidden2, axis=0)
        mem_part = dot(dk2, wck, NT) + dot(dv2, wcv, NT)
        memory_grad = links.from_row(links.pair_sum_half(mem_part).astype(BF)).astype(F32)

        gh1 = grad_hidden1.astype(BF)
        grad_att1 = dot(gh1, wo, NT).astype(BF)
        dq1, dk1, dv1 = attend_back(q1, k1, v1, grad_att1, att1, sums1, *reach_self)
        t_o = links.weight_total(cut_slots(dot(att1, gh1, TN).astype(BF), 0), 1)
        t_q = links.weight_total(cut_slots(dot(n1, dq1, TN).astype(BF), 1), 2)
        t_k = links.weight_total(cut_slots(dot(n1, dk1, TN).astype(BF), 1), 1)
        t_v = links.weight_total(cut_slots(dot(n1, dv1, TN).astype(BF), 1), 2)
        grad_norm1 = dot(dq1, wq, NT) + dot(dk1, wk, NT) + dot(dv1, wv, NT)
        grad_from1, g_self_gain, g_self_shift = norm_backward(links.pair_sum(grad_norm1), inputs, self_gain)
        input_half = links.half_row(grad_hidden1 + grad_from1)
        input_grad = links.from_row(input_half.astype(BF)).astype(F32)
        g_attend_bias = jnp.sum(grad_hidden1, axis=0)

        shared = links.chip_sum(
            jnp.stack([
                g_self_gain, g_self_shift, g_attend_bias, g_cross_gain, g_cross_shift, g_cross_attend_bias,
                g_feed_gain, g_feed_shift, g_outer_bias,
            ])
        )
        split = cat(
            [
                jnp.sum(g.astype(F32), axis=0).reshape(4, -1)
                for g in (dq1, dv1, dq2, dv2, cat(grad_inner, 1))
            ],
            1,
        )
        split = links.quarter_sum(split)
        split_both = links.other_core(split)

        def split_of(at, size):
            mine, theirs = split[at:at + size], split_both[at:at + size]
            return jnp.where(core == 0, cat([mine, theirs], 0), cat([theirs, mine], 0))

        full = lambda total, axis: links.halves(total, axis).astype(F32)
        return (
            block_out, input_grad, memory_grad,
            shared[0], shared[1],
            full(t_q, 1), split_of(0, head), full(t_k, 1), full(t_v, 1), split_of(head, head),
            full(t_o, 0), shared[2],
            shared[3], shared[4],
            full(t_cq, 1), split_of(2 * head, head), full(t_ck, 1), full(t_cv, 1), split_of(3 * head, head),
            full(t_co, 0), shared[5],
            shared[6], shared[7],
            full(t_inner, 1), split_of(4 * head, unit), full(t_outer, 0), shared[8],
        )

    row, one, by_column, by_row = P("dp", "tensor", None), P(), P(None, "tensor"), P("tensor", None)
    part, ids = P("tensor"), P("dp", None)
    return jax.shard_map(
        local,
        mesh=mesh,
        in_specs=(
            row, row, row, ids, ids,
            one, one, by_column, part, by_column, by_column, part, by_row, one,
            one, one, by_column, part, by_column, by_column, part, by_row, one,
            one, one, by_column, part, by_row, one,
        ),
        out_specs=(
            row, row, row,
            one, one, by_column, part, by_column, by_column, part, by_row, one,
            one, one, by_column, part, by_column, by_column, part, by_row, one,
            one, one, by_column, part, by_row, one,
        ),
        check_vma=False,
    )


BLOCK_ROWS = 512


def general_norm_forward(values, gain, shift):
    average = jnp.mean(values, axis=-1, keepdims=True)
    center = values - average
    inverse = lax.rsqrt(jnp.mean(center * center, axis=-1, keepdims=True) + EPSILON)
    normed = center * inverse
    return ((normed * gain + shift).astype(jnp.bfloat16), normed, inverse)


def general_norm_backward(grad_in, normed, inverse, gain):
    scaled = grad_in * gain
    first_mean = jnp.mean(scaled, axis=-1, keepdims=True)
    second_mean = jnp.mean(scaled * normed, axis=-1, keepdims=True)
    grad_values = inverse * (scaled - first_mean - normed * second_mean)
    return (grad_values, jnp.sum(grad_in * normed, axis=(0, 1)), jnp.sum(grad_in, axis=(0, 1)))


def gather_rows(values):
    return lax.all_gather(values, "tensor", axis=1, tiled=True)


def gather_grads(values):
    return lax.all_gather(values, "tensor", axis=1, tiled=True)


def reduce_inputs(partial_sum):
    return lax.psum_scatter(partial_sum, "tensor", scatter_dimension=1, tiled=True)


def advance(base, partial_sum, bias):
    return base + lax.psum_scatter(partial_sum, "tensor", scatter_dimension=1, tiled=True) + bias


def next_rows(values, gain, shift):
    return gather_rows(general_norm_forward(values, gain, shift)[0])


def backward_rows(normed_low):
    return gather_rows(normed_low)


def project(rows_in, weight):
    return jnp.einsum("rtd,dc->rtc", rows_in, weight, preferred_element_type=jnp.float32)


def project_back(grads, weight):
    return jnp.einsum("rtc,dc->rtd", grads, weight, preferred_element_type=jnp.float32)


def outer_sum(rows_in, grads):
    return jnp.einsum("rtd,rtc->dc", rows_in, grads, preferred_element_type=jnp.float32)


def bias_sum(grads):
    return jnp.sum(grads.astype(jnp.float32), axis=(0, 1))


def split_heads(values):
    return values.reshape(values.shape[0], values.shape[1], values.shape[2] // HD, HD)


def block_scores(query_block, key_row, query_ids, key_ids, row_start, causal):
    raw_scores = jnp.einsum(
        "qhd,khd->hqk", query_block, key_row, preferred_element_type=jnp.float32
    ) * float(HD) ** (-0.5)
    allowed = query_ids[:, None] == key_ids[None, :]
    if causal:
        query_place = row_start + jnp.arange(query_block.shape[0], dtype=jnp.int32)
        key_place = jnp.arange(key_row.shape[0], dtype=jnp.int32)
        allowed = allowed & (key_place[None, :] <= query_place[:, None])
    return jnp.where(allowed[None], raw_scores, jnp.full(raw_scores.shape, MASKED, jnp.float32))


def block_inputs(
    query_heads, key_heads, value_heads, query_ids, key_ids, position, block_count, block_size
):
    row_index = position // block_count
    row_start = position % block_count * block_size
    query_row = lax.dynamic_index_in_dim(query_heads, row_index, 0, keepdims=False)
    query_block = lax.dynamic_slice_in_dim(query_row, row_start, block_size, 0)
    key_row = lax.dynamic_index_in_dim(key_heads, row_index, 0, keepdims=False)
    value_row = lax.dynamic_index_in_dim(value_heads, row_index, 0, keepdims=False)
    query_seg = lax.dynamic_slice_in_dim(
        lax.dynamic_index_in_dim(query_ids, row_index, 0, keepdims=False), row_start, block_size, 0
    )
    key_seg = lax.dynamic_index_in_dim(key_ids, row_index, 0, keepdims=False)
    return (row_index, row_start, query_block, key_row, value_row, query_seg, key_seg)


def attend_forward(query, keys, values, query_ids, key_ids, causal):
    query_heads = split_heads(query)
    key_heads = split_heads(keys)
    value_heads = split_heads(values)
    block_size = min(BLOCK_ROWS, query.shape[1])
    block_count = query.shape[1] // block_size

    def one_block(position):
        row_index, row_start, query_block, key_row, value_row, query_seg, key_seg = block_inputs(
            query_heads,
            key_heads,
            value_heads,
            query_ids,
            key_ids,
            position,
            block_count,
            block_size,
        )
        scores = block_scores(query_block, key_row, query_seg, key_seg, row_start, causal)
        row_max = jnp.max(scores, axis=-1, keepdims=True)
        expo_scores = jnp.exp(scores - row_max)
        row_total = jnp.sum(expo_scores, axis=-1, keepdims=True)
        softmax_out = expo_scores / row_total
        attended = jnp.einsum(
            "hqk,khd->qhd",
            softmax_out.astype(jnp.bfloat16),
            value_row,
            preferred_element_type=jnp.float32,
        ).astype(jnp.bfloat16)
        return (attended, (row_max + jnp.log(row_total))[..., 0])

    attended_all, log_sums = lax.map(
        one_block, jnp.arange(query.shape[0] * block_count, dtype=jnp.int32)
    )
    return (attended_all.reshape(query.shape), log_sums)


def attend_backward(query, keys, values, grad_att, log_sums, query_ids, key_ids, causal):
    query_heads = split_heads(query)
    key_heads = split_heads(keys)
    value_heads = split_heads(values)
    grad_heads = split_heads(grad_att)
    block_size = min(BLOCK_ROWS, query.shape[1])
    block_count = query.shape[1] // block_size
    score_scale = float(HD) ** (-0.5)

    def one_block(carry, inputs):
        grad_keys, grad_values = carry
        position, log_sum = inputs
        row_index, row_start, query_block, key_row, value_row, query_seg, key_seg = block_inputs(
            query_heads,
            key_heads,
            value_heads,
            query_ids,
            key_ids,
            position,
            block_count,
            block_size,
        )
        grad_row = lax.dynamic_index_in_dim(grad_heads, row_index, 0, keepdims=False)
        grad_block = lax.dynamic_slice_in_dim(grad_row, row_start, block_size, 0)
        scores = block_scores(query_block, key_row, query_seg, key_seg, row_start, causal)
        softmax_out = jnp.exp(scores - log_sum[..., None])
        softmax_low = softmax_out.astype(jnp.bfloat16)
        attended = jnp.einsum(
            "hqk,khd->qhd", softmax_low, value_row, preferred_element_type=jnp.float32
        ).astype(jnp.bfloat16)
        grad_prob = jnp.einsum(
            "qhd,khd->hqk", grad_block, value_row, preferred_element_type=jnp.float32
        )
        correction = jnp.sum(softmax_out * grad_prob, axis=-1, keepdims=True)
        grad_score = (softmax_out * (grad_prob - correction)).astype(jnp.bfloat16)
        grad_query = (
            jnp.einsum("hqk,khd->qhd", grad_score, key_row, preferred_element_type=jnp.float32)
            * score_scale
        ).astype(jnp.bfloat16)
        key_added = (
            jnp.einsum("hqk,qhd->khd", grad_score, query_block, preferred_element_type=jnp.float32)
            * score_scale
        )
        value_added = jnp.einsum(
            "hqk,qhd->khd", softmax_low, grad_block, preferred_element_type=jnp.float32
        )
        grad_keys = grad_keys.at[row_index].add(key_added)
        grad_values = grad_values.at[row_index].add(value_added)
        return ((grad_keys, grad_values), (grad_query, attended))

    empty_grads = jnp.zeros(key_heads.shape, jnp.float32)
    positions = jnp.arange(query.shape[0] * block_count, dtype=jnp.int32)
    (grad_keys, grad_values), (grad_query, attended_all) = lax.scan(
        one_block, (empty_grads, empty_grads), (positions, log_sums)
    )
    return (
        grad_query.reshape(query.shape),
        grad_keys.reshape(keys.shape).astype(jnp.bfloat16),
        grad_values.reshape(values.shape).astype(jnp.bfloat16),
        attended_all.reshape(query.shape),
    )


def general_local(
    layer_input,
    memory,
    grad_out,
    target_segments,
    source_segments,
    self_gain,
    self_shift,
    query_weight,
    query_bias,
    key_weight,
    value_weight,
    value_bias,
    attend_weight,
    attend_bias,
    cross_gain,
    cross_shift,
    cross_query,
    cross_query_bias,
    cross_key,
    cross_value,
    cross_value_bias,
    cross_attend,
    cross_attend_bias,
    feed_gain,
    feed_shift,
    inner_weight,
    inner_bias,
    outer_weight,
    outer_bias,
):
    inputs = layer_input.astype(jnp.float32)
    rows_first = next_rows(inputs, self_gain, self_shift)
    query_first = (project(rows_first, query_weight) + query_bias).astype(jnp.bfloat16)
    keys_first = project(rows_first, key_weight).astype(jnp.bfloat16)
    values_first = (project(rows_first, value_weight) + value_bias).astype(jnp.bfloat16)
    attended_first, sums_first = attend_forward(
        query_first, keys_first, values_first, target_segments, target_segments, True
    )
    base_first = advance(inputs, project(attended_first, attend_weight), attend_bias)
    memory_rows = lax.all_gather(memory, "tensor", axis=1, tiled=True)
    rows_second = next_rows(base_first, cross_gain, cross_shift)
    query_second = (project(rows_second, cross_query) + cross_query_bias).astype(jnp.bfloat16)
    keys_second = project(memory_rows, cross_key).astype(jnp.bfloat16)
    values_second = (project(memory_rows, cross_value) + cross_value_bias).astype(jnp.bfloat16)
    attended_second, sums_second = attend_forward(
        query_second, keys_second, values_second, target_segments, source_segments, False
    )
    base_second = advance(base_first, project(attended_second, cross_attend), cross_attend_bias)
    rows_third = next_rows(base_second, feed_gain, feed_shift)
    pre_active = project(rows_third, inner_weight) + inner_bias
    active = jax.nn.silu(pre_active).astype(jnp.bfloat16)
    base_out = advance(base_second, project(active, outer_weight), outer_bias)
    block_out = base_out.astype(jnp.bfloat16)
    kept_input, kept_first, kept_second, kept_memory, kept_sums_first, kept_sums_second = (
        lax.optimization_barrier(
            (inputs, base_first, base_second, memory_rows, sums_first, sums_second)
        )
    )
    grad_top = grad_out.astype(jnp.float32)
    normed_low3, unit_third, inverse_third = general_norm_forward(kept_second, feed_gain, feed_shift)
    rows_back3 = backward_rows(normed_low3)
    pre_back = project(rows_back3, inner_weight) + inner_bias
    sigmoid_back = jax.nn.sigmoid(pre_back)
    active_back = (pre_back * sigmoid_back).astype(jnp.bfloat16)
    grad_rows3 = gather_grads(grad_top.astype(jnp.bfloat16))
    grad_outer_weight = outer_sum(active_back, grad_rows3)
    grad_outer_bias = jnp.sum(grad_top, axis=(0, 1))
    grad_active = project_back(grad_rows3, outer_weight)
    grad_inner = (grad_active * sigmoid_back * (1.0 + pre_back * (1.0 - sigmoid_back))).astype(
        jnp.bfloat16
    )
    grad_inner_weight = outer_sum(rows_back3, grad_inner)
    grad_inner_bias = bias_sum(grad_inner)
    grad_norm3 = reduce_inputs(project_back(grad_inner, inner_weight))
    grad_from3, grad_feed_gain, grad_feed_shift = general_norm_backward(
        grad_norm3, unit_third, inverse_third, feed_gain
    )
    grad_hidden2 = grad_top + grad_from3
    normed_low2, unit_second, inverse_second = general_norm_forward(kept_first, cross_gain, cross_shift)
    rows_back2 = backward_rows(normed_low2)
    query_back2 = (project(rows_back2, cross_query) + cross_query_bias).astype(jnp.bfloat16)
    keys_back2 = project(kept_memory, cross_key).astype(jnp.bfloat16)
    values_back2 = (project(kept_memory, cross_value) + cross_value_bias).astype(jnp.bfloat16)
    grad_rows2 = gather_grads(grad_hidden2.astype(jnp.bfloat16))
    grad_att2 = project_back(grad_rows2, cross_attend).astype(jnp.bfloat16)
    grad_query2, grad_keys2, grad_values2, attended_back2 = attend_backward(
        query_back2,
        keys_back2,
        values_back2,
        grad_att2,
        kept_sums_second,
        target_segments,
        source_segments,
        False,
    )
    grad_cross_attend = outer_sum(attended_back2, grad_rows2)
    grad_cross_attend_bias = jnp.sum(grad_hidden2, axis=(0, 1))
    grad_cross_query = outer_sum(rows_back2, grad_query2)
    grad_cross_query_bias = bias_sum(grad_query2)
    grad_cross_key = outer_sum(kept_memory, grad_keys2)
    grad_cross_value = outer_sum(kept_memory, grad_values2)
    grad_cross_value_bias = bias_sum(grad_values2)
    memory_grad = lax.psum_scatter(
        (project_back(grad_keys2, cross_key) + project_back(grad_values2, cross_value)).astype(
            jnp.bfloat16
        ),
        "tensor",
        scatter_dimension=1,
        tiled=True,
    ).astype(jnp.float32)
    grad_norm2 = reduce_inputs(project_back(grad_query2, cross_query))
    grad_from2, grad_cross_gain, grad_cross_shift = general_norm_backward(
        grad_norm2, unit_second, inverse_second, cross_gain
    )
    grad_hidden1 = grad_hidden2 + grad_from2
    normed_low1, unit_first, inverse_first = general_norm_forward(kept_input, self_gain, self_shift)
    rows_back1 = backward_rows(normed_low1)
    query_back1 = (project(rows_back1, query_weight) + query_bias).astype(jnp.bfloat16)
    keys_back1 = project(rows_back1, key_weight).astype(jnp.bfloat16)
    values_back1 = (project(rows_back1, value_weight) + value_bias).astype(jnp.bfloat16)
    grad_rows1 = gather_grads(grad_hidden1.astype(jnp.bfloat16))
    grad_att1 = project_back(grad_rows1, attend_weight).astype(jnp.bfloat16)
    grad_query1, grad_keys1, grad_values1, attended_back1 = attend_backward(
        query_back1,
        keys_back1,
        values_back1,
        grad_att1,
        kept_sums_first,
        target_segments,
        target_segments,
        True,
    )
    grad_attend_weight = outer_sum(attended_back1, grad_rows1)
    grad_attend_bias = jnp.sum(grad_hidden1, axis=(0, 1))
    grad_query_weight = outer_sum(rows_back1, grad_query1)
    grad_query_bias = bias_sum(grad_query1)
    grad_key_weight = outer_sum(rows_back1, grad_keys1)
    grad_value_weight = outer_sum(rows_back1, grad_values1)
    grad_value_bias = bias_sum(grad_values1)
    grad_norm1 = reduce_inputs(
        project_back(grad_query1, query_weight)
        + project_back(grad_keys1, key_weight)
        + project_back(grad_values1, value_weight)
    )
    grad_from1, grad_self_gain, grad_self_shift = general_norm_backward(
        grad_norm1, unit_first, inverse_first, self_gain
    )
    input_grad = grad_hidden1 + grad_from1
    (
        grad_query_weight,
        grad_query_bias,
        grad_key_weight,
        grad_value_weight,
        grad_value_bias,
        grad_attend_weight,
        grad_cross_query,
        grad_cross_query_bias,
        grad_cross_key,
        grad_cross_value,
        grad_cross_value_bias,
        grad_cross_attend,
        grad_inner_weight,
        grad_inner_bias,
        grad_outer_weight,
    ) = (
        lax.psum(grad_query_weight.astype(jnp.bfloat16), "dp").astype(jnp.float32),
        lax.psum(grad_query_bias.astype(jnp.bfloat16), "dp").astype(jnp.float32),
        lax.psum(grad_key_weight.astype(jnp.bfloat16), "dp").astype(jnp.float32),
        lax.psum(grad_value_weight.astype(jnp.bfloat16), "dp").astype(jnp.float32),
        lax.psum(grad_value_bias.astype(jnp.bfloat16), "dp").astype(jnp.float32),
        lax.psum(grad_attend_weight.astype(jnp.bfloat16), "dp").astype(jnp.float32),
        lax.psum(grad_cross_query.astype(jnp.bfloat16), "dp").astype(jnp.float32),
        lax.psum(grad_cross_query_bias.astype(jnp.bfloat16), "dp").astype(jnp.float32),
        lax.psum(grad_cross_key.astype(jnp.bfloat16), "dp").astype(jnp.float32),
        lax.psum(grad_cross_value.astype(jnp.bfloat16), "dp").astype(jnp.float32),
        lax.psum(grad_cross_value_bias.astype(jnp.bfloat16), "dp").astype(jnp.float32),
        lax.psum(grad_cross_attend.astype(jnp.bfloat16), "dp").astype(jnp.float32),
        lax.psum(grad_inner_weight.astype(jnp.bfloat16), "dp").astype(jnp.float32),
        lax.psum(grad_inner_bias.astype(jnp.bfloat16), "dp").astype(jnp.float32),
        lax.psum(grad_outer_weight.astype(jnp.bfloat16), "dp").astype(jnp.float32),
    )
    (
        grad_self_gain,
        grad_self_shift,
        grad_attend_bias,
        grad_cross_gain,
        grad_cross_shift,
        grad_cross_attend_bias,
        grad_feed_gain,
        grad_feed_shift,
        grad_outer_bias,
    ) = lax.psum(
        (
            grad_self_gain,
            grad_self_shift,
            grad_attend_bias,
            grad_cross_gain,
            grad_cross_shift,
            grad_cross_attend_bias,
            grad_feed_gain,
            grad_feed_shift,
            grad_outer_bias,
        ),
        ("dp", "tensor"),
    )
    return (
        block_out,
        input_grad,
        memory_grad,
        grad_self_gain,
        grad_self_shift,
        grad_query_weight,
        grad_query_bias,
        grad_key_weight,
        grad_value_weight,
        grad_value_bias,
        grad_attend_weight,
        grad_attend_bias,
        grad_cross_gain,
        grad_cross_shift,
        grad_cross_query,
        grad_cross_query_bias,
        grad_cross_key,
        grad_cross_value,
        grad_cross_value_bias,
        grad_cross_attend,
        grad_cross_attend_bias,
        grad_feed_gain,
        grad_feed_shift,
        grad_inner_weight,
        grad_inner_bias,
        grad_outer_weight,
        grad_outer_bias,
    )


def general_solution(mesh):
    placed = (
        P("dp", "tensor", None),
        P("dp", "tensor", None),
        P("dp", "tensor", None),
        P("dp", None),
        P("dp", None),
        P(),
        P(),
        P(None, "tensor"),
        P("tensor"),
        P(None, "tensor"),
        P(None, "tensor"),
        P("tensor"),
        P("tensor", None),
        P(),
        P(),
        P(),
        P(None, "tensor"),
        P("tensor"),
        P(None, "tensor"),
        P(None, "tensor"),
        P("tensor"),
        P("tensor", None),
        P(),
        P(),
        P(),
        P(None, "tensor"),
        P("tensor"),
        P("tensor", None),
        P(),
    )
    return jax.shard_map(
        general_local,
        mesh=mesh,
        in_specs=placed,
        out_specs=(
            P("dp", "tensor", None),
            P("dp", "tensor", None),
            P("dp", "tensor", None),
            P(),
            P(),
            P(None, "tensor"),
            P("tensor"),
            P(None, "tensor"),
            P(None, "tensor"),
            P("tensor"),
            P("tensor", None),
            P(),
            P(),
            P(),
            P(None, "tensor"),
            P("tensor"),
            P(None, "tensor"),
            P(None, "tensor"),
            P("tensor"),
            P("tensor", None),
            P(),
            P(),
            P(),
            P(None, "tensor"),
            P("tensor"),
            P("tensor", None),
            P(),
        ),
        check_vma=False,
    )
```

```python
import jax
import jax.numpy as jnp
from jax import lax
from jax.experimental import pallas as pl
from jax.experimental.pallas import tpu as pltpu
from jax.sharding import PartitionSpec as P

HD = 64
MASKED = -1000000000.0
QUERIES = 128
KEYS = 256
NT = (((1,), (1,)), ((), ()))
TN = (((0,), (0,)), ((), ()))
NN = (((1,), (0,)), ((), ()))


def dot(a, b, dims):
    return lax.dot_general(a, b, dims, preferred_element_type=jnp.float32)


def both_heads(block):
    first = lax.broadcasted_iota(jnp.int32, block.shape, 1) < HD
    zero = jnp.zeros_like(block)
    return jnp.concatenate([jnp.where(first, block, zero), jnp.where(first, zero, block)], axis=0)


def key_span(bounds, place, count, step):
    start = bounds[0, place] + step * KEYS
    at = pl.multiple_of(jnp.minimum(start, count - KEYS), 16)
    return start, at


def allowed_keys(low_ref, high_ref, start, at):
    key_place = at + lax.broadcasted_iota(jnp.int32, (KEYS, 1), 0)
    least = jnp.maximum(low_ref[...], start)
    seen = (key_place >= least) & (key_place < high_ref[...])
    return jnp.concatenate([seen, seen], axis=1)


def attend_kernel(bounds, low_ref, high_ref, q_ref, k_ref, v_ref, out_ref, sums_ref, acc, top, total):
    pairs = q_ref.shape[1] // 128
    count = k_ref.shape[0]
    place = pl.program_id(0)
    acc[...] = jnp.zeros_like(acc)
    total[...] = jnp.zeros_like(total)
    top[...] = jnp.full_like(top, -1e30)
    queries = [both_heads(q_ref[:, p * 128:(p + 1) * 128] * jnp.bfloat16(HD ** -0.5)) for p in range(pairs)]

    def step(j, _):
        start, at = key_span(bounds, place, count, j)
        seen = allowed_keys(low_ref, high_ref, start, at)
        for p in range(pairs):
            keys = k_ref[pl.ds(at, KEYS), p * 128:(p + 1) * 128]
            values = v_ref[pl.ds(at, KEYS), p * 128:(p + 1) * 128]
            scores = jnp.where(seen, dot(keys, queries[p], NT), MASKED)
            before = top[p:p + 1]
            now = jnp.maximum(before, jnp.max(scores, axis=0, keepdims=True))
            weight = jnp.exp(scores - now)
            keep = jnp.exp(before - now)
            top[p:p + 1] = now
            total[p:p + 1] = total[p:p + 1] * keep + jnp.sum(weight, axis=0, keepdims=True)
            acc[p] = acc[p] * keep + dot(values, weight.astype(jnp.bfloat16), TN)
        return 0

    lax.fori_loop(0, bounds[1, place], step, 0)
    for p in range(pairs):
        sums = total[p:p + 1]
        mixed = acc[p] / sums
        joined = jnp.concatenate([mixed[:HD, :QUERIES], mixed[HD:, QUERIES:]], axis=0)
        out_ref[:, p * 128:(p + 1) * 128] = joined.T.astype(jnp.bfloat16)
        sums_ref[p:p + 1] = top[p:p + 1] + jnp.log(sums)


def attend(q, q_at, kv, k_at, bounds, low, high):
    count, width = q.shape[0], 512
    source = kv.shape[0]
    pairs = width // 128
    return pl.pallas_call(
        attend_kernel,
        grid_spec=pltpu.PrefetchScalarGridSpec(
            num_scalar_prefetch=1,
            grid=(count // QUERIES,),
            in_specs=[
                pl.BlockSpec((1, QUERIES), lambda i, b: (0, i)),
                pl.BlockSpec((1, QUERIES), lambda i, b: (0, i)),
                pl.BlockSpec((QUERIES, width), lambda i, b: (i, q_at)),
                pl.BlockSpec((source, width), lambda i, b: (0, k_at)),
                pl.BlockSpec((source, width), lambda i, b: (0, k_at + 1)),
            ],
            out_specs=[
                pl.BlockSpec((QUERIES, width), lambda i, b: (i, 0)),
                pl.BlockSpec((None, pairs, 2 * QUERIES), lambda i, b: (i, 0, 0)),
            ],
            scratch_shapes=[
                pltpu.VMEM((pairs, 128, 2 * QUERIES), jnp.float32),
                pltpu.VMEM((pairs, 2 * QUERIES), jnp.float32),
                pltpu.VMEM((pairs, 2 * QUERIES), jnp.float32),
            ],
        ),
        out_shape=[
            jax.ShapeDtypeStruct((count, width), jnp.bfloat16),
            jax.ShapeDtypeStruct((count // QUERIES, pairs, 2 * QUERIES), jnp.float32),
        ],
        compiler_params=pltpu.CompilerParams(vmem_limit_bytes=32 << 20),
        cost_estimate=pl.CostEstimate(flops=4 * count * 400 * width, bytes_accessed=8 * count * width, transcendentals=0),
        name="attend",
    )(bounds, low, high, q, kv, kv)


def attend_back_kernel(
    bounds, low_ref, high_ref, q_ref, grad_ref, out_ref, sums_ref, k_ref, v_ref,
    dq_ref, dk_ref, dv_ref, acc, acc_k, acc_v,
):
    pairs = q_ref.shape[1] // 128
    count = k_ref.shape[0]
    place = pl.program_id(0)

    @pl.when(place == 0)
    def _():
        acc_k[...] = jnp.zeros_like(acc_k)
        acc_v[...] = jnp.zeros_like(acc_v)

    acc[...] = jnp.zeros_like(acc)
    queries, grads, fixes = [], [], []
    ones = jnp.ones((8, 128), jnp.bfloat16)
    for p in range(pairs):
        cut = slice(p * 128, (p + 1) * 128)
        queries.append(both_heads(q_ref[:, cut] * jnp.bfloat16(HD ** -0.5)))
        grad = both_heads(grad_ref[:, cut])
        grads.append(grad)
        out = out_ref[:, cut].astype(jnp.float32)
        product = grad.astype(jnp.float32) * jnp.concatenate([out, out], axis=0)
        coarse = product.astype(jnp.bfloat16)
        fine = (product - coarse.astype(jnp.float32)).astype(jnp.bfloat16)
        fixes.append((dot(ones, coarse, NT) + dot(ones, fine, NT))[:1])

    def step(j, _):
        start, at = key_span(bounds, place, count, j)
        seen = allowed_keys(low_ref, high_ref, start, at)
        rows = pl.ds(at, KEYS)
        for p in range(pairs):
            cut = slice(p * 128, (p + 1) * 128)
            keys = k_ref[rows, cut]
            values = v_ref[rows, cut]
            scores = dot(keys, queries[p], NT)
            prob = jnp.exp(jnp.where(seen, scores - sums_ref[p:p + 1], MASKED))
            dprob = dot(values, grads[p], NT)
            dscore = (prob * (dprob - fixes[p])).astype(jnp.bfloat16)
            acc_v[rows, cut] += dot(prob.astype(jnp.bfloat16), grads[p], NN)
            acc_k[rows, cut] += dot(dscore, queries[p], NN)
            acc[p] += dot(keys, dscore, TN)
        return 0

    lax.fori_loop(0, bounds[1, place], step, 0)
    for p in range(pairs):
        mixed = acc[p] * (HD ** -0.5)
        joined = jnp.concatenate([mixed[:HD, :QUERIES], mixed[HD:, QUERIES:]], axis=0)
        dq_ref[:, p * 128:(p + 1) * 128] = joined.T.astype(jnp.bfloat16)

    @pl.when(place == pl.num_programs(0) - 1)
    def _():
        dk_ref[...] = acc_k[...].astype(jnp.bfloat16)
        dv_ref[...] = acc_v[...].astype(jnp.bfloat16)


def attend_back(q, q_at, kv, k_at, grad, out, sums, bounds, low, high):
    count, width = grad.shape
    source = kv.shape[0]
    pairs = width // 128
    whole = lambda i, b: (0, 0)
    rows = lambda i, b: (i, 0)
    return pl.pallas_call(
        attend_back_kernel,
        grid_spec=pltpu.PrefetchScalarGridSpec(
            num_scalar_prefetch=1,
            grid=(count // QUERIES,),
            in_specs=[
                pl.BlockSpec((1, QUERIES), lambda i, b: (0, i)),
                pl.BlockSpec((1, QUERIES), lambda i, b: (0, i)),
                pl.BlockSpec((QUERIES, width), lambda i, b: (i, q_at)),
                pl.BlockSpec((QUERIES, width), rows),
                pl.BlockSpec((QUERIES, width), rows),
                pl.BlockSpec((None, pairs, 2 * QUERIES), lambda i, b: (i, 0, 0)),
                pl.BlockSpec((source, width), lambda i, b: (0, k_at)),
                pl.BlockSpec((source, width), lambda i, b: (0, k_at + 1)),
            ],
            out_specs=[
                pl.BlockSpec((QUERIES, width), rows),
                pl.BlockSpec((source, width), whole),
                pl.BlockSpec((source, width), whole),
            ],
            scratch_shapes=[
                pltpu.VMEM((pairs, 128, 2 * QUERIES), jnp.float32),
                pltpu.VMEM((source, width), jnp.float32),
                pltpu.VMEM((source, width), jnp.float32),
            ],
        ),
        out_shape=[
            jax.ShapeDtypeStruct((count, width), jnp.bfloat16),
            jax.ShapeDtypeStruct((source, width), jnp.bfloat16),
            jax.ShapeDtypeStruct((source, width), jnp.bfloat16),
        ],
        compiler_params=pltpu.CompilerParams(vmem_limit_bytes=40 << 20),
        cost_estimate=pl.CostEstimate(flops=10 * count * 400 * width, bytes_accessed=16 * count * width, transcendentals=0),
        name="attend_back",
    )(bounds, low, high, q, grad, out, sums, kv, kv)


def reach(query_ids, key_ids, causal):
    count = query_ids.shape[0]
    low = jnp.sum((key_ids[None, :] < query_ids[:, None]).astype(jnp.int32), axis=1)
    if causal:
        high = jnp.arange(count, dtype=jnp.int32) + 1
    else:
        high = jnp.sum((key_ids[None, :] <= query_ids[:, None]).astype(jnp.int32), axis=1)
    first = low[::QUERIES] // 16 * 16
    steps = (high[QUERIES - 1::QUERIES] - first + KEYS - 1) // KEYS
    return jnp.stack([first, steps]), low[None], high[None]


EPSILON = 1e-05
BF = jnp.bfloat16
F32 = jnp.float32


class Links:
    def __init__(self, mesh):
        self.dp = mesh.shape["dp"]
        self.tensor = mesh.shape["tensor"]
        self.planes = self.dp // 2

    def enter(self):
        place = lax.axis_index("dp")
        self.core = place % 2
        self.plane = place // 2
        self.chip = lax.axis_index("tensor")

    def move(self, value, target):
        pairs = []
        for place in range(self.dp):
            for chip in range(self.tensor):
                to = target(place // 2, place % 2, chip)
                if to is not None:
                    pairs.append((place * self.tensor + chip, (to[0] * 2 + to[1]) * self.tensor + to[2]))
        return lax.ppermute(value, ("dp", "tensor"), pairs)

    def other_core(self, value):
        return self.move(value, lambda plane, core, chip: (plane, 1 - core, chip))

    def across(self, value, step):
        return self.move(value, lambda plane, core, chip: (plane, core, chip ^ step))

    def plane_pair(self, value, step):
        return self.move(value, lambda plane, core, chip: (plane ^ step, core, chip))

    def slot(self, value, which):
        def target(plane, core, chip):
            step = 3 if which == 3 else which if plane % 2 == 0 else 3 - which
            return (plane, core, chip ^ step)

        return self.move(value, target)

    def gather_weight(self, own):
        first = self.slot(own, 1)
        diagonal = self.slot(first, 2)
        second = self.plane_pair(first, 1)
        return [own, first, second, diagonal]

    def plane_sum(self, parts, first):
        second = 3 - first
        near = self.slot(parts[first], first)
        passed = self.slot(parts[3], first)
        middle = (parts[second].astype(F32) + passed.astype(F32)).astype(BF)
        far = self.slot(middle, second)
        return parts[0].astype(F32) + near.astype(F32) + far.astype(F32)

    def line_sum(self, total):
        if self.planes % 4:
            low = total.astype(BF)
            step = 1
            while step < self.planes:
                low = (low.astype(F32) + self.plane_pair(low, step).astype(F32)).astype(BF)
                step *= 2
            return low
        inward = {0: 1, 3: 2}
        outward = {1: 0, 2: 3}
        middle = {1: 2, 2: 1}

        def along(table):
            def target(plane, core, chip):
                to = table.get(plane % 4)
                return None if to is None else (plane - plane % 4 + to, core, chip)

            return target

        low = (total + self.move(total.astype(BF), along(inward)).astype(F32)).astype(BF)
        low = (low.astype(F32) + self.move(low, along(middle)).astype(F32)).astype(BF)
        step = 4
        while step < self.planes:
            low = (low.astype(F32) + self.plane_pair(low, step).astype(F32)).astype(BF)
            step *= 2
        back = self.move(low, along(outward))
        inner = (self.plane % 4 == 1) | (self.plane % 4 == 2)
        return jnp.where(inner, low, back)

    def weight_total(self, parts, first):
        return self.line_sum(self.plane_sum(parts, first))

    def halves(self, mine, axis):
        theirs = self.other_core(mine)
        return jnp.where(
            self.core == 0,
            jnp.concatenate([mine, theirs], axis=axis),
            jnp.concatenate([theirs, mine], axis=axis),
        )

    def take_half(self, value, axis, which):
        size = value.shape[axis] // 2
        return lax.dynamic_slice_in_dim(value, which * size, size, axis)

    def swap_parts(self, parts):
        got = [lax.dynamic_index_in_dim(parts, self.chip, 0, keepdims=False)]
        for step in range(1, self.tensor):
            got.append(self.across(lax.dynamic_index_in_dim(parts, self.chip ^ step, 0, keepdims=False), step))
        got = jnp.stack(got)
        return jnp.stack(
            [lax.dynamic_index_in_dim(got, self.chip ^ at, 0, keepdims=False) for at in range(self.tensor)]
        )

    def to_row(self, value):
        keep = self.take_half(value, 1, self.core)
        theirs = self.other_core(self.take_half(value, 1, 1 - self.core))
        rows = jnp.where(self.core == 0, jnp.concatenate([keep, theirs]), jnp.concatenate([theirs, keep]))
        mine = self.swap_parts(rows)
        both = self.halves(mine[:, None], 1)
        return both.reshape(-1, value.shape[-1])

    def half_row(self, row):
        cut = row.reshape(self.tensor, 2, -1, row.shape[-1])
        return lax.dynamic_index_in_dim(cut, self.core, 1, keepdims=False)

    def other_half_row(self, row):
        cut = row.reshape(self.tensor, 2, -1, row.shape[-1])
        return lax.dynamic_index_in_dim(cut, 1 - self.core, 1, keepdims=False)

    def from_row(self, mine):
        rows = self.swap_parts(mine)
        keep = self.take_half(rows, 0, self.core)
        theirs = self.other_core(self.take_half(rows, 0, 1 - self.core))
        return jnp.where(
            self.core == 0,
            jnp.concatenate([keep, theirs], axis=1),
            jnp.concatenate([theirs, keep], axis=1),
        )

    def pair_sum(self, partial):
        low = lax.optimization_barrier(partial.astype(BF))
        return low.astype(F32) + self.other_core(low).astype(F32)

    def pair_sum_half(self, partial):
        low = lax.optimization_barrier(partial.astype(BF))
        return self.half_row(low).astype(F32) + self.other_core(self.other_half_row(low)).astype(F32)

    def chip_sum(self, value):
        for step in (1, 2):
            value = value + self.across(value, step)
        step = 1
        while step < self.planes:
            value = value + self.plane_pair(value, step)
            step *= 2
        return value

    def quarter_sum(self, parts):
        total = parts[0]
        for which in (1, 2, 3):
            total = total + self.slot(parts[which], which)
        step = 1
        while step < self.planes:
            total = total + self.plane_pair(total, step)
            step *= 2
        return total


def norm_stats(values):
    average = jnp.mean(values, axis=-1, keepdims=True)
    center = values - average
    inverse = lax.rsqrt(jnp.mean(center * center, axis=-1, keepdims=True) + EPSILON)
    return center * inverse, inverse


def norm_forward(values, gain, shift):
    unit, _ = norm_stats(values)
    return (unit * gain + shift).astype(BF)


def norm_backward(grad_in, values, gain):
    unit, inverse = norm_stats(values)
    scaled = grad_in * gain
    first_mean = jnp.mean(scaled, axis=-1, keepdims=True)
    second_mean = jnp.mean(scaled * unit, axis=-1, keepdims=True)
    grad_values = inverse * (scaled - first_mean - unit * second_mean)
    return grad_values, jnp.sum(grad_in * unit, axis=0), jnp.sum(grad_in, axis=0)


def cat(parts, axis):
    return jnp.concatenate(parts, axis=axis)


def cut_slots(value, axis):
    return jnp.split(value, 4, axis=axis)


class Net:
    def __init__(self, sems, local_sems):
        place = lax.axis_index("dp")
        chip = lax.axis_index("tensor")
        core, plane = place % 2, place // 2
        odd = plane % 2
        beside, over, corner = chip + 1 - 2 * (chip % 2), (chip + 2) % 4, 3 - chip
        self.chip, self.core_index, self.odd, self.plane = chip, core, odd, plane
        self.chips = (beside, over, corner)
        self.core = (plane * 2 + 1 - core, chip)
        self.first = (place, beside + odd * (over - beside))
        self.second = (place, over + odd * (beside - over))
        self.corner = (place, corner)
        self.near_plane = ((plane + 1 - 2 * odd) * 2 + core, chip)
        self.far_plane = ((plane + 2) % 4 * 2 + core, chip)
        self.sems, self.local_sems = sems, local_sems
        self.count = self.local_count = 0
        self.unsent, self.unmoved = [], []

    def meet(self):
        barrier = pltpu.get_barrier_semaphore()
        partners = (self.core, self.first, self.second, self.corner, self.near_plane, self.far_plane)
        for partner in partners:
            pl.semaphore_signal(barrier, inc=1, device_id=partner, device_id_type=pl.DeviceIdType.MESH)
        pl.semaphore_wait(barrier, len(partners))

    def send(self, source, target, device):
        copy = pltpu.make_async_remote_copy(
            src_ref=source,
            dst_ref=target,
            send_sem=self.sems.at[0, self.count],
            recv_sem=self.sems.at[1, self.count],
            device_id=device,
            device_id_type=pl.DeviceIdType.MESH,
        )
        self.count += 1
        copy.start()
        self.unsent.append(copy)
        return copy

    def move(self, source, target):
        copy = pltpu.make_async_copy(source, target, self.local_sems.at[self.local_count])
        self.local_count += 1
        copy.start()
        self.unmoved.append(copy)
        return copy

    def moved(self, copy):
        copy.wait()
        self.unmoved = [other for other in self.unmoved if other is not copy]

    def sent(self, copy):
        copy.wait_send()
        self.unsent = [other for other in self.unsent if other is not copy]

    def finish(self):
        for copy in self.unmoved:
            copy.wait()
        for copy in self.unsent:
            copy.wait_send()
        self.unsent, self.unmoved = [], []


def row_in(net, given, rows, row):
    core, chip = net.core_index, net.chip
    mine = pl.ds(2 * core, 2)
    swap = net.send(given.at[:, 1 - core], rows.at[mine], net.core)
    keep = net.move(given.at[:, core], rows.at[mine])
    yield
    net.moved(keep)
    swap.wait_recv()
    own = net.move(rows.at[chip], row.at[chip, core])
    sends = [
        net.send(rows.at[other], row.at[chip, core], (lax.axis_index("dp"), other)) for other in net.chips
    ]
    yield
    net.moved(own)
    shares = [net.send(row.at[chip, core], row.at[chip, core], net.core)]
    for other, copy in zip(net.chips, sends):
        copy.wait_recv()
        shares.append(net.send(row.at[other, core], row.at[other, core], net.core))
    yield
    for copy in shares:
        copy.wait_recv()


def row_out(net, pieces, rows, result):
    core, chip = net.core_index, net.chip
    own = net.move(pieces.at[chip], rows.at[chip])
    sends = [net.send(pieces.at[other], rows.at[chip], (lax.axis_index("dp"), other)) for other in net.chips]
    yield
    net.moved(own)
    for copy in sends:
        copy.wait_recv()
    keep = net.move(rows.at[pl.ds(2 * core, 2)], result.at[:, core])
    swap = net.send(rows.at[pl.ds(2 * (1 - core), 2)], result.at[:, core], net.core)
    yield
    swap.wait_recv()
    net.moved(keep)


class Gather:
    def __init__(self, net, own, slot):
        self.net, self.slot = net, slot
        self.near = net.send(own, slot(1), net.first)
        self.own = net.move(own, slot(0))

    def relay(self):
        self.near.wait_recv()
        self.corner = self.net.send(self.slot(1), self.slot(3), self.net.second)
        self.other = self.net.send(self.slot(1), self.slot(2), self.net.near_plane)

    def finish(self):
        self.net.moved(self.own)
        self.corner.wait_recv()
        self.other.wait_recv()


ANY = pl.BlockSpec(memory_space=pl.ANY)
VM = pl.BlockSpec(memory_space=pltpu.VMEM)
SENDS = 96


def half_columns(net, weight, width):
    return weight.at[:, pl.ds(pl.multiple_of(net.core_index * width, width), width)]


def half_rows(net, weight, height):
    return weight.at[pl.ds(pl.multiple_of(net.core_index * height, height), height)]


def tile_rows(i, size=256):
    return pl.ds(pl.multiple_of(i * size, size), size)


def call_remote(kernel, ident, ins, in_specs, outs, out_specs, scratch, vmem=48, name=None):
    return pl.pallas_call(
        kernel,
        in_specs=in_specs,
        out_specs=out_specs,
        out_shape=outs,
        scratch_shapes=list(scratch) + [pltpu.SemaphoreType.DMA((2, SENDS)), pltpu.SemaphoreType.DMA((SENDS,))],
        compiler_params=pltpu.CompilerParams(
            collective_id=ident, has_side_effects=True, vmem_limit_bytes=vmem << 20
        ),
        name=name,
    )(*ins)


def begin_kernel(
    given, ids, bias, wq, wk, wv, wo, gain, shift,
    x_out, n_out, qkv_out, w_out, wo_out, ids_out, bias_out,
    rows, row, weights, normed, qkv, biases, sems, local_sems,
):
    net = Net(sems, local_sems)
    net.meet()
    core = net.core_index
    enter = row_in(net, given, rows, row)
    next(enter)
    ids_swap = net.send(ids, ids_out.at[pl.ds(2 * core, 2)], net.core)
    net.move(ids, ids_out.at[pl.ds(2 * core, 2)])
    bias_copies = [
        net.send(bias, biases.at[1], net.first),
        net.send(bias, biases.at[2], net.second),
        net.send(bias, biases.at[3], net.corner),
    ]
    bias_own = net.move(bias, biases.at[0])
    gathers = []
    for kind, weight in enumerate((wq, wk, wv)):
        slot = lambda s, kind=kind: weights.at[:, kind * 512 + s * 128:kind * 512 + s * 128 + 128]
        gathers.append(Gather(net, half_columns(net, weight, 128), slot))
    next(enter)
    gather_o = Gather(net, half_rows(net, wo, 128), lambda s: wo_out.at[pl.ds(s * 128, 128)])
    for gather in gathers:
        gather.relay()
    next(enter)
    gather_o.relay()
    for _ in enter:
        pass
    net.move(row, x_out)

    def norm(i, _):
        values = row[i].reshape(256, -1).astype(F32)
        normed[tile_rows(i)] = norm_forward(values, gain[...], shift[...])
        return 0

    lax.fori_loop(0, 4, norm, 0)
    net.move(normed, n_out)
    net.moved(bias_own)
    for copy in bias_copies:
        copy.wait_recv()
    net.move(biases, bias_out)
    for gather in gathers:
        gather.finish()
    net.move(weights, w_out)

    def project(i, _):
        tokens = normed[tile_rows(i)]
        for kind in range(3):
            cut = slice(kind * 512, kind * 512 + 512)
            value = dot(tokens, weights[:, cut], NN)
            if kind != 1:
                at = 0 if kind == 0 else 1
                value = value + jnp.concatenate([biases[s, at:at + 1] for s in range(4)], axis=1)
            qkv[tile_rows(i), cut] = value.astype(BF)
        return 0

    lax.fori_loop(0, 4, project, 0)
    net.move(qkv, qkv_out)
    gather_o.finish()
    ids_swap.wait_recv()
    net.finish()


def begin(given, ids, bias, wq, wk, wv, wo, gain, shift):
    length, width = 1024, given.shape[-1]
    shape = jax.ShapeDtypeStruct
    return call_remote(
        begin_kernel, 1,
        (given.reshape(2, 2, -1, width), ids, bias, wq, wk, wv, wo, gain[None], shift[None]),
        [ANY] * 7 + [VM] * 2,
        [
            shape((4, 2, 128, width), BF), shape((length, width), BF), shape((length, 1536), BF),
            shape((width, 1536), BF), shape((512, width), BF), shape((4, 16, 128), jnp.int32), shape((4, 8, 128), F32),
        ],
        [ANY] * 7,
        [
            pltpu.VMEM((4, 128, width), BF), pltpu.VMEM((4, 2, 128, width), BF), pltpu.VMEM((width, 1536), BF),
            pltpu.VMEM((length, width), BF), pltpu.VMEM((length, 1536), BF), pltpu.VMEM((4, 8, 128), F32),
        ],
        name="begin",
    )


def middle_kernel(
    att, x, wo, bias_o, gain, shift, given, wcq, wck, wcv, wco, bias_in,
    h_out, n_out, q_out, kv_out, mem_out, w_out, wco_out,
    att_vm, x_vm, wo_vm, part, part_in, hidden, normed, rows, row, weights, queries, keys, biases, sems, local_sems,
):
    net = Net(sems, local_sems)
    loads = [net.move(att, att_vm), net.move(wo, wo_vm), net.move(x, x_vm), net.move(bias_in, biases)]
    net.meet()
    enter = row_in(net, given, rows, row)
    next(enter)
    gathers = []
    for kind, weight in ((1, wck), (2, wcv), (0, wcq)):
        slot = lambda s, kind=kind: weights.at[:, kind * 512 + s * 128:kind * 512 + s * 128 + 128]
        gathers.append(Gather(net, half_columns(net, weight, 128), slot))
    gathers.append(Gather(net, half_rows(net, wco, 128), lambda s: wco_out.at[pl.ds(s * 128, 128)]))
    for copy in loads:
        net.moved(copy)
    swaps = []
    for i in range(4):
        part[i] = dot(att_vm[i * 256:i * 256 + 256], wo_vm[...], NN).astype(BF)
        swaps.append(net.send(part.at[i], part_in.at[i], net.core))
        if i == 1:
            next(enter)
    for i in range(4):
        swaps[i].wait_recv()
        rows_i = slice(i * 256, i * 256 + 256)
        value = x_vm[i].reshape(256, -1).astype(F32) + part[i].astype(F32) + part_in[i].astype(F32) + bias_o[...]
        hidden[rows_i] = value
        normed[rows_i] = norm_forward(value, gain[...], shift[...])
        if i == 1:
            gathers[0].relay()
            gathers[1].relay()
    net.move(hidden, h_out)
    net.move(normed, n_out)
    next(enter)
    gathers[2].relay()
    gathers[3].relay()
    for _ in enter:
        pass
    net.move(row, mem_out)
    for gather in gathers[:3]:
        gather.finish()
    net.move(weights, w_out)
    values_bias = jnp.concatenate([biases[s, 3:4] for s in range(4)], axis=1)
    query_bias = jnp.concatenate([biases[s, 2:3] for s in range(4)], axis=1)

    def project(i, _):
        tokens = row[i].reshape(256, -1)
        keys[tile_rows(i), :512] = dot(tokens, weights[:, 512:1024], NN).astype(BF)
        keys[tile_rows(i), 512:] = (dot(tokens, weights[:, 1024:], NN) + values_bias).astype(BF)
        queries[tile_rows(i)] = (dot(normed[tile_rows(i)], weights[:, :512], NN) + query_bias).astype(BF)
        return 0

    lax.fori_loop(0, 4, project, 0)
    net.move(keys, kv_out)
    net.move(queries, q_out)
    gathers[3].finish()
    net.finish()


def middle(att, x, wo, bias_o, gain, shift, given, wcq, wck, wcv, wco, bias_in):
    length, width = att.shape[0], given.shape[-1]
    shape = jax.ShapeDtypeStruct
    return call_remote(
        middle_kernel, 2,
        (att, x, wo, bias_o[None], gain[None], shift[None], given.reshape(2, 2, -1, width), wcq, wck, wcv, wco, bias_in),
        [ANY] * 3 + [VM] * 3 + [ANY] * 6,
        [
            shape((length, width), F32), shape((length, width), BF), shape((length, 512), BF),
            shape((length, 1024), BF), shape((4, 2, 128, width), BF), shape((width, 1536), BF), shape((512, width), BF),
        ],
        [ANY] * 7,
        [
            pltpu.VMEM((length, 512), BF), pltpu.VMEM((4, 2, 128, width), BF), pltpu.VMEM((512, width), BF),
            pltpu.VMEM((4, 256, width), BF), pltpu.VMEM((4, 256, width), BF), pltpu.VMEM((length, width), F32),
            pltpu.VMEM((length, width), BF), pltpu.VMEM((4, 128, width), BF), pltpu.VMEM((4, 2, 128, width), BF),
            pltpu.VMEM((width, 1536), BF), pltpu.VMEM((length, 512), BF), pltpu.VMEM((length, 1024), BF),
            pltpu.VMEM((4, 8, 128), F32),
        ],
        name="middle",
    )


def add_up(target, sources, step=64):
    def some(i, _):
        cut = pl.ds(pl.multiple_of(i * step, step), step)
        total = sources[0][cut].astype(F32)
        for source in sources[1:]:
            total = total + source[cut].astype(F32)
        target[cut] = total.astype(BF)
        return 0

    lax.fori_loop(0, target.shape[0] // step, some, 0)


class Scatter:
    def __init__(self, net, part, first, landing, result):
        self.net, self.part, self.result = net, part, result
        self.near_in, self.pass_in, self.far_in, self.one_in, self.two_in = landing
        self.one, self.two = (1, 2) if first == 1 else (2, 1)
        self.to_one, self.to_two = (net.first, net.second) if first == 1 else (net.second, net.first)
        self.size = self.one_in.shape[0]

    def half(self, ref, which):
        return ref.at[pl.ds(pl.multiple_of(which * self.size, self.size), self.size)]

    def start(self):
        self.passed = self.net.send(self.part(3), self.pass_in, self.to_one)
        self.near = self.net.send(self.part(self.one), self.near_in, self.to_one)

    def middle(self):
        self.passed.wait_recv()
        add_up(self.part(self.two), [self.part(self.two), self.pass_in])
        self.far = self.net.send(self.part(self.two), self.far_in, self.to_two)

    def own(self):
        self.near.wait_recv()
        self.far.wait_recv()
        add_up(self.part(0), [self.part(0), self.near_in, self.far_in])
        self.line = self.net.send(self.half(self.part(0), 1 - self.net.odd), self.one_in, self.net.near_plane)

    def line1(self):
        self.line.wait_recv()
        mine = self.half(self.part(0), self.net.odd)
        add_up(mine, [mine, self.one_in])
        self.line = self.net.send(mine, self.two_in, self.net.far_plane)

    def line2(self):
        self.line.wait_recv()
        mine = self.half(self.part(0), self.net.odd)
        place = self.result(self.net.core_index, self.net.odd)
        add_up(place, [mine, self.two_in])
        self.line = self.net.send(place, place, self.net.near_plane)
        self.cores = [self.net.send(place, place, self.net.core)]

    def line3(self):
        self.line.wait_recv()
        place = self.result(self.net.core_index, 1 - self.net.odd)
        self.cores.append(self.net.send(place, place, self.net.core))

    def end(self):
        for copy in self.cores:
            copy.wait_recv()


def landing(rows, columns):
    return [pltpu.VMEM((rows, columns), BF)] * 3 + [pltpu.VMEM((rows // 2, columns), BF)] * 2


def weight_grad(lhs, rhs, target, start, count, columns=slice(None), size=256):
    def some(i, _):
        cut = pl.ds(pl.multiple_of(start + i * size, size), size)
        target[cut, columns] = dot(lhs[:, cut], rhs(), TN).astype(BF)
        return 0

    lax.fori_loop(0, count // size, some, 0)


def norm_back_tile(grad_in, values, gain):
    unit, inverse = norm_stats(values)
    scaled = grad_in * gain
    first_mean = jnp.mean(scaled, axis=-1, keepdims=True)
    second_mean = jnp.mean(scaled * unit, axis=-1, keepdims=True)
    grad_values = inverse * (scaled - first_mean - unit * second_mean)
    return grad_values, jnp.sum(grad_in * unit, axis=0, keepdims=True), jnp.sum(grad_in, axis=0, keepdims=True)


def feed_kernel(
    att, h_in, wco, given, inner, outer, bias_in, bias_c, gain, shift, bias_u,
    block_out, gh_out, gatt_out, outer_out, inner_out, sums_out, split_out,
    att_vm, wco_vm, hidden, part, part_in, back_in, out_in, normed, rows, row, wi, wu, act, slope, g_outer,
    biases, sums, split, gatt, pieces, rows_back, full_outer, full_inner, *rest,
):
    lands, (sems, local_sems) = rest[:-2], rest[-2:]
    net = Net(sems, local_sems)
    core = net.core_index
    loads = [net.move(att, att_vm), net.move(wco, wco_vm), net.move(h_in, hidden), net.move(bias_in, biases)]
    net.meet()
    enter = row_in(net, given, rows, row)
    next(enter)

    def gather_inner(k):
        own = inner.at[pl.ds(k * 512, 512), pl.ds(pl.multiple_of(core * 512, 512), 512)]
        return Gather(net, own, lambda s: wi.at[pl.ds(k * 512, 512), s * 512:s * 512 + 512])

    def gather_outer(k):
        own = outer.at[pl.ds(pl.multiple_of(core * 512 + k * 256, 256), 256)]
        return Gather(net, own, lambda s: wu.at[pl.ds(s * 512 + k * 256, 256)])

    gathers = [gather_inner(0), gather_inner(1)]
    for copy in loads:
        net.moved(copy)
    swaps = []
    for i in range(4):
        value = dot(att_vm[i * 256:i * 256 + 256], wco_vm[...], NN)
        part[i] = value.astype(BF).reshape(2, 128, -1)
        swaps.append(net.send(part.at[i], part_in.at[i], net.core))
    next(enter)
    for i in range(4):
        swaps[i].wait_recv()
        value = hidden[i] + part[i].astype(F32) + part_in[i].astype(F32) + bias_c[...][None]
        hidden[i] = value
        normed[i * 256:i * 256 + 256] = norm_forward(value.reshape(256, -1), gain[...], shift[...])
    gathers[0].relay()
    gathers.append(gather_outer(0))
    next(enter)
    gathers[1].relay()
    gathers.append(gather_outer(1))
    for _ in enter:
        pass
    gathers[0].finish()
    gathers[1].finish()

    def feed(i, _):
        tokens = normed[tile_rows(i)]
        for s in range(4):
            cut = slice(s * 512, s * 512 + 512)
            bias = jnp.concatenate([biases[s, 4 + k:5 + k] for k in range(4)], axis=1)
            pre = dot(tokens, wi[:, cut], NN) + bias
            sigmoid = jax.nn.sigmoid(pre)
            act[tile_rows(i), cut] = (pre * sigmoid).astype(BF)
            slope[tile_rows(i), cut] = (sigmoid * (1.0 + pre * (1.0 - sigmoid))).astype(BF)
        return 0

    lax.fori_loop(0, 2, feed, 0)
    gathers[2].relay()
    lax.fori_loop(2, 4, feed, 0)
    whole_row = lambda: row[...].reshape(1024, -1)
    outer_result = lambda k: lambda c, h: full_outer.at[pl.ds(pl.multiple_of(c * 512 + k * 256 + h * 128, 128), 128)]
    inner_result = lambda k: lambda c, h: full_inner.at[
        pl.ds(pl.multiple_of(k * 512 + h * 256, 256), 256), pl.ds(pl.multiple_of(c * 512, 512), 512)
    ]
    outers = [
        Scatter(net, lambda s, k=k: g_outer.at[pl.ds(s * 512 + k * 256, 256)], 1, lands[k * 5:k * 5 + 5], outer_result(k))
        for k in range(2)
    ]
    inners = [
        Scatter(
            net, lambda s, k=k: act.at[pl.ds(k * 512, 512), s * 512:s * 512 + 512], 2,
            lands[10 + k * 5:15 + k * 5], inner_result(k),
        )
        for k in range(2)
    ]
    for k in range(2):
        for s in (3, 1):
            weight_grad(act, whole_row, g_outer, s * 512 + k * 256, 256)
        outers[k].start()
        if k == 0:
            gathers[3].relay()
    for k in range(2):
        for s in (2, 0):
            weight_grad(act, whole_row, g_outer, s * 512 + k * 256, 256)
    gathers[2].finish()
    gathers[3].finish()
    split[...] = jnp.zeros_like(split)
    sums[...] = jnp.zeros_like(sums)

    def feed_back(i, _):
        tokens = row[i].reshape(256, -1)
        for s in range(4):
            cut = slice(s * 512, s * 512 + 512)
            value = (dot(tokens, wu[cut], NT) * slope[tile_rows(i), cut].astype(F32)).astype(BF)
            slope[tile_rows(i), cut] = value
            split[0:1, cut] += jnp.sum(value.astype(F32), axis=0, keepdims=True)
        return 0

    lax.fori_loop(0, 4, feed_back, 0)
    outers[0].middle()
    for copy in swaps:
        net.sent(copy)

    def feed_out(i, _):
        part[i] = dot(act[tile_rows(i)], wu[...], NN).astype(BF).reshape(2, 128, -1)
        return 0

    lax.fori_loop(0, 4, feed_out, 0)
    out_swap = net.send(part.at[:, 1 - core], out_in, net.core)
    outers[1].middle()
    for k in range(2):
        for s in (3, 2):
            for h in range(2):
                cut = slice(s * 512, s * 512 + 512)
                weight_grad(normed, lambda: slope[:, cut], act, k * 512 + h * 256, 256, cut)
        inners[k].start()
    out_swap.wait_recv()
    for i in range(4):
        pieces[i] = (hidden[i, core] + part[i, core].astype(F32) + out_in[i].astype(F32) + bias_u[...]).astype(BF)
    leave = row_out(net, pieces, rows_back, block_out)
    next(leave)
    net.sent(out_swap)
    swaps = []
    for i in range(4):
        value = dot(slope[i * 256:i * 256 + 256], wi[...], NT)
        part[i] = value.astype(BF).reshape(2, 128, -1)
        swaps.append(net.send(part.at[i], back_in.at[i], net.core))
    for k in range(2):
        for s in (1, 0):
            cut = slice(s * 512, s * 512 + 512)
            weight_grad(normed, lambda: slope[:, cut], act, k * 512, 512, cut)
    outers[0].own()
    for copy in swaps:
        copy.wait_recv()

    def back(i, _):
        grad = (part[i].astype(F32) + back_in[i].astype(F32)).reshape(256, -1)
        change, by_gain, by_shift = norm_back_tile(grad, hidden[i].reshape(256, -1), gain[...])
        top = row[i].reshape(256, -1).astype(F32)
        value = top + change
        hidden[i] = value.reshape(2, 128, -1)
        gatt[tile_rows(i)] = dot(value.astype(BF), wco_vm[...], NT).astype(BF)
        sums[0:1] += by_gain
        sums[1:2] += by_shift
        sums[2:3] += jnp.sum(top, axis=0, keepdims=True)
        sums[3:4] += jnp.sum(value, axis=0, keepdims=True)
        return 0

    lax.fori_loop(0, 4, back, 0)
    net.move(hidden, gh_out)
    net.move(gatt, gatt_out)
    net.move(sums, sums_out)
    net.move(split, split_out)
    next(leave)
    outers[0].line1()
    outers[1].own()
    inners[0].middle()
    outers[0].line2()
    outers[1].line1()
    for _ in leave:
        pass
    inners[1].middle()
    outers[0].line3()
    outers[1].line2()
    inners[0].own()
    outers[1].line3()
    inners[0].line1()
    inners[1].own()
    inners[0].line2()
    inners[1].line1()
    inners[0].line3()
    inners[1].line2()
    inners[1].line3()
    for scatter in outers:
        scatter.end()
    net.move(full_outer, outer_out)
    for scatter in inners:
        scatter.end()
    net.move(full_inner, inner_out)
    net.finish()


def feed(att, hidden, wco, given, inner, outer, bias_in, bias_c, gain, shift, bias_u):
    length, width = att.shape[0], given.shape[-1]
    shape = jax.ShapeDtypeStruct
    quarters = (4, 2, 128, width)
    block, gh, gatt, g_outer, g_inner, sums, split = call_remote(
        feed_kernel, 3,
        (
            att, hidden.reshape(quarters), wco, given.reshape(2, 2, -1, width), inner, outer, bias_in,
            bias_c[None], gain[None], shift[None], bias_u[None],
        ),
        [ANY] * 7 + [VM] * 4,
        [
            shape((2, 2, 128, width), BF), shape(quarters, F32), shape((length, 512), BF),
            shape((1024, width), BF), shape((width, 1024), BF), shape((8, width), F32), shape((8, 2048), F32),
        ],
        [ANY] * 7,
        [
            pltpu.VMEM((length, 512), BF), pltpu.VMEM((512, width), BF), pltpu.VMEM(quarters, F32),
            pltpu.VMEM(quarters, BF), pltpu.VMEM(quarters, BF), pltpu.VMEM(quarters, BF), pltpu.VMEM((4, 128, width), BF),
            pltpu.VMEM((length, width), BF), pltpu.VMEM((4, 128, width), BF), pltpu.VMEM(quarters, BF),
            pltpu.VMEM((width, 2048), BF), pltpu.VMEM((2048, width), BF),
            pltpu.VMEM((length, 2048), BF), pltpu.VMEM((length, 2048), BF), pltpu.VMEM((2048, width), BF),
            pltpu.VMEM((4, 8, 128), F32), pltpu.VMEM((8, width), F32), pltpu.VMEM((8, 2048), F32),
            pltpu.VMEM((length, 512), BF), pltpu.VMEM((4, 128, width), BF), pltpu.VMEM((4, 128, width), BF),
            pltpu.VMEM((1024, width), BF), pltpu.VMEM((width, 1024), BF),
        ]
        + landing(256, width) * 2 + landing(512, 512) * 2,
        vmem=62, name="feed",
    )
    return block.reshape(given.shape), gh.reshape(hidden.shape), gatt, g_outer, g_inner, sums, split[0]


def run_scatters(scatters, between=()):
    steps = ("middle", "own", "line1", "line2", "line3", "end")
    between = list(between)
    for at in range(len(steps) + len(scatters) - 1):
        for place, scatter in enumerate(scatters):
            if 0 <= at - place < len(steps):
                getattr(scatter, steps[at - place])()
        if between:
            between.pop(0)()
    for rest in between:
        rest()


def head_scatters(net, g_heads, g_out, full_heads, full_out, lands):
    result = lambda kind: lambda c, h: full_heads.at[
        kind, pl.ds(pl.multiple_of(h * 512, 512), 512), pl.ds(pl.multiple_of(c * 128, 128), 128)
    ]
    found = [
        Scatter(
            net, lambda s, kind=kind: g_heads.at[:, kind * 512 + s * 128:kind * 512 + s * 128 + 128], first,
            lands[kind * 5:kind * 5 + 5], result(kind),
        )
        for kind, first in ((0, 1), (1, 1), (2, 2))
    ]
    found.append(
        Scatter(
            net, lambda s: g_out.at[pl.ds(s * 128, 128)], 2, lands[15:20],
            lambda c, h: full_out.at[pl.ds(pl.multiple_of(c * 128 + h * 64, 64), 64)],
        )
    )
    return found


def cross_kernel(
    dq, dk, dv, n_in, mem, att, gh_in, h_in, wc, wo, gain,
    mem_out, gh_out, gatt_out, heads_out, o_out, sums_out, split_out,
    dq_vm, dk_vm, dv_vm, normed, tokens, att_vm, grads, hidden, weights, wo_vm,
    part, part_in, mem_part, mem_in, pieces, rows_back, g_heads, g_out, full_heads, full_out, gatt, sums, split, *rest,
):
    lands, (sems, local_sems) = rest[:-2], rest[-2:]
    net = Net(sems, local_sems)
    core = net.core_index
    loads = [
        net.move(source, target)
        for source, target in (
            (dq, dq_vm), (wc, weights), (mem, tokens), (dk, dk_vm), (dv, dv_vm), (n_in, normed), (att, att_vm),
            (gh_in, grads), (h_in, hidden), (wo, wo_vm),
        )
    ]
    net.meet()
    for copy in loads[:2]:
        net.moved(copy)
    swaps = []
    for i in range(4):
        value = dot(dq_vm[i * 256:i * 256 + 256], weights[:, :512], NT)
        part[i] = value.astype(BF).reshape(2, 128, -1)
        swaps.append(net.send(part.at[i], part_in.at[i], net.core))
    for copy in loads[2:]:
        net.moved(copy)
    scatters = head_scatters(net, g_heads, g_out, full_heads, full_out, lands)
    weight_grad(tokens, lambda: dk_vm[...], g_heads, 0, 1024, slice(512, 1024))
    scatters[1].start()
    weight_grad(tokens, lambda: dv_vm[...], g_heads, 0, 1024, slice(1024, 1536))
    scatters[2].start()
    for i in range(4):
        cut = slice(i * 256, i * 256 + 256)
        value = dot(dk_vm[cut], weights[:, 512:1024], NT) + dot(dv_vm[cut], weights[:, 1024:], NT)
        mem_part[i] = value.astype(BF).reshape(2, 128, -1)
    mem_swap = net.send(mem_part.at[:, 1 - core], mem_in, net.core)
    weight_grad(normed, lambda: dq_vm[...], g_heads, 0, 1024, slice(0, 512))
    scatters[0].start()
    weight_grad(att_vm, lambda: grads[...].reshape(1024, -1).astype(BF), g_out, 0, 512)
    scatters[3].start()
    mem_swap.wait_recv()
    for i in range(4):
        pieces[i] = (mem_part[i, core].astype(F32) + mem_in[i].astype(F32)).astype(BF)
    leave = row_out(net, pieces, rows_back, mem_out)
    next(leave)
    scatters[1].middle()
    for copy in swaps:
        copy.wait_recv()
    sums[...] = jnp.zeros_like(sums)
    split[...] = jnp.zeros_like(split)
    split[0:1, :512] = jnp.sum(dq_vm[...].astype(F32), axis=0, keepdims=True)
    split[0:1, 512:] = jnp.sum(dv_vm[...].astype(F32), axis=0, keepdims=True)

    def back(i, _):
        grad = (part[i].astype(F32) + part_in[i].astype(F32)).reshape(256, -1)
        change, by_gain, by_shift = norm_back_tile(grad, hidden[i].reshape(256, -1), gain[...])
        value = grads[i].reshape(256, -1) + change
        grads[i] = value.reshape(2, 128, -1)
        gatt[tile_rows(i)] = dot(value.astype(BF), wo_vm[...], NT).astype(BF)
        sums[0:1] += by_gain
        sums[1:2] += by_shift
        sums[2:3] += jnp.sum(value, axis=0, keepdims=True)
        return 0

    lax.fori_loop(0, 4, back, 0)
    net.move(grads, gh_out)
    net.move(gatt, gatt_out)
    net.move(sums, sums_out)
    net.move(split, split_out)
    scatters[2].middle()
    next(leave)
    scatters[0].middle()
    scatters[1].own()
    scatters[3].middle()
    scatters[2].own()
    scatters[1].line1()
    for _ in leave:
        pass
    scatters[0].own()
    scatters[2].line1()
    scatters[3].own()
    scatters[1].line2()
    scatters[0].line1()
    scatters[2].line2()
    scatters[3].line1()
    scatters[1].line3()
    scatters[0].line2()
    scatters[2].line3()
    scatters[3].line2()
    scatters[0].line3()
    scatters[3].line3()
    for scatter in scatters:
        scatter.end()
    net.move(full_heads, heads_out)
    net.move(full_out, o_out)
    net.finish()


def head_landing(width):
    return landing(1024, 128) * 3 + landing(128, width)


def cross(dq, dk, dv, n, mem, att, gh, hidden, wc, wo, gain):
    length, width = dq.shape[0], n.shape[-1]
    shape = jax.ShapeDtypeStruct
    quarters = (4, 2, 128, width)
    mem_grad, gh, gatt, heads, out, sums, split = call_remote(
        cross_kernel, 4,
        (
            dq, dk, dv, n, mem.reshape(length, width), att, gh.reshape(quarters), hidden.reshape(quarters), wc, wo,
            gain[None],
        ),
        [ANY] * 10 + [VM],
        [
            shape((2, 2, 128, width), BF), shape(quarters, F32), shape((length, 512), BF),
            shape((3, width, 256), BF), shape((256, width), BF), shape((8, width), F32), shape((8, 1024), F32),
        ],
        [ANY] * 7,
        [pltpu.VMEM((length, 512), BF)] * 3
        + [
            pltpu.VMEM((length, width), BF), pltpu.VMEM((length, width), BF), pltpu.VMEM((length, 512), BF),
            pltpu.VMEM(quarters, F32), pltpu.VMEM(quarters, F32), pltpu.VMEM((width, 1536), BF),
            pltpu.VMEM((512, width), BF), pltpu.VMEM(quarters, BF), pltpu.VMEM(quarters, BF),
            pltpu.VMEM(quarters, BF), pltpu.VMEM((4, 128, width), BF), pltpu.VMEM((4, 128, width), BF),
            pltpu.VMEM((4, 128, width), BF), pltpu.VMEM((width, 1536), BF), pltpu.VMEM((512, width), BF),
            pltpu.VMEM((3, width, 256), BF), pltpu.VMEM((256, width), BF), pltpu.VMEM((length, 512), BF),
            pltpu.VMEM((8, width), F32), pltpu.VMEM((8, 1024), F32),
        ]
        + head_landing(width),
        vmem=60, name="cross",
    )
    return mem_grad.reshape(2, -1, width), gh, gatt, heads, out, sums, split[0]


def end_kernel(
    dq, dk, dv, n_in, att, gh_in, x_in, wqkv, gain, shared_in, split_in,
    grad_out, heads_out, o_out, shared_out, late_out, split_out,
    dqkv, normed, att_vm, grads, values, weights, part, part_in, pieces, rows_back,
    g_heads, g_out, full_heads, full_out, shared, shared_land, late, late_land, split, split_land, split_full, *rest,
):
    lands, (sems, local_sems) = rest[:-2], rest[-2:]
    net = Net(sems, local_sems)
    core, chip = net.core_index, net.chip
    place = lax.axis_index("dp")
    loads = [
        net.move(source, target)
        for source, target in (
            (dq, dqkv.at[:, :512]), (dk, dqkv.at[:, 512:1024]), (dv, dqkv.at[:, 1024:]), (wqkv, weights), (n_in, normed),
            (att, att_vm), (gh_in, grads), (x_in, values), (shared_in, shared), (split_in, split),
        )
    ]
    net.meet()
    for copy in loads[:4]:
        net.moved(copy)

    def back(i, _):
        value = dot(dqkv[tile_rows(i)], weights[...], NT)
        part[i] = value.astype(BF).reshape(2, 128, -1)
        return 0

    lax.fori_loop(0, 4, back, 0)
    swap = net.send(part.at[:, 1 - core], part_in, net.core)
    for copy in loads[4:]:
        net.moved(copy)
    stages = [(place, net.chips[0]), (place, net.chips[1]), net.near_plane, net.far_plane]
    shared_copy = net.send(shared, shared_land.at[0], stages[0])
    scatters = head_scatters(net, g_heads, g_out, full_heads, full_out, lands)
    order = [scatters[0], scatters[2], scatters[1], scatters[3]]
    for kind in (0, 2, 1):
        cut = slice(kind * 512, kind * 512 + 512)
        weight_grad(normed, lambda: dqkv[:, cut], g_heads, 0, 1024, cut)
        scatters[kind].start()
        if kind == 0:
            swap.wait_recv()
            late[...] = jnp.zeros_like(late)
            for i in range(4):
                grad = part[i, core].astype(F32) + part_in[i].astype(F32)
                change, by_gain, by_shift = norm_back_tile(grad, values[i, core].astype(F32), gain[...])
                pieces[i] = (grads[i, core] + change).astype(BF)
                late[0:1] += by_gain
                late[1:2] += by_shift
            leave = row_out(net, pieces, rows_back, grad_out)
            next(leave)
            late_copy = net.send(late, late_land.at[0], net.core)
    weight_grad(att_vm, lambda: grads[...].reshape(1024, -1).astype(BF), g_out, 0, 512)
    scatters[3].start()
    for at, kind in ((0, 0), (1, 2)):
        total = jnp.sum(dqkv[:, kind * 512:kind * 512 + 512].astype(F32), axis=0, keepdims=True)
        for s in range(4):
            split[s, at:at + 1] = total[:, s * 128:s * 128 + 128]
    split_copies = [
        net.send(split.at[s], split_land.at[s - 1], device)
        for s, device in ((1, net.first), (2, net.second), (3, net.corner))
    ]

    def shared_stage(at):
        def step():
            nonlocal shared_copy
            shared_copy.wait_recv()
            net.sent(shared_copy)
            shared[...] += shared_land[at]
            if at < 3:
                shared_copy = net.send(shared, shared_land.at[at + 1], stages[at + 1])

        return step

    def late_stage(at):
        def step():
            nonlocal late_copy
            late_copy.wait_recv()
            net.sent(late_copy)
            late[...] += late_land[at]
            if at < 4:
                late_copy = net.send(late, late_land.at[at + 1], stages[at])

        return step

    def split_stage(at):
        def step():
            nonlocal split_copies
            for copy in split_copies:
                copy.wait_recv()
                net.sent(copy)
            if at == 0:
                split[0] = split[0] + split_land[0] + split_land[1] + split_land[2]
            else:
                split[0] = split[0] + split_land[2 + at]
            if at < 2:
                device = (net.near_plane, net.far_plane)[at]
                split_copies = [net.send(split.at[0], split_land.at[3 + at], device)]
            else:
                split_full[core] = split[0]
                split_copies = [net.send(split_full.at[core], split_full.at[core], net.core)]

        return step

    def row_step():
        next(leave, None)

    def both(*steps):
        def step():
            for one in steps:
                one()

        return step

    run_scatters(
        order,
        [
            both(shared_stage(0), late_stage(0), split_stage(0)),
            both(row_step, shared_stage(1), late_stage(1)),
            both(late_stage(2), split_stage(1)),
            both(shared_stage(2), late_stage(3), row_step),
            both(shared_stage(3), late_stage(4), split_stage(2)),
        ],
    )
    split_copies[0].wait_recv()
    net.move(full_heads, heads_out)
    net.move(full_out, o_out)
    net.move(shared, shared_out)
    net.move(late, late_out)
    net.move(split_full, split_out)
    net.finish()


def end(dq, dk, dv, n, att, gh, x, wqkv, gain, shared, split):
    length, width = dq.shape[0], n.shape[-1]
    shape = jax.ShapeDtypeStruct
    quarters = (4, 2, 128, width)
    grad, *others = call_remote(
        end_kernel, 5,
        (dq, dk, dv, n, att, gh, x, wqkv, gain[None], shared, split),
        [ANY] * 8 + [VM] + [ANY] * 2,
        [
            shape((2, 2, 128, width), BF), shape((3, width, 256), BF), shape((256, width), BF),
            shape((8, width), F32), shape((8, width), F32), shape((2, 8, 128), F32),
        ],
        [ANY] * 6,
        [
            pltpu.VMEM((length, 1536), BF), pltpu.VMEM((length, width), BF), pltpu.VMEM((length, 512), BF),
            pltpu.VMEM(quarters, F32), pltpu.VMEM(quarters, BF), pltpu.VMEM((width, 1536), BF),
            pltpu.VMEM(quarters, BF), pltpu.VMEM((4, 128, width), BF), pltpu.VMEM((4, 128, width), BF),
            pltpu.VMEM((4, 128, width), BF), pltpu.VMEM((width, 1536), BF), pltpu.VMEM((512, width), BF),
            pltpu.VMEM((3, width, 256), BF), pltpu.VMEM((256, width), BF),
            pltpu.VMEM((8, width), F32), pltpu.VMEM((4, 8, width), F32),
            pltpu.VMEM((8, width), F32), pltpu.VMEM((5, 8, width), F32),
            pltpu.VMEM((4, 8, 128), F32), pltpu.VMEM((5, 8, 128), F32), pltpu.VMEM((2, 8, 128), F32),
        ]
        + head_landing(width),
        vmem=60, name="end",
    )
    return [grad.reshape(2, -1, width)] + others


def solution(mesh):
    if mesh.shape["tensor"] != 4 or mesh.shape["dp"] != 8:
        return general_solution(mesh)
    links = Links(mesh)

    def local(
        layer_input, memory, grad_out, target_segments, source_segments,
        self_gain, self_shift, query_weight, query_bias, key_weight, value_weight, value_bias,
        attend_weight, attend_bias,
        cross_gain, cross_shift, cross_query, cross_query_bias, cross_key, cross_value, cross_value_bias,
        cross_attend, cross_attend_bias,
        feed_gain, feed_shift, inner_weight, inner_bias, outer_weight, outer_bias,
    ):
        links.enter()
        core, chip = links.core, links.chip
        columns = lambda w: links.take_half(w, 1, core)
        rows = lambda w: links.take_half(w, 0, core)

        head, unit = 128, 512
        ids = jnp.stack([target_segments, source_segments], axis=1).reshape(2, 16, 128)
        biases = cat([rows(b) for b in (query_bias, value_bias, cross_query_bias, cross_value_bias, inner_bias)], 0)
        x_row, n1, qkv1, wqkv, wo, row_ids, bias_slots = begin(
            layer_input, ids, biases.reshape(8, 128), query_weight, key_weight, value_weight, attend_weight,
            self_gain, self_shift,
        )
        inputs = x_row.reshape(1024, 1024).astype(F32)
        row_ids = lax.dynamic_index_in_dim(row_ids, chip, 0, keepdims=False).reshape(2, 1024)
        target_ids, source_ids = row_ids[0], row_ids[1]
        reach_self = reach(target_ids, target_ids, True)
        reach_cross = reach(target_ids, source_ids, False)
        bi = bias_slots[:, 4:].reshape(-1)
        wq, wk, wv = wqkv[:, :512], wqkv[:, 512:1024], wqkv[:, 1024:]

        att1, sums1 = attend(qkv1, 0, qkv1, 1, *reach_self)
        hidden1, n2, q2, kv2, mem, wc, wco = middle(
            att1, x_row, wo, attend_bias, cross_gain, cross_shift, memory, cross_query, cross_key, cross_value,
            cross_attend, bias_slots,
        )
        mem = mem.reshape(1024, 1024)
        wcq, wck, wcv = wc[:, :512], wc[:, 512:1024], wc[:, 1024:]
        att2, sums2 = attend(q2, 0, kv2, 0, *reach_cross)

        block_out, grad_hidden2, grad_att2, f_outer, f_inner, feed_sums, feed_split = feed(
            att2, hidden1, wco, grad_out, inner_weight, outer_weight, bias_slots, cross_attend_bias, feed_gain,
            feed_shift, outer_bias,
        )

        dq2, dk2, dv2 = attend_back(q2, 0, kv2, 0, grad_att2, att2, sums2, *reach_cross)
        memory_grad, grad_hidden1, grad_att1, c_heads, c_out, cross_sums, cross_split = cross(
            dq2, dk2, dv2, n2, mem, att2, grad_hidden2, hidden1, wc, wo, cross_gain
        )
        dq1, dk1, dv1 = attend_back(qkv1, 0, qkv1, 1, grad_att1, att1, sums1, *reach_self)
        shared = cat([cross_sums[2:3], cross_sums[:2], feed_sums[3:4], feed_sums[:3], jnp.zeros((1, 1024), F32)], 0)
        split = cat(
            [
                jnp.zeros((4, 2, 128), F32), cross_split[:512].reshape(4, 1, 128), cross_split[512:].reshape(4, 1, 128),
                feed_split.reshape(4, 4, 128),
            ],
            1,
        )
        input_grad, s_heads, s_out, shared, late, split = end(
            dq1, dk1, dv1, n1, att1, grad_hidden1, x_row, wqkv, self_gain, shared, split
        )
        split_of = lambda at, rows: split[:, at:at + rows].reshape(-1)
        return (
            block_out, input_grad.astype(F32), memory_grad.astype(F32),
            late[0], late[1],
            s_heads[0].astype(F32), split_of(0, 1), s_heads[1].astype(F32), s_heads[2].astype(F32), split_of(1, 1),
            s_out.astype(F32), shared[0],
            shared[1], shared[2],
            c_heads[0].astype(F32), split_of(2, 1), c_heads[1].astype(F32), c_heads[2].astype(F32), split_of(3, 1),
            c_out.astype(F32), shared[3],
            shared[4], shared[5],
            f_inner.astype(F32), split_of(4, 4), f_outer.astype(F32), shared[6],
        )

    row, one, by_column, by_row = P("dp", "tensor", None), P(), P(None, "tensor"), P("tensor", None)
    part, ids = P("tensor"), P("dp", None)
    return jax.shard_map(
        local,
        mesh=mesh,
        in_specs=(
            row, row, row, ids, ids,
            one, one, by_column, part, by_column, by_column, part, by_row, one,
            one, one, by_column, part, by_column, by_column, part, by_row, one,
            one, one, by_column, part, by_row, one,
        ),
        out_specs=(
            row, row, row,
            one, one, by_column, part, by_column, by_column, part, by_row, one,
            one, one, by_column, part, by_column, by_column, part, by_row, one,
            one, one, by_column, part, by_row, one,
        ),
        check_vma=False,
    )


BLOCK_ROWS = 512


def general_norm_forward(values, gain, shift):
    average = jnp.mean(values, axis=-1, keepdims=True)
    center = values - average
    inverse = lax.rsqrt(jnp.mean(center * center, axis=-1, keepdims=True) + EPSILON)
    normed = center * inverse
    return ((normed * gain + shift).astype(jnp.bfloat16), normed, inverse)


def general_norm_backward(grad_in, normed, inverse, gain):
    scaled = grad_in * gain
    first_mean = jnp.mean(scaled, axis=-1, keepdims=True)
    second_mean = jnp.mean(scaled * normed, axis=-1, keepdims=True)
    grad_values = inverse * (scaled - first_mean - normed * second_mean)
    return (grad_values, jnp.sum(grad_in * normed, axis=(0, 1)), jnp.sum(grad_in, axis=(0, 1)))


def gather_rows(values):
    return lax.all_gather(values, "tensor", axis=1, tiled=True)


def gather_grads(values):
    return lax.all_gather(values, "tensor", axis=1, tiled=True)


def reduce_inputs(partial_sum):
    return lax.psum_scatter(partial_sum, "tensor", scatter_dimension=1, tiled=True)


def advance(base, partial_sum, bias):
    return base + lax.psum_scatter(partial_sum, "tensor", scatter_dimension=1, tiled=True) + bias


def next_rows(values, gain, shift):
    return gather_rows(general_norm_forward(values, gain, shift)[0])


def backward_rows(normed_low):
    return gather_rows(normed_low)


def project(rows_in, weight):
    return jnp.einsum("rtd,dc->rtc", rows_in, weight, preferred_element_type=jnp.float32)


def project_back(grads, weight):
    return jnp.einsum("rtc,dc->rtd", grads, weight, preferred_element_type=jnp.float32)


def outer_sum(rows_in, grads):
    return jnp.einsum("rtd,rtc->dc", rows_in, grads, preferred_element_type=jnp.float32)


def bias_sum(grads):
    return jnp.sum(grads.astype(jnp.float32), axis=(0, 1))


def split_heads(values):
    return values.reshape(values.shape[0], values.shape[1], values.shape[2] // HD, HD)


def block_scores(query_block, key_row, query_ids, key_ids, row_start, causal):
    raw_scores = jnp.einsum(
        "qhd,khd->hqk", query_block, key_row, preferred_element_type=jnp.float32
    ) * float(HD) ** (-0.5)
    allowed = query_ids[:, None] == key_ids[None, :]
    if causal:
        query_place = row_start + jnp.arange(query_block.shape[0], dtype=jnp.int32)
        key_place = jnp.arange(key_row.shape[0], dtype=jnp.int32)
        allowed = allowed & (key_place[None, :] <= query_place[:, None])
    return jnp.where(allowed[None], raw_scores, jnp.full(raw_scores.shape, MASKED, jnp.float32))


def block_inputs(
    query_heads, key_heads, value_heads, query_ids, key_ids, position, block_count, block_size
):
    row_index = position // block_count
    row_start = position % block_count * block_size
    query_row = lax.dynamic_index_in_dim(query_heads, row_index, 0, keepdims=False)
    query_block = lax.dynamic_slice_in_dim(query_row, row_start, block_size, 0)
    key_row = lax.dynamic_index_in_dim(key_heads, row_index, 0, keepdims=False)
    value_row = lax.dynamic_index_in_dim(value_heads, row_index, 0, keepdims=False)
    query_seg = lax.dynamic_slice_in_dim(
        lax.dynamic_index_in_dim(query_ids, row_index, 0, keepdims=False), row_start, block_size, 0
    )
    key_seg = lax.dynamic_index_in_dim(key_ids, row_index, 0, keepdims=False)
    return (row_index, row_start, query_block, key_row, value_row, query_seg, key_seg)


def attend_forward(query, keys, values, query_ids, key_ids, causal):
    query_heads = split_heads(query)
    key_heads = split_heads(keys)
    value_heads = split_heads(values)
    block_size = min(BLOCK_ROWS, query.shape[1])
    block_count = query.shape[1] // block_size

    def one_block(position):
        row_index, row_start, query_block, key_row, value_row, query_seg, key_seg = block_inputs(
            query_heads,
            key_heads,
            value_heads,
            query_ids,
            key_ids,
            position,
            block_count,
            block_size,
        )
        scores = block_scores(query_block, key_row, query_seg, key_seg, row_start, causal)
        row_max = jnp.max(scores, axis=-1, keepdims=True)
        expo_scores = jnp.exp(scores - row_max)
        row_total = jnp.sum(expo_scores, axis=-1, keepdims=True)
        softmax_out = expo_scores / row_total
        attended = jnp.einsum(
            "hqk,khd->qhd",
            softmax_out.astype(jnp.bfloat16),
            value_row,
            preferred_element_type=jnp.float32,
        ).astype(jnp.bfloat16)
        return (attended, (row_max + jnp.log(row_total))[..., 0])

    attended_all, log_sums = lax.map(
        one_block, jnp.arange(query.shape[0] * block_count, dtype=jnp.int32)
    )
    return (attended_all.reshape(query.shape), log_sums)


def attend_backward(query, keys, values, grad_att, log_sums, query_ids, key_ids, causal):
    query_heads = split_heads(query)
    key_heads = split_heads(keys)
    value_heads = split_heads(values)
    grad_heads = split_heads(grad_att)
    block_size = min(BLOCK_ROWS, query.shape[1])
    block_count = query.shape[1] // block_size
    score_scale = float(HD) ** (-0.5)

    def one_block(carry, inputs):
        grad_keys, grad_values = carry
        position, log_sum = inputs
        row_index, row_start, query_block, key_row, value_row, query_seg, key_seg = block_inputs(
            query_heads,
            key_heads,
            value_heads,
            query_ids,
            key_ids,
            position,
            block_count,
            block_size,
        )
        grad_row = lax.dynamic_index_in_dim(grad_heads, row_index, 0, keepdims=False)
        grad_block = lax.dynamic_slice_in_dim(grad_row, row_start, block_size, 0)
        scores = block_scores(query_block, key_row, query_seg, key_seg, row_start, causal)
        softmax_out = jnp.exp(scores - log_sum[..., None])
        softmax_low = softmax_out.astype(jnp.bfloat16)
        attended = jnp.einsum(
            "hqk,khd->qhd", softmax_low, value_row, preferred_element_type=jnp.float32
        ).astype(jnp.bfloat16)
        grad_prob = jnp.einsum(
            "qhd,khd->hqk", grad_block, value_row, preferred_element_type=jnp.float32
        )
        correction = jnp.sum(softmax_out * grad_prob, axis=-1, keepdims=True)
        grad_score = (softmax_out * (grad_prob - correction)).astype(jnp.bfloat16)
        grad_query = (
            jnp.einsum("hqk,khd->qhd", grad_score, key_row, preferred_element_type=jnp.float32)
            * score_scale
        ).astype(jnp.bfloat16)
        key_added = (
            jnp.einsum("hqk,qhd->khd", grad_score, query_block, preferred_element_type=jnp.float32)
            * score_scale
        )
        value_added = jnp.einsum(
            "hqk,qhd->khd", softmax_low, grad_block, preferred_element_type=jnp.float32
        )
        grad_keys = grad_keys.at[row_index].add(key_added)
        grad_values = grad_values.at[row_index].add(value_added)
        return ((grad_keys, grad_values), (grad_query, attended))

    empty_grads = jnp.zeros(key_heads.shape, jnp.float32)
    positions = jnp.arange(query.shape[0] * block_count, dtype=jnp.int32)
    (grad_keys, grad_values), (grad_query, attended_all) = lax.scan(
        one_block, (empty_grads, empty_grads), (positions, log_sums)
    )
    return (
        grad_query.reshape(query.shape),
        grad_keys.reshape(keys.shape).astype(jnp.bfloat16),
        grad_values.reshape(values.shape).astype(jnp.bfloat16),
        attended_all.reshape(query.shape),
    )


def general_local(
    layer_input,
    memory,
    grad_out,
    target_segments,
    source_segments,
    self_gain,
    self_shift,
    query_weight,
    query_bias,
    key_weight,
    value_weight,
    value_bias,
    attend_weight,
    attend_bias,
    cross_gain,
    cross_shift,
    cross_query,
    cross_query_bias,
    cross_key,
    cross_value,
    cross_value_bias,
    cross_attend,
    cross_attend_bias,
    feed_gain,
    feed_shift,
    inner_weight,
    inner_bias,
    outer_weight,
    outer_bias,
):
    inputs = layer_input.astype(jnp.float32)
    rows_first = next_rows(inputs, self_gain, self_shift)
    query_first = (project(rows_first, query_weight) + query_bias).astype(jnp.bfloat16)
    keys_first = project(rows_first, key_weight).astype(jnp.bfloat16)
    values_first = (project(rows_first, value_weight) + value_bias).astype(jnp.bfloat16)
    attended_first, sums_first = attend_forward(
        query_first, keys_first, values_first, target_segments, target_segments, True
    )
    base_first = advance(inputs, project(attended_first, attend_weight), attend_bias)
    memory_rows = lax.all_gather(memory, "tensor", axis=1, tiled=True)
    rows_second = next_rows(base_first, cross_gain, cross_shift)
    query_second = (project(rows_second, cross_query) + cross_query_bias).astype(jnp.bfloat16)
    keys_second = project(memory_rows, cross_key).astype(jnp.bfloat16)
    values_second = (project(memory_rows, cross_value) + cross_value_bias).astype(jnp.bfloat16)
    attended_second, sums_second = attend_forward(
        query_second, keys_second, values_second, target_segments, source_segments, False
    )
    base_second = advance(base_first, project(attended_second, cross_attend), cross_attend_bias)
    rows_third = next_rows(base_second, feed_gain, feed_shift)
    pre_active = project(rows_third, inner_weight) + inner_bias
    active = jax.nn.silu(pre_active).astype(jnp.bfloat16)
    base_out = advance(base_second, project(active, outer_weight), outer_bias)
    block_out = base_out.astype(jnp.bfloat16)
    kept_input, kept_first, kept_second, kept_memory, kept_sums_first, kept_sums_second = (
        lax.optimization_barrier(
            (inputs, base_first, base_second, memory_rows, sums_first, sums_second)
        )
    )
    grad_top = grad_out.astype(jnp.float32)
    normed_low3, unit_third, inverse_third = general_norm_forward(kept_second, feed_gain, feed_shift)
    rows_back3 = backward_rows(normed_low3)
    pre_back = project(rows_back3, inner_weight) + inner_bias
    sigmoid_back = jax.nn.sigmoid(pre_back)
    active_back = (pre_back * sigmoid_back).astype(jnp.bfloat16)
    grad_rows3 = gather_grads(grad_top.astype(jnp.bfloat16))
    grad_outer_weight = outer_sum(active_back, grad_rows3)
    grad_outer_bias = jnp.sum(grad_top, axis=(0, 1))
    grad_active = project_back(grad_rows3, outer_weight)
    grad_inner = (grad_active * sigmoid_back * (1.0 + pre_back * (1.0 - sigmoid_back))).astype(
        jnp.bfloat16
    )
    grad_inner_weight = outer_sum(rows_back3, grad_inner)
    grad_inner_bias = bias_sum(grad_inner)
    grad_norm3 = reduce_inputs(project_back(grad_inner, inner_weight))
    grad_from3, grad_feed_gain, grad_feed_shift = general_norm_backward(
        grad_norm3, unit_third, inverse_third, feed_gain
    )
    grad_hidden2 = grad_top + grad_from3
    normed_low2, unit_second, inverse_second = general_norm_forward(kept_first, cross_gain, cross_shift)
    rows_back2 = backward_rows(normed_low2)
    query_back2 = (project(rows_back2, cross_query) + cross_query_bias).astype(jnp.bfloat16)
    keys_back2 = project(kept_memory, cross_key).astype(jnp.bfloat16)
    values_back2 = (project(kept_memory, cross_value) + cross_value_bias).astype(jnp.bfloat16)
    grad_rows2 = gather_grads(grad_hidden2.astype(jnp.bfloat16))
    grad_att2 = project_back(grad_rows2, cross_attend).astype(jnp.bfloat16)
    grad_query2, grad_keys2, grad_values2, attended_back2 = attend_backward(
        query_back2,
        keys_back2,
        values_back2,
        grad_att2,
        kept_sums_second,
        target_segments,
        source_segments,
        False,
    )
    grad_cross_attend = outer_sum(attended_back2, grad_rows2)
    grad_cross_attend_bias = jnp.sum(grad_hidden2, axis=(0, 1))
    grad_cross_query = outer_sum(rows_back2, grad_query2)
    grad_cross_query_bias = bias_sum(grad_query2)
    grad_cross_key = outer_sum(kept_memory, grad_keys2)
    grad_cross_value = outer_sum(kept_memory, grad_values2)
    grad_cross_value_bias = bias_sum(grad_values2)
    memory_grad = lax.psum_scatter(
        (project_back(grad_keys2, cross_key) + project_back(grad_values2, cross_value)).astype(
            jnp.bfloat16
        ),
        "tensor",
        scatter_dimension=1,
        tiled=True,
    ).astype(jnp.float32)
    grad_norm2 = reduce_inputs(project_back(grad_query2, cross_query))
    grad_from2, grad_cross_gain, grad_cross_shift = general_norm_backward(
        grad_norm2, unit_second, inverse_second, cross_gain
    )
    grad_hidden1 = grad_hidden2 + grad_from2
    normed_low1, unit_first, inverse_first = general_norm_forward(kept_input, self_gain, self_shift)
    rows_back1 = backward_rows(normed_low1)
    query_back1 = (project(rows_back1, query_weight) + query_bias).astype(jnp.bfloat16)
    keys_back1 = project(rows_back1, key_weight).astype(jnp.bfloat16)
    values_back1 = (project(rows_back1, value_weight) + value_bias).astype(jnp.bfloat16)
    grad_rows1 = gather_grads(grad_hidden1.astype(jnp.bfloat16))
    grad_att1 = project_back(grad_rows1, attend_weight).astype(jnp.bfloat16)
    grad_query1, grad_keys1, grad_values1, attended_back1 = attend_backward(
        query_back1,
        keys_back1,
        values_back1,
        grad_att1,
        kept_sums_first,
        target_segments,
        target_segments,
        True,
    )
    grad_attend_weight = outer_sum(attended_back1, grad_rows1)
    grad_attend_bias = jnp.sum(grad_hidden1, axis=(0, 1))
    grad_query_weight = outer_sum(rows_back1, grad_query1)
    grad_query_bias = bias_sum(grad_query1)
    grad_key_weight = outer_sum(rows_back1, grad_keys1)
    grad_value_weight = outer_sum(rows_back1, grad_values1)
    grad_value_bias = bias_sum(grad_values1)
    grad_norm1 = reduce_inputs(
        project_back(grad_query1, query_weight)
        + project_back(grad_keys1, key_weight)
        + project_back(grad_values1, value_weight)
    )
    grad_from1, grad_self_gain, grad_self_shift = general_norm_backward(
        grad_norm1, unit_first, inverse_first, self_gain
    )
    input_grad = grad_hidden1 + grad_from1
    (
        grad_query_weight,
        grad_query_bias,
        grad_key_weight,
        grad_value_weight,
        grad_value_bias,
        grad_attend_weight,
        grad_cross_query,
        grad_cross_query_bias,
        grad_cross_key,
        grad_cross_value,
        grad_cross_value_bias,
        grad_cross_attend,
        grad_inner_weight,
        grad_inner_bias,
        grad_outer_weight,
    ) = (
        lax.psum(grad_query_weight.astype(jnp.bfloat16), "dp").astype(jnp.float32),
        lax.psum(grad_query_bias.astype(jnp.bfloat16), "dp").astype(jnp.float32),
        lax.psum(grad_key_weight.astype(jnp.bfloat16), "dp").astype(jnp.float32),
        lax.psum(grad_value_weight.astype(jnp.bfloat16), "dp").astype(jnp.float32),
        lax.psum(grad_value_bias.astype(jnp.bfloat16), "dp").astype(jnp.float32),
        lax.psum(grad_attend_weight.astype(jnp.bfloat16), "dp").astype(jnp.float32),
        lax.psum(grad_cross_query.astype(jnp.bfloat16), "dp").astype(jnp.float32),
        lax.psum(grad_cross_query_bias.astype(jnp.bfloat16), "dp").astype(jnp.float32),
        lax.psum(grad_cross_key.astype(jnp.bfloat16), "dp").astype(jnp.float32),
        lax.psum(grad_cross_value.astype(jnp.bfloat16), "dp").astype(jnp.float32),
        lax.psum(grad_cross_value_bias.astype(jnp.bfloat16), "dp").astype(jnp.float32),
        lax.psum(grad_cross_attend.astype(jnp.bfloat16), "dp").astype(jnp.float32),
        lax.psum(grad_inner_weight.astype(jnp.bfloat16), "dp").astype(jnp.float32),
        lax.psum(grad_inner_bias.astype(jnp.bfloat16), "dp").astype(jnp.float32),
        lax.psum(grad_outer_weight.astype(jnp.bfloat16), "dp").astype(jnp.float32),
    )
    (
        grad_self_gain,
        grad_self_shift,
        grad_attend_bias,
        grad_cross_gain,
        grad_cross_shift,
        grad_cross_attend_bias,
        grad_feed_gain,
        grad_feed_shift,
        grad_outer_bias,
    ) = lax.psum(
        (
            grad_self_gain,
            grad_self_shift,
            grad_attend_bias,
            grad_cross_gain,
            grad_cross_shift,
            grad_cross_attend_bias,
            grad_feed_gain,
            grad_feed_shift,
            grad_outer_bias,
        ),
        ("dp", "tensor"),
    )
    return (
        block_out,
        input_grad,
        memory_grad,
        grad_self_gain,
        grad_self_shift,
        grad_query_weight,
        grad_query_bias,
        grad_key_weight,
        grad_value_weight,
        grad_value_bias,
        grad_attend_weight,
        grad_attend_bias,
        grad_cross_gain,
        grad_cross_shift,
        grad_cross_query,
        grad_cross_query_bias,
        grad_cross_key,
        grad_cross_value,
        grad_cross_value_bias,
        grad_cross_attend,
        grad_cross_attend_bias,
        grad_feed_gain,
        grad_feed_shift,
        grad_inner_weight,
        grad_inner_bias,
        grad_outer_weight,
        grad_outer_bias,
    )


def general_solution(mesh):
    placed = (
        P("dp", "tensor", None),
        P("dp", "tensor", None),
        P("dp", "tensor", None),
        P("dp", None),
        P("dp", None),
        P(),
        P(),
        P(None, "tensor"),
        P("tensor"),
        P(None, "tensor"),
        P(None, "tensor"),
        P("tensor"),
        P("tensor", None),
        P(),
        P(),
        P(),
        P(None, "tensor"),
        P("tensor"),
        P(None, "tensor"),
        P(None, "tensor"),
        P("tensor"),
        P("tensor", None),
        P(),
        P(),
        P(),
        P(None, "tensor"),
        P("tensor"),
        P("tensor", None),
        P(),
    )
    return jax.shard_map(
        general_local,
        mesh=mesh,
        in_specs=placed,
        out_specs=(
            P("dp", "tensor", None),
            P("dp", "tensor", None),
            P("dp", "tensor", None),
            P(),
            P(),
            P(None, "tensor"),
            P("tensor"),
            P(None, "tensor"),
            P(None, "tensor"),
            P("tensor"),
            P("tensor", None),
            P(),
            P(),
            P(),
            P(None, "tensor"),
            P("tensor"),
            P(None, "tensor"),
            P(None, "tensor"),
            P("tensor"),
            P("tensor", None),
            P(),
            P(),
            P(),
            P(None, "tensor"),
            P("tensor"),
            P("tensor", None),
            P(),
        ),
        check_vma=False,
    )
```

```python
import jax
import jax.numpy as jnp
from jax import lax
from jax.experimental import pallas as pl
from jax.experimental.pallas import tpu as pltpu
from jax.sharding import PartitionSpec as P

HD = 64
MASKED = -1000000000.0
QUERIES = 128
KEYS = 256
NT = (((1,), (1,)), ((), ()))
TN = (((0,), (0,)), ((), ()))
NN = (((1,), (0,)), ((), ()))


def dot(a, b, dims):
    return lax.dot_general(a, b, dims, preferred_element_type=jnp.float32)


def both_heads(block):
    first = lax.broadcasted_iota(jnp.int32, block.shape, 1) < HD
    zero = jnp.zeros_like(block)
    return jnp.concatenate([jnp.where(first, block, zero), jnp.where(first, zero, block)], axis=0)


def key_span(bounds, place, count, step):
    start = bounds[0, place] + step * KEYS
    at = pl.multiple_of(jnp.minimum(start, count - KEYS), 16)
    return start, at


def allowed_keys(low_ref, high_ref, start, at):
    key_place = at + lax.broadcasted_iota(jnp.int32, (KEYS, 1), 0)
    least = jnp.maximum(low_ref[...], start)
    seen = (key_place >= least) & (key_place < high_ref[...])
    return jnp.concatenate([seen, seen], axis=1)


def attend_step(queries, k_ref, v_ref, rows, seen, acc, top, total):
    pairs = range(len(queries))
    cuts = [slice(p * 128, (p + 1) * 128) for p in pairs]
    scores = [jnp.where(seen, dot(k_ref[rows, cuts[p]], queries[p], NT), MASKED) for p in pairs]
    before = [top[p:p + 1] for p in pairs]
    now = [jnp.maximum(before[p], jnp.max(scores[p], axis=0, keepdims=True)) for p in pairs]
    weight = [jnp.exp(scores[p] - now[p]) for p in pairs]
    keep = [jnp.exp(before[p] - now[p]) for p in pairs]
    added = [dot(v_ref[rows, cuts[p]], weight[p].astype(jnp.bfloat16), TN) for p in pairs]
    sums = [jnp.sum(weight[p], axis=0, keepdims=True) for p in pairs]
    for p in pairs:
        top[p:p + 1] = now[p]
        total[p:p + 1] = total[p:p + 1] * keep[p] + sums[p]
        acc[p] = acc[p] * keep[p] + added[p]


def attend_back_step(queries, grads, fixes, sums, k_ref, v_ref, rows, seen, acc, acc_k, acc_v):
    pairs = range(len(queries))
    cuts = [slice(p * 128, (p + 1) * 128) for p in pairs]
    scores = [dot(k_ref[rows, cuts[p]], queries[p], NT) for p in pairs]
    dprob = [dot(v_ref[rows, cuts[p]], grads[p], NT) for p in pairs]
    prob = [jnp.exp(jnp.where(seen, scores[p] - sums[p], MASKED)) for p in pairs]
    low = [prob[p].astype(jnp.bfloat16) for p in pairs]
    dscore = [(prob[p] * (dprob[p] - fixes[p])).astype(jnp.bfloat16) for p in pairs]
    added_v = [dot(low[p], grads[p], NN) for p in pairs]
    added_k = [dot(dscore[p], queries[p], NN) for p in pairs]
    added_q = [dot(k_ref[rows, cuts[p]], dscore[p], TN) for p in pairs]
    for p in pairs:
        acc_v[rows, cuts[p]] += added_v[p]
        acc_k[rows, cuts[p]] += added_k[p]
        acc[p] += added_q[p]


def attend_kernel(bounds, low_ref, high_ref, q_ref, k_ref, v_ref, out_ref, sums_ref, acc, top, total):
    pairs = q_ref.shape[1] // 128
    count = k_ref.shape[0]
    place = pl.program_id(0)
    acc[...] = jnp.zeros_like(acc)
    total[...] = jnp.zeros_like(total)
    top[...] = jnp.full_like(top, -1e30)
    queries = [both_heads(q_ref[:, p * 128:(p + 1) * 128] * jnp.bfloat16(HD ** -0.5)) for p in range(pairs)]

    def step(j, _):
        start, at = key_span(bounds, place, count, j)
        seen = allowed_keys(low_ref, high_ref, start, at)
        attend_step(queries, k_ref, v_ref, pl.ds(at, KEYS), seen, acc, top, total)
        return 0

    lax.fori_loop(0, bounds[1, place], step, 0)
    for p in range(pairs):
        sums = total[p:p + 1]
        mixed = acc[p] / sums
        joined = jnp.concatenate([mixed[:HD, :QUERIES], mixed[HD:, QUERIES:]], axis=0)
        out_ref[:, p * 128:(p + 1) * 128] = joined.T.astype(jnp.bfloat16)
        sums_ref[p:p + 1] = top[p:p + 1] + jnp.log(sums)


def attend(q, q_at, kv, k_at, bounds, low, high):
    count, width = q.shape[0], 512
    source = kv.shape[0]
    pairs = width // 128
    return pl.pallas_call(
        attend_kernel,
        grid_spec=pltpu.PrefetchScalarGridSpec(
            num_scalar_prefetch=1,
            grid=(count // QUERIES,),
            in_specs=[
                pl.BlockSpec((1, QUERIES), lambda i, b: (0, i)),
                pl.BlockSpec((1, QUERIES), lambda i, b: (0, i)),
                pl.BlockSpec((QUERIES, width), lambda i, b: (i, q_at)),
                pl.BlockSpec((source, width), lambda i, b: (0, k_at)),
                pl.BlockSpec((source, width), lambda i, b: (0, k_at + 1)),
            ],
            out_specs=[
                pl.BlockSpec((QUERIES, width), lambda i, b: (i, 0)),
                pl.BlockSpec((None, pairs, 2 * QUERIES), lambda i, b: (i, 0, 0)),
            ],
            scratch_shapes=[
                pltpu.VMEM((pairs, 128, 2 * QUERIES), jnp.float32),
                pltpu.VMEM((pairs, 2 * QUERIES), jnp.float32),
                pltpu.VMEM((pairs, 2 * QUERIES), jnp.float32),
            ],
        ),
        out_shape=[
            jax.ShapeDtypeStruct((count, width), jnp.bfloat16),
            jax.ShapeDtypeStruct((count // QUERIES, pairs, 2 * QUERIES), jnp.float32),
        ],
        compiler_params=pltpu.CompilerParams(vmem_limit_bytes=32 << 20),
        cost_estimate=pl.CostEstimate(flops=4 * count * 400 * width, bytes_accessed=8 * count * width, transcendentals=0),
        name="attend",
    )(bounds, low, high, q, kv, kv)


def attend_back_kernel(
    bounds, low_ref, high_ref, q_ref, grad_ref, out_ref, sums_ref, k_ref, v_ref,
    dq_ref, dk_ref, dv_ref, acc, acc_k, acc_v,
):
    pairs = q_ref.shape[1] // 128
    count = k_ref.shape[0]
    place = pl.program_id(0)

    @pl.when(place == 0)
    def _():
        acc_k[...] = jnp.zeros_like(acc_k)
        acc_v[...] = jnp.zeros_like(acc_v)

    acc[...] = jnp.zeros_like(acc)
    queries, grads, fixes = [], [], []
    ones = jnp.ones((8, 128), jnp.bfloat16)
    for p in range(pairs):
        cut = slice(p * 128, (p + 1) * 128)
        queries.append(both_heads(q_ref[:, cut] * jnp.bfloat16(HD ** -0.5)))
        grad = both_heads(grad_ref[:, cut])
        grads.append(grad)
        out = out_ref[:, cut].astype(jnp.float32)
        product = grad.astype(jnp.float32) * jnp.concatenate([out, out], axis=0)
        coarse = product.astype(jnp.bfloat16)
        fine = (product - coarse.astype(jnp.float32)).astype(jnp.bfloat16)
        fixes.append((dot(ones, coarse, NT) + dot(ones, fine, NT))[:1])

    def step(j, _):
        start, at = key_span(bounds, place, count, j)
        seen = allowed_keys(low_ref, high_ref, start, at)
        sums = [sums_ref[p:p + 1] for p in range(pairs)]
        attend_back_step(queries, grads, fixes, sums, k_ref, v_ref, pl.ds(at, KEYS), seen, acc, acc_k, acc_v)
        return 0

    lax.fori_loop(0, bounds[1, place], step, 0)
    for p in range(pairs):
        mixed = acc[p] * (HD ** -0.5)
        joined = jnp.concatenate([mixed[:HD, :QUERIES], mixed[HD:, QUERIES:]], axis=0)
        dq_ref[:, p * 128:(p + 1) * 128] = joined.T.astype(jnp.bfloat16)

    @pl.when(place == pl.num_programs(0) - 1)
    def _():
        dk_ref[...] = acc_k[...].astype(jnp.bfloat16)
        dv_ref[...] = acc_v[...].astype(jnp.bfloat16)


def attend_back(q, q_at, kv, k_at, grad, out, sums, bounds, low, high):
    count, width = grad.shape
    source = kv.shape[0]
    pairs = width // 128
    whole = lambda i, b: (0, 0)
    rows = lambda i, b: (i, 0)
    return pl.pallas_call(
        attend_back_kernel,
        grid_spec=pltpu.PrefetchScalarGridSpec(
            num_scalar_prefetch=1,
            grid=(count // QUERIES,),
            in_specs=[
                pl.BlockSpec((1, QUERIES), lambda i, b: (0, i)),
                pl.BlockSpec((1, QUERIES), lambda i, b: (0, i)),
                pl.BlockSpec((QUERIES, width), lambda i, b: (i, q_at)),
                pl.BlockSpec((QUERIES, width), rows),
                pl.BlockSpec((QUERIES, width), rows),
                pl.BlockSpec((None, pairs, 2 * QUERIES), lambda i, b: (i, 0, 0)),
                pl.BlockSpec((source, width), lambda i, b: (0, k_at)),
                pl.BlockSpec((source, width), lambda i, b: (0, k_at + 1)),
            ],
            out_specs=[
                pl.BlockSpec((QUERIES, width), rows),
                pl.BlockSpec((source, width), whole),
                pl.BlockSpec((source, width), whole),
            ],
            scratch_shapes=[
                pltpu.VMEM((pairs, 128, 2 * QUERIES), jnp.float32),
                pltpu.VMEM((source, width), jnp.float32),
                pltpu.VMEM((source, width), jnp.float32),
            ],
        ),
        out_shape=[
            jax.ShapeDtypeStruct((count, width), jnp.bfloat16),
            jax.ShapeDtypeStruct((source, width), jnp.bfloat16),
            jax.ShapeDtypeStruct((source, width), jnp.bfloat16),
        ],
        compiler_params=pltpu.CompilerParams(vmem_limit_bytes=40 << 20),
        cost_estimate=pl.CostEstimate(flops=10 * count * 400 * width, bytes_accessed=16 * count * width, transcendentals=0),
        name="attend_back",
    )(bounds, low, high, q, grad, out, sums, kv, kv)


def reach(query_ids, key_ids, causal):
    count = query_ids.shape[0]
    low = jnp.sum((key_ids[None, :] < query_ids[:, None]).astype(jnp.int32), axis=1)
    if causal:
        high = jnp.arange(count, dtype=jnp.int32) + 1
    else:
        high = jnp.sum((key_ids[None, :] <= query_ids[:, None]).astype(jnp.int32), axis=1)
    first = low[::QUERIES] // 16 * 16
    steps = (high[QUERIES - 1::QUERIES] - first + KEYS - 1) // KEYS
    return jnp.stack([first, steps]), low[None], high[None]


EPSILON = 1e-05
BF = jnp.bfloat16
F32 = jnp.float32


class Links:
    def __init__(self, mesh):
        self.dp = mesh.shape["dp"]
        self.tensor = mesh.shape["tensor"]
        self.planes = self.dp // 2

    def enter(self):
        place = lax.axis_index("dp")
        self.core = place % 2
        self.plane = place // 2
        self.chip = lax.axis_index("tensor")

    def move(self, value, target):
        pairs = []
        for place in range(self.dp):
            for chip in range(self.tensor):
                to = target(place // 2, place % 2, chip)
                if to is not None:
                    pairs.append((place * self.tensor + chip, (to[0] * 2 + to[1]) * self.tensor + to[2]))
        return lax.ppermute(value, ("dp", "tensor"), pairs)

    def other_core(self, value):
        return self.move(value, lambda plane, core, chip: (plane, 1 - core, chip))

    def across(self, value, step):
        return self.move(value, lambda plane, core, chip: (plane, core, chip ^ step))

    def plane_pair(self, value, step):
        return self.move(value, lambda plane, core, chip: (plane ^ step, core, chip))

    def slot(self, value, which):
        def target(plane, core, chip):
            step = 3 if which == 3 else which if plane % 2 == 0 else 3 - which
            return (plane, core, chip ^ step)

        return self.move(value, target)

    def gather_weight(self, own):
        first = self.slot(own, 1)
        diagonal = self.slot(first, 2)
        second = self.plane_pair(first, 1)
        return [own, first, second, diagonal]

    def plane_sum(self, parts, first):
        second = 3 - first
        near = self.slot(parts[first], first)
        passed = self.slot(parts[3], first)
        middle = (parts[second].astype(F32) + passed.astype(F32)).astype(BF)
        far = self.slot(middle, second)
        return parts[0].astype(F32) + near.astype(F32) + far.astype(F32)

    def line_sum(self, total):
        if self.planes % 4:
            low = total.astype(BF)
            step = 1
            while step < self.planes:
                low = (low.astype(F32) + self.plane_pair(low, step).astype(F32)).astype(BF)
                step *= 2
            return low
        inward = {0: 1, 3: 2}
        outward = {1: 0, 2: 3}
        middle = {1: 2, 2: 1}

        def along(table):
            def target(plane, core, chip):
                to = table.get(plane % 4)
                return None if to is None else (plane - plane % 4 + to, core, chip)

            return target

        low = (total + self.move(total.astype(BF), along(inward)).astype(F32)).astype(BF)
        low = (low.astype(F32) + self.move(low, along(middle)).astype(F32)).astype(BF)
        step = 4
        while step < self.planes:
            low = (low.astype(F32) + self.plane_pair(low, step).astype(F32)).astype(BF)
            step *= 2
        back = self.move(low, along(outward))
        inner = (self.plane % 4 == 1) | (self.plane % 4 == 2)
        return jnp.where(inner, low, back)

    def weight_total(self, parts, first):
        return self.line_sum(self.plane_sum(parts, first))

    def halves(self, mine, axis):
        theirs = self.other_core(mine)
        return jnp.where(
            self.core == 0,
            jnp.concatenate([mine, theirs], axis=axis),
            jnp.concatenate([theirs, mine], axis=axis),
        )

    def take_half(self, value, axis, which):
        size = value.shape[axis] // 2
        return lax.dynamic_slice_in_dim(value, which * size, size, axis)

    def swap_parts(self, parts):
        got = [lax.dynamic_index_in_dim(parts, self.chip, 0, keepdims=False)]
        for step in range(1, self.tensor):
            got.append(self.across(lax.dynamic_index_in_dim(parts, self.chip ^ step, 0, keepdims=False), step))
        got = jnp.stack(got)
        return jnp.stack(
            [lax.dynamic_index_in_dim(got, self.chip ^ at, 0, keepdims=False) for at in range(self.tensor)]
        )

    def to_row(self, value):
        keep = self.take_half(value, 1, self.core)
        theirs = self.other_core(self.take_half(value, 1, 1 - self.core))
        rows = jnp.where(self.core == 0, jnp.concatenate([keep, theirs]), jnp.concatenate([theirs, keep]))
        mine = self.swap_parts(rows)
        both = self.halves(mine[:, None], 1)
        return both.reshape(-1, value.shape[-1])

    def half_row(self, row):
        cut = row.reshape(self.tensor, 2, -1, row.shape[-1])
        return lax.dynamic_index_in_dim(cut, self.core, 1, keepdims=False)

    def other_half_row(self, row):
        cut = row.reshape(self.tensor, 2, -1, row.shape[-1])
        return lax.dynamic_index_in_dim(cut, 1 - self.core, 1, keepdims=False)

    def from_row(self, mine):
        rows = self.swap_parts(mine)
        keep = self.take_half(rows, 0, self.core)
        theirs = self.other_core(self.take_half(rows, 0, 1 - self.core))
        return jnp.where(
            self.core == 0,
            jnp.concatenate([keep, theirs], axis=1),
            jnp.concatenate([theirs, keep], axis=1),
        )

    def pair_sum(self, partial):
        low = lax.optimization_barrier(partial.astype(BF))
        return low.astype(F32) + self.other_core(low).astype(F32)

    def pair_sum_half(self, partial):
        low = lax.optimization_barrier(partial.astype(BF))
        return self.half_row(low).astype(F32) + self.other_core(self.other_half_row(low)).astype(F32)

    def chip_sum(self, value):
        for step in (1, 2):
            value = value + self.across(value, step)
        step = 1
        while step < self.planes:
            value = value + self.plane_pair(value, step)
            step *= 2
        return value

    def quarter_sum(self, parts):
        total = parts[0]
        for which in (1, 2, 3):
            total = total + self.slot(parts[which], which)
        step = 1
        while step < self.planes:
            total = total + self.plane_pair(total, step)
            step *= 2
        return total


def norm_stats(values):
    average = jnp.mean(values, axis=-1, keepdims=True)
    center = values - average
    inverse = lax.rsqrt(jnp.mean(center * center, axis=-1, keepdims=True) + EPSILON)
    return center * inverse, inverse


def norm_forward(values, gain, shift):
    unit, _ = norm_stats(values)
    return (unit * gain + shift).astype(BF)


def norm_backward(grad_in, values, gain):
    unit, inverse = norm_stats(values)
    scaled = grad_in * gain
    first_mean = jnp.mean(scaled, axis=-1, keepdims=True)
    second_mean = jnp.mean(scaled * unit, axis=-1, keepdims=True)
    grad_values = inverse * (scaled - first_mean - unit * second_mean)
    return grad_values, jnp.sum(grad_in * unit, axis=0), jnp.sum(grad_in, axis=0)


def cat(parts, axis):
    return jnp.concatenate(parts, axis=axis)


def cut_slots(value, axis):
    return jnp.split(value, 4, axis=axis)


class Net:
    def __init__(self, sems, local_sems):
        place = lax.axis_index("dp")
        chip = lax.axis_index("tensor")
        core, plane = place % 2, place // 2
        odd = plane % 2
        beside, over, corner = chip + 1 - 2 * (chip % 2), (chip + 2) % 4, 3 - chip
        self.chip, self.core_index, self.odd, self.plane = chip, core, odd, plane
        self.chips = (beside, over, corner)
        self.core = (plane * 2 + 1 - core, chip)
        self.first = (place, beside + odd * (over - beside))
        self.second = (place, over + odd * (beside - over))
        self.corner = (place, corner)
        self.near_plane = ((plane + 1 - 2 * odd) * 2 + core, chip)
        self.far_plane = ((plane + 2) % 4 * 2 + core, chip)
        self.sems, self.local_sems = sems, local_sems
        self.count = self.local_count = 0
        self.unsent, self.unmoved = [], []

    def meet(self):
        barrier = pltpu.get_barrier_semaphore()
        partners = (self.core, self.first, self.second, self.corner, self.near_plane, self.far_plane)
        for partner in partners:
            pl.semaphore_signal(barrier, inc=1, device_id=partner, device_id_type=pl.DeviceIdType.MESH)
        pl.semaphore_wait(barrier, len(partners))

    def send(self, source, target, device):
        copy = pltpu.make_async_remote_copy(
            src_ref=source,
            dst_ref=target,
            send_sem=self.sems.at[0, self.count],
            recv_sem=self.sems.at[1, self.count],
            device_id=device,
            device_id_type=pl.DeviceIdType.MESH,
        )
        self.count += 1
        copy.start()
        self.unsent.append(copy)
        return copy

    def move(self, source, target):
        copy = pltpu.make_async_copy(source, target, self.local_sems.at[self.local_count])
        self.local_count += 1
        copy.start()
        self.unmoved.append(copy)
        return copy

    def moved(self, copy):
        copy.wait()
        self.unmoved = [other for other in self.unmoved if other is not copy]

    def sent(self, copy):
        copy.wait_send()
        self.unsent = [other for other in self.unsent if other is not copy]

    def finish(self):
        for copy in self.unmoved:
            copy.wait()
        for copy in self.unsent:
            copy.wait_send()
        self.unsent, self.unmoved = [], []


def row_in(net, given, rows, row):
    core, chip = net.core_index, net.chip
    mine = pl.ds(2 * core, 2)
    swap = net.send(given.at[:, 1 - core], rows.at[mine], net.core)
    keep = net.move(given.at[:, core], rows.at[mine])
    yield
    net.moved(keep)
    swap.wait_recv()
    own = net.move(rows.at[chip], row.at[chip, core])
    sends = [
        net.send(rows.at[other], row.at[chip, core], (lax.axis_index("dp"), other)) for other in net.chips
    ]
    yield
    net.moved(own)
    shares = [net.send(row.at[chip, core], row.at[chip, core], net.core)]
    for other, copy in zip(net.chips, sends):
        copy.wait_recv()
        shares.append(net.send(row.at[other, core], row.at[other, core], net.core))
    yield
    for copy in shares:
        copy.wait_recv()


def row_out(net, pieces, rows, result):
    core, chip = net.core_index, net.chip
    own = net.move(pieces.at[chip], rows.at[chip])
    sends = [net.send(pieces.at[other], rows.at[chip], (lax.axis_index("dp"), other)) for other in net.chips]
    yield
    net.moved(own)
    for copy in sends:
        copy.wait_recv()
    keep = net.move(rows.at[pl.ds(2 * core, 2)], result.at[:, core])
    swap = net.send(rows.at[pl.ds(2 * (1 - core), 2)], result.at[:, core], net.core)
    yield
    swap.wait_recv()
    net.moved(keep)


class Gather:
    def __init__(self, net, own, slot, flip=False):
        self.net, self.slot = net, slot
        self.one, self.two = (2, 1) if flip else (1, 2)
        to_one, self.to_two = (net.second, net.first) if flip else (net.first, net.second)
        self.near = net.send(own, slot(self.one), to_one)
        self.own = net.move(own, slot(0))

    def relay(self):
        self.near.wait_recv()
        self.corner = self.net.send(self.slot(self.one), self.slot(3), self.to_two)
        self.other = self.net.send(self.slot(self.one), self.slot(self.two), self.net.near_plane)

    def finish(self):
        self.net.moved(self.own)
        self.corner.wait_recv()
        self.other.wait_recv()


ANY = pl.BlockSpec(memory_space=pl.ANY)
VM = pl.BlockSpec(memory_space=pltpu.VMEM)
SENDS = 112


def half_columns(net, weight, width):
    return weight.at[:, pl.ds(pl.multiple_of(net.core_index * width, width), width)]


def half_rows(net, weight, height):
    return weight.at[pl.ds(pl.multiple_of(net.core_index * height, height), height)]


def tile_rows(i, size=256):
    return pl.ds(pl.multiple_of(i * size, size), size)


def call_remote(kernel, ident, ins, in_specs, outs, out_specs, scratch, vmem=48, name=None):
    return pl.pallas_call(
        kernel,
        in_specs=in_specs,
        out_specs=out_specs,
        out_shape=outs,
        scratch_shapes=list(scratch) + [pltpu.SemaphoreType.DMA((2, SENDS)), pltpu.SemaphoreType.DMA((SENDS,))],
        compiler_params=pltpu.CompilerParams(
            collective_id=ident, has_side_effects=True, vmem_limit_bytes=vmem << 20
        ),
        name=name,
    )(*ins)


def begin_kernel(
    given, ids, bias, wq, wk, wv, wo, gain, shift,
    x_out, n_out, qkv_out, w_out, wo_out, ids_out, bias_out,
    rows, row, weights, normed, qkv, biases, sems, local_sems,
):
    net = Net(sems, local_sems)
    net.meet()
    core = net.core_index
    enter = row_in(net, given, rows, row)
    next(enter)
    ids_swap = net.send(ids, ids_out.at[pl.ds(2 * core, 2)], net.core)
    net.move(ids, ids_out.at[pl.ds(2 * core, 2)])
    bias_copies = [
        net.send(bias, biases.at[1], net.first),
        net.send(bias, biases.at[2], net.second),
        net.send(bias, biases.at[3], net.corner),
    ]
    bias_own = net.move(bias, biases.at[0])
    gathers = []
    for kind, weight in enumerate((wq, wk, wv)):
        slot = lambda s, kind=kind: weights.at[:, kind * 512 + s * 128:kind * 512 + s * 128 + 128]
        gathers.append(Gather(net, half_columns(net, weight, 128), slot, kind == 1))
    next(enter)
    gather_o = Gather(net, half_rows(net, wo, 128), lambda s: wo_out.at[pl.ds(s * 128, 128)], True)
    for gather in gathers:
        gather.relay()
    next(enter)
    gather_o.relay()
    for _ in enter:
        pass
    net.move(row, x_out)

    def norm(i, _):
        values = row[i].reshape(256, -1).astype(F32)
        normed[tile_rows(i)] = norm_forward(values, gain[...], shift[...])
        return 0

    lax.fori_loop(0, 4, norm, 0)
    net.move(normed, n_out)
    net.moved(bias_own)
    for copy in bias_copies:
        copy.wait_recv()
    net.move(biases, bias_out)
    for gather in gathers:
        gather.finish()
    net.move(weights, w_out)

    def project(i, _):
        tokens = normed[tile_rows(i)]
        for kind in range(3):
            cut = slice(kind * 512, kind * 512 + 512)
            value = dot(tokens, weights[:, cut], NN)
            if kind != 1:
                at = 0 if kind == 0 else 1
                value = value + jnp.concatenate([biases[s, at:at + 1] for s in range(4)], axis=1)
            qkv[tile_rows(i), cut] = value.astype(BF)
        return 0

    lax.fori_loop(0, 4, project, 0)
    net.move(qkv, qkv_out)
    gather_o.finish()
    ids_swap.wait_recv()
    net.finish()


def begin(given, ids, bias, wq, wk, wv, wo, gain, shift):
    length, width = 1024, given.shape[-1]
    shape = jax.ShapeDtypeStruct
    return call_remote(
        begin_kernel, 1,
        (given.reshape(2, 2, -1, width), ids, bias, wq, wk, wv, wo, gain[None], shift[None]),
        [ANY] * 7 + [VM] * 2,
        [
            shape((4, 2, 128, width), BF), shape((length, width), BF), shape((length, 1536), BF),
            shape((width, 1536), BF), shape((512, width), BF), shape((4, 16, 128), jnp.int32), shape((4, 8, 128), F32),
        ],
        [ANY] * 7,
        [
            pltpu.VMEM((4, 128, width), BF), pltpu.VMEM((4, 2, 128, width), BF), pltpu.VMEM((width, 1536), BF),
            pltpu.VMEM((length, width), BF), pltpu.VMEM((length, 1536), BF), pltpu.VMEM((4, 8, 128), F32),
        ],
        name="begin",
    )


def middle_kernel(
    att, x, wo, bias_o, gain, shift, given, wcq, wck, wcv, wco, bias_in,
    h_out, n_out, q_out, kv_out, mem_out, w_out, wco_out,
    att_vm, x_vm, wo_vm, part, part_in, hidden, normed, rows, row, weights, queries, keys, biases, sems, local_sems,
):
    net = Net(sems, local_sems)
    loads = [net.move(att, att_vm), net.move(wo, wo_vm), net.move(x, x_vm), net.move(bias_in, biases)]
    net.meet()
    enter = row_in(net, given, rows, row)
    next(enter)
    gathers = []
    for kind, weight in ((1, wck), (2, wcv), (0, wcq)):
        slot = lambda s, kind=kind: weights.at[:, kind * 512 + s * 128:kind * 512 + s * 128 + 128]
        gathers.append(Gather(net, half_columns(net, weight, 128), slot, kind == 2))
    gathers.append(Gather(net, half_rows(net, wco, 128), lambda s: wco_out.at[pl.ds(s * 128, 128)], True))
    for copy in loads:
        net.moved(copy)
    swaps = []
    for i in range(4):
        part[i] = dot(att_vm[i * 256:i * 256 + 256], wo_vm[...], NN).astype(BF)
        swaps.append(net.send(part.at[i], part_in.at[i], net.core))
        if i == 1:
            next(enter)
    for i in range(4):
        swaps[i].wait_recv()
        rows_i = slice(i * 256, i * 256 + 256)
        value = x_vm[i].reshape(256, -1).astype(F32) + part[i].astype(F32) + part_in[i].astype(F32) + bias_o[...]
        hidden[rows_i] = value
        normed[rows_i] = norm_forward(value, gain[...], shift[...])
        if i == 1:
            gathers[0].relay()
            gathers[1].relay()
    net.move(hidden, h_out)
    net.move(normed, n_out)
    next(enter)
    gathers[2].relay()
    gathers[3].relay()
    for _ in enter:
        pass
    net.move(row, mem_out)
    for gather in gathers[:3]:
        gather.finish()
    net.move(weights, w_out)
    values_bias = jnp.concatenate([biases[s, 3:4] for s in range(4)], axis=1)
    query_bias = jnp.concatenate([biases[s, 2:3] for s in range(4)], axis=1)

    def project(i, _):
        tokens = row[i].reshape(256, -1)
        keys[tile_rows(i), :512] = dot(tokens, weights[:, 512:1024], NN).astype(BF)
        keys[tile_rows(i), 512:] = (dot(tokens, weights[:, 1024:], NN) + values_bias).astype(BF)
        queries[tile_rows(i)] = (dot(normed[tile_rows(i)], weights[:, :512], NN) + query_bias).astype(BF)
        return 0

    lax.fori_loop(0, 4, project, 0)
    net.move(keys, kv_out)
    net.move(queries, q_out)
    gathers[3].finish()
    net.finish()


def middle(att, x, wo, bias_o, gain, shift, given, wcq, wck, wcv, wco, bias_in):
    length, width = att.shape[0], given.shape[-1]
    shape = jax.ShapeDtypeStruct
    return call_remote(
        middle_kernel, 2,
        (att, x, wo, bias_o[None], gain[None], shift[None], given.reshape(2, 2, -1, width), wcq, wck, wcv, wco, bias_in),
        [ANY] * 3 + [VM] * 3 + [ANY] * 6,
        [
            shape((length, width), F32), shape((length, width), BF), shape((length, 512), BF),
            shape((length, 1024), BF), shape((4, 2, 128, width), BF), shape((width, 1536), BF), shape((512, width), BF),
        ],
        [ANY] * 7,
        [
            pltpu.VMEM((length, 512), BF), pltpu.VMEM((4, 2, 128, width), BF), pltpu.VMEM((512, width), BF),
            pltpu.VMEM((4, 256, width), BF), pltpu.VMEM((4, 256, width), BF), pltpu.VMEM((length, width), F32),
            pltpu.VMEM((length, width), BF), pltpu.VMEM((4, 128, width), BF), pltpu.VMEM((4, 2, 128, width), BF),
            pltpu.VMEM((width, 1536), BF), pltpu.VMEM((length, 512), BF), pltpu.VMEM((length, 1024), BF),
            pltpu.VMEM((4, 8, 128), F32),
        ],
        name="middle",
    )


def add_up(target, sources, step=64):
    def some(i, _):
        cut = pl.ds(pl.multiple_of(i * step, step), step)
        total = sources[0][cut].astype(F32)
        for source in sources[1:]:
            total = total + source[cut].astype(F32)
        target[cut] = total.astype(BF)
        return 0

    lax.fori_loop(0, target.shape[0] // step, some, 0)


class Line:
    def __init__(self, net, total, landing, result):
        self.net, self.total, self.result = net, total, result
        self.one_in, self.two_in = landing
        self.size = self.one_in.shape[0]

    def half(self, which):
        return self.total.at[pl.ds(pl.multiple_of(which * self.size, self.size), self.size)]

    def line0(self):
        self.line = self.net.send(self.half(1 - self.net.odd), self.one_in, self.net.near_plane)

    def line1(self):
        self.line.wait_recv()
        mine = self.half(self.net.odd)
        add_up(mine, [mine, self.one_in])
        self.line = self.net.send(mine, self.two_in, self.net.far_plane)

    def line2(self):
        self.line.wait_recv()
        place = self.result(self.net.core_index, self.net.odd)
        add_up(place, [self.half(self.net.odd), self.two_in])
        self.line = self.net.send(place, place, self.net.near_plane)
        self.cores = [self.net.send(place, place, self.net.core)]

    def line3(self):
        self.line.wait_recv()
        place = self.result(self.net.core_index, 1 - self.net.odd)
        self.cores.append(self.net.send(place, place, self.net.core))

    def end(self):
        for copy in self.cores:
            copy.wait_recv()


class Scatter:
    def __init__(self, net, part, first, landing):
        self.net, self.part = net, part
        self.near_in, self.pass_in, self.far_in = landing
        self.one, self.two = (1, 2) if first == 1 else (2, 1)
        self.to_one, self.to_two = (net.first, net.second) if first == 1 else (net.second, net.first)

    def start(self):
        self.passed = self.net.send(self.part(3), self.pass_in, self.to_one)
        self.near = self.net.send(self.part(self.one), self.near_in, self.to_one)

    def middle(self):
        self.passed.wait_recv()
        add_up(self.part(self.two), [self.part(self.two), self.pass_in])
        self.far = self.net.send(self.part(self.two), self.far_in, self.to_two)

    def own(self):
        self.near.wait_recv()
        self.far.wait_recv()
        add_up(self.part(0), [self.part(0), self.near_in, self.far_in])


def landing(rows, columns):
    return [pltpu.VMEM((rows, columns), BF)] * 3


def line_landing(rows, columns):
    return [pltpu.VMEM((rows // 2, columns), BF)] * 2


def staggered(items, steps):
    calls = []
    for at in range(len(steps) + len(items) - 1):
        for place, item in enumerate(items):
            if 0 <= at - place < len(steps):
                calls.append(getattr(item, steps[at - place]))
    return calls


def weight_grad(lhs, rhs, target, start, count, columns=slice(None), size=256):
    def some(i, _):
        cut = pl.ds(pl.multiple_of(start + i * size, size), size)
        target[cut, columns] = dot(lhs[:, cut], rhs(), TN).astype(BF)
        return 0

    lax.fori_loop(0, count // size, some, 0)


def norm_back_tile(grad_in, values, gain):
    unit, inverse = norm_stats(values)
    scaled = grad_in * gain
    first_mean = jnp.mean(scaled, axis=-1, keepdims=True)
    second_mean = jnp.mean(scaled * unit, axis=-1, keepdims=True)
    grad_values = inverse * (scaled - first_mean - unit * second_mean)
    return grad_values, jnp.sum(grad_in * unit, axis=0, keepdims=True), jnp.sum(grad_in, axis=0, keepdims=True)


def feed_kernel(
    att, h_in, wco, given, inner, outer, bias_in, bias_c, gain, shift, bias_u,
    block_out, gh_out, gatt_out, outer_out, inner_out, sums_out, split_out,
    att_vm, wco_vm, hidden, part, part_in, back_in, out_in, normed, rows, row, wi, wu, act, slope, g_outer,
    g_inner, biases, sums, split, gatt, pieces, rows_back, full_outer, *rest,
):
    lands, (sems, local_sems) = rest[:-2], rest[-2:]
    net = Net(sems, local_sems)
    core = net.core_index
    loads = [net.move(att, att_vm), net.move(wco, wco_vm), net.move(h_in, hidden), net.move(bias_in, biases)]
    net.meet()
    enter = row_in(net, given, rows, row)
    next(enter)

    def gather_inner(k):
        own = inner.at[pl.ds(k * 512, 512), pl.ds(pl.multiple_of(core * 512, 512), 512)]
        return Gather(net, own, lambda s: wi.at[pl.ds(k * 512, 512), s * 512:s * 512 + 512], k == 1)

    def gather_outer(k):
        own = outer.at[pl.ds(pl.multiple_of(core * 512 + k * 256, 256), 256)]
        return Gather(net, own, lambda s: wu.at[pl.ds(s * 512 + k * 256, 256)], k == 1)

    gathers = [gather_inner(0), gather_inner(1)]
    for copy in loads:
        net.moved(copy)
    swaps = []
    for i in range(4):
        value = dot(att_vm[i * 256:i * 256 + 256], wco_vm[...], NN)
        part[i] = value.astype(BF).reshape(2, 128, -1)
        swaps.append(net.send(part.at[i], part_in.at[i], net.core))
    next(enter)
    for i in range(4):
        swaps[i].wait_recv()
        value = hidden[i] + part[i].astype(F32) + part_in[i].astype(F32) + bias_c[...][None]
        hidden[i] = value
        normed[i * 256:i * 256 + 256] = norm_forward(value.reshape(256, -1), gain[...], shift[...])
    gathers[0].relay()
    gathers.append(gather_outer(0))
    next(enter)
    gathers[1].relay()
    gathers.append(gather_outer(1))
    for _ in enter:
        pass
    gathers[0].finish()
    gathers[1].finish()

    def feed(i, _):
        tokens = normed[tile_rows(i)]
        for s in range(4):
            cut = slice(s * 512, s * 512 + 512)
            bias = jnp.concatenate([biases[s, 4 + k:5 + k] for k in range(4)], axis=1)
            pre = dot(tokens, wi[:, cut], NN) + bias
            sigmoid = jax.nn.sigmoid(pre)
            act[tile_rows(i), cut] = (pre * sigmoid).astype(BF)
            slope[tile_rows(i), cut] = (sigmoid * (1.0 + pre * (1.0 - sigmoid))).astype(BF)
        return 0

    lax.fori_loop(0, 2, feed, 0)
    gathers[2].relay()
    lax.fori_loop(2, 4, feed, 0)
    whole_row = lambda: row[...].reshape(1024, -1)
    outers = [
        Scatter(net, lambda s, k=k: g_outer.at[pl.ds(s * 512 + k * 256, 256)], 1 + k, lands[k * 3:k * 3 + 3])
        for k in range(2)
    ]
    outer_lines = [
        Line(
            net, g_outer.at[pl.ds(k * 256, 256)], lands[12 + k * 2:14 + k * 2],
            lambda c, h, k=k: full_outer.at[pl.ds(pl.multiple_of(c * 512 + k * 256 + h * 128, 128), 128)],
        )
        for k in range(2)
    ]
    inners = [
        Scatter(
            net, lambda s, k=k: g_inner.at[pl.ds(k * 512, 512), s * 512:s * 512 + 512], 1 + k,
            lands[6 + k * 3:9 + k * 3],
        )
        for k in range(2)
    ]

    def outer_grad(k, s):
        weight_grad(act, whole_row, g_outer, s * 512 + k * 256, 256)

    def inner_grad(k, s):
        cut = slice(s * 512, s * 512 + 512)
        weight_grad(normed, lambda: slope[:, cut], g_inner, k * 512, 512, cut)

    for k in range(2):
        outer_grad(k, 3)
        outer_grad(k, 1 + k)
        outers[k].start()
    gathers[3].relay()
    for k in range(2):
        outer_grad(k, 2 - k)
        outer_grad(k, 0)
    gathers[2].finish()
    gathers[3].finish()
    split[...] = jnp.zeros_like(split)
    sums[...] = jnp.zeros_like(sums)

    def feed_back(i, _):
        tokens = row[i].reshape(256, -1)
        for s in range(4):
            cut = slice(s * 512, s * 512 + 512)
            value = (dot(tokens, wu[cut], NT) * slope[tile_rows(i), cut].astype(F32)).astype(BF)
            slope[tile_rows(i), cut] = value
            split[0:1, cut] += jnp.sum(value.astype(F32), axis=0, keepdims=True)
        return 0

    lax.fori_loop(0, 4, feed_back, 0)
    for k in range(2):
        inner_grad(k, 3)
        inner_grad(k, 1 + k)
        inners[k].start()
    for copy in swaps:
        net.sent(copy)
    swaps = []
    for i in range(4):
        value = dot(slope[i * 256:i * 256 + 256], wi[...], NT)
        part[i] = value.astype(BF).reshape(2, 128, -1)
        swaps.append(net.send(part.at[i], back_in.at[i], net.core))
    outers[0].middle()
    outers[1].middle()

    def feed_out(i, _):
        part_in[i] = dot(act[tile_rows(i)], wu[...], NN).astype(BF).reshape(2, 128, -1)
        return 0

    lax.fori_loop(0, 4, feed_out, 0)
    out_swap = net.send(part_in.at[:, 1 - core], out_in, net.core)
    for k in range(2):
        inner_grad(k, 2 - k)
        inner_grad(k, 0)
    out_swap.wait_recv()
    for i in range(4):
        pieces[i] = (hidden[i, core] + part_in[i, core].astype(F32) + out_in[i].astype(F32) + bias_u[...]).astype(BF)
    leave = row_out(net, pieces, rows_back, block_out)
    next(leave)
    outers[0].own()
    outer_lines[0].line0()
    outers[1].own()
    outer_lines[1].line0()
    for copy in swaps:
        copy.wait_recv()

    def back(i, _):
        grad = (part[i].astype(F32) + back_in[i].astype(F32)).reshape(256, -1)
        change, by_gain, by_shift = norm_back_tile(grad, hidden[i].reshape(256, -1), gain[...])
        top = row[i].reshape(256, -1).astype(F32)
        value = top + change
        hidden[i] = value.reshape(2, 128, -1)
        gatt[tile_rows(i)] = dot(value.astype(BF), wco_vm[...], NT).astype(BF)
        sums[0:1] += by_gain
        sums[1:2] += by_shift
        sums[2:3] += jnp.sum(top, axis=0, keepdims=True)
        sums[3:4] += jnp.sum(value, axis=0, keepdims=True)
        return 0

    lax.fori_loop(0, 4, back, 0)
    net.move(hidden, gh_out)
    net.move(gatt, gatt_out)
    net.move(sums, sums_out)
    net.move(split, split_out)
    inners[0].middle()
    outer_lines[0].line1()
    inners[1].middle()
    outer_lines[1].line1()
    next(leave)
    outer_lines[0].line2()
    outer_lines[1].line2()
    inners[0].own()
    net.move(g_inner.at[pl.ds(0, 512), :512], inner_out.at[pl.ds(0, 512)])
    outer_lines[0].line3()
    inners[1].own()
    net.move(g_inner.at[pl.ds(512, 512), :512], inner_out.at[pl.ds(512, 512)])
    outer_lines[1].line3()
    for line in outer_lines:
        line.end()
    net.move(full_outer, outer_out)
    for _ in leave:
        pass
    net.finish()


def feed(att, hidden, wco, given, inner, outer, bias_in, bias_c, gain, shift, bias_u):
    length, width = att.shape[0], given.shape[-1]
    shape = jax.ShapeDtypeStruct
    quarters = (4, 2, 128, width)
    block, gh, gatt, g_outer, g_inner, sums, split = call_remote(
        feed_kernel, 3,
        (
            att, hidden.reshape(quarters), wco, given.reshape(2, 2, -1, width), inner, outer, bias_in,
            bias_c[None], gain[None], shift[None], bias_u[None],
        ),
        [ANY] * 7 + [VM] * 4,
        [
            shape((2, 2, 128, width), BF), shape(quarters, F32), shape((length, 512), BF),
            shape((1024, width), BF), shape((width, 512), BF), shape((8, width), F32), shape((8, 2048), F32),
        ],
        [ANY] * 7,
        [
            pltpu.VMEM((length, 512), BF), pltpu.VMEM((512, width), BF), pltpu.VMEM(quarters, F32),
            pltpu.VMEM(quarters, BF), pltpu.VMEM(quarters, BF), pltpu.VMEM(quarters, BF), pltpu.VMEM((4, 128, width), BF),
            pltpu.VMEM((length, width), BF), pltpu.VMEM((4, 128, width), BF), pltpu.VMEM(quarters, BF),
            pltpu.VMEM((width, 2048), BF), pltpu.VMEM((2048, width), BF),
            pltpu.VMEM((length, 2048), BF), pltpu.VMEM((length, 2048), BF), pltpu.VMEM((2048, width), BF),
            pltpu.VMEM((width, 2048), BF), pltpu.VMEM((4, 8, 128), F32), pltpu.VMEM((8, width), F32), pltpu.VMEM((8, 2048), F32),
            pltpu.VMEM((length, 512), BF), pltpu.VMEM((4, 128, width), BF), pltpu.VMEM((4, 128, width), BF),
            pltpu.VMEM((1024, width), BF),
        ]
        + landing(256, width) * 2 + landing(512, 512) * 2 + line_landing(256, width) * 2,
        vmem=62, name="feed",
    )
    return block.reshape(given.shape), gh.reshape(hidden.shape), gatt, g_outer, g_inner, sums, split[0]


def head_scatters(net, g_heads, g_out, lands):
    found = []
    for kind in range(3):
        found.append(
            Scatter(
                net, lambda s, kind=kind: g_heads.at[:, kind * 512 + s * 128:kind * 512 + s * 128 + 128],
                (1, 1, 2)[kind], lands[kind * 3:kind * 3 + 3],
            )
        )
    found.append(Scatter(net, lambda s: g_out.at[pl.ds(s * 128, 128)], 2, lands[9:12]))
    return found


def head_lines(net, totals, total_out, full_heads, full_out, lands):
    lines = []
    for kind in range(3):
        lines.append(
            Line(
                net, totals(kind), lands[kind * 2:kind * 2 + 2],
                lambda c, h, kind=kind: full_heads.at[
                    kind, pl.ds(pl.multiple_of(h * 512, 512), 512), pl.ds(pl.multiple_of(c * 128, 128), 128)
                ],
            )
        )
    lines.append(
        Line(
            net, total_out, lands[6:8],
            lambda c, h: full_out.at[pl.ds(pl.multiple_of(c * 128 + h * 64, 64), 64)],
        )
    )
    return lines


def cross_kernel(
    dq, dk, dv, n_in, mem, att, gh_in, h_in, wc, wo, inner_in, gain,
    mem_out, gh_out, gatt_out, heads_out, o_out, inner_out, sums_out, split_out,
    dq_vm, dk_vm, dv_vm, normed, tokens, att_vm, grads, hidden, weights, wo_vm,
    part, part_in, mem_part, mem_in, pieces, rows_back, g_heads, g_out, inner_total, full_inner, gatt, sums, split, *rest,
):
    lands, (sems, local_sems) = rest[:-2], rest[-2:]
    net = Net(sems, local_sems)
    core = net.core_index
    loads = [
        net.move(source, target)
        for source, target in (
            (dq, dq_vm), (wc, weights), (mem, tokens), (dk, dk_vm), (dv, dv_vm), (n_in, normed), (att, att_vm),
            (gh_in, grads), (h_in, hidden), (wo, wo_vm),
        )
    ]
    inner_load = net.move(inner_in, inner_total)
    net.meet()
    for copy in loads[:2]:
        net.moved(copy)
    lines = [
        Line(
            net, inner_total.at[pl.ds(k * 512, 512)], lands[12 + k * 2:14 + k * 2],
            lambda c, h, k=k: full_inner.at[
                pl.ds(pl.multiple_of(k * 512 + h * 256, 256), 256), pl.ds(pl.multiple_of(c * 512, 512), 512)
            ],
        )
        for k in range(2)
    ]
    swaps = []
    for i in range(4):
        value = dot(dq_vm[i * 256:i * 256 + 256], weights[:, :512], NT)
        part[i] = value.astype(BF).reshape(2, 128, -1)
        swaps.append(net.send(part.at[i], part_in.at[i], net.core))
    for copy in loads[2:] + [inner_load]:
        net.moved(copy)
    lines[0].line0()
    lines[1].line0()
    scatters = head_scatters(net, g_heads, g_out, lands)
    weight_grad(tokens, lambda: dk_vm[...], g_heads, 0, 1024, slice(512, 1024))
    scatters[1].start()
    weight_grad(tokens, lambda: dv_vm[...], g_heads, 0, 1024, slice(1024, 1536))
    scatters[2].start()
    for i in range(4):
        cut = slice(i * 256, i * 256 + 256)
        value = dot(dk_vm[cut], weights[:, 512:1024], NT) + dot(dv_vm[cut], weights[:, 1024:], NT)
        mem_part[i] = value.astype(BF).reshape(2, 128, -1)
    mem_swap = net.send(mem_part.at[:, 1 - core], mem_in, net.core)
    weight_grad(normed, lambda: dq_vm[...], g_heads, 0, 1024, slice(0, 512))
    scatters[0].start()
    weight_grad(att_vm, lambda: grads[...].reshape(1024, -1).astype(BF), g_out, 0, 512)
    scatters[3].start()
    lines[0].line1()
    lines[1].line1()
    mem_swap.wait_recv()
    for i in range(4):
        pieces[i] = (mem_part[i, core].astype(F32) + mem_in[i].astype(F32)).astype(BF)
    leave = row_out(net, pieces, rows_back, mem_out)
    next(leave)
    scatters[1].middle()
    scatters[2].middle()
    for copy in swaps:
        copy.wait_recv()
    sums[...] = jnp.zeros_like(sums)
    split[...] = jnp.zeros_like(split)
    split[0:1, :512] = jnp.sum(dq_vm[...].astype(F32), axis=0, keepdims=True)
    split[0:1, 512:] = jnp.sum(dv_vm[...].astype(F32), axis=0, keepdims=True)

    def back(i, _):
        grad = (part[i].astype(F32) + part_in[i].astype(F32)).reshape(256, -1)
        change, by_gain, by_shift = norm_back_tile(grad, hidden[i].reshape(256, -1), gain[...])
        value = grads[i].reshape(256, -1) + change
        grads[i] = value.reshape(2, 128, -1)
        gatt[tile_rows(i)] = dot(value.astype(BF), wo_vm[...], NT).astype(BF)
        sums[0:1] += by_gain
        sums[1:2] += by_shift
        sums[2:3] += jnp.sum(value, axis=0, keepdims=True)
        return 0

    lax.fori_loop(0, 4, back, 0)
    net.move(grads, gh_out)
    net.move(gatt, gatt_out)
    net.move(sums, sums_out)
    net.move(split, split_out)
    lines[0].line2()
    lines[1].line2()
    scatters[0].middle()
    scatters[3].middle()
    next(leave)
    lines[0].line3()
    lines[1].line3()
    for kind in (1, 2, 0):
        scatters[kind].own()
        net.move(g_heads.at[:, kind * 512:kind * 512 + 128], heads_out.at[kind])
    scatters[3].own()
    net.move(g_out.at[pl.ds(0, 128)], o_out)
    for line in lines:
        line.end()
    net.move(full_inner, inner_out)
    for _ in leave:
        pass
    net.finish()


def head_landing(width):
    return landing(1024, 128) * 3 + landing(128, width)


def head_line_landing(width):
    return line_landing(1024, 128) * 3 + line_landing(128, width)


def cross(dq, dk, dv, n, mem, att, gh, hidden, wc, wo, inner_total, gain):
    length, width = dq.shape[0], n.shape[-1]
    shape = jax.ShapeDtypeStruct
    quarters = (4, 2, 128, width)
    mem_grad, gh, gatt, heads, out, g_inner, sums, split = call_remote(
        cross_kernel, 4,
        (
            dq, dk, dv, n, mem.reshape(length, width), att, gh.reshape(quarters), hidden.reshape(quarters), wc, wo,
            inner_total, gain[None],
        ),
        [ANY] * 11 + [VM],
        [
            shape((2, 2, 128, width), BF), shape(quarters, F32), shape((length, 512), BF),
            shape((3, width, 128), BF), shape((128, width), BF), shape((width, 1024), BF),
            shape((8, width), F32), shape((8, 1024), F32),
        ],
        [ANY] * 8,
        [pltpu.VMEM((length, 512), BF)] * 3
        + [
            pltpu.VMEM((length, width), BF), pltpu.VMEM((length, width), BF), pltpu.VMEM((length, 512), BF),
            pltpu.VMEM(quarters, F32), pltpu.VMEM(quarters, F32), pltpu.VMEM((width, 1536), BF),
            pltpu.VMEM((512, width), BF), pltpu.VMEM(quarters, BF), pltpu.VMEM(quarters, BF),
            pltpu.VMEM(quarters, BF), pltpu.VMEM((4, 128, width), BF), pltpu.VMEM((4, 128, width), BF),
            pltpu.VMEM((4, 128, width), BF), pltpu.VMEM((width, 1536), BF), pltpu.VMEM((512, width), BF),
            pltpu.VMEM((width, 512), BF), pltpu.VMEM((width, 1024), BF), pltpu.VMEM((length, 512), BF),
            pltpu.VMEM((8, width), F32), pltpu.VMEM((8, 1024), F32),
        ]
        + head_landing(width) + line_landing(512, 512) * 2,
        vmem=60, name="cross",
    )
    return mem_grad.reshape(2, -1, width), gh, gatt, heads, out, g_inner, sums, split[0]


def end_kernel(
    dq, dk, dv, n_in, att, gh_in, x_in, wqkv, gain, shared_in, split_in, cross_heads, cross_o,
    grad_out, heads_out, o_out, cross_out, cross_o_out, shared_out, late_out, split_out,
    dqkv, normed, att_vm, grads, values, weights, part, part_in, pieces, rows_back,
    g_heads, g_out, full_heads, full_out, heads_total, o_total, cross_full, cross_full_o,
    shared, shared_land, late, late_land, split, split_land, split_full, *rest,
):
    lands, (sems, local_sems) = rest[:-2], rest[-2:]
    net = Net(sems, local_sems)
    core, chip = net.core_index, net.chip
    place = lax.axis_index("dp")
    loads = [
        net.move(source, target)
        for source, target in (
            (dq, dqkv.at[:, :512]), (dk, dqkv.at[:, 512:1024]), (dv, dqkv.at[:, 1024:]), (wqkv, weights), (n_in, normed),
            (cross_heads, heads_total), (cross_o, o_total),
            (att, att_vm), (gh_in, grads), (x_in, values), (shared_in, shared), (split_in, split),
        )
    ]
    net.meet()
    for copy in loads[:4]:
        net.moved(copy)

    def back(i, _):
        value = dot(dqkv[tile_rows(i)], weights[...], NT)
        part[i] = value.astype(BF).reshape(2, 128, -1)
        return 0

    lax.fori_loop(0, 4, back, 0)
    swap = net.send(part.at[:, 1 - core], part_in, net.core)
    for copy in loads[4:]:
        net.moved(copy)
    stages = [(place, net.chips[0]), (place, net.chips[1]), net.near_plane, net.far_plane]
    shared_copy = net.send(shared, shared_land.at[0], stages[0])
    scatters = head_scatters(net, g_heads, g_out, lands[:12])
    lines = head_lines(
        net, lambda kind: g_heads.at[:, kind * 512:kind * 512 + 128], g_out.at[pl.ds(0, 128)], full_heads, full_out,
        lands[12:20],
    )
    cross_lines = head_lines(net, lambda kind: heads_total.at[kind], o_total, cross_full, cross_full_o, lands[20:28])
    for line in cross_lines:
        line.line0()
    for kind in (0, 2, 1):
        cut = slice(kind * 512, kind * 512 + 512)
        weight_grad(normed, lambda: dqkv[:, cut], g_heads, 0, 1024, cut)
        scatters[kind].start()
        if kind == 0:
            swap.wait_recv()
            late[...] = jnp.zeros_like(late)
            for i in range(4):
                grad = part[i, core].astype(F32) + part_in[i].astype(F32)
                change, by_gain, by_shift = norm_back_tile(grad, values[i, core].astype(F32), gain[...])
                pieces[i] = (grads[i, core] + change).astype(BF)
                late[0:1] += by_gain
                late[1:2] += by_shift
            leave = row_out(net, pieces, rows_back, grad_out)
            next(leave)
            late_copy = net.send(late, late_land.at[0], net.core)
    weight_grad(att_vm, lambda: grads[...].reshape(1024, -1).astype(BF), g_out, 0, 512)
    scatters[3].start()
    for line in cross_lines:
        line.line1()
    for at, kind in ((0, 0), (1, 2)):
        total = jnp.sum(dqkv[:, kind * 512:kind * 512 + 512].astype(F32), axis=0, keepdims=True)
        for s in range(4):
            split[s, at:at + 1] = total[:, s * 128:s * 128 + 128]
    split_copies = [
        net.send(split.at[s], split_land.at[s - 1], device)
        for s, device in ((1, net.first), (2, net.second), (3, net.corner))
    ]

    def shared_stage(at):
        def step():
            nonlocal shared_copy
            shared_copy.wait_recv()
            net.sent(shared_copy)
            shared[...] += shared_land[at]
            if at < 3:
                shared_copy = net.send(shared, shared_land.at[at + 1], stages[at + 1])

        return step

    def late_stage(at):
        def step():
            nonlocal late_copy
            late_copy.wait_recv()
            net.sent(late_copy)
            late[...] += late_land[at]
            if at < 4:
                late_copy = net.send(late, late_land.at[at + 1], stages[at])

        return step

    def split_stage(at):
        def step():
            nonlocal split_copies
            for copy in split_copies:
                copy.wait_recv()
                net.sent(copy)
            if at == 0:
                split[0] = split[0] + split_land[0] + split_land[1] + split_land[2]
            else:
                split[0] = split[0] + split_land[2 + at]
            if at < 2:
                device = (net.near_plane, net.far_plane)[at]
                split_copies = [net.send(split.at[0], split_land.at[3 + at], device)]
            else:
                split_full[core] = split[0]
                split_copies = [net.send(split_full.at[core], split_full.at[core], net.core)]

        return step

    def calls(items, step):
        for item in items:
            getattr(item, step)()

    scatters[0].middle()
    scatters[2].middle()
    shared_stage(0)()
    late_stage(0)()
    split_stage(0)()
    next(leave)
    scatters[1].middle()
    scatters[3].middle()
    calls(cross_lines, "line2")
    shared_stage(1)()
    late_stage(1)()
    for kind in (0, 2):
        scatters[kind].own()
        lines[kind].line0()
    late_stage(2)()
    split_stage(1)()
    calls(cross_lines, "line3")
    for kind in (1, 3):
        scatters[kind].own()
        lines[kind].line0()
    shared_stage(2)()
    late_stage(3)()
    lines[0].line1()
    lines[2].line1()
    lines[1].line1()
    lines[3].line1()
    shared_stage(3)()
    late_stage(4)()
    split_stage(2)()
    for step in ("line2", "line3", "end"):
        for kind in (0, 2, 1, 3):
            getattr(lines[kind], step)()
    calls(cross_lines, "end")
    net.move(cross_full, cross_out)
    net.move(cross_full_o, cross_o_out)
    for _ in leave:
        pass
    split_copies[0].wait_recv()
    net.move(full_heads, heads_out)
    net.move(full_out, o_out)
    net.move(shared, shared_out)
    net.move(late, late_out)
    net.move(split_full, split_out)
    net.finish()


def end(dq, dk, dv, n, att, gh, x, wqkv, gain, shared, split, cross_heads, cross_o):
    length, width = dq.shape[0], n.shape[-1]
    shape = jax.ShapeDtypeStruct
    quarters = (4, 2, 128, width)
    heads = [shape((3, width, 256), BF), shape((256, width), BF)]
    grad, *others = call_remote(
        end_kernel, 5,
        (dq, dk, dv, n, att, gh, x, wqkv, gain[None], shared, split, cross_heads, cross_o),
        [ANY] * 8 + [VM] + [ANY] * 4,
        [shape((2, 2, 128, width), BF)] + heads + heads
        + [shape((8, width), F32), shape((8, width), F32), shape((2, 8, 128), F32)],
        [ANY] * 8,
        [
            pltpu.VMEM((length, 1536), BF), pltpu.VMEM((length, width), BF), pltpu.VMEM((length, 512), BF),
            pltpu.VMEM(quarters, F32), pltpu.VMEM(quarters, BF), pltpu.VMEM((width, 1536), BF),
            pltpu.VMEM(quarters, BF), pltpu.VMEM((4, 128, width), BF), pltpu.VMEM((4, 128, width), BF),
            pltpu.VMEM((4, 128, width), BF), pltpu.VMEM((width, 1536), BF), pltpu.VMEM((512, width), BF),
            pltpu.VMEM((3, width, 256), BF), pltpu.VMEM((256, width), BF),
            pltpu.VMEM((3, width, 128), BF), pltpu.VMEM((128, width), BF),
            pltpu.VMEM((3, width, 256), BF), pltpu.VMEM((256, width), BF),
            pltpu.VMEM((8, width), F32), pltpu.VMEM((4, 8, width), F32),
            pltpu.VMEM((8, width), F32), pltpu.VMEM((5, 8, width), F32),
            pltpu.VMEM((4, 8, 128), F32), pltpu.VMEM((5, 8, 128), F32), pltpu.VMEM((2, 8, 128), F32),
        ]
        + head_landing(width) + head_line_landing(width) * 2,
        vmem=60, name="end",
    )
    return [grad.reshape(2, -1, width)] + others


def solution(mesh):
    if mesh.shape["tensor"] != 4 or mesh.shape["dp"] != 8:
        return general_solution(mesh)
    links = Links(mesh)

    def local(
        layer_input, memory, grad_out, target_segments, source_segments,
        self_gain, self_shift, query_weight, query_bias, key_weight, value_weight, value_bias,
        attend_weight, attend_bias,
        cross_gain, cross_shift, cross_query, cross_query_bias, cross_key, cross_value, cross_value_bias,
        cross_attend, cross_attend_bias,
        feed_gain, feed_shift, inner_weight, inner_bias, outer_weight, outer_bias,
    ):
        links.enter()
        core, chip = links.core, links.chip
        columns = lambda w: links.take_half(w, 1, core)
        rows = lambda w: links.take_half(w, 0, core)

        head, unit = 128, 512
        ids = jnp.stack([target_segments, source_segments], axis=1).reshape(2, 16, 128)
        biases = cat([rows(b) for b in (query_bias, value_bias, cross_query_bias, cross_value_bias, inner_bias)], 0)
        x_row, n1, qkv1, wqkv, wo, row_ids, bias_slots = begin(
            layer_input, ids, biases.reshape(8, 128), query_weight, key_weight, value_weight, attend_weight,
            self_gain, self_shift,
        )
        inputs = x_row.reshape(1024, 1024).astype(F32)
        row_ids = lax.dynamic_index_in_dim(row_ids, chip, 0, keepdims=False).reshape(2, 1024)
        target_ids, source_ids = row_ids[0], row_ids[1]
        reach_self = reach(target_ids, target_ids, True)
        reach_cross = reach(target_ids, source_ids, False)
        bi = bias_slots[:, 4:].reshape(-1)
        wq, wk, wv = wqkv[:, :512], wqkv[:, 512:1024], wqkv[:, 1024:]

        att1, sums1 = attend(qkv1, 0, qkv1, 1, *reach_self)
        hidden1, n2, q2, kv2, mem, wc, wco = middle(
            att1, x_row, wo, attend_bias, cross_gain, cross_shift, memory, cross_query, cross_key, cross_value,
            cross_attend, bias_slots,
        )
        mem = mem.reshape(1024, 1024)
        wcq, wck, wcv = wc[:, :512], wc[:, 512:1024], wc[:, 1024:]
        att2, sums2 = attend(q2, 0, kv2, 0, *reach_cross)

        block_out, grad_hidden2, grad_att2, f_outer, f_inner, feed_sums, feed_split = feed(
            att2, hidden1, wco, grad_out, inner_weight, outer_weight, bias_slots, cross_attend_bias, feed_gain,
            feed_shift, outer_bias,
        )

        dq2, dk2, dv2 = attend_back(q2, 0, kv2, 0, grad_att2, att2, sums2, *reach_cross)
        memory_grad, grad_hidden1, grad_att1, c_heads, c_out, f_inner, cross_sums, cross_split = cross(
            dq2, dk2, dv2, n2, mem, att2, grad_hidden2, hidden1, wc, wo, f_inner, cross_gain
        )
        dq1, dk1, dv1 = attend_back(qkv1, 0, qkv1, 1, grad_att1, att1, sums1, *reach_self)
        shared = cat([cross_sums[2:3], cross_sums[:2], feed_sums[3:4], feed_sums[:3], jnp.zeros((1, 1024), F32)], 0)
        split = cat(
            [
                jnp.zeros((4, 2, 128), F32), cross_split[:512].reshape(4, 1, 128), cross_split[512:].reshape(4, 1, 128),
                feed_split.reshape(4, 4, 128),
            ],
            1,
        )
        input_grad, s_heads, s_out, c_heads, c_out, shared, late, split = end(
            dq1, dk1, dv1, n1, att1, grad_hidden1, x_row, wqkv, self_gain, shared, split, c_heads, c_out
        )
        split_of = lambda at, rows: split[:, at:at + rows].reshape(-1)
        return (
            block_out, input_grad.astype(F32), memory_grad.astype(F32),
            late[0], late[1],
            s_heads[0].astype(F32), split_of(0, 1), s_heads[1].astype(F32), s_heads[2].astype(F32), split_of(1, 1),
            s_out.astype(F32), shared[0],
            shared[1], shared[2],
            c_heads[0].astype(F32), split_of(2, 1), c_heads[1].astype(F32), c_heads[2].astype(F32), split_of(3, 1),
            c_out.astype(F32), shared[3],
            shared[4], shared[5],
            f_inner.astype(F32), split_of(4, 4), f_outer.astype(F32), shared[6],
        )

    row, one, by_column, by_row = P("dp", "tensor", None), P(), P(None, "tensor"), P("tensor", None)
    part, ids = P("tensor"), P("dp", None)
    return jax.shard_map(
        local,
        mesh=mesh,
        in_specs=(
            row, row, row, ids, ids,
            one, one, by_column, part, by_column, by_column, part, by_row, one,
            one, one, by_column, part, by_column, by_column, part, by_row, one,
            one, one, by_column, part, by_row, one,
        ),
        out_specs=(
            row, row, row,
            one, one, by_column, part, by_column, by_column, part, by_row, one,
            one, one, by_column, part, by_column, by_column, part, by_row, one,
            one, one, by_column, part, by_row, one,
        ),
        check_vma=False,
    )


BLOCK_ROWS = 512


def general_norm_forward(values, gain, shift):
    average = jnp.mean(values, axis=-1, keepdims=True)
    center = values - average
    inverse = lax.rsqrt(jnp.mean(center * center, axis=-1, keepdims=True) + EPSILON)
    normed = center * inverse
    return ((normed * gain + shift).astype(jnp.bfloat16), normed, inverse)


def general_norm_backward(grad_in, normed, inverse, gain):
    scaled = grad_in * gain
    first_mean = jnp.mean(scaled, axis=-1, keepdims=True)
    second_mean = jnp.mean(scaled * normed, axis=-1, keepdims=True)
    grad_values = inverse * (scaled - first_mean - normed * second_mean)
    return (grad_values, jnp.sum(grad_in * normed, axis=(0, 1)), jnp.sum(grad_in, axis=(0, 1)))


def gather_rows(values):
    return lax.all_gather(values, "tensor", axis=1, tiled=True)


def gather_grads(values):
    return lax.all_gather(values, "tensor", axis=1, tiled=True)


def reduce_inputs(partial_sum):
    return lax.psum_scatter(partial_sum, "tensor", scatter_dimension=1, tiled=True)


def advance(base, partial_sum, bias):
    return base + lax.psum_scatter(partial_sum, "tensor", scatter_dimension=1, tiled=True) + bias


def next_rows(values, gain, shift):
    return gather_rows(general_norm_forward(values, gain, shift)[0])


def backward_rows(normed_low):
    return gather_rows(normed_low)


def project(rows_in, weight):
    return jnp.einsum("rtd,dc->rtc", rows_in, weight, preferred_element_type=jnp.float32)


def project_back(grads, weight):
    return jnp.einsum("rtc,dc->rtd", grads, weight, preferred_element_type=jnp.float32)


def outer_sum(rows_in, grads):
    return jnp.einsum("rtd,rtc->dc", rows_in, grads, preferred_element_type=jnp.float32)


def bias_sum(grads):
    return jnp.sum(grads.astype(jnp.float32), axis=(0, 1))


def split_heads(values):
    return values.reshape(values.shape[0], values.shape[1], values.shape[2] // HD, HD)


def block_scores(query_block, key_row, query_ids, key_ids, row_start, causal):
    raw_scores = jnp.einsum(
        "qhd,khd->hqk", query_block, key_row, preferred_element_type=jnp.float32
    ) * float(HD) ** (-0.5)
    allowed = query_ids[:, None] == key_ids[None, :]
    if causal:
        query_place = row_start + jnp.arange(query_block.shape[0], dtype=jnp.int32)
        key_place = jnp.arange(key_row.shape[0], dtype=jnp.int32)
        allowed = allowed & (key_place[None, :] <= query_place[:, None])
    return jnp.where(allowed[None], raw_scores, jnp.full(raw_scores.shape, MASKED, jnp.float32))


def block_inputs(
    query_heads, key_heads, value_heads, query_ids, key_ids, position, block_count, block_size
):
    row_index = position // block_count
    row_start = position % block_count * block_size
    query_row = lax.dynamic_index_in_dim(query_heads, row_index, 0, keepdims=False)
    query_block = lax.dynamic_slice_in_dim(query_row, row_start, block_size, 0)
    key_row = lax.dynamic_index_in_dim(key_heads, row_index, 0, keepdims=False)
    value_row = lax.dynamic_index_in_dim(value_heads, row_index, 0, keepdims=False)
    query_seg = lax.dynamic_slice_in_dim(
        lax.dynamic_index_in_dim(query_ids, row_index, 0, keepdims=False), row_start, block_size, 0
    )
    key_seg = lax.dynamic_index_in_dim(key_ids, row_index, 0, keepdims=False)
    return (row_index, row_start, query_block, key_row, value_row, query_seg, key_seg)


def attend_forward(query, keys, values, query_ids, key_ids, causal):
    query_heads = split_heads(query)
    key_heads = split_heads(keys)
    value_heads = split_heads(values)
    block_size = min(BLOCK_ROWS, query.shape[1])
    block_count = query.shape[1] // block_size

    def one_block(position):
        row_index, row_start, query_block, key_row, value_row, query_seg, key_seg = block_inputs(
            query_heads,
            key_heads,
            value_heads,
            query_ids,
            key_ids,
            position,
            block_count,
            block_size,
        )
        scores = block_scores(query_block, key_row, query_seg, key_seg, row_start, causal)
        row_max = jnp.max(scores, axis=-1, keepdims=True)
        expo_scores = jnp.exp(scores - row_max)
        row_total = jnp.sum(expo_scores, axis=-1, keepdims=True)
        softmax_out = expo_scores / row_total
        attended = jnp.einsum(
            "hqk,khd->qhd",
            softmax_out.astype(jnp.bfloat16),
            value_row,
            preferred_element_type=jnp.float32,
        ).astype(jnp.bfloat16)
        return (attended, (row_max + jnp.log(row_total))[..., 0])

    attended_all, log_sums = lax.map(
        one_block, jnp.arange(query.shape[0] * block_count, dtype=jnp.int32)
    )
    return (attended_all.reshape(query.shape), log_sums)


def attend_backward(query, keys, values, grad_att, log_sums, query_ids, key_ids, causal):
    query_heads = split_heads(query)
    key_heads = split_heads(keys)
    value_heads = split_heads(values)
    grad_heads = split_heads(grad_att)
    block_size = min(BLOCK_ROWS, query.shape[1])
    block_count = query.shape[1] // block_size
    score_scale = float(HD) ** (-0.5)

    def one_block(carry, inputs):
        grad_keys, grad_values = carry
        position, log_sum = inputs
        row_index, row_start, query_block, key_row, value_row, query_seg, key_seg = block_inputs(
            query_heads,
            key_heads,
            value_heads,
            query_ids,
            key_ids,
            position,
            block_count,
            block_size,
        )
        grad_row = lax.dynamic_index_in_dim(grad_heads, row_index, 0, keepdims=False)
        grad_block = lax.dynamic_slice_in_dim(grad_row, row_start, block_size, 0)
        scores = block_scores(query_block, key_row, query_seg, key_seg, row_start, causal)
        softmax_out = jnp.exp(scores - log_sum[..., None])
        softmax_low = softmax_out.astype(jnp.bfloat16)
        attended = jnp.einsum(
            "hqk,khd->qhd", softmax_low, value_row, preferred_element_type=jnp.float32
        ).astype(jnp.bfloat16)
        grad_prob = jnp.einsum(
            "qhd,khd->hqk", grad_block, value_row, preferred_element_type=jnp.float32
        )
        correction = jnp.sum(softmax_out * grad_prob, axis=-1, keepdims=True)
        grad_score = (softmax_out * (grad_prob - correction)).astype(jnp.bfloat16)
        grad_query = (
            jnp.einsum("hqk,khd->qhd", grad_score, key_row, preferred_element_type=jnp.float32)
            * score_scale
        ).astype(jnp.bfloat16)
        key_added = (
            jnp.einsum("hqk,qhd->khd", grad_score, query_block, preferred_element_type=jnp.float32)
            * score_scale
        )
        value_added = jnp.einsum(
            "hqk,qhd->khd", softmax_low, grad_block, preferred_element_type=jnp.float32
        )
        grad_keys = grad_keys.at[row_index].add(key_added)
        grad_values = grad_values.at[row_index].add(value_added)
        return ((grad_keys, grad_values), (grad_query, attended))

    empty_grads = jnp.zeros(key_heads.shape, jnp.float32)
    positions = jnp.arange(query.shape[0] * block_count, dtype=jnp.int32)
    (grad_keys, grad_values), (grad_query, attended_all) = lax.scan(
        one_block, (empty_grads, empty_grads), (positions, log_sums)
    )
    return (
        grad_query.reshape(query.shape),
        grad_keys.reshape(keys.shape).astype(jnp.bfloat16),
        grad_values.reshape(values.shape).astype(jnp.bfloat16),
        attended_all.reshape(query.shape),
    )


def general_local(
    layer_input,
    memory,
    grad_out,
    target_segments,
    source_segments,
    self_gain,
    self_shift,
    query_weight,
    query_bias,
    key_weight,
    value_weight,
    value_bias,
    attend_weight,
    attend_bias,
    cross_gain,
    cross_shift,
    cross_query,
    cross_query_bias,
    cross_key,
    cross_value,
    cross_value_bias,
    cross_attend,
    cross_attend_bias,
    feed_gain,
    feed_shift,
    inner_weight,
    inner_bias,
    outer_weight,
    outer_bias,
):
    inputs = layer_input.astype(jnp.float32)
    rows_first = next_rows(inputs, self_gain, self_shift)
    query_first = (project(rows_first, query_weight) + query_bias).astype(jnp.bfloat16)
    keys_first = project(rows_first, key_weight).astype(jnp.bfloat16)
    values_first = (project(rows_first, value_weight) + value_bias).astype(jnp.bfloat16)
    attended_first, sums_first = attend_forward(
        query_first, keys_first, values_first, target_segments, target_segments, True
    )
    base_first = advance(inputs, project(attended_first, attend_weight), attend_bias)
    memory_rows = lax.all_gather(memory, "tensor", axis=1, tiled=True)
    rows_second = next_rows(base_first, cross_gain, cross_shift)
    query_second = (project(rows_second, cross_query) + cross_query_bias).astype(jnp.bfloat16)
    keys_second = project(memory_rows, cross_key).astype(jnp.bfloat16)
    values_second = (project(memory_rows, cross_value) + cross_value_bias).astype(jnp.bfloat16)
    attended_second, sums_second = attend_forward(
        query_second, keys_second, values_second, target_segments, source_segments, False
    )
    base_second = advance(base_first, project(attended_second, cross_attend), cross_attend_bias)
    rows_third = next_rows(base_second, feed_gain, feed_shift)
    pre_active = project(rows_third, inner_weight) + inner_bias
    active = jax.nn.silu(pre_active).astype(jnp.bfloat16)
    base_out = advance(base_second, project(active, outer_weight), outer_bias)
    block_out = base_out.astype(jnp.bfloat16)
    kept_input, kept_first, kept_second, kept_memory, kept_sums_first, kept_sums_second = (
        lax.optimization_barrier(
            (inputs, base_first, base_second, memory_rows, sums_first, sums_second)
        )
    )
    grad_top = grad_out.astype(jnp.float32)
    normed_low3, unit_third, inverse_third = general_norm_forward(kept_second, feed_gain, feed_shift)
    rows_back3 = backward_rows(normed_low3)
    pre_back = project(rows_back3, inner_weight) + inner_bias
    sigmoid_back = jax.nn.sigmoid(pre_back)
    active_back = (pre_back * sigmoid_back).astype(jnp.bfloat16)
    grad_rows3 = gather_grads(grad_top.astype(jnp.bfloat16))
    grad_outer_weight = outer_sum(active_back, grad_rows3)
    grad_outer_bias = jnp.sum(grad_top, axis=(0, 1))
    grad_active = project_back(grad_rows3, outer_weight)
    grad_inner = (grad_active * sigmoid_back * (1.0 + pre_back * (1.0 - sigmoid_back))).astype(
        jnp.bfloat16
    )
    grad_inner_weight = outer_sum(rows_back3, grad_inner)
    grad_inner_bias = bias_sum(grad_inner)
    grad_norm3 = reduce_inputs(project_back(grad_inner, inner_weight))
    grad_from3, grad_feed_gain, grad_feed_shift = general_norm_backward(
        grad_norm3, unit_third, inverse_third, feed_gain
    )
    grad_hidden2 = grad_top + grad_from3
    normed_low2, unit_second, inverse_second = general_norm_forward(kept_first, cross_gain, cross_shift)
    rows_back2 = backward_rows(normed_low2)
    query_back2 = (project(rows_back2, cross_query) + cross_query_bias).astype(jnp.bfloat16)
    keys_back2 = project(kept_memory, cross_key).astype(jnp.bfloat16)
    values_back2 = (project(kept_memory, cross_value) + cross_value_bias).astype(jnp.bfloat16)
    grad_rows2 = gather_grads(grad_hidden2.astype(jnp.bfloat16))
    grad_att2 = project_back(grad_rows2, cross_attend).astype(jnp.bfloat16)
    grad_query2, grad_keys2, grad_values2, attended_back2 = attend_backward(
        query_back2,
        keys_back2,
        values_back2,
        grad_att2,
        kept_sums_second,
        target_segments,
        source_segments,
        False,
    )
    grad_cross_attend = outer_sum(attended_back2, grad_rows2)
    grad_cross_attend_bias = jnp.sum(grad_hidden2, axis=(0, 1))
    grad_cross_query = outer_sum(rows_back2, grad_query2)
    grad_cross_query_bias = bias_sum(grad_query2)
    grad_cross_key = outer_sum(kept_memory, grad_keys2)
    grad_cross_value = outer_sum(kept_memory, grad_values2)
    grad_cross_value_bias = bias_sum(grad_values2)
    memory_grad = lax.psum_scatter(
        (project_back(grad_keys2, cross_key) + project_back(grad_values2, cross_value)).astype(
            jnp.bfloat16
        ),
        "tensor",
        scatter_dimension=1,
        tiled=True,
    ).astype(jnp.float32)
    grad_norm2 = reduce_inputs(project_back(grad_query2, cross_query))
    grad_from2, grad_cross_gain, grad_cross_shift = general_norm_backward(
        grad_norm2, unit_second, inverse_second, cross_gain
    )
    grad_hidden1 = grad_hidden2 + grad_from2
    normed_low1, unit_first, inverse_first = general_norm_forward(kept_input, self_gain, self_shift)
    rows_back1 = backward_rows(normed_low1)
    query_back1 = (project(rows_back1, query_weight) + query_bias).astype(jnp.bfloat16)
    keys_back1 = project(rows_back1, key_weight).astype(jnp.bfloat16)
    values_back1 = (project(rows_back1, value_weight) + value_bias).astype(jnp.bfloat16)
    grad_rows1 = gather_grads(grad_hidden1.astype(jnp.bfloat16))
    grad_att1 = project_back(grad_rows1, attend_weight).astype(jnp.bfloat16)
    grad_query1, grad_keys1, grad_values1, attended_back1 = attend_backward(
        query_back1,
        keys_back1,
        values_back1,
        grad_att1,
        kept_sums_first,
        target_segments,
        target_segments,
        True,
    )
    grad_attend_weight = outer_sum(attended_back1, grad_rows1)
    grad_attend_bias = jnp.sum(grad_hidden1, axis=(0, 1))
    grad_query_weight = outer_sum(rows_back1, grad_query1)
    grad_query_bias = bias_sum(grad_query1)
    grad_key_weight = outer_sum(rows_back1, grad_keys1)
    grad_value_weight = outer_sum(rows_back1, grad_values1)
    grad_value_bias = bias_sum(grad_values1)
    grad_norm1 = reduce_inputs(
        project_back(grad_query1, query_weight)
        + project_back(grad_keys1, key_weight)
        + project_back(grad_values1, value_weight)
    )
    grad_from1, grad_self_gain, grad_self_shift = general_norm_backward(
        grad_norm1, unit_first, inverse_first, self_gain
    )
    input_grad = grad_hidden1 + grad_from1
    (
        grad_query_weight,
        grad_query_bias,
        grad_key_weight,
        grad_value_weight,
        grad_value_bias,
        grad_attend_weight,
        grad_cross_query,
        grad_cross_query_bias,
        grad_cross_key,
        grad_cross_value,
        grad_cross_value_bias,
        grad_cross_attend,
        grad_inner_weight,
        grad_inner_bias,
        grad_outer_weight,
    ) = (
        lax.psum(grad_query_weight.astype(jnp.bfloat16), "dp").astype(jnp.float32),
        lax.psum(grad_query_bias.astype(jnp.bfloat16), "dp").astype(jnp.float32),
        lax.psum(grad_key_weight.astype(jnp.bfloat16), "dp").astype(jnp.float32),
        lax.psum(grad_value_weight.astype(jnp.bfloat16), "dp").astype(jnp.float32),
        lax.psum(grad_value_bias.astype(jnp.bfloat16), "dp").astype(jnp.float32),
        lax.psum(grad_attend_weight.astype(jnp.bfloat16), "dp").astype(jnp.float32),
        lax.psum(grad_cross_query.astype(jnp.bfloat16), "dp").astype(jnp.float32),
        lax.psum(grad_cross_query_bias.astype(jnp.bfloat16), "dp").astype(jnp.float32),
        lax.psum(grad_cross_key.astype(jnp.bfloat16), "dp").astype(jnp.float32),
        lax.psum(grad_cross_value.astype(jnp.bfloat16), "dp").astype(jnp.float32),
        lax.psum(grad_cross_value_bias.astype(jnp.bfloat16), "dp").astype(jnp.float32),
        lax.psum(grad_cross_attend.astype(jnp.bfloat16), "dp").astype(jnp.float32),
        lax.psum(grad_inner_weight.astype(jnp.bfloat16), "dp").astype(jnp.float32),
        lax.psum(grad_inner_bias.astype(jnp.bfloat16), "dp").astype(jnp.float32),
        lax.psum(grad_outer_weight.astype(jnp.bfloat16), "dp").astype(jnp.float32),
    )
    (
        grad_self_gain,
        grad_self_shift,
        grad_attend_bias,
        grad_cross_gain,
        grad_cross_shift,
        grad_cross_attend_bias,
        grad_feed_gain,
        grad_feed_shift,
        grad_outer_bias,
    ) = lax.psum(
        (
            grad_self_gain,
            grad_self_shift,
            grad_attend_bias,
            grad_cross_gain,
            grad_cross_shift,
            grad_cross_attend_bias,
            grad_feed_gain,
            grad_feed_shift,
            grad_outer_bias,
        ),
        ("dp", "tensor"),
    )
    return (
        block_out,
        input_grad,
        memory_grad,
        grad_self_gain,
        grad_self_shift,
        grad_query_weight,
        grad_query_bias,
        grad_key_weight,
        grad_value_weight,
        grad_value_bias,
        grad_attend_weight,
        grad_attend_bias,
        grad_cross_gain,
        grad_cross_shift,
        grad_cross_query,
        grad_cross_query_bias,
        grad_cross_key,
        grad_cross_value,
        grad_cross_value_bias,
        grad_cross_attend,
        grad_cross_attend_bias,
        grad_feed_gain,
        grad_feed_shift,
        grad_inner_weight,
        grad_inner_bias,
        grad_outer_weight,
        grad_outer_bias,
    )


def general_solution(mesh):
    placed = (
        P("dp", "tensor", None),
        P("dp", "tensor", None),
        P("dp", "tensor", None),
        P("dp", None),
        P("dp", None),
        P(),
        P(),
        P(None, "tensor"),
        P("tensor"),
        P(None, "tensor"),
        P(None, "tensor"),
        P("tensor"),
        P("tensor", None),
        P(),
        P(),
        P(),
        P(None, "tensor"),
        P("tensor"),
        P(None, "tensor"),
        P(None, "tensor"),
        P("tensor"),
        P("tensor", None),
        P(),
        P(),
        P(),
        P(None, "tensor"),
        P("tensor"),
        P("tensor", None),
        P(),
    )
    return jax.shard_map(
        general_local,
        mesh=mesh,
        in_specs=placed,
        out_specs=(
            P("dp", "tensor", None),
            P("dp", "tensor", None),
            P("dp", "tensor", None),
            P(),
            P(),
            P(None, "tensor"),
            P("tensor"),
            P(None, "tensor"),
            P(None, "tensor"),
            P("tensor"),
            P("tensor", None),
            P(),
            P(),
            P(),
            P(None, "tensor"),
            P("tensor"),
            P(None, "tensor"),
            P(None, "tensor"),
            P("tensor"),
            P("tensor", None),
            P(),
            P(),
            P(),
            P(None, "tensor"),
            P("tensor"),
            P("tensor", None),
            P(),
        ),
        check_vma=False,
    )
```

```python
import jax
import jax.numpy as jnp
from jax import lax
from jax.experimental import pallas as pl
from jax.experimental.pallas import tpu as pltpu
from jax.sharding import PartitionSpec as P

HD = 64
MASKED = -1000000000.0
QUERIES = 128
KEYS = 256
NT = (((1,), (1,)), ((), ()))
TN = (((0,), (0,)), ((), ()))
NN = (((1,), (0,)), ((), ()))


def dot(a, b, dims):
    return lax.dot_general(a, b, dims, preferred_element_type=jnp.float32)


def both_heads(block):
    first = lax.broadcasted_iota(jnp.int32, block.shape, 1) < HD
    zero = jnp.zeros_like(block)
    return jnp.concatenate([jnp.where(first, block, zero), jnp.where(first, zero, block)], axis=0)


def allowed_keys(least, limit, at):
    key_place = at + lax.broadcasted_iota(jnp.int32, (KEYS, 1), 0)
    seen = (key_place >= least) & (key_place < limit)
    return jnp.concatenate([seen, seen], axis=1)


def attend_step(queries, k_ref, k_at, v_at, rows, seen, acc, top, total):
    pairs = range(len(queries))
    keys = [k_ref[rows, k_at + p * 128:k_at + p * 128 + 128] for p in pairs]
    values = [k_ref[rows, v_at + p * 128:v_at + p * 128 + 128] for p in pairs]
    scores = [jnp.where(seen, dot(keys[p], queries[p], NT), MASKED) for p in pairs]
    before = [top[p:p + 1] for p in pairs]
    now = [jnp.maximum(before[p], jnp.max(scores[p], axis=0, keepdims=True)) for p in pairs]
    weight = [jnp.exp(scores[p] - now[p]) for p in pairs]
    keep = [jnp.exp(before[p] - now[p]) for p in pairs]
    added = [dot(values[p], weight[p].astype(jnp.bfloat16), TN) for p in pairs]
    sums = [jnp.sum(weight[p], axis=0, keepdims=True) for p in pairs]
    for p in pairs:
        top[p:p + 1] = now[p]
        total[p:p + 1] = total[p:p + 1] * keep[p] + sums[p]
        acc[p] = acc[p] * keep[p] + added[p]


def attend_back_step(queries, grads, fixes, sums, k_ref, k_at, v_at, rows, seen, acc, acc_k, acc_v):
    pairs = range(len(queries))
    cuts = [slice(p * 128, (p + 1) * 128) for p in pairs]
    keys = [k_ref[rows, k_at + p * 128:k_at + p * 128 + 128] for p in pairs]
    values = [k_ref[rows, v_at + p * 128:v_at + p * 128 + 128] for p in pairs]
    scores = [dot(keys[p], queries[p], NT) for p in pairs]
    dprob = [dot(values[p], grads[p], NT) for p in pairs]
    prob = [jnp.exp(jnp.where(seen, scores[p] - sums[p], MASKED)) for p in pairs]
    low = [prob[p].astype(jnp.bfloat16) for p in pairs]
    dscore = [(prob[p] * (dprob[p] - fixes[p])).astype(jnp.bfloat16) for p in pairs]
    added_v = [dot(low[p], grads[p], NN) for p in pairs]
    added_k = [dot(dscore[p], queries[p], NN) for p in pairs]
    added_q = [dot(keys[p], dscore[p], TN) for p in pairs]
    for p in pairs:
        acc_v[rows, cuts[p]] += added_v[p]
        acc_k[rows, cuts[p]] += added_k[p]
        acc[p] += added_q[p]


EPSILON = 1e-05
BF = jnp.bfloat16
F32 = jnp.float32


def norm_stats(values):
    average = jnp.mean(values, axis=-1, keepdims=True)
    center = values - average
    inverse = lax.rsqrt(jnp.mean(center * center, axis=-1, keepdims=True) + EPSILON)
    return center * inverse, inverse


def norm_forward(values, gain, shift):
    unit, _ = norm_stats(values)
    return (unit * gain + shift).astype(BF)


class Net:
    def __init__(self, sems, local_sems):
        place = lax.axis_index("dp")
        chip = lax.axis_index("tensor")
        core, plane = place % 2, place // 2
        odd = plane % 2
        beside, over, corner = chip + 1 - 2 * (chip % 2), (chip + 2) % 4, 3 - chip
        self.chip, self.core_index, self.odd, self.plane = chip, core, odd, plane
        self.chips = (beside, over, corner)
        self.core = (plane * 2 + 1 - core, chip)
        self.first = (place, beside + odd * (over - beside))
        self.second = (place, over + odd * (beside - over))
        self.corner = (place, corner)
        self.near_plane = ((plane + 1 - 2 * odd) * 2 + core, chip)
        self.far_plane = ((plane + 2) % 4 * 2 + core, chip)
        self.sems, self.local_sems = sems, local_sems
        self.count = self.local_count = 0
        self.unsent, self.unmoved = [], []

    def meet(self):
        barrier = pltpu.get_barrier_semaphore()
        partners = (self.core, self.first, self.second, self.corner, self.near_plane, self.far_plane)
        for partner in partners:
            pl.semaphore_signal(barrier, inc=1, device_id=partner, device_id_type=pl.DeviceIdType.MESH)
        pl.semaphore_wait(barrier, len(partners))

    def send(self, source, target, device):
        copy = pltpu.make_async_remote_copy(
            src_ref=source,
            dst_ref=target,
            send_sem=self.sems.at[0, self.count],
            recv_sem=self.sems.at[1, self.count],
            device_id=device,
            device_id_type=pl.DeviceIdType.MESH,
        )
        self.count += 1
        copy.start()
        self.unsent.append(copy)
        return copy

    def move(self, source, target):
        copy = pltpu.make_async_copy(source, target, self.local_sems.at[self.local_count])
        self.local_count += 1
        copy.start()
        self.unmoved.append(copy)
        return copy

    def moved(self, copy):
        copy.wait()
        self.unmoved = [other for other in self.unmoved if other is not copy]

    def sent(self, copy):
        copy.wait_send()
        self.unsent = [other for other in self.unsent if other is not copy]

    def finish(self):
        for copy in self.unmoved:
            copy.wait()
        for copy in self.unsent:
            copy.wait_send()
        self.unsent, self.unmoved = [], []


def row_in(net, given, rows, row):
    core, chip = net.core_index, net.chip
    mine = pl.ds(2 * core, 2)
    swap = net.send(given.at[:, 1 - core], rows.at[mine], net.core)
    keep = net.move(given.at[:, core], rows.at[mine])
    yield
    net.moved(keep)
    swap.wait_recv()
    own = net.move(rows.at[chip], row.at[chip, core])
    sends = [
        net.send(rows.at[other], row.at[chip, core], (lax.axis_index("dp"), other)) for other in net.chips
    ]
    yield
    net.moved(own)
    shares = [net.send(row.at[chip, core], row.at[chip, core], net.core)]
    for other, copy in zip(net.chips, sends):
        copy.wait_recv()
        shares.append(net.send(row.at[other, core], row.at[other, core], net.core))
    yield
    for copy in shares:
        copy.wait_recv()


def row_out(net, pieces, rows, result):
    core, chip = net.core_index, net.chip
    own = net.move(pieces.at[chip], rows.at[chip])
    sends = [net.send(pieces.at[other], rows.at[chip], (lax.axis_index("dp"), other)) for other in net.chips]
    yield
    net.moved(own)
    for copy in sends:
        copy.wait_recv()
    keep = net.move(rows.at[pl.ds(2 * core, 2)], result.at[:, core])
    swap = net.send(rows.at[pl.ds(2 * (1 - core), 2)], result.at[:, core], net.core)
    yield
    swap.wait_recv()
    net.moved(keep)


class Gather:
    def __init__(self, net, own, slot, flip=False):
        self.net, self.slot = net, slot
        self.one, self.two = (2, 1) if flip else (1, 2)
        to_one, self.to_two = (net.second, net.first) if flip else (net.first, net.second)
        self.near = net.send(own, slot(self.one), to_one)
        self.own = net.move(own, slot(0))

    def relay(self):
        self.near.wait_recv()
        self.corner = self.net.send(self.slot(self.one), self.slot(3), self.to_two)
        self.other = self.net.send(self.slot(self.one), self.slot(self.two), self.net.near_plane)

    def finish(self):
        self.net.moved(self.own)
        self.corner.wait_recv()
        self.other.wait_recv()


ANY = pl.BlockSpec(memory_space=pl.ANY)
VM = pl.BlockSpec(memory_space=pltpu.VMEM)
SENDS = 160


def half_columns(net, weight, width):
    return weight.at[:, pl.ds(pl.multiple_of(net.core_index * width, width), width)]


def half_rows(net, weight, height):
    return weight.at[pl.ds(pl.multiple_of(net.core_index * height, height), height)]


def tile_rows(i, size=256):
    return pl.ds(pl.multiple_of(i * size, size), size)


def call_remote(kernel, ident, ins, in_specs, outs, out_specs, scratch, vmem=48, name=None):
    return pl.pallas_call(
        kernel,
        in_specs=in_specs,
        out_specs=out_specs,
        out_shape=outs,
        scratch_shapes=list(scratch) + [pltpu.SemaphoreType.DMA((2, SENDS)), pltpu.SemaphoreType.DMA((SENDS,))],
        compiler_params=pltpu.CompilerParams(
            collective_id=ident, has_side_effects=True, vmem_limit_bytes=vmem << 20
        ),
        name=name,
    )(*ins)


def add_up(target, sources, step=64):
    def some(i, _):
        cut = pl.ds(pl.multiple_of(i * step, step), step)
        total = sources[0][cut].astype(F32)
        for source in sources[1:]:
            total = total + source[cut].astype(F32)
        target[cut] = total.astype(BF)
        return 0

    lax.fori_loop(0, target.shape[0] // step, some, 0)


class Line:
    def __init__(self, net, total, landing, result):
        self.net, self.total, self.result = net, total, result
        self.one_in, self.two_in = landing
        self.size = self.one_in.shape[0]

    def half(self, which):
        return self.total.at[pl.ds(pl.multiple_of(which * self.size, self.size), self.size)]

    def line0(self):
        self.line = self.net.send(self.half(1 - self.net.odd), self.one_in, self.net.near_plane)

    def line1(self):
        self.line.wait_recv()
        mine = self.half(self.net.odd)
        add_up(mine, [mine, self.one_in])
        self.line = self.net.send(mine, self.two_in, self.net.far_plane)

    def line2(self):
        self.line.wait_recv()
        place = self.result(self.net.core_index, self.net.odd)
        add_up(self.two_in, [self.half(self.net.odd), self.two_in])
        self.net.move(self.two_in, place)
        self.line = self.net.send(self.two_in, place, self.net.near_plane)
        self.cores = [self.net.send(self.two_in, place, self.net.core)]

    def line3(self):
        self.line.wait_recv()
        place = self.result(self.net.core_index, 1 - self.net.odd)
        self.cores.append(self.net.send(place, place, self.net.core))

    def end(self):
        for copy in self.cores:
            copy.wait_recv()


class Scatter:
    def __init__(self, net, part, first, landing):
        self.net, self.part = net, part
        self.near_in, self.pass_in, self.far_in = landing
        self.one, self.two = (1, 2) if first == 1 else (2, 1)
        self.to_one, self.to_two = (net.first, net.second) if first == 1 else (net.second, net.first)

    def start(self):
        self.passed = self.net.send(self.part(3), self.pass_in, self.to_one)
        self.near = self.net.send(self.part(self.one), self.near_in, self.to_one)

    def middle(self):
        self.passed.wait_recv()
        add_up(self.part(self.two), [self.part(self.two), self.pass_in])
        self.far = self.net.send(self.part(self.two), self.far_in, self.to_two)

    def own(self):
        self.near.wait_recv()
        self.far.wait_recv()
        add_up(self.part(0), [self.part(0), self.near_in, self.far_in])


def landing(rows, columns):
    return [pltpu.VMEM((rows, columns), BF)] * 3


def line_landing(rows, columns):
    return [pltpu.VMEM((rows // 2, columns), BF)] * 2


def weight_grad(lhs, rhs, target, start, count, columns=slice(None), size=256):
    def some(i, _):
        cut = pl.ds(pl.multiple_of(start + i * size, size), size)
        target[cut, columns] = dot(lhs(cut), rhs(), TN).astype(BF)
        return 0

    lax.fori_loop(0, count // size, some, 0)


def norm_back_tile(grad_in, values, gain):
    unit, inverse = norm_stats(values)
    scaled = grad_in * gain
    first_mean = jnp.mean(scaled, axis=-1, keepdims=True)
    second_mean = jnp.mean(scaled * unit, axis=-1, keepdims=True)
    grad_values = inverse * (scaled - first_mean - unit * second_mean)
    return grad_values, jnp.sum(grad_in * unit, axis=0, keepdims=True), jnp.sum(grad_in, axis=0, keepdims=True)


def head_scatters(net, g_heads, g_out, lands):
    found = []
    for kind in range(3):
        found.append(
            Scatter(
                net, lambda s, kind=kind: g_heads.at[:, kind * 512 + s * 128:kind * 512 + s * 128 + 128],
                (1, 1, 2)[kind], lands[kind * 3:kind * 3 + 3],
            )
        )
    found.append(Scatter(net, lambda s: g_out.at[pl.ds(s * 128, 128)], 2, lands[9:12]))
    return found


def head_lines(net, totals, total_out, full_heads, full_out, lands):
    lines = []
    for kind in range(3):
        lines.append(
            Line(
                net, totals(kind), lands[kind * 2:kind * 2 + 2],
                lambda c, h, kind=kind: full_heads.at[
                    kind, pl.ds(pl.multiple_of(h * 512, 512), 512), pl.ds(pl.multiple_of(c * 128, 128), 128)
                ],
            )
        )
    lines.append(
        Line(
            net, total_out, lands[6:8],
            lambda c, h: full_out.at[pl.ds(pl.multiple_of(c * 128 + h * 64, 64), 64)],
        )
    )
    return lines


def head_landing(width):
    return landing(1024, 128) * 3 + landing(128, width)


def head_line_landing(width):
    return line_landing(1024, 128) * 3 + line_landing(128, width)


def attend_block(i, q_ref, q_at, k_ref, k_at, v_at, low, high, causal, out_ref, sums_ref, acc, top, total):
    pairs = range(4)
    rows = tile_rows(i, QUERIES)
    queries = [
        both_heads(q_ref[rows, q_at + p * 128:q_at + p * 128 + 128] * jnp.bfloat16(HD ** -0.5)) for p in pairs
    ]
    least, limit = low[pl.ds(i, 1)], high[pl.ds(i, 1)]
    acc[...] = jnp.zeros_like(acc)
    total[...] = jnp.zeros_like(total)
    top[...] = jnp.full_like(top, -1e30)

    def step(j, _):
        at = pl.multiple_of(j * KEYS, KEYS)
        seen = allowed_keys(least, limit, at)
        attend_step(queries, k_ref, k_at, v_at, pl.ds(at, KEYS), seen, acc, top, total)
        return 0

    lax.fori_loop(0, i // 2 + 1 if causal else k_ref.shape[0] // KEYS, step, 0)
    for p in pairs:
        sums = total[p:p + 1]
        mixed = acc[p] / sums
        joined = jnp.concatenate([mixed[:HD, :QUERIES], mixed[HD:, QUERIES:]], axis=0)
        out_ref[rows, p * 128:(p + 1) * 128] = joined.T.astype(BF)
        sums_ref[i, p:p + 1] = top[p:p + 1] + jnp.log(sums)


def attend_back_block(
    i, q_ref, q_at, k_ref, k_at, v_at, grad_ref, out_ref, out_at, sums_ref, low, high, causal, dq_ref, dq_at, acc, acc_k, acc_v
):
    pairs = range(4)
    rows = tile_rows(i, QUERIES)
    least, limit = low[pl.ds(i, 1)], high[pl.ds(i, 1)]
    queries, grads, fixes, sums = [], [], [], []
    ones = jnp.ones((8, 128), BF)
    for p in pairs:
        queries.append(both_heads(q_ref[rows, q_at + p * 128:q_at + p * 128 + 128] * jnp.bfloat16(HD ** -0.5)))
        grad = both_heads(grad_ref[rows, p * 128:(p + 1) * 128])
        grads.append(grad)
        out = out_ref[rows, out_at + p * 128:out_at + p * 128 + 128].astype(F32)
        product = grad.astype(F32) * jnp.concatenate([out, out], axis=0)
        coarse = product.astype(BF)
        fine = (product - coarse.astype(F32)).astype(BF)
        fixes.append((dot(ones, coarse, NT) + dot(ones, fine, NT))[:1])
        sums.append(sums_ref[i, p:p + 1])
    acc[...] = jnp.zeros_like(acc)

    def step(j, _):
        at = pl.multiple_of(j * KEYS, KEYS)
        seen = allowed_keys(least, limit, at)
        attend_back_step(queries, grads, fixes, sums, k_ref, k_at, v_at, pl.ds(at, KEYS), seen, acc, acc_k, acc_v)
        return 0

    lax.fori_loop(0, i // 2 + 1 if causal else k_ref.shape[0] // KEYS, step, 0)
    for p in pairs:
        mixed = acc[p] * (HD ** -0.5)
        joined = jnp.concatenate([mixed[:HD, :QUERIES], mixed[HD:, QUERIES:]], axis=0)
        dq_ref[rows, dq_at + p * 128:dq_at + p * 128 + 128] = joined.T.astype(BF)


def reach(query_ids, key_ids):
    low = jnp.zeros(query_ids.shape, F32)
    high = jnp.zeros(query_ids.shape, F32)
    for segment in range(16):
        here = query_ids == segment
        before = jnp.sum((key_ids < segment).astype(F32), axis=(0, 1), keepdims=True)
        upto = jnp.sum((key_ids <= segment).astype(F32), axis=(0, 1), keepdims=True)
        low = low + jnp.where(here, before, 0.0)
        high = high + jnp.where(here, upto, 0.0)
    return low.astype(jnp.int32), high.astype(jnp.int32)


def project_out(net, att, weight, part, part_in):
    swaps = []
    for i in range(4):
        part[i] = dot(att[i * 256:i * 256 + 256], weight[...], NN).astype(BF).reshape(2, 128, -1)
        swaps.append(net.send(part.at[i], part_in.at[i], net.core))
    return swaps


def ahead_kernel(
    x_in, mem_in, top_in, ids, bias, wq, wk, wv, wo, wcq, wck, wcv, wco, inner, outer,
    gain1, shift1, bias_o, gain2, shift2, bias_c, gain3, shift3,
    x_out, mem_out, top_out, n1_out, qkv_out, att1_out, sums1_out, h1_out, n2_out, q2_out, kv2_out, att2_out, sums2_out,
    h2_out, n3_out, act_out, slope_out, wqkv_out, wo_out, wc_out, wco_out, wi_out, wu_out, reach_out,
    rows_x, rows_mem, rows_top, row, mem, weights, weights2, wo_vm, wco_vm, wi, normed, qkv, att, part, part_in, part_in2,
    hidden, queries, keys, act, slope, biases, all_ids, spans, sums1, sums2, acc, top, total, sems, local_sems,
):
    net = Net(sems, local_sems)
    core, chip = net.core_index, net.chip
    net.meet()
    enter_x = row_in(net, x_in, rows_x, row)
    next(enter_x)
    mine = pl.ds(2 * core, 2)
    ids_copies = [net.move(ids, all_ids.at[mine]), net.send(ids, all_ids.at[mine], net.core)]
    bias_own = net.move(bias, biases.at[0])
    bias_copies = [
        net.send(bias, biases.at[1], net.first),
        net.send(bias, biases.at[2], net.second),
        net.send(bias, biases.at[3], net.corner),
    ]

    def gather_columns(weight, target, kind, flip):
        slot = lambda s: target.at[:, kind * 512 + s * 128:kind * 512 + s * 128 + 128]
        return Gather(net, half_columns(net, weight, 128), slot, flip)

    def gather_rows_of(weight, target, flip):
        return Gather(net, half_rows(net, weight, 128), lambda s: target.at[pl.ds(s * 128, 128)], flip)

    def gather_inner(k):
        own = inner.at[pl.ds(k * 512, 512), pl.ds(pl.multiple_of(core * 512, 512), 512)]
        return Gather(net, own, lambda s: wi.at[pl.ds(k * 512, 512), s * 512:s * 512 + 512], k == 1)

    def gather_outer(k):
        own = outer.at[pl.ds(pl.multiple_of(core * 512 + k * 256, 256), 256)]
        return Gather(net, own, lambda s: wu_out.at[pl.ds(s * 512 + k * 256, 256)], k == 1)

    gather_q = gather_columns(wq, weights, 0, False)
    gather_k = gather_columns(wk, weights, 1, True)
    gather_v = gather_columns(wv, weights, 2, False)
    next(enter_x)
    enter_mem = row_in(net, mem_in, rows_mem, mem)
    next(enter_mem)
    gather_o = gather_rows_of(wo, wo_vm, True)
    gather_q.relay()
    gather_k.relay()
    gather_v.relay()
    next(enter_x)
    next(enter_mem)
    for _ in enter_x:
        pass
    net.move(row, x_out)

    def norm_first(i, _):
        normed[tile_rows(i)] = norm_forward(row[i].reshape(256, -1).astype(F32), gain1[...], shift1[...])
        return 0

    lax.fori_loop(0, 4, norm_first, 0)
    n1_move = net.move(normed, n1_out)
    gather_o.relay()
    gather_ck = gather_columns(wck, weights2, 1, False)
    gather_cv = gather_columns(wcv, weights2, 2, True)
    net.moved(bias_own)
    for copy in bias_copies:
        copy.wait_recv()
    for gather in (gather_q, gather_k, gather_v):
        gather.finish()
    net.move(weights, wqkv_out)

    def project_first(i, _):
        tokens = normed[tile_rows(i)]
        for kind in range(3):
            cut = slice(kind * 512, kind * 512 + 512)
            value = dot(tokens, weights[:, cut], NN)
            if kind != 1:
                at = 0 if kind == 0 else 1
                value = value + jnp.concatenate([biases[s, at:at + 1] for s in range(4)], axis=1)
            qkv[tile_rows(i), cut] = value.astype(BF)
        return 0

    lax.fori_loop(0, 4, project_first, 0)
    net.move(qkv, qkv_out)
    net.moved(ids_copies[0])
    ids_copies[1].wait_recv()
    target_ids, source_ids = all_ids[chip, :8], all_ids[chip, 8:]
    low, _ = reach(target_ids, target_ids)
    spans[0] = low
    place = lax.broadcasted_iota(jnp.int32, (8, 128), 0) * 128 + lax.broadcasted_iota(jnp.int32, (8, 128), 1)
    spans[1] = place + 1
    low, high = reach(target_ids, source_ids)
    spans[2] = low
    spans[3] = high
    net.move(spans, reach_out)

    def attend_first(i, _):
        attend_block(i, qkv, 0, qkv, 512, 1024, spans.at[0], spans.at[1], True, att, sums1, acc, top, total)
        return 0

    lax.fori_loop(0, 4, attend_first, 0)
    gather_ck.relay()
    gather_cv.relay()
    gather_cq = gather_columns(wcq, weights2, 0, False)
    gather_co = gather_rows_of(wco, wco_vm, True)
    next(enter_mem)
    lax.fori_loop(4, 7, attend_first, 0)
    gather_cq.relay()
    gather_co.relay()
    enter_top = row_in(net, top_in, rows_top, top_out)
    next(enter_top)
    for _ in enter_mem:
        pass
    net.move(mem, mem_out)
    lax.fori_loop(7, 8, attend_first, 0)
    att1_move = net.move(att, att1_out)
    net.move(sums1, sums1_out)
    next(enter_top)
    gather_o.finish()
    net.move(wo_vm, wo_out)
    swaps = project_out(net, att, wo_vm, part, part_in)
    inners = [gather_inner(0), gather_inner(1)]
    for gather in (gather_ck, gather_cv):
        gather.finish()
    values_bias = jnp.concatenate([biases[s, 3:4] for s in range(4)], axis=1)
    query_bias = jnp.concatenate([biases[s, 2:3] for s in range(4)], axis=1)

    def project_memory(i, _):
        tokens = mem[i].reshape(256, -1)
        keys[tile_rows(i), :512] = dot(tokens, weights2[:, 512:1024], NN).astype(BF)
        keys[tile_rows(i), 512:] = (dot(tokens, weights2[:, 1024:], NN) + values_bias).astype(BF)
        return 0

    lax.fori_loop(0, 4, project_memory, 0)
    net.move(keys, kv2_out)
    net.moved(n1_move)
    for i in range(4):
        swaps[i].wait_recv()

    def middle_rows(i, _):
        value = row[i].astype(F32) + part[i].astype(F32) + part_in[i].astype(F32)
        value = value.reshape(256, -1) + bias_o[...]
        hidden[tile_rows(i)] = value
        normed[tile_rows(i)] = norm_forward(value, gain2[...], shift2[...])
        return 0

    lax.fori_loop(0, 4, middle_rows, 0)
    h1_move = net.move(hidden, h1_out)
    n2_move = net.move(normed, n2_out)
    gather_cq.finish()
    net.move(weights2, wc_out)

    def project_query(i, _):
        queries[tile_rows(i)] = (dot(normed[tile_rows(i)], weights2[:, :512], NN) + query_bias).astype(BF)
        return 0

    lax.fori_loop(0, 4, project_query, 0)
    net.move(queries, q2_out)
    net.moved(att1_move)
    next(enter_top)
    inners[0].relay()
    inners[1].relay()
    outers = [gather_outer(0), gather_outer(1)]

    def attend_second(i, _):
        attend_block(i, queries, 0, keys, 0, 512, spans.at[2], spans.at[3], False, att, sums2, acc, top, total)
        return 0

    lax.fori_loop(0, 4, attend_second, 0)
    outers[0].relay()
    outers[1].relay()
    for _ in enter_top:
        pass
    lax.fori_loop(4, 8, attend_second, 0)
    net.move(att, att2_out)
    net.move(sums2, sums2_out)
    gather_co.finish()
    net.move(wco_vm, wco_out)
    for copy in swaps:
        net.sent(copy)
    swaps = project_out(net, att, wco_vm, part, part_in2)
    net.moved(h1_move)
    net.moved(n2_move)
    for i in range(4):
        swaps[i].wait_recv()

    def last_rows(i, _):
        value = part[i].astype(F32) + part_in2[i].astype(F32)
        value = hidden[tile_rows(i)] + value.reshape(256, -1) + bias_c[...]
        hidden[tile_rows(i)] = value
        normed[tile_rows(i)] = norm_forward(value, gain3[...], shift3[...])
        return 0

    lax.fori_loop(0, 4, last_rows, 0)
    net.move(hidden, h2_out)
    net.move(normed, n3_out)
    inners[0].finish()
    inners[1].finish()
    net.move(wi, wi_out)

    def feed(i, _):
        tokens = normed[tile_rows(i)]
        for s in range(4):
            cut = slice(s * 512, s * 512 + 512)
            unit_bias = jnp.concatenate([biases[s, 4 + k:5 + k] for k in range(4)], axis=1)
            pre = dot(tokens, wi[:, cut], NN) + unit_bias
            sigmoid = jax.nn.sigmoid(pre)
            act[tile_rows(i), cut] = (pre * sigmoid).astype(BF)
            slope[tile_rows(i), cut] = (sigmoid * (1.0 + pre * (1.0 - sigmoid))).astype(BF)
        return 0

    lax.fori_loop(0, 4, feed, 0)
    net.move(act, act_out)
    net.move(slope, slope_out)
    for gather in outers:
        gather.finish()
    net.finish()


def ahead(x, mem, top, ids, bias, weights, vectors):
    length, width = 1024, x.shape[-1]
    shape = jax.ShapeDtypeStruct
    quarters = (4, 2, 128, width)
    rows = lambda columns, kind=BF: shape((length, columns), kind)
    sums = shape((8, 4, 256), F32)
    return call_remote(
        ahead_kernel, 1,
        [a.reshape(2, 2, -1, width) for a in (x, mem, top)] + [ids, bias] + list(weights) + [v[None] for v in vectors],
        [ANY] * 15 + [VM] * 8,
        [
            shape(quarters, BF), shape(quarters, BF), shape(quarters, BF), rows(width), rows(1536), rows(512), sums,
            rows(width, F32), rows(width), rows(512), rows(1024), rows(512), sums,
            rows(width, F32), rows(width), rows(2048), rows(2048),
            shape((width, 1536), BF), shape((512, width), BF), shape((width, 1536), BF), shape((512, width), BF),
            shape((width, 2048), BF), shape((2048, width), BF), shape((4, 8, 128), jnp.int32),
        ],
        [ANY] * 24,
        [pltpu.VMEM((4, 128, width), BF)] * 3 + [pltpu.VMEM(quarters, BF)] * 2 + [pltpu.VMEM((width, 1536), BF)] * 2
        + [pltpu.VMEM((512, width), BF)] * 2
        + [
            pltpu.VMEM((width, 2048), BF), pltpu.VMEM((length, width), BF), pltpu.VMEM((length, 1536), BF),
            pltpu.VMEM((length, 512), BF), pltpu.VMEM(quarters, BF), pltpu.VMEM(quarters, BF), pltpu.VMEM(quarters, BF),
            pltpu.VMEM((length, width), F32), pltpu.VMEM((length, 512), BF), pltpu.VMEM((length, 1024), BF),
            pltpu.VMEM((length, 2048), BF), pltpu.VMEM((length, 2048), BF), pltpu.VMEM((4, 8, 128), F32),
            pltpu.VMEM((4, 16, 128), jnp.int32), pltpu.VMEM((4, 8, 128), jnp.int32),
            pltpu.VMEM((8, 4, 256), F32), pltpu.VMEM((8, 4, 256), F32),
            pltpu.VMEM((4, 128, 256), F32), pltpu.VMEM((4, 256), F32), pltpu.VMEM((4, 256), F32),
        ],
        vmem=62, name="ahead",
    )


def turn_kernel(
    act_in, slope_in, n3_in, h2_in, top_in, wi_in, wu_in, wco_in, q_in, kv_in, att_in, sums_in, reach_in, gain, bias_u,
    block_out, gh_out, outer_out, inner_out, heads_out, vectors_out, split_out,
    act, slope, wu, wi, g_outer, g_inner, hidden, row, normed, wco, part, back_in, out_part, out_in, gatt,
    pieces, rows_back, acc_k, acc_v, acc, spans, sums, vectors, split, *rest,
):
    lands, (sems, local_sems) = rest[:-2], rest[-2:]
    net = Net(sems, local_sems)
    core = net.core_index
    loads = [
        net.move(source, target)
        for source, target in (
            (act_in, act), (top_in, row), (wu_in, wu), (slope_in, slope), (n3_in, normed), (wi_in, wi), (h2_in, hidden),
            (wco_in, wco), (reach_in, spans), (sums_in, sums),
        )
    ]
    net.meet()
    whole_row = lambda: row[...].reshape(1024, -1)
    outers = [
        Scatter(net, lambda s, k=k: g_outer.at[pl.ds(s * 512 + k * 256, 256)], 1 + k, lands[k * 3:k * 3 + 3])
        for k in range(2)
    ]
    outer_lines = [
        Line(
            net, g_outer.at[pl.ds(k * 256, 256)], lands[12 + k * 2:14 + k * 2],
            lambda c, h, k=k: outer_out.at[pl.ds(pl.multiple_of(c * 512 + k * 256 + h * 128, 128), 128)],
        )
        for k in range(2)
    ]
    inners = [
        Scatter(
            net, lambda s, k=k: g_inner.at[pl.ds(k * 512, 512), s * 512:s * 512 + 512], 1 + k,
            lands[6 + k * 3:9 + k * 3],
        )
        for k in range(2)
    ]

    def outer_grad(k, s):
        weight_grad(lambda cut: act[:, cut], whole_row, g_outer, s * 512 + k * 256, 256)

    def inner_grad(k, s):
        cut = slice(s * 512, s * 512 + 512)
        weight_grad(lambda rows: normed[:, rows], lambda: slope[:, cut], g_inner, k * 512, 512, cut)

    net.moved(loads[0])
    net.moved(loads[1])
    for k in range(2):
        outer_grad(k, 3)
        outer_grad(k, 1 + k)
        outers[k].start()
    for k in range(2):
        outer_grad(k, 2 - k)
        outer_grad(k, 0)
    for copy in loads[2:]:
        net.moved(copy)
    split[...] = jnp.zeros_like(split)
    vectors[...] = jnp.zeros_like(vectors)

    def feed_back(i, _):
        tokens = row[i].reshape(256, -1)
        for s in range(4):
            cut = slice(s * 512, s * 512 + 512)
            value = (dot(tokens, wu[cut], NT) * slope[tile_rows(i), cut].astype(F32)).astype(BF)
            slope[tile_rows(i), cut] = value
            split[0:1, cut] += jnp.sum(value.astype(F32), axis=0, keepdims=True)
        return 0

    lax.fori_loop(0, 4, feed_back, 0)
    swaps = []
    for i in range(4):
        value = dot(slope[i * 256:i * 256 + 256], wi[...], NT)
        part[i] = value.astype(BF).reshape(2, 128, -1)
        swaps.append(net.send(part.at[i], back_in.at[i], net.core))
    for k in range(2):
        inner_grad(k, 3)
        inner_grad(k, 1 + k)
        inners[k].start()
    outers[0].middle()
    outers[1].middle()
    for copy in swaps:
        copy.wait_recv()

    def feed_out(i, _):
        out_part[i] = dot(act[tile_rows(i)], wu[...], NN).astype(BF).reshape(2, 128, -1)
        return 0

    lax.fori_loop(0, 4, feed_out, 0)
    out_swap = net.send(out_part.at[:, 1 - core], out_in, net.core)
    loads = [
        net.move(kv_in, act.at[:, :1024]), net.move(q_in, act.at[:, 1024:1536]), net.move(att_in, act.at[:, 1536:]),
    ]
    for k in range(2):
        inner_grad(k, 2 - k)
        inner_grad(k, 0)
    out_swap.wait_recv()
    for i in range(4):
        pieces[i] = (hidden[i, core] + out_part[i, core].astype(F32) + out_in[i].astype(F32) + bias_u[...]).astype(BF)
    leave = row_out(net, pieces, rows_back, block_out)
    next(leave)

    def back(i, _):
        grad = (part[i].astype(F32) + back_in[i].astype(F32)).reshape(256, -1)
        change, by_gain, by_shift = norm_back_tile(grad, hidden[i].reshape(256, -1), gain[...])
        top = row[i].reshape(256, -1).astype(F32)
        value = top + change
        hidden[i] = value.reshape(2, 128, -1)
        gatt[tile_rows(i)] = dot(value.astype(BF), wco[...], NT).astype(BF)
        vectors[4:5] += by_gain
        vectors[5:6] += by_shift
        vectors[6:7] += jnp.sum(top, axis=0, keepdims=True)
        vectors[3:4] += jnp.sum(value, axis=0, keepdims=True)
        return 0

    lax.fori_loop(0, 4, back, 0)
    net.move(hidden, gh_out)
    net.move(vectors, vectors_out)
    net.move(split, split_out)
    outers[0].own()
    outer_lines[0].line0()
    outers[1].own()
    outer_lines[1].line0()
    inners[0].middle()
    inners[1].middle()
    for copy in loads:
        net.moved(copy)
    acc_k[...] = jnp.zeros_like(acc_k)
    acc_v[...] = jnp.zeros_like(acc_v)

    def attend_back(i, _):
        attend_back_block(
            i, act, 1024, act, 0, 512, gatt, act, 1536, sums, spans.at[2], spans.at[3], False, slope, 0, acc, acc_k, acc_v
        )
        return 0

    lax.fori_loop(0, 3, attend_back, 0)
    outer_lines[0].line1()
    outer_lines[1].line1()
    next(leave)
    lax.fori_loop(3, 6, attend_back, 0)
    outer_lines[0].line2()
    outer_lines[1].line2()
    inners[0].own()
    net.move(g_inner.at[pl.ds(0, 512), :512], inner_out.at[pl.ds(0, 512)])
    inners[1].own()
    net.move(g_inner.at[pl.ds(512, 512), :512], inner_out.at[pl.ds(512, 512)])
    lax.fori_loop(6, 8, attend_back, 0)
    slope[:, 512:1024] = acc_k[...].astype(BF)
    slope[:, 1024:1536] = acc_v[...].astype(BF)
    net.move(slope.at[:, :1536], heads_out)
    outer_lines[0].line3()
    outer_lines[1].line3()
    for line in outer_lines:
        line.end()
    for _ in leave:
        pass
    net.finish()


def turn(act, slope, n3, h2, top, wi, wu, wco, q, kv, att, sums, reach_rows, gain, bias_u):
    length, width = act.shape[0], n3.shape[-1]
    shape = jax.ShapeDtypeStruct
    quarters = (4, 2, 128, width)
    return call_remote(
        turn_kernel, 2,
        (
            act, slope, n3, h2.reshape(quarters), top, wi, wu, wco, q, kv, att, sums, reach_rows, gain[None], bias_u[None],
        ),
        [ANY] * 13 + [VM] * 2,
        [
            shape((2, 2, 128, width), BF), shape(quarters, F32), shape((1024, width), BF), shape((width, 512), BF),
            shape((length, 1536), BF), shape((8, width), F32), shape((8, 2048), F32),
        ],
        [ANY] * 7,
        [
            pltpu.VMEM((length, 2048), BF), pltpu.VMEM((length, 2048), BF), pltpu.VMEM((2048, width), BF),
            pltpu.VMEM((width, 2048), BF), pltpu.VMEM((2048, width), BF), pltpu.VMEM((width, 2048), BF),
            pltpu.VMEM(quarters, F32), pltpu.VMEM(quarters, BF), pltpu.VMEM((length, width), BF),
            pltpu.VMEM((512, width), BF), pltpu.VMEM(quarters, BF), pltpu.VMEM(quarters, BF), pltpu.VMEM(quarters, BF),
            pltpu.VMEM((4, 128, width), BF), pltpu.VMEM((length, 512), BF),
            pltpu.VMEM((4, 128, width), BF), pltpu.VMEM((4, 128, width), BF),
            pltpu.VMEM((length, 512), F32), pltpu.VMEM((length, 512), F32), pltpu.VMEM((4, 128, 256), F32),
            pltpu.VMEM((4, 8, 128), jnp.int32), pltpu.VMEM((8, 4, 256), F32),
            pltpu.VMEM((8, width), F32), pltpu.VMEM((8, 2048), F32),
        ]
        + landing(256, width) * 2 + landing(512, 512) * 2 + line_landing(256, width) * 2,
        vmem=62, name="turn",
    )


def last_kernel(
    heads_in, n2_in, mem_in, att2_in, gh_in, h1_in, wc_in, wo_in, inner_in, qkv_in, att1_in, sums_in, reach_in, n1_in, x_in,
    wqkv_in, shared_in, split_in, gain2, gain1,
    mem_out, grad_out, cross_out, cross_o_out, heads_out, o_out, inner_out, shared_out, late_out, split_out,
    dqkv, normed, tokens, att, grads, hidden, weights, wo, part, part_in, mem_part, mem_back, grad_in,
    pieces_mem, rows_mem, pieces, rows_back, g_cross, g_cross_o, g_heads, g_o, gatt, acc, spans, sums,
    inner_total,
    shared, shared_land, late, late_land, split, split_land, split_full, *rest,
):
    lands, (sems, local_sems) = rest[:-2], rest[-2:]
    net = Net(sems, local_sems)
    core, chip = net.core_index, net.chip
    place = lax.axis_index("dp")
    loads = [
        net.move(source, target)
        for source, target in (
            (heads_in, dqkv), (wc_in, weights), (inner_in, inner_total), (mem_in, tokens), (n2_in, normed), (att2_in, att),
            (gh_in, grads), (h1_in, hidden), (wo_in, wo), (reach_in, spans), (sums_in, sums), (shared_in, shared),
            (split_in, split),
        )
    ]
    net.meet()
    inner_lines = [
        Line(
            net, inner_total.at[pl.ds(k * 512, 512)], lands[40 + k * 2:42 + k * 2],
            lambda c, h, k=k: inner_out.at[
                pl.ds(pl.multiple_of(k * 512 + h * 256, 256), 256), pl.ds(pl.multiple_of(c * 512, 512), 512)
            ],
        )
        for k in range(2)
    ]
    scatters = head_scatters(net, g_cross, g_cross_o, lands[:12])
    lines = head_lines(
        net, lambda kind: g_cross.at[:, kind * 512:kind * 512 + 128], g_cross_o.at[pl.ds(0, 128)], cross_out,
        cross_o_out, lands[12:20],
    )
    for copy in loads[:3]:
        net.moved(copy)
    inner_lines[0].line0()
    inner_lines[1].line0()
    swaps = []
    for i in range(4):
        value = dot(dqkv[i * 256:i * 256 + 256, :512], weights[:, :512], NT)
        part[i] = value.astype(BF).reshape(2, 128, -1)
        swaps.append(net.send(part.at[i], part_in.at[i], net.core))
    for copy in loads[3:]:
        net.moved(copy)
    memory = lambda cut: tokens[:, :, :, cut].reshape(1024, -1)
    for kind in (1, 2):
        cut = slice(kind * 512, kind * 512 + 512)
        weight_grad(memory, lambda: dqkv[:, cut], g_cross, 0, 1024, cut)
        scatters[kind].start()

    def memory_back(i, _):
        rows = tile_rows(i)
        value = dot(dqkv[rows, 512:1024], weights[:, 512:1024], NT) + dot(dqkv[rows, 1024:], weights[:, 1024:], NT)
        mem_part[i] = value.astype(BF).reshape(2, 128, -1)
        return 0

    lax.fori_loop(0, 4, memory_back, 0)
    mem_swap = net.send(mem_part.at[:, 1 - core], mem_back, net.core)
    load_qkv = net.move(qkv_in, weights)
    load_x = net.move(x_in, tokens)
    weight_grad(lambda cut: normed[:, cut], lambda: dqkv[:, :512], g_cross, 0, 1024, slice(0, 512))
    load_n1 = net.move(n1_in, normed)
    weight_grad(lambda cut: att[:, cut], lambda: grads[...].reshape(1024, -1).astype(BF), g_cross_o, 0, 512)
    load_att = net.move(att1_in, att)
    for at, kind in ((2, 0), (3, 2)):
        total = jnp.sum(dqkv[:, kind * 512:kind * 512 + 512].astype(F32), axis=0, keepdims=True)
        for s in range(4):
            split[s, at:at + 1] = total[:, s * 128:s * 128 + 128]
    for copy in swaps:
        copy.wait_recv()

    def back(i, _):
        grad = (part[i].astype(F32) + part_in[i].astype(F32)).reshape(256, -1)
        change, by_gain, by_shift = norm_back_tile(grad, hidden[tile_rows(i)], gain2[...])
        value = grads[i].reshape(256, -1) + change
        grads[i] = value.reshape(2, 128, -1)
        gatt[tile_rows(i)] = dot(value.astype(BF), wo[...], NT).astype(BF)
        shared[1:2] += by_gain
        shared[2:3] += by_shift
        shared[0:1] += jnp.sum(value, axis=0, keepdims=True)
        return 0

    lax.fori_loop(0, 4, back, 0)
    scatters[1].middle()
    scatters[2].middle()
    scatters[0].start()
    scatters[3].start()
    mem_swap.wait_recv()
    for i in range(4):
        pieces_mem[i] = (mem_part[i, core].astype(F32) + mem_back[i].astype(F32)).astype(BF)
    leave_mem = row_out(net, pieces_mem, rows_mem, mem_out)
    next(leave_mem)
    inner_lines[0].line1()
    inner_lines[1].line1()
    stages = [(place, net.chips[0]), (place, net.chips[1]), net.near_plane, net.far_plane]
    shared_copy = net.send(shared, shared_land.at[0], stages[0])

    def shared_stage(at):
        nonlocal shared_copy
        shared_copy.wait_recv()
        net.sent(shared_copy)
        shared[...] += shared_land[at]
        if at < 3:
            shared_copy = net.send(shared, shared_land.at[at + 1], stages[at + 1])

    hidden[...] = jnp.zeros_like(hidden)
    for copy in (load_qkv, load_att):
        net.moved(copy)

    def attend_back(i, _):
        attend_back_block(
            i, weights, 0, weights, 512, 1024, gatt, att, 0, sums, spans.at[0], spans.at[1], True, dqkv, 0, acc,
            hidden.at[:, :512], hidden.at[:, 512:],
        )
        return 0

    lax.fori_loop(0, 4, attend_back, 0)
    scatters[1].own()
    lines[1].line0()
    scatters[2].own()
    lines[2].line0()
    scatters[0].middle()
    scatters[3].middle()
    inner_lines[0].line2()
    inner_lines[1].line2()
    next(leave_mem)
    shared_stage(0)
    lax.fori_loop(4, 6, attend_back, 0)
    lines[1].line1()
    lines[2].line1()
    scatters[0].own()
    scatters[3].own()
    lines[0].line0()
    lines[3].line0()
    inner_lines[0].line3()
    inner_lines[1].line3()
    shared_stage(1)
    lax.fori_loop(6, 8, attend_back, 0)
    load_w = net.move(wqkv_in, weights)
    dqkv[:, 512:] = hidden[...].astype(BF)
    lines[1].line2()
    lines[2].line2()
    lines[0].line1()
    lines[3].line1()
    shared_stage(2)
    for copy in (load_n1, load_x):
        net.moved(copy)
    own_scatters = head_scatters(net, g_heads, g_o, lands[20:32])
    own_lines = head_lines(
        net, lambda kind: g_heads.at[:, kind * 512:kind * 512 + 128], g_o.at[pl.ds(0, 128)], heads_out, o_out,
        lands[32:40],
    )

    def head_grad(kind):
        cut = slice(kind * 512, kind * 512 + 512)
        weight_grad(lambda rows: normed[:, rows], lambda: dqkv[:, cut], g_heads, 0, 1024, cut)

    head_grad(0)
    own_scatters[0].start()
    head_grad(2)
    own_scatters[2].start()
    net.moved(load_w)
    for copy in swaps:
        net.sent(copy)

    def first_back(i, _):
        part[i] = dot(dqkv[tile_rows(i)], weights[...], NT).astype(BF).reshape(2, 128, -1)
        return 0

    lax.fori_loop(0, 4, first_back, 0)
    swap = net.send(part.at[:, 1 - core], grad_in, net.core)
    head_grad(1)
    weight_grad(lambda cut: att[:, cut], lambda: grads[...].reshape(1024, -1).astype(BF), g_o, 0, 512)
    own_scatters[0].middle()
    own_scatters[2].middle()
    own_scatters[1].start()
    own_scatters[3].start()
    lines[1].line3()
    lines[2].line3()
    lines[0].line2()
    lines[3].line2()
    shared_stage(3)
    for at, kind in ((0, 0), (1, 2)):
        total = jnp.sum(dqkv[:, kind * 512:kind * 512 + 512].astype(F32), axis=0, keepdims=True)
        for s in range(4):
            split[s, at:at + 1] = total[:, s * 128:s * 128 + 128]
    split_copies = [
        net.send(split.at[s], split_land.at[s - 1], device)
        for s, device in ((1, net.first), (2, net.second), (3, net.corner))
    ]
    swap.wait_recv()
    late[...] = jnp.zeros_like(late)
    for i in range(4):
        grad = part[i, core].astype(F32) + grad_in[i].astype(F32)
        change, by_gain, by_shift = norm_back_tile(grad, tokens[i, core].astype(F32), gain1[...])
        pieces[i] = (grads[i, core] + change).astype(BF)
        late[0:1] += by_gain
        late[1:2] += by_shift
    late_copy = net.send(late, late_land.at[0], net.core)
    leave = row_out(net, pieces, rows_back, grad_out)

    def late_stage(at):
        nonlocal late_copy
        late_copy.wait_recv()
        net.sent(late_copy)
        late[...] += late_land[at]
        if at < 4:
            late_copy = net.send(late, late_land.at[at + 1], stages[at])

    def split_stage(at):
        nonlocal split_copies
        for copy in split_copies:
            copy.wait_recv()
            net.sent(copy)
        if at == 0:
            split[0] = split[0] + split_land[0] + split_land[1] + split_land[2]
        else:
            split[0] = split[0] + split_land[2 + at]
        if at < 2:
            device = (net.near_plane, net.far_plane)[at]
            split_copies = [net.send(split.at[0], split_land.at[3 + at], device)]
        else:
            split_full[core] = split[0]
            split_copies = [net.send(split_full.at[core], split_full.at[core], net.core)]

    own_scatters[0].own()
    own_lines[0].line0()
    own_scatters[2].own()
    own_lines[2].line0()
    lines[0].line3()
    lines[3].line3()
    late_stage(0)
    split_stage(0)
    own_scatters[1].middle()
    own_scatters[3].middle()
    next(leave)
    late_stage(1)
    own_lines[0].line1()
    own_lines[2].line1()
    split_stage(1)
    late_stage(2)
    own_scatters[1].own()
    own_lines[1].line0()
    own_scatters[3].own()
    own_lines[3].line0()
    own_lines[0].line2()
    own_lines[2].line2()
    late_stage(3)
    split_stage(2)
    own_lines[1].line1()
    own_lines[3].line1()
    next(leave)
    late_stage(4)
    own_lines[0].line3()
    own_lines[2].line3()
    own_lines[1].line2()
    own_lines[3].line2()
    own_lines[1].line3()
    own_lines[3].line3()
    for line in inner_lines + lines + own_lines:
        line.end()
    for _ in leave_mem:
        pass
    for _ in leave:
        pass
    split_copies[0].wait_recv()
    for source, target in (
        (shared, shared_out), (late, late_out), (split_full, split_out),
    ):
        net.move(source, target)
    net.finish()


def last(heads, n2, mem, att2, gh, h1, wc, wo, inner_total, qkv, att1, sums, reach_rows, n1, x, wqkv, shared, split, gain2, gain1):
    length, width = heads.shape[0], n1.shape[-1]
    shape = jax.ShapeDtypeStruct
    quarters = (4, 2, 128, width)
    own = [shape((3, width, 256), BF), shape((256, width), BF)]
    return call_remote(
        last_kernel, 3,
        (
            heads, n2, mem, att2, gh, h1, wc, wo, inner_total, qkv, att1, sums, reach_rows, n1, x, wqkv, shared, split,
            gain2[None], gain1[None],
        ),
        [ANY] * 18 + [VM] * 2,
        [shape((2, 2, 128, width), BF)] * 2 + own + own
        + [shape((width, 1024), BF), shape((8, width), F32), shape((8, width), F32), shape((2, 8, 128), F32)],
        [ANY] * 10,
        [
            pltpu.VMEM((length, 1536), BF), pltpu.VMEM((length, width), BF), pltpu.VMEM(quarters, BF),
            pltpu.VMEM((length, 512), BF), pltpu.VMEM(quarters, F32), pltpu.VMEM((length, width), F32),
            pltpu.VMEM((width, 1536), BF), pltpu.VMEM((512, width), BF), pltpu.VMEM(quarters, BF),
            pltpu.VMEM(quarters, BF), pltpu.VMEM(quarters, BF), pltpu.VMEM((4, 128, width), BF),
            pltpu.VMEM((4, 128, width), BF),
        ]
        + [pltpu.VMEM((4, 128, width), BF)] * 4
        + [pltpu.VMEM((width, 1536), BF), pltpu.VMEM((512, width), BF)] * 2
        + [
            pltpu.VMEM((length, 512), BF), pltpu.VMEM((4, 128, 256), F32), pltpu.VMEM((4, 8, 128), jnp.int32),
            pltpu.VMEM((8, 4, 256), F32), pltpu.VMEM((width, 512), BF),
        ]
        + [
            pltpu.VMEM((8, width), F32), pltpu.VMEM((4, 8, width), F32),
            pltpu.VMEM((8, width), F32), pltpu.VMEM((5, 8, width), F32),
            pltpu.VMEM((4, 8, 128), F32), pltpu.VMEM((5, 8, 128), F32), pltpu.VMEM((2, 8, 128), F32),
        ]
        + (head_landing(width) + head_line_landing(width)) * 2 + line_landing(512, 512) * 2,
        vmem=63, name="last",
    )


def solution(mesh):
    if mesh.shape["tensor"] != 4 or mesh.shape["dp"] != 8:
        return general_solution(mesh)

    def local(
        layer_input, memory, grad_out, target_segments, source_segments,
        self_gain, self_shift, query_weight, query_bias, key_weight, value_weight, value_bias,
        attend_weight, attend_bias,
        cross_gain, cross_shift, cross_query, cross_query_bias, cross_key, cross_value, cross_value_bias,
        cross_attend, cross_attend_bias,
        feed_gain, feed_shift, inner_weight, inner_bias, outer_weight, outer_bias,
    ):
        core = lax.axis_index("dp") % 2
        half = lambda b: lax.dynamic_slice_in_dim(b, core * (b.shape[0] // 2), b.shape[0] // 2)
        ids = jnp.stack([target_segments, source_segments], axis=1).reshape(2, 16, 128)
        biases = jnp.concatenate([half(b) for b in (query_bias, value_bias, cross_query_bias, cross_value_bias, inner_bias)])
        (
            x, mem, top, n1, qkv1, att1, sums1, h1, n2, q2, kv2, att2, sums2, h2, n3, act, slope,
            wqkv, wo, wc, wco, wi, wu, spans,
        ) = ahead(
            layer_input, memory, grad_out, ids, biases.reshape(8, 128),
            (
                query_weight, key_weight, value_weight, attend_weight, cross_query, cross_key, cross_value, cross_attend,
                inner_weight, outer_weight,
            ),
            (self_gain, self_shift, attend_bias, cross_gain, cross_shift, cross_attend_bias, feed_gain, feed_shift),
        )
        block_out, gh2, f_outer, f_inner, heads2, shared, split = turn(
            act, slope, n3, h2, top, wi, wu, wco, q2, kv2, att2, sums2, spans, feed_gain, outer_bias
        )
        split = jnp.concatenate([jnp.zeros((4, 4, 128), F32), split[0].reshape(4, 4, 128)], axis=1)
        memory_grad, input_grad, c_heads, c_out, s_heads, s_out, f_inner, shared, late, split = last(
            heads2, n2, mem, att2, gh2, h1, wc, wo, f_inner, qkv1, att1, sums1, spans, n1, x, wqkv, shared, split,
            cross_gain, self_gain,
        )
        split_of = lambda at, rows: split[:, at:at + rows].reshape(-1)
        tokens = layer_input.shape
        return (
            block_out.reshape(tokens), input_grad.reshape(tokens).astype(F32), memory_grad.reshape(tokens).astype(F32),
            late[0], late[1],
            s_heads[0].astype(F32), split_of(0, 1), s_heads[1].astype(F32), s_heads[2].astype(F32), split_of(1, 1),
            s_out.astype(F32), shared[0],
            shared[1], shared[2],
            c_heads[0].astype(F32), split_of(2, 1), c_heads[1].astype(F32), c_heads[2].astype(F32), split_of(3, 1),
            c_out.astype(F32), shared[3],
            shared[4], shared[5],
            f_inner.astype(F32), split_of(4, 4), f_outer.astype(F32), shared[6],
        )

    row, one, by_column, by_row = P("dp", "tensor", None), P(), P(None, "tensor"), P("tensor", None)
    part, ids = P("tensor"), P("dp", None)
    return jax.shard_map(
        local,
        mesh=mesh,
        in_specs=(
            row, row, row, ids, ids,
            one, one, by_column, part, by_column, by_column, part, by_row, one,
            one, one, by_column, part, by_column, by_column, part, by_row, one,
            one, one, by_column, part, by_row, one,
        ),
        out_specs=(
            row, row, row,
            one, one, by_column, part, by_column, by_column, part, by_row, one,
            one, one, by_column, part, by_column, by_column, part, by_row, one,
            one, one, by_column, part, by_row, one,
        ),
        check_vma=False,
    )


BLOCK_ROWS = 512


def general_norm_forward(values, gain, shift):
    average = jnp.mean(values, axis=-1, keepdims=True)
    center = values - average
    inverse = lax.rsqrt(jnp.mean(center * center, axis=-1, keepdims=True) + EPSILON)
    normed = center * inverse
    return ((normed * gain + shift).astype(jnp.bfloat16), normed, inverse)


def general_norm_backward(grad_in, normed, inverse, gain):
    scaled = grad_in * gain
    first_mean = jnp.mean(scaled, axis=-1, keepdims=True)
    second_mean = jnp.mean(scaled * normed, axis=-1, keepdims=True)
    grad_values = inverse * (scaled - first_mean - normed * second_mean)
    return (grad_values, jnp.sum(grad_in * normed, axis=(0, 1)), jnp.sum(grad_in, axis=(0, 1)))


def gather_rows(values):
    return lax.all_gather(values, "tensor", axis=1, tiled=True)


def gather_grads(values):
    return lax.all_gather(values, "tensor", axis=1, tiled=True)


def reduce_inputs(partial_sum):
    return lax.psum_scatter(partial_sum, "tensor", scatter_dimension=1, tiled=True)


def advance(base, partial_sum, bias):
    return base + lax.psum_scatter(partial_sum, "tensor", scatter_dimension=1, tiled=True) + bias


def next_rows(values, gain, shift):
    return gather_rows(general_norm_forward(values, gain, shift)[0])


def backward_rows(normed_low):
    return gather_rows(normed_low)


def project(rows_in, weight):
    return jnp.einsum("rtd,dc->rtc", rows_in, weight, preferred_element_type=jnp.float32)


def project_back(grads, weight):
    return jnp.einsum("rtc,dc->rtd", grads, weight, preferred_element_type=jnp.float32)


def outer_sum(rows_in, grads):
    return jnp.einsum("rtd,rtc->dc", rows_in, grads, preferred_element_type=jnp.float32)


def bias_sum(grads):
    return jnp.sum(grads.astype(jnp.float32), axis=(0, 1))


def split_heads(values):
    return values.reshape(values.shape[0], values.shape[1], values.shape[2] // HD, HD)


def block_scores(query_block, key_row, query_ids, key_ids, row_start, causal):
    raw_scores = jnp.einsum(
        "qhd,khd->hqk", query_block, key_row, preferred_element_type=jnp.float32
    ) * float(HD) ** (-0.5)
    allowed = query_ids[:, None] == key_ids[None, :]
    if causal:
        query_place = row_start + jnp.arange(query_block.shape[0], dtype=jnp.int32)
        key_place = jnp.arange(key_row.shape[0], dtype=jnp.int32)
        allowed = allowed & (key_place[None, :] <= query_place[:, None])
    return jnp.where(allowed[None], raw_scores, jnp.full(raw_scores.shape, MASKED, jnp.float32))


def block_inputs(
    query_heads, key_heads, value_heads, query_ids, key_ids, position, block_count, block_size
):
    row_index = position // block_count
    row_start = position % block_count * block_size
    query_row = lax.dynamic_index_in_dim(query_heads, row_index, 0, keepdims=False)
    query_block = lax.dynamic_slice_in_dim(query_row, row_start, block_size, 0)
    key_row = lax.dynamic_index_in_dim(key_heads, row_index, 0, keepdims=False)
    value_row = lax.dynamic_index_in_dim(value_heads, row_index, 0, keepdims=False)
    query_seg = lax.dynamic_slice_in_dim(
        lax.dynamic_index_in_dim(query_ids, row_index, 0, keepdims=False), row_start, block_size, 0
    )
    key_seg = lax.dynamic_index_in_dim(key_ids, row_index, 0, keepdims=False)
    return (row_index, row_start, query_block, key_row, value_row, query_seg, key_seg)


def attend_forward(query, keys, values, query_ids, key_ids, causal):
    query_heads = split_heads(query)
    key_heads = split_heads(keys)
    value_heads = split_heads(values)
    block_size = min(BLOCK_ROWS, query.shape[1])
    block_count = query.shape[1] // block_size

    def one_block(position):
        row_index, row_start, query_block, key_row, value_row, query_seg, key_seg = block_inputs(
            query_heads,
            key_heads,
            value_heads,
            query_ids,
            key_ids,
            position,
            block_count,
            block_size,
        )
        scores = block_scores(query_block, key_row, query_seg, key_seg, row_start, causal)
        row_max = jnp.max(scores, axis=-1, keepdims=True)
        expo_scores = jnp.exp(scores - row_max)
        row_total = jnp.sum(expo_scores, axis=-1, keepdims=True)
        softmax_out = expo_scores / row_total
        attended = jnp.einsum(
            "hqk,khd->qhd",
            softmax_out.astype(jnp.bfloat16),
            value_row,
            preferred_element_type=jnp.float32,
        ).astype(jnp.bfloat16)
        return (attended, (row_max + jnp.log(row_total))[..., 0])

    attended_all, log_sums = lax.map(
        one_block, jnp.arange(query.shape[0] * block_count, dtype=jnp.int32)
    )
    return (attended_all.reshape(query.shape), log_sums)


def attend_backward(query, keys, values, grad_att, log_sums, query_ids, key_ids, causal):
    query_heads = split_heads(query)
    key_heads = split_heads(keys)
    value_heads = split_heads(values)
    grad_heads = split_heads(grad_att)
    block_size = min(BLOCK_ROWS, query.shape[1])
    block_count = query.shape[1] // block_size
    score_scale = float(HD) ** (-0.5)

    def one_block(carry, inputs):
        grad_keys, grad_values = carry
        position, log_sum = inputs
        row_index, row_start, query_block, key_row, value_row, query_seg, key_seg = block_inputs(
            query_heads,
            key_heads,
            value_heads,
            query_ids,
            key_ids,
            position,
            block_count,
            block_size,
        )
        grad_row = lax.dynamic_index_in_dim(grad_heads, row_index, 0, keepdims=False)
        grad_block = lax.dynamic_slice_in_dim(grad_row, row_start, block_size, 0)
        scores = block_scores(query_block, key_row, query_seg, key_seg, row_start, causal)
        softmax_out = jnp.exp(scores - log_sum[..., None])
        softmax_low = softmax_out.astype(jnp.bfloat16)
        attended = jnp.einsum(
            "hqk,khd->qhd", softmax_low, value_row, preferred_element_type=jnp.float32
        ).astype(jnp.bfloat16)
        grad_prob = jnp.einsum(
            "qhd,khd->hqk", grad_block, value_row, preferred_element_type=jnp.float32
        )
        correction = jnp.sum(softmax_out * grad_prob, axis=-1, keepdims=True)
        grad_score = (softmax_out * (grad_prob - correction)).astype(jnp.bfloat16)
        grad_query = (
            jnp.einsum("hqk,khd->qhd", grad_score, key_row, preferred_element_type=jnp.float32)
            * score_scale
        ).astype(jnp.bfloat16)
        key_added = (
            jnp.einsum("hqk,qhd->khd", grad_score, query_block, preferred_element_type=jnp.float32)
            * score_scale
        )
        value_added = jnp.einsum(
            "hqk,qhd->khd", softmax_low, grad_block, preferred_element_type=jnp.float32
        )
        grad_keys = grad_keys.at[row_index].add(key_added)
        grad_values = grad_values.at[row_index].add(value_added)
        return ((grad_keys, grad_values), (grad_query, attended))

    empty_grads = jnp.zeros(key_heads.shape, jnp.float32)
    positions = jnp.arange(query.shape[0] * block_count, dtype=jnp.int32)
    (grad_keys, grad_values), (grad_query, attended_all) = lax.scan(
        one_block, (empty_grads, empty_grads), (positions, log_sums)
    )
    return (
        grad_query.reshape(query.shape),
        grad_keys.reshape(keys.shape).astype(jnp.bfloat16),
        grad_values.reshape(values.shape).astype(jnp.bfloat16),
        attended_all.reshape(query.shape),
    )


def general_local(
    layer_input,
    memory,
    grad_out,
    target_segments,
    source_segments,
    self_gain,
    self_shift,
    query_weight,
    query_bias,
    key_weight,
    value_weight,
    value_bias,
    attend_weight,
    attend_bias,
    cross_gain,
    cross_shift,
    cross_query,
    cross_query_bias,
    cross_key,
    cross_value,
    cross_value_bias,
    cross_attend,
    cross_attend_bias,
    feed_gain,
    feed_shift,
    inner_weight,
    inner_bias,
    outer_weight,
    outer_bias,
):
    inputs = layer_input.astype(jnp.float32)
    rows_first = next_rows(inputs, self_gain, self_shift)
    query_first = (project(rows_first, query_weight) + query_bias).astype(jnp.bfloat16)
    keys_first = project(rows_first, key_weight).astype(jnp.bfloat16)
    values_first = (project(rows_first, value_weight) + value_bias).astype(jnp.bfloat16)
    attended_first, sums_first = attend_forward(
        query_first, keys_first, values_first, target_segments, target_segments, True
    )
    base_first = advance(inputs, project(attended_first, attend_weight), attend_bias)
    memory_rows = lax.all_gather(memory, "tensor", axis=1, tiled=True)
    rows_second = next_rows(base_first, cross_gain, cross_shift)
    query_second = (project(rows_second, cross_query) + cross_query_bias).astype(jnp.bfloat16)
    keys_second = project(memory_rows, cross_key).astype(jnp.bfloat16)
    values_second = (project(memory_rows, cross_value) + cross_value_bias).astype(jnp.bfloat16)
    attended_second, sums_second = attend_forward(
        query_second, keys_second, values_second, target_segments, source_segments, False
    )
    base_second = advance(base_first, project(attended_second, cross_attend), cross_attend_bias)
    rows_third = next_rows(base_second, feed_gain, feed_shift)
    pre_active = project(rows_third, inner_weight) + inner_bias
    active = jax.nn.silu(pre_active).astype(jnp.bfloat16)
    base_out = advance(base_second, project(active, outer_weight), outer_bias)
    block_out = base_out.astype(jnp.bfloat16)
    kept_input, kept_first, kept_second, kept_memory, kept_sums_first, kept_sums_second = (
        lax.optimization_barrier(
            (inputs, base_first, base_second, memory_rows, sums_first, sums_second)
        )
    )
    grad_top = grad_out.astype(jnp.float32)
    normed_low3, unit_third, inverse_third = general_norm_forward(kept_second, feed_gain, feed_shift)
    rows_back3 = backward_rows(normed_low3)
    pre_back = project(rows_back3, inner_weight) + inner_bias
    sigmoid_back = jax.nn.sigmoid(pre_back)
    active_back = (pre_back * sigmoid_back).astype(jnp.bfloat16)
    grad_rows3 = gather_grads(grad_top.astype(jnp.bfloat16))
    grad_outer_weight = outer_sum(active_back, grad_rows3)
    grad_outer_bias = jnp.sum(grad_top, axis=(0, 1))
    grad_active = project_back(grad_rows3, outer_weight)
    grad_inner = (grad_active * sigmoid_back * (1.0 + pre_back * (1.0 - sigmoid_back))).astype(
        jnp.bfloat16
    )
    grad_inner_weight = outer_sum(rows_back3, grad_inner)
    grad_inner_bias = bias_sum(grad_inner)
    grad_norm3 = reduce_inputs(project_back(grad_inner, inner_weight))
    grad_from3, grad_feed_gain, grad_feed_shift = general_norm_backward(
        grad_norm3, unit_third, inverse_third, feed_gain
    )
    grad_hidden2 = grad_top + grad_from3
    normed_low2, unit_second, inverse_second = general_norm_forward(kept_first, cross_gain, cross_shift)
    rows_back2 = backward_rows(normed_low2)
    query_back2 = (project(rows_back2, cross_query) + cross_query_bias).astype(jnp.bfloat16)
    keys_back2 = project(kept_memory, cross_key).astype(jnp.bfloat16)
    values_back2 = (project(kept_memory, cross_value) + cross_value_bias).astype(jnp.bfloat16)
    grad_rows2 = gather_grads(grad_hidden2.astype(jnp.bfloat16))
    grad_att2 = project_back(grad_rows2, cross_attend).astype(jnp.bfloat16)
    grad_query2, grad_keys2, grad_values2, attended_back2 = attend_backward(
        query_back2,
        keys_back2,
        values_back2,
        grad_att2,
        kept_sums_second,
        target_segments,
        source_segments,
        False,
    )
    grad_cross_attend = outer_sum(attended_back2, grad_rows2)
    grad_cross_attend_bias = jnp.sum(grad_hidden2, axis=(0, 1))
    grad_cross_query = outer_sum(rows_back2, grad_query2)
    grad_cross_query_bias = bias_sum(grad_query2)
    grad_cross_key = outer_sum(kept_memory, grad_keys2)
    grad_cross_value = outer_sum(kept_memory, grad_values2)
    grad_cross_value_bias = bias_sum(grad_values2)
    memory_grad = lax.psum_scatter(
        (project_back(grad_keys2, cross_key) + project_back(grad_values2, cross_value)).astype(
            jnp.bfloat16
        ),
        "tensor",
        scatter_dimension=1,
        tiled=True,
    ).astype(jnp.float32)
    grad_norm2 = reduce_inputs(project_back(grad_query2, cross_query))
    grad_from2, grad_cross_gain, grad_cross_shift = general_norm_backward(
        grad_norm2, unit_second, inverse_second, cross_gain
    )
    grad_hidden1 = grad_hidden2 + grad_from2
    normed_low1, unit_first, inverse_first = general_norm_forward(kept_input, self_gain, self_shift)
    rows_back1 = backward_rows(normed_low1)
    query_back1 = (project(rows_back1, query_weight) + query_bias).astype(jnp.bfloat16)
    keys_back1 = project(rows_back1, key_weight).astype(jnp.bfloat16)
    values_back1 = (project(rows_back1, value_weight) + value_bias).astype(jnp.bfloat16)
    grad_rows1 = gather_grads(grad_hidden1.astype(jnp.bfloat16))
    grad_att1 = project_back(grad_rows1, attend_weight).astype(jnp.bfloat16)
    grad_query1, grad_keys1, grad_values1, attended_back1 = attend_backward(
        query_back1,
        keys_back1,
        values_back1,
        grad_att1,
        kept_sums_first,
        target_segments,
        target_segments,
        True,
    )
    grad_attend_weight = outer_sum(attended_back1, grad_rows1)
    grad_attend_bias = jnp.sum(grad_hidden1, axis=(0, 1))
    grad_query_weight = outer_sum(rows_back1, grad_query1)
    grad_query_bias = bias_sum(grad_query1)
    grad_key_weight = outer_sum(rows_back1, grad_keys1)
    grad_value_weight = outer_sum(rows_back1, grad_values1)
    grad_value_bias = bias_sum(grad_values1)
    grad_norm1 = reduce_inputs(
        project_back(grad_query1, query_weight)
        + project_back(grad_keys1, key_weight)
        + project_back(grad_values1, value_weight)
    )
    grad_from1, grad_self_gain, grad_self_shift = general_norm_backward(
        grad_norm1, unit_first, inverse_first, self_gain
    )
    input_grad = grad_hidden1 + grad_from1
    (
        grad_query_weight,
        grad_query_bias,
        grad_key_weight,
        grad_value_weight,
        grad_value_bias,
        grad_attend_weight,
        grad_cross_query,
        grad_cross_query_bias,
        grad_cross_key,
        grad_cross_value,
        grad_cross_value_bias,
        grad_cross_attend,
        grad_inner_weight,
        grad_inner_bias,
        grad_outer_weight,
    ) = (
        lax.psum(grad_query_weight.astype(jnp.bfloat16), "dp").astype(jnp.float32),
        lax.psum(grad_query_bias.astype(jnp.bfloat16), "dp").astype(jnp.float32),
        lax.psum(grad_key_weight.astype(jnp.bfloat16), "dp").astype(jnp.float32),
        lax.psum(grad_value_weight.astype(jnp.bfloat16), "dp").astype(jnp.float32),
        lax.psum(grad_value_bias.astype(jnp.bfloat16), "dp").astype(jnp.float32),
        lax.psum(grad_attend_weight.astype(jnp.bfloat16), "dp").astype(jnp.float32),
        lax.psum(grad_cross_query.astype(jnp.bfloat16), "dp").astype(jnp.float32),
        lax.psum(grad_cross_query_bias.astype(jnp.bfloat16), "dp").astype(jnp.float32),
        lax.psum(grad_cross_key.astype(jnp.bfloat16), "dp").astype(jnp.float32),
        lax.psum(grad_cross_value.astype(jnp.bfloat16), "dp").astype(jnp.float32),
        lax.psum(grad_cross_value_bias.astype(jnp.bfloat16), "dp").astype(jnp.float32),
        lax.psum(grad_cross_attend.astype(jnp.bfloat16), "dp").astype(jnp.float32),
        lax.psum(grad_inner_weight.astype(jnp.bfloat16), "dp").astype(jnp.float32),
        lax.psum(grad_inner_bias.astype(jnp.bfloat16), "dp").astype(jnp.float32),
        lax.psum(grad_outer_weight.astype(jnp.bfloat16), "dp").astype(jnp.float32),
    )
    (
        grad_self_gain,
        grad_self_shift,
        grad_attend_bias,
        grad_cross_gain,
        grad_cross_shift,
        grad_cross_attend_bias,
        grad_feed_gain,
        grad_feed_shift,
        grad_outer_bias,
    ) = lax.psum(
        (
            grad_self_gain,
            grad_self_shift,
            grad_attend_bias,
            grad_cross_gain,
            grad_cross_shift,
            grad_cross_attend_bias,
            grad_feed_gain,
            grad_feed_shift,
            grad_outer_bias,
        ),
        ("dp", "tensor"),
    )
    return (
        block_out,
        input_grad,
        memory_grad,
        grad_self_gain,
        grad_self_shift,
        grad_query_weight,
        grad_query_bias,
        grad_key_weight,
        grad_value_weight,
        grad_value_bias,
        grad_attend_weight,
        grad_attend_bias,
        grad_cross_gain,
        grad_cross_shift,
        grad_cross_query,
        grad_cross_query_bias,
        grad_cross_key,
        grad_cross_value,
        grad_cross_value_bias,
        grad_cross_attend,
        grad_cross_attend_bias,
        grad_feed_gain,
        grad_feed_shift,
        grad_inner_weight,
        grad_inner_bias,
        grad_outer_weight,
        grad_outer_bias,
    )


def general_solution(mesh):
    placed = (
        P("dp", "tensor", None),
        P("dp", "tensor", None),
        P("dp", "tensor", None),
        P("dp", None),
        P("dp", None),
        P(),
        P(),
        P(None, "tensor"),
        P("tensor"),
        P(None, "tensor"),
        P(None, "tensor"),
        P("tensor"),
        P("tensor", None),
        P(),
        P(),
        P(),
        P(None, "tensor"),
        P("tensor"),
        P(None, "tensor"),
        P(None, "tensor"),
        P("tensor"),
        P("tensor", None),
        P(),
        P(),
        P(),
        P(None, "tensor"),
        P("tensor"),
        P("tensor", None),
        P(),
    )
    return jax.shard_map(
        general_local,
        mesh=mesh,
        in_specs=placed,
        out_specs=(
            P("dp", "tensor", None),
            P("dp", "tensor", None),
            P("dp", "tensor", None),
            P(),
            P(),
            P(None, "tensor"),
            P("tensor"),
            P(None, "tensor"),
            P(None, "tensor"),
            P("tensor"),
            P("tensor", None),
            P(),
            P(),
            P(),
            P(None, "tensor"),
            P("tensor"),
            P(None, "tensor"),
            P(None, "tensor"),
            P("tensor"),
            P("tensor", None),
            P(),
            P(),
            P(),
            P(None, "tensor"),
            P("tensor"),
            P("tensor", None),
            P(),
        ),
        check_vma=False,
    )
```

```python
import jax
import jax.numpy as jnp
from jax import lax
from jax.experimental import pallas as pl
from jax.experimental.pallas import tpu as pltpu
from jax.sharding import PartitionSpec as P

HD = 64
MASKED = -1000000000.0
QUERIES = 128
KEYS = 256
NT = (((1,), (1,)), ((), ()))
TN = (((0,), (0,)), ((), ()))
NN = (((1,), (0,)), ((), ()))


def dot(a, b, dims):
    return lax.dot_general(a, b, dims, preferred_element_type=jnp.float32)


def both_heads(block):
    first = lax.broadcasted_iota(jnp.int32, block.shape, 1) < HD
    zero = jnp.zeros_like(block)
    return jnp.concatenate([jnp.where(first, block, zero), jnp.where(first, zero, block)], axis=0)


def allowed_keys(least, limit, at):
    key_place = at + lax.broadcasted_iota(jnp.int32, (KEYS, 1), 0)
    seen = (key_place >= least) & (key_place < limit)
    return jnp.concatenate([seen, seen], axis=1)


def attend_step(queries, k_ref, k_at, v_at, rows, seen, acc, top, total):
    pairs = range(len(queries))
    keys = [k_ref[rows, k_at + p * 128:k_at + p * 128 + 128] for p in pairs]
    values = [k_ref[rows, v_at + p * 128:v_at + p * 128 + 128] for p in pairs]
    scores = [jnp.where(seen, dot(keys[p], queries[p], NT), MASKED) for p in pairs]
    before = [top[p:p + 1] for p in pairs]
    now = [jnp.maximum(before[p], jnp.max(scores[p], axis=0, keepdims=True)) for p in pairs]
    weight = [jnp.exp(scores[p] - now[p]) for p in pairs]
    keep = [jnp.exp(before[p] - now[p]) for p in pairs]
    added = [dot(values[p], weight[p].astype(jnp.bfloat16), TN) for p in pairs]
    sums = [jnp.sum(weight[p], axis=0, keepdims=True) for p in pairs]
    for p in pairs:
        top[p:p + 1] = now[p]
        total[p:p + 1] = total[p:p + 1] * keep[p] + sums[p]
        acc[p] = acc[p] * keep[p] + added[p]


def attend_back_step(queries, grads, fixes, sums, k_ref, k_at, v_at, rows, seen, acc, acc_k, acc_v):
    pairs = range(len(queries))
    cuts = [slice(p * 128, (p + 1) * 128) for p in pairs]
    keys = [k_ref[rows, k_at + p * 128:k_at + p * 128 + 128] for p in pairs]
    values = [k_ref[rows, v_at + p * 128:v_at + p * 128 + 128] for p in pairs]
    scores = [dot(keys[p], queries[p], NT) for p in pairs]
    dprob = [dot(values[p], grads[p], NT) for p in pairs]
    prob = [jnp.exp(jnp.where(seen, scores[p] - sums[p], MASKED)) for p in pairs]
    low = [prob[p].astype(jnp.bfloat16) for p in pairs]
    dscore = [(prob[p] * (dprob[p] - fixes[p])).astype(jnp.bfloat16) for p in pairs]
    added_v = [dot(low[p], grads[p], NN) for p in pairs]
    added_k = [dot(dscore[p], queries[p], NN) for p in pairs]
    added_q = [dot(keys[p], dscore[p], TN) for p in pairs]
    for p in pairs:
        acc_v[rows, cuts[p]] += added_v[p]
        acc_k[rows, cuts[p]] += added_k[p]
        acc[p] += added_q[p]


EPSILON = 1e-05
BF = jnp.bfloat16
F32 = jnp.float32


def norm_stats(values):
    average = jnp.mean(values, axis=-1, keepdims=True)
    center = values - average
    inverse = lax.rsqrt(jnp.mean(center * center, axis=-1, keepdims=True) + EPSILON)
    return center * inverse, inverse


def norm_forward(values, gain, shift):
    unit, _ = norm_stats(values)
    return (unit * gain + shift).astype(BF)


class Net:
    def __init__(self, sems, local_sems):
        place = lax.axis_index("dp")
        chip = lax.axis_index("tensor")
        core, plane = place % 2, place // 2
        odd = plane % 2
        beside, over, corner = chip + 1 - 2 * (chip % 2), (chip + 2) % 4, 3 - chip
        self.chip, self.core_index, self.odd, self.plane = chip, core, odd, plane
        self.chips = (beside, over, corner)
        self.core = (plane * 2 + 1 - core, chip)
        self.first = (place, beside + odd * (over - beside))
        self.second = (place, over + odd * (beside - over))
        self.corner = (place, corner)
        self.near_plane = ((plane + 1 - 2 * odd) * 2 + core, chip)
        self.far_plane = ((plane + 2) % 4 * 2 + core, chip)
        self.inside = (plane + 1) // 2 == 1
        self.outside = (plane + 1) // 2 != 1
        self.across = ((3 - plane) * 2 + core, chip)
        self.sems, self.local_sems = sems, local_sems
        self.count = self.local_count = 0
        self.unsent, self.unmoved = [], []

    def meet(self):
        barrier = pltpu.get_barrier_semaphore()
        partners = (
            self.core, self.first, self.second, self.corner, self.near_plane, self.far_plane, self.across,
        )
        for partner in partners:
            pl.semaphore_signal(barrier, inc=1, device_id=partner, device_id_type=pl.DeviceIdType.MESH)
        pl.semaphore_wait(barrier, len(partners))

    def describe(self, source, target, device):
        self.count += 1
        return pltpu.make_async_remote_copy(
            src_ref=source,
            dst_ref=target,
            send_sem=self.sems.at[0, self.count - 1],
            recv_sem=self.sems.at[1, self.count - 1],
            device_id=device,
            device_id_type=pl.DeviceIdType.MESH,
        )

    def describe_move(self, source, target):
        self.local_count += 1
        return pltpu.make_async_copy(source, target, self.local_sems.at[self.local_count - 1])

    def send(self, source, target, device):
        copy = self.describe(source, target, device)
        copy.start()
        self.unsent.append(copy)
        return copy

    def move(self, source, target):
        copy = self.describe_move(source, target)
        copy.start()
        self.unmoved.append(copy)
        return copy

    def moved(self, copy):
        copy.wait()
        self.unmoved = [other for other in self.unmoved if other is not copy]

    def sent(self, copy):
        copy.wait_send()
        self.unsent = [other for other in self.unsent if other is not copy]

    def finish(self):
        for copy in self.unmoved:
            copy.wait()
        for copy in self.unsent:
            copy.wait_send()
        self.unsent, self.unmoved = [], []


def row_in(net, given, rows, row):
    core, chip = net.core_index, net.chip
    mine = pl.ds(2 * core, 2)
    swap = net.send(given.at[:, 1 - core], rows.at[mine], net.core)
    keep = net.move(given.at[:, core], rows.at[mine])
    yield
    net.moved(keep)
    swap.wait_recv()
    own = net.move(rows.at[chip], row.at[chip, core])
    sends = [
        net.send(rows.at[other], row.at[chip, core], (lax.axis_index("dp"), other)) for other in net.chips
    ]
    yield
    net.moved(own)
    shares = [net.send(row.at[chip, core], row.at[chip, core], net.core)]
    for other, copy in zip(net.chips, sends):
        copy.wait_recv()
        shares.append(net.send(row.at[other, core], row.at[other, core], net.core))
    yield
    for copy in shares:
        copy.wait_recv()
        net.sent(copy)


def row_out(net, pieces, rows, result):
    core, chip = net.core_index, net.chip
    own = net.move(pieces.at[chip], rows.at[chip])
    sends = [net.send(pieces.at[other], rows.at[chip], (lax.axis_index("dp"), other)) for other in net.chips]
    yield
    net.moved(own)
    for copy in sends:
        copy.wait_recv()
    keep = net.move(rows.at[pl.ds(2 * core, 2)], result.at[:, core])
    swap = net.send(rows.at[pl.ds(2 * (1 - core), 2)], result.at[:, core], net.core)
    yield
    swap.wait_recv()
    net.moved(keep)


class Gather:
    def __init__(self, net, own, slot, flip=False):
        self.net, self.slot = net, slot
        self.one, self.two = (2, 1) if flip else (1, 2)
        to_one, self.to_two = (net.second, net.first) if flip else (net.first, net.second)
        self.near = net.send(own, slot(self.one), to_one)
        self.own = net.move(own, slot(0))

    def relay(self):
        self.near.wait_recv()
        self.corner = self.net.send(self.slot(self.one), self.slot(3), self.to_two)
        self.other = self.net.send(self.slot(self.one), self.slot(self.two), self.net.near_plane)

    def finish(self):
        self.net.moved(self.own)
        self.corner.wait_recv()
        self.other.wait_recv()


ANY = pl.BlockSpec(memory_space=pl.ANY)
VM = pl.BlockSpec(memory_space=pltpu.VMEM)
SENDS = 224


def half_columns(net, weight, width):
    return weight.at[:, pl.ds(pl.multiple_of(net.core_index * width, width), width)]


def half_rows(net, weight, height):
    return weight.at[pl.ds(pl.multiple_of(net.core_index * height, height), height)]


def tile_rows(i, size=256):
    return pl.ds(pl.multiple_of(i * size, size), size)


def call_remote(kernel, ident, ins, in_specs, outs, out_specs, scratch, vmem=48, name=None):
    return pl.pallas_call(
        kernel,
        in_specs=in_specs,
        out_specs=out_specs,
        out_shape=outs,
        scratch_shapes=list(scratch) + [pltpu.SemaphoreType.DMA((2, SENDS)), pltpu.SemaphoreType.DMA((SENDS,))],
        compiler_params=pltpu.CompilerParams(
            collective_id=ident, has_side_effects=True, vmem_limit_bytes=vmem << 20
        ),
        name=name,
    )(*ins)


def add_up(target, sources):
    step = min(64, target.shape[0])

    def some(i, _):
        cut = pl.ds(pl.multiple_of(i * step, step), step)
        total = sources[0][cut].astype(F32)
        for source in sources[1:]:
            total = total + source[cut].astype(F32)
        target[cut] = total.astype(BF)
        return 0

    lax.fori_loop(0, target.shape[0] // step, some, 0)


class Line:
    def __init__(self, net, total, landing, result):
        self.net, self.total = net, total
        self.one_in, self.two_in = landing
        place = result(net.core_index)
        self.inward = net.describe(total, self.one_in, net.near_plane)
        self.across = net.describe(total, self.two_in, net.across)
        self.outward = net.describe(self.two_in, place, net.near_plane)
        self.keep = net.describe_move(self.two_in, place)
        self.inside_core = net.describe(self.two_in, place, net.core)
        self.outside_core = net.describe(place, place, net.core)

    def line0(self):
        pl.when(self.net.outside)(self.inward.start)

    def line1(self):
        @pl.when(self.net.inside)
        def _():
            self.inward.wait_recv()
            add_up(self.total, [self.total, self.one_in])
            self.across.start()

    def line2(self):
        @pl.when(self.net.inside)
        def _():
            self.across.wait_recv()
            add_up(self.two_in, [self.total, self.two_in])
            self.outward.start()
            self.inside_core.start()
            self.keep.start()

    def line3(self):
        @pl.when(self.net.outside)
        def _():
            self.outward.wait_recv()
            self.outside_core.start()

    def end(self):
        @pl.when(self.net.inside)
        def _():
            self.inside_core.wait_recv()
            for copy in (self.across, self.outward, self.inside_core):
                copy.wait_send()
            self.keep.wait()

        @pl.when(self.net.outside)
        def _():
            self.outside_core.wait_recv()
            for copy in (self.inward, self.outside_core):
                copy.wait_send()


class Scatter:
    def __init__(self, net, part, first, landing, source=None):
        self.net, self.part, self.source = net, part, source or part
        self.near_in, self.pass_in, self.far_in = landing
        self.one, self.two = (1, 2) if first == 1 else (2, 1)
        self.to_one, self.to_two = (net.first, net.second) if first == 1 else (net.second, net.first)

    def start(self):
        self.passed = self.net.send(self.source(3), self.pass_in, self.to_one)
        self.near = self.net.send(self.source(self.one), self.near_in, self.to_one)

    def middle(self):
        self.passed.wait_recv()
        add_up(self.part(self.two), [self.part(self.two), self.pass_in])
        self.far = self.net.send(self.part(self.two), self.far_in, self.to_two)

    def own(self):
        self.near.wait_recv()
        self.far.wait_recv()
        add_up(self.part(0), [self.part(0), self.near_in, self.far_in])


def landing(rows, columns):
    return [pltpu.VMEM((rows, columns), BF)] * 3


def line_landing(rows, columns):
    return [pltpu.VMEM((rows, columns), BF)] * 2


def weight_grad(lhs, rhs, target, start, count, columns=slice(None), size=256):
    def some(i, _):
        cut = pl.ds(pl.multiple_of(start + i * size, size), size)
        target[cut, columns] = dot(lhs(cut), rhs(), TN).astype(BF)
        return 0

    lax.fori_loop(0, count // size, some, 0)


def norm_back_tile(grad_in, values, gain):
    unit, inverse = norm_stats(values)
    scaled = grad_in * gain
    first_mean = jnp.mean(scaled, axis=-1, keepdims=True)
    second_mean = jnp.mean(scaled * unit, axis=-1, keepdims=True)
    grad_values = inverse * (scaled - first_mean - unit * second_mean)
    return grad_values, jnp.sum(grad_in * unit, axis=0, keepdims=True), jnp.sum(grad_in, axis=0, keepdims=True)


def head_scatters(net, g_heads, g_out, lands):
    columns = lambda kind, s: slice(kind * 512 + s * 128, kind * 512 + s * 128 + 128)
    found = {
        "q": Scatter(net, lambda s: g_heads.at[:, columns(0, s)], 1, lands[:3]),
        "v": Scatter(net, lambda s: g_heads.at[:, columns(2, s)], 2, lands[3:6]),
    }
    for half in range(2):
        found["k%d" % half] = Scatter(
            net, lambda s, half=half: g_heads.at[pl.ds(half * 512, 512), columns(1, s)], 1 + half,
            lands[6 + half * 3:9 + half * 3],
        )
        found["o%d" % half] = Scatter(
            net, lambda s, half=half: g_out.at[pl.ds(s * 128 + half * 64, 64)], 1 + half,
            lands[12 + half * 3:15 + half * 3],
        )
    return found


def head_lines(net, g_heads, g_out, full_heads, full_out, lands):
    found = {}
    for kind, name in enumerate("qkv"):
        for half in range(2):
            at = (kind * 2 + half) * 2
            found[name + str(half)] = Line(
                net, g_heads.at[pl.ds(half * 512, 512), kind * 512:kind * 512 + 128], lands[at:at + 2],
                lambda c, kind=kind, half=half: full_heads.at[
                    kind, pl.ds(half * 512, 512), pl.ds(pl.multiple_of(c * 128, 128), 128)
                ],
            )
    for half in range(2):
        found["o%d" % half] = Line(
            net, g_out.at[pl.ds(half * 64, 64)], lands[12 + half * 2:14 + half * 2],
            lambda c, half=half: full_out.at[pl.ds(pl.multiple_of(c * 128 + half * 64, 64), 64)],
        )
    return found


def head_landing(width):
    return landing(1024, 128) * 2 + (landing(512, 128)) * 2 + landing(64, width) * 2


def head_line_landing(width):
    return line_landing(512, 128) * 6 + line_landing(64, width) * 2


def attend_block(i, q_ref, q_at, k_ref, k_at, v_at, low, high, causal, out_ref, sums_ref, acc, top, total):
    pairs = range(4)
    rows = tile_rows(i, QUERIES)
    queries = [
        both_heads(q_ref[rows, q_at + p * 128:q_at + p * 128 + 128] * jnp.bfloat16(HD ** -0.5)) for p in pairs
    ]
    least, limit = low[pl.ds(i, 1)], high[pl.ds(i, 1)]
    acc[...] = jnp.zeros_like(acc)
    total[...] = jnp.zeros_like(total)
    top[...] = jnp.full_like(top, -1e30)

    def step(j, _):
        at = pl.multiple_of(j * KEYS, KEYS)
        seen = allowed_keys(least, limit, at)
        attend_step(queries, k_ref, k_at, v_at, pl.ds(at, KEYS), seen, acc, top, total)
        return 0

    lax.fori_loop(0, i // 2 + 1 if causal else k_ref.shape[0] // KEYS, step, 0)
    for p in pairs:
        sums = total[p:p + 1]
        mixed = acc[p] / sums
        joined = jnp.concatenate([mixed[:HD, :QUERIES], mixed[HD:, QUERIES:]], axis=0)
        out_ref[rows, p * 128:(p + 1) * 128] = joined.T.astype(BF)
        sums_ref[i, p:p + 1] = top[p:p + 1] + jnp.log(sums)


def attend_back_block(
    i, q_ref, q_at, k_ref, k_at, v_at, grad_ref, out_ref, out_at, sums_ref, low, high, causal, dq_ref, dq_at, acc, acc_k, acc_v
):
    pairs = range(4)
    rows = tile_rows(i, QUERIES)
    least, limit = low[pl.ds(i, 1)], high[pl.ds(i, 1)]
    queries, grads, fixes, sums = [], [], [], []
    ones = jnp.ones((8, 128), BF)
    for p in pairs:
        queries.append(both_heads(q_ref[rows, q_at + p * 128:q_at + p * 128 + 128] * jnp.bfloat16(HD ** -0.5)))
        grad = both_heads(grad_ref[rows, p * 128:(p + 1) * 128])
        grads.append(grad)
        out = out_ref[rows, out_at + p * 128:out_at + p * 128 + 128].astype(F32)
        product = grad.astype(F32) * jnp.concatenate([out, out], axis=0)
        coarse = product.astype(BF)
        fine = (product - coarse.astype(F32)).astype(BF)
        fixes.append((dot(ones, coarse, NT) + dot(ones, fine, NT))[:1])
        sums.append(sums_ref[i, p:p + 1])
    acc[...] = jnp.zeros_like(acc)

    def step(j, _):
        at = pl.multiple_of(j * KEYS, KEYS)
        seen = allowed_keys(least, limit, at)
        attend_back_step(queries, grads, fixes, sums, k_ref, k_at, v_at, pl.ds(at, KEYS), seen, acc, acc_k, acc_v)
        return 0

    lax.fori_loop(0, i // 2 + 1 if causal else k_ref.shape[0] // KEYS, step, 0)
    for p in pairs:
        mixed = acc[p] * (HD ** -0.5)
        joined = jnp.concatenate([mixed[:HD, :QUERIES], mixed[HD:, QUERIES:]], axis=0)
        dq_ref[rows, dq_at + p * 128:dq_at + p * 128 + 128] = joined.T.astype(BF)


def reach(query_ids, key_ids):
    low = jnp.zeros(query_ids.shape, F32)
    high = jnp.zeros(query_ids.shape, F32)
    for segment in range(16):
        here = query_ids == segment
        before = jnp.sum((key_ids < segment).astype(F32), axis=(0, 1), keepdims=True)
        upto = jnp.sum((key_ids <= segment).astype(F32), axis=(0, 1), keepdims=True)
        low = low + jnp.where(here, before, 0.0)
        high = high + jnp.where(here, upto, 0.0)
    return low.astype(jnp.int32), high.astype(jnp.int32)


def project_out(net, att, weight, part, part_in):
    swaps = []
    for i in range(4):
        part[i] = dot(att[i * 256:i * 256 + 256], weight[...], NN).astype(BF).reshape(2, 128, -1)
        swaps.append(net.send(part.at[i], part_in.at[i], net.core))
    return swaps


def ahead_kernel(
    x_in, mem_in, top_in, target_ids_in, source_ids_in, bias_q, bias_v, bias_cq, bias_cv, bias_i, wq, wk, wv, wo, wcq, wck, wcv, wco, inner, outer,
    gain1, shift1, bias_o, gain2, shift2, bias_c, gain3, shift3,
    x_out, mem_out, top_out, n1_out, qkv_out, att1_out, sums1_out, h1_out, n2_out, q2_out, kv2_out, att2_out, sums2_out,
    h2_out, n3_out, act_out, slope_out, g_outer_out, wqkv_out, wo_out, wc_out, wco_out, wi_out, wu_out, reach_out,
    rows_x, rows_mem, rows_top, row, mem, weights, weights2, wo_vm, wco_vm, wi, normed, qkv, att, part, part_in, part_in2,
    hidden, queries, keys, act, slope, g_outer, bias, biases, ids, all_ids, spans, sums1, sums2, acc, top, total, sems, local_sems,
):
    net = Net(sems, local_sems)
    core, chip = net.core_index, net.chip
    net.meet()
    enter_x = row_in(net, x_in, rows_x, row)
    next(enter_x)
    mine = pl.ds(2 * core, 2)
    for i in range(2):
        for r in range(8):
            cut = slice(r * 128, r * 128 + 128)
            ids[i, r:r + 1] = target_ids_in[i:i + 1, cut]
            ids[i, 8 + r:9 + r] = source_ids_in[i:i + 1, cut]
    at = 0
    for value in (bias_q, bias_v, bias_cq, bias_cv, bias_i):
        for r in range(value.shape[1] // 128):
            bias[at:at + 1] = value[:, r * 128:r * 128 + 128]
            at += 1
    ids_copies = [net.move(ids, all_ids.at[mine]), net.send(ids, all_ids.at[mine], net.core)]
    bias_own = net.move(bias, biases.at[0])
    bias_copies = [
        net.send(bias, biases.at[1], net.first),
        net.send(bias, biases.at[2], net.second),
        net.send(bias, biases.at[3], net.corner),
    ]

    def gather_columns(weight, target, kind, flip):
        slot = lambda s: target.at[:, kind * 512 + s * 128:kind * 512 + s * 128 + 128]
        return Gather(net, half_columns(net, weight, 128), slot, flip)

    def gather_rows_of(weight, target, flip):
        return Gather(net, half_rows(net, weight, 128), lambda s: target.at[pl.ds(s * 128, 128)], flip)

    def gather_inner(k):
        own = inner.at[pl.ds(k * 512, 512), pl.ds(pl.multiple_of(core * 512, 512), 512)]
        return Gather(net, own, lambda s: wi.at[pl.ds(k * 512, 512), s * 512:s * 512 + 512], k == 1)

    def gather_outer(k):
        own = outer.at[pl.ds(pl.multiple_of(core * 512 + k * 256, 256), 256)]
        return Gather(net, own, lambda s: wu_out.at[pl.ds(s * 512 + k * 256, 256)], k == 1)

    gather_q = gather_columns(wq, weights, 0, False)
    gather_k = gather_columns(wk, weights, 1, True)
    next(enter_x)
    gather_v = gather_columns(wv, weights, 2, False)
    gather_o = gather_rows_of(wo, wo_vm, True)
    enter_mem = row_in(net, mem_in, rows_mem, mem)
    next(enter_mem)
    enter_top = row_in(net, top_in, rows_top, top_out)
    next(enter_top)
    gather_q.relay()
    gather_k.relay()
    next(enter_x)
    for _ in enter_x:
        pass
    x_move = net.move(row, x_out)

    def norm_first(i, _):
        normed[tile_rows(i)] = norm_forward(row[i].reshape(256, -1).astype(F32), gain1[...], shift1[...])
        return 0

    lax.fori_loop(0, 4, norm_first, 0)
    n1_move = net.move(normed, n1_out)
    gather_v.relay()
    gather_o.relay()
    next(enter_mem)
    gather_ck = gather_columns(wck, weights2, 1, False)
    gather_cv = gather_columns(wcv, weights2, 2, True)
    net.moved(bias_own)
    for copy in bias_copies:
        copy.wait_recv()

    def project_first(kind):
        cut = slice(kind * 512, kind * 512 + 512)
        bias = None
        if kind != 1:
            bias = jnp.concatenate([biases[s, pl.ds(kind + core, 1)] for s in range(4)], axis=1)

        def some(i, _):
            value = dot(normed[tile_rows(i)], weights[:, cut], NN)
            if kind != 1:
                value = value + bias
            qkv[tile_rows(i), cut] = value.astype(BF)
            return 0

        lax.fori_loop(0, 4, some, 0)

    for kind, gather in enumerate((gather_q, gather_k, gather_v)):
        gather.finish()
        project_first(kind)
    net.move(weights, wqkv_out)
    gather_cq = gather_columns(wcq, weights2, 0, False)
    gather_co = gather_rows_of(wco, wco_vm, True)
    net.move(qkv, qkv_out)
    net.moved(ids_copies[0])
    ids_copies[1].wait_recv()
    target_ids, source_ids = all_ids[chip, :8], all_ids[chip, 8:]
    low, _ = reach(target_ids, target_ids)
    spans[0] = low
    place = lax.broadcasted_iota(jnp.int32, (8, 128), 0) * 128 + lax.broadcasted_iota(jnp.int32, (8, 128), 1)
    spans[1] = place + 1
    low, high = reach(target_ids, source_ids)
    spans[2] = low
    spans[3] = high
    net.move(spans, reach_out)

    def attend_first(i, _):
        attend_block(i, qkv, 0, qkv, 512, 1024, spans.at[0], spans.at[1], True, att, sums1, acc, top, total)
        return 0

    lax.fori_loop(0, 8, attend_first, 0)
    next(enter_mem)
    gather_ck.relay()
    gather_cv.relay()
    gather_cq.relay()
    gather_co.relay()
    att1_move = net.move(att, att1_out)
    net.move(sums1, sums1_out)
    gather_o.finish()
    net.move(wo_vm, wo_out)
    swaps = project_out(net, att, wo_vm, part, part_in)
    inners = [gather_inner(0), gather_inner(1)]
    next(enter_top)
    for _ in enter_mem:
        pass
    net.move(mem, mem_out)
    for gather in (gather_ck, gather_cv):
        gather.finish()
    values_bias = jnp.concatenate([biases[s, pl.ds(6 + core, 1)] for s in range(4)], axis=1)
    query_bias = jnp.concatenate([biases[s, pl.ds(4 + core, 1)] for s in range(4)], axis=1)

    def project_memory(i, _):
        tokens = mem[i].reshape(256, -1)
        keys[tile_rows(i), :512] = dot(tokens, weights2[:, 512:1024], NN).astype(BF)
        keys[tile_rows(i), 512:] = (dot(tokens, weights2[:, 1024:], NN) + values_bias).astype(BF)
        return 0

    lax.fori_loop(0, 4, project_memory, 0)
    net.move(keys, kv2_out)
    net.moved(n1_move)
    for i in range(4):
        swaps[i].wait_recv()

    def middle_rows(i, _):
        value = row[i].astype(F32) + part[i].astype(F32) + part_in[i].astype(F32)
        value = value.reshape(256, -1) + bias_o[...]
        hidden[tile_rows(i)] = value
        normed[tile_rows(i)] = norm_forward(value, gain2[...], shift2[...])
        return 0

    lax.fori_loop(0, 4, middle_rows, 0)
    net.moved(x_move)
    h1_move = net.move(hidden, h1_out)
    n2_move = net.move(normed, n2_out)
    gather_cq.finish()
    net.move(weights2, wc_out)

    def project_query(i, _):
        queries[tile_rows(i)] = (dot(normed[tile_rows(i)], weights2[:, :512], NN) + query_bias).astype(BF)
        return 0

    lax.fori_loop(0, 4, project_query, 0)
    net.move(queries, q2_out)
    net.moved(att1_move)

    def attend_second(i, _):
        attend_block(i, queries, 0, keys, 0, 512, spans.at[2], spans.at[3], False, att, sums2, acc, top, total)
        return 0

    lax.fori_loop(0, 3, attend_second, 0)
    inners[0].relay()
    inners[1].relay()
    outers = [gather_outer(0), gather_outer(1)]
    lax.fori_loop(3, 8, attend_second, 0)
    net.move(att, att2_out)
    net.move(sums2, sums2_out)
    gather_co.finish()
    net.move(wco_vm, wco_out)
    for copy in swaps:
        net.sent(copy)
    swaps = project_out(net, att, wco_vm, part, part_in2)
    next(enter_top)
    net.moved(h1_move)
    net.moved(n2_move)
    for i in range(4):
        swaps[i].wait_recv()

    def last_rows(i, _):
        value = part[i].astype(F32) + part_in2[i].astype(F32)
        value = hidden[tile_rows(i)] + value.reshape(256, -1) + bias_c[...]
        hidden[tile_rows(i)] = value
        normed[tile_rows(i)] = norm_forward(value, gain3[...], shift3[...])
        return 0

    lax.fori_loop(0, 4, last_rows, 0)
    net.move(hidden, h2_out)
    net.move(normed, n3_out)
    inners[0].finish()
    inners[1].finish()
    net.move(wi, wi_out)

    def feed(i, _):
        tokens = normed[tile_rows(i)]
        for s in range(4):
            cut = slice(s * 512, s * 512 + 512)
            unit_bias = jnp.concatenate([biases[s, pl.ds(8 + core * 4 + k, 1)] for k in range(4)], axis=1)
            pre = dot(tokens, wi[:, cut], NN) + unit_bias
            sigmoid = jax.nn.sigmoid(pre)
            act[tile_rows(i), cut] = (pre * sigmoid).astype(BF)
            slope[tile_rows(i), cut] = (sigmoid * (1.0 + pre * (1.0 - sigmoid))).astype(BF)
        return 0

    lax.fori_loop(0, 1, feed, 0)
    outers[0].relay()
    outers[1].relay()
    for _ in enter_top:
        pass
    top_load = net.move(top_out, row)
    lax.fori_loop(1, 4, feed, 0)
    net.move(act, act_out)
    net.move(slope, slope_out)
    net.moved(top_load)
    weight_grad(lambda cut: act[:, cut], lambda: row[...].reshape(1024, -1), g_outer, 0, 2048, size=512)
    net.move(g_outer, g_outer_out)
    for gather in outers:
        gather.finish()
    net.finish()


def ahead(x, mem, top, ids, biases, weights, vectors):
    length, width = 1024, x.shape[-1]
    shape = jax.ShapeDtypeStruct
    quarters = (4, 2, 128, width)
    rows = lambda columns, kind=BF: shape((length, columns), kind)
    sums = shape((8, 4, 256), F32)
    return call_remote(
        ahead_kernel, 1,
        [a.reshape(2, 2, -1, width) for a in (x, mem, top)] + list(ids) + [v[None] for v in biases] + list(weights)
        + [v[None] for v in vectors],
        [ANY] * 3 + [VM] * 7 + [ANY] * 10 + [VM] * 8,
        [
            shape(quarters, BF), shape(quarters, BF), shape(quarters, BF), rows(width), rows(1536), rows(512), sums,
            rows(width, F32), rows(width), rows(512), rows(1024), rows(512), sums,
            rows(width, F32), rows(width), rows(2048), rows(2048), shape((2048, width), BF),
            shape((width, 1536), BF), shape((512, width), BF), shape((width, 1536), BF), shape((512, width), BF),
            shape((width, 2048), BF), shape((2048, width), BF), shape((4, 8, 128), jnp.int32),
        ],
        [ANY] * 25,
        [pltpu.VMEM((4, 128, width), BF)] * 3 + [pltpu.VMEM(quarters, BF)] * 2 + [pltpu.VMEM((width, 1536), BF)] * 2
        + [pltpu.VMEM((512, width), BF)] * 2
        + [
            pltpu.VMEM((width, 2048), BF), pltpu.VMEM((length, width), BF), pltpu.VMEM((length, 1536), BF),
            pltpu.VMEM((length, 512), BF), pltpu.VMEM(quarters, BF), pltpu.VMEM(quarters, BF), pltpu.VMEM(quarters, BF),
            pltpu.VMEM((length, width), F32), pltpu.VMEM((length, 512), BF), pltpu.VMEM((length, 1024), BF),
            pltpu.VMEM((length, 2048), BF), pltpu.VMEM((length, 2048), BF), pltpu.VMEM((2048, width), BF),
            pltpu.VMEM((16, 128), F32),
            pltpu.VMEM((4, 16, 128), F32), pltpu.VMEM((2, 16, 128), jnp.int32),
            pltpu.VMEM((4, 16, 128), jnp.int32), pltpu.VMEM((4, 8, 128), jnp.int32),
            pltpu.VMEM((8, 4, 256), F32), pltpu.VMEM((8, 4, 256), F32),
            pltpu.VMEM((4, 128, 256), F32), pltpu.VMEM((4, 256), F32), pltpu.VMEM((4, 256), F32),
        ],
        vmem=62, name="ahead",
    )


def turn_kernel(
    g_outer_in, act_in, slope_in, n3_in, h2_in, top_in, wi_in, wu_in, wco_in, q_in, kv_in, att_in, sums_in, reach_in, gain, bias_u,
    block_out, gh_out, outer_out, inner_out, heads_out, vectors_out, split_out,
    act, slope, wu, wi, g_outer, g_inner, hidden, row, normed, wco, part, back_in, out_part, out_in, gatt,
    pieces, result, rows_back, acc_k, acc_v, acc, spans, sums, vectors, split, *rest,
):
    lands, (sems, local_sems) = rest[:-2], rest[-2:]
    net = Net(sems, local_sems)
    core = net.core_index
    loads = [
        net.move(source, target)
        for source, target in (
            (top_in, row), (wu_in, wu), (slope_in, slope), (wi_in, wi), (n3_in, normed), (act_in, act), (g_outer_in, g_outer),
            (h2_in, hidden), (wco_in, wco), (reach_in, spans), (sums_in, sums),
        )
    ]
    net.meet()
    outers = [
        Scatter(
            net, lambda s, k=k: g_outer.at[pl.ds(s * 512 + k * 256, 256)], 1 + k, lands[k * 3:k * 3 + 3],
            lambda s, k=k: g_outer_in.at[pl.ds(s * 512 + k * 256, 256)],
        )
        for k in range(2)
    ]
    outer_lines = [
        Line(
            net, g_outer.at[pl.ds(k * 128, 128)], lands[12 + k * 2:14 + k * 2],
            lambda c, k=k: outer_out.at[pl.ds(pl.multiple_of(c * 512 + k * 128, 128), 128)],
        )
        for k in range(4)
    ]
    inners = [
        Scatter(
            net, lambda s, k=k: g_inner.at[pl.ds(k * 512, 512), s * 512:s * 512 + 512], 1 + k,
            lands[6 + k * 3:9 + k * 3],
        )
        for k in range(2)
    ]

    def inner_grad(k, s):
        cut = slice(s * 512, s * 512 + 512)
        weight_grad(lambda rows: normed[:, rows], lambda: slope[:, cut], g_inner, k * 512, 512, cut)

    for k in range(2):
        outers[k].start()
    for copy in loads[:3]:
        net.moved(copy)
    split[...] = jnp.zeros_like(split)
    vectors[...] = jnp.zeros_like(vectors)

    def feed_back(i, _):
        tokens = row[i].reshape(256, -1)
        for s in range(4):
            cut = slice(s * 512, s * 512 + 512)
            value = (dot(tokens, wu[cut], NT) * slope[tile_rows(i), cut].astype(F32)).astype(BF)
            slope[tile_rows(i), cut] = value
            split[0:1, cut] += jnp.sum(value.astype(F32), axis=0, keepdims=True)
        return 0

    lax.fori_loop(0, 4, feed_back, 0)
    for copy in loads[3:]:
        net.moved(copy)
    swaps = []
    for i in range(4):
        value = dot(slope[i * 256:i * 256 + 256], wi[...], NT)
        part[i] = value.astype(BF).reshape(2, 128, -1)
        swaps.append(net.send(part.at[i], back_in.at[i], net.core))
    outers[0].middle()
    outers[1].middle()
    for k in range(2):
        inner_grad(k, 3)
        inner_grad(k, 1 + k)
        inners[k].start()

    def feed_out(i, _):
        out_part[i] = dot(act[tile_rows(i)], wu[...], NN).astype(BF).reshape(2, 128, -1)
        return 0

    lax.fori_loop(0, 4, feed_out, 0)
    out_swap = net.send(out_part.at[:, 1 - core], out_in, net.core)
    loads = [
        net.move(kv_in, act.at[:, :1024]), net.move(q_in, act.at[:, 1024:1536]), net.move(att_in, act.at[:, 1536:]),
    ]
    for copy in swaps:
        copy.wait_recv()

    def back(i, _):
        grad = (part[i].astype(F32) + back_in[i].astype(F32)).reshape(256, -1)
        before = hidden[i]
        change, by_gain, by_shift = norm_back_tile(grad, before.reshape(256, -1), gain[...])
        top = row[i].reshape(256, -1).astype(F32)
        value = top + change
        pieces[i] = hidden[i, core]
        hidden[i] = value.reshape(2, 128, -1)
        gatt[tile_rows(i)] = dot(value.astype(BF), wco[...], NT).astype(BF)
        vectors[4:5] += by_gain
        vectors[5:6] += by_shift
        vectors[6:7] += jnp.sum(top, axis=0, keepdims=True)
        vectors[3:4] += jnp.sum(value, axis=0, keepdims=True)
        return 0

    lax.fori_loop(0, 4, back, 0)
    net.move(hidden, gh_out)
    net.move(vectors, vectors_out)
    net.move(split, split_out)
    out_swap.wait_recv()
    for i in range(4):
        result[i] = (pieces[i] + out_part[i, core].astype(F32) + out_in[i].astype(F32) + bias_u[...]).astype(BF)
    leave = row_out(net, result, rows_back, block_out)
    next(leave)
    for k in range(2):
        inner_grad(k, 2 - k)
        inner_grad(k, 0)
    for k in range(2):
        outers[k].own()
        outer_lines[2 * k].line0()
        outer_lines[2 * k + 1].line0()
    for copy in loads:
        net.moved(copy)
    acc_k[...] = jnp.zeros_like(acc_k)
    acc_v[...] = jnp.zeros_like(acc_v)

    def attend_back(i, _):
        attend_back_block(
            i, act, 1024, act, 0, 512, gatt, act, 1536, sums, spans.at[2], spans.at[3], False, slope, 0, acc, acc_k, acc_v
        )
        return 0

    lax.fori_loop(0, 3, attend_back, 0)
    inners[0].middle()
    inners[1].middle()
    outer_lines[0].line1()
    outer_lines[1].line1()
    lax.fori_loop(3, 5, attend_back, 0)
    outer_lines[2].line1()
    outer_lines[3].line1()
    outer_lines[0].line2()
    lax.fori_loop(5, 7, attend_back, 0)
    outer_lines[1].line2()
    outer_lines[2].line2()
    lax.fori_loop(7, 8, attend_back, 0)
    outer_lines[3].line2()
    slope[:, 512:1024] = acc_k[...].astype(BF)
    slope[:, 1024:1536] = acc_v[...].astype(BF)
    net.move(slope.at[:, :1536], heads_out)
    inners[0].own()
    net.move(g_inner.at[pl.ds(0, 512), :512], inner_out.at[pl.ds(0, 512)])
    inners[1].own()
    net.move(g_inner.at[pl.ds(512, 512), :512], inner_out.at[pl.ds(512, 512)])
    next(leave)
    for line in outer_lines:
        line.line3()
    for line in outer_lines:
        line.end()
    for _ in leave:
        pass
    net.finish()


def turn(g_outer, act, slope, n3, h2, top, wi, wu, wco, q, kv, att, sums, reach_rows, gain, bias_u):
    length, width = act.shape[0], n3.shape[-1]
    shape = jax.ShapeDtypeStruct
    quarters = (4, 2, 128, width)
    return call_remote(
        turn_kernel, 2,
        (
            g_outer, act, slope, n3, h2.reshape(quarters), top, wi, wu, wco, q, kv, att, sums, reach_rows, gain[None], bias_u[None],
        ),
        [ANY] * 14 + [VM] * 2,
        [
            shape((2, 2, 128, width), BF), shape(quarters, F32), shape((1024, width), BF), shape((width, 512), BF),
            shape((length, 1536), BF), shape((8, width), F32), shape((8, 2048), F32),
        ],
        [ANY] * 7,
        [
            pltpu.VMEM((length, 2048), BF), pltpu.VMEM((length, 2048), BF), pltpu.VMEM((2048, width), BF),
            pltpu.VMEM((width, 2048), BF), pltpu.VMEM((2048, width), BF), pltpu.VMEM((width, 2048), BF),
            pltpu.VMEM(quarters, F32), pltpu.VMEM(quarters, BF), pltpu.VMEM((length, width), BF),
            pltpu.VMEM((512, width), BF), pltpu.VMEM(quarters, BF), pltpu.VMEM(quarters, BF), pltpu.VMEM(quarters, BF),
            pltpu.VMEM((4, 128, width), BF), pltpu.VMEM((length, 512), BF),
            pltpu.VMEM((4, 128, width), F32), pltpu.VMEM((4, 128, width), BF), pltpu.VMEM((4, 128, width), BF),
            pltpu.VMEM((length, 512), F32), pltpu.VMEM((length, 512), F32), pltpu.VMEM((4, 128, 256), F32),
            pltpu.VMEM((4, 8, 128), jnp.int32), pltpu.VMEM((8, 4, 256), F32),
            pltpu.VMEM((8, width), F32), pltpu.VMEM((8, 2048), F32),
        ]
        + landing(256, width) * 2 + landing(512, 512) * 2 + line_landing(128, width) * 4,
        vmem=62, name="turn",
    )


def last_kernel(
    heads_in, n2_in, mem_in, att2_in, gh_in, h1_in, wc_in, wo_in, inner_in, qkv_in, att1_in, sums_in, reach_in, n1_in, x_in,
    wqkv_in, shared_in, split_in, gain2, gain1,
    mem_out, grad_out, cross_out, cross_o_out, heads_out, o_out, inner_out, shared_out, late_out, split_out,
    dqkv, normed, tokens, att, grads, hidden, weights, wo, part, part_in, mem_part, mem_back, grad_in,
    pieces_mem, rows_mem, pieces, rows_back, g_cross, g_cross_o, g_heads, g_o, gatt, acc, spans, sums,
    inner_total,
    shared, shared_land, late, late_land, split_load, split, split_sum, split_plane, split_land, split_full, *rest,
):
    lands, (sems, local_sems) = rest[:-2], rest[-2:]
    net = Net(sems, local_sems)
    core, chip = net.core_index, net.chip
    place = lax.axis_index("dp")
    loads = [
        net.move(source, target)
        for source, target in (
            (heads_in, dqkv), (wc_in, weights), (inner_in, inner_total), (mem_in, tokens), (n2_in, normed), (att2_in, att),
            (gh_in, grads), (h1_in, hidden), (wo_in, wo), (reach_in, spans), (sums_in, sums), (shared_in, shared.at[0]),
            (split_in, split_load),
        )
    ]
    net.meet()
    inner_lines = [
        Line(
            net, inner_total.at[pl.ds(k * 512, 512)], lands[68 + k * 2:70 + k * 2],
            lambda c, k=k: inner_out.at[pl.ds(k * 512, 512), pl.ds(pl.multiple_of(c * 512, 512), 512)],
        )
        for k in range(2)
    ]
    scatters = head_scatters(net, g_cross, g_cross_o, lands[:18])
    lines = head_lines(net, g_cross, g_cross_o, cross_out, cross_o_out, lands[18:34])
    own_scatters = head_scatters(net, g_heads, g_o, lands[34:52])
    own_lines = head_lines(net, g_heads, g_o, heads_out, o_out, lands[52:68])

    def each(group, names, *steps):
        for step in steps:
            for name in names.split():
                getattr(group[name], step)()

    for copy in loads[:3]:
        net.moved(copy)
    inner_lines[0].line0()
    inner_lines[1].line0()
    swaps = []
    for i in range(4):
        value = dot(dqkv[i * 256:i * 256 + 256, :512], weights[:, :512], NT)
        part[i] = value.astype(BF).reshape(2, 128, -1)
        swaps.append(net.send(part.at[i], part_in.at[i], net.core))
    for copy in loads[3:]:
        net.moved(copy)
    memory = lambda cut: tokens[:, :, :, cut].reshape(1024, -1)
    for kind in (1, 2):
        cut = slice(kind * 512, kind * 512 + 512)
        weight_grad(memory, lambda: dqkv[:, cut], g_cross, 0, 1024, cut)
        each(scatters, "k0 k1" if kind == 1 else "v", "start")
    weight_grad(lambda cut: normed[:, cut], lambda: dqkv[:, :512], g_cross, 0, 1024, slice(0, 512))
    each(scatters, "q", "start")
    load_n1 = net.move(n1_in, normed)
    weight_grad(lambda cut: att[:, cut], lambda: grads[...].astype(BF), g_cross_o, 0, 512)
    each(scatters, "o0 o1", "start")
    load_att = net.move(att1_in, att)
    for copy in swaps:
        copy.wait_recv()

    def back(i, _):
        grad = (part[i].astype(F32) + part_in[i].astype(F32)).reshape(256, -1)
        change, by_gain, by_shift = norm_back_tile(grad, hidden[tile_rows(i)], gain2[...])
        value = grads[tile_rows(i)] + change
        mem_part[i] = value.astype(BF).reshape(2, 128, -1)
        gatt[tile_rows(i)] = dot(value.astype(BF), wo[...], NT).astype(BF)
        shared[0, 1:2] += by_gain
        shared[0, 2:3] += by_shift
        shared[0, 0:1] += jnp.sum(value, axis=0, keepdims=True)
        hidden[tile_rows(i)] = value
        return 0

    lax.fori_loop(0, 4, back, 0)
    each(scatters, "k0 k1", "middle")
    inner_lines[0].line1()
    net.moved(load_att)
    weight_grad(lambda cut: att[:, cut], lambda: mem_part[...].reshape(1024, -1), g_o, 0, 512)

    def memory_back(i, _):
        rows = tile_rows(i)
        value = dot(dqkv[rows, 512:1024], weights[:, 512:1024], NT) + dot(dqkv[rows, 1024:], weights[:, 1024:], NT)
        mem_part[i] = value.astype(BF).reshape(2, 128, -1)
        return 0

    lax.fori_loop(0, 4, memory_back, 0)
    mem_swap = net.send(mem_part.at[:, 1 - core], mem_back, net.core)
    load_qkv = net.move(qkv_in, weights)
    load_x = net.move(x_in, tokens)
    each(scatters, "v q o0 o1", "middle")
    each(own_scatters, "o0 o1", "start")
    for s in range(4):
        for k in range(4):
            split[s, 4 + k:5 + k] = split_load[0:1, s * 512 + k * 128:s * 512 + k * 128 + 128]
    for at, kind in ((2, 0), (3, 2)):
        total = jnp.sum(dqkv[:, kind * 512:kind * 512 + 512].astype(F32), axis=0, keepdims=True)
        for s in range(4):
            split[s, at:at + 1] = total[:, s * 128:s * 128 + 128]
    inner_lines[1].line1()
    stages = [(place, net.chips[0]), (place, net.chips[1]), net.near_plane, net.far_plane]
    shared_copy = net.send(shared.at[0], shared_land.at[0], stages[0])

    def shared_stage(at):
        nonlocal shared_copy
        shared_copy.wait_recv()
        shared[at + 1] = shared[at] + shared_land[at]
        if at < 3:
            shared_copy = net.send(shared.at[at + 1], shared_land.at[at + 1], stages[at + 1])

    grads[...] = jnp.zeros_like(grads)
    mem_swap.wait_recv()
    for i in range(4):
        pieces_mem[i] = (mem_part[i, core].astype(F32) + mem_back[i].astype(F32)).astype(BF)
    leave_mem = row_out(net, pieces_mem, rows_mem, mem_out)
    next(leave_mem)
    net.moved(load_qkv)

    def attend_back(i, _):
        attend_back_block(
            i, weights, 0, weights, 512, 1024, gatt, att, 0, sums, spans.at[0], spans.at[1], True, dqkv, 0, acc,
            grads.at[:, :512], grads.at[:, 512:],
        )
        return 0

    lax.fori_loop(0, 4, attend_back, 0)
    each(scatters, "k0 k1", "own")
    each(lines, "k0 k1", "line0")
    inner_lines[0].line2()
    lax.fori_loop(4, 6, attend_back, 0)
    each(scatters, "v q", "own")
    each(lines, "v0 v1 q0 q1", "line0")
    each(scatters, "o0 o1", "own")
    each(lines, "o0 o1", "line0")
    each(lines, "k0 k1", "line1")
    inner_lines[1].line2()
    shared_stage(0)
    each(own_scatters, "o0 o1", "middle")
    lax.fori_loop(6, 8, attend_back, 0)
    load_w = net.move(wqkv_in, weights)
    dqkv[:, 512:] = grads[...].astype(BF)
    net.moved(load_n1)

    def head_grad(kind):
        cut = slice(kind * 512, kind * 512 + 512)
        weight_grad(lambda rows: normed[:, rows], lambda: dqkv[:, cut], g_heads, 0, 1024, cut)

    each(lines, "v0 v1", "line1")
    head_grad(0)
    each(own_scatters, "q", "start")
    each(lines, "q0 q1", "line1")
    head_grad(2)
    each(own_scatters, "v", "start")
    each(lines, "k0 k1", "line2")
    inner_lines[0].line3()
    next(leave_mem)
    each(lines, "v0 v1", "line2")
    net.moved(load_w)
    for copy in swaps:
        net.sent(copy)

    def first_back(i, _):
        part[i] = dot(dqkv[tile_rows(i)], weights[...], NT).astype(BF).reshape(2, 128, -1)
        return 0

    lax.fori_loop(0, 4, first_back, 0)
    swap = net.send(part.at[:, 1 - core], grad_in, net.core)
    each(lines, "q0 q1", "line2")
    each(own_scatters, "q v", "middle")
    head_grad(1)
    each(own_scatters, "k0 k1", "start")
    shared_stage(1)
    each(own_scatters, "o0 o1", "own")
    each(own_lines, "o0 o1", "line0")
    each(lines, "o0 o1", "line1")
    for at, kind in ((0, 0), (1, 2)):
        total = jnp.sum(dqkv[:, kind * 512:kind * 512 + 512].astype(F32), axis=0, keepdims=True)
        for s in range(4):
            split[s, at:at + 1] = total[:, s * 128:s * 128 + 128]
    split_copies = [net.send(split, split_plane.at[0], net.near_plane)]
    net.moved(load_x)
    swap.wait_recv()
    late[0] = jnp.zeros(late.shape[1:], F32)
    for i in range(4):
        grad = part[i, core].astype(F32) + grad_in[i].astype(F32)
        change, by_gain, by_shift = norm_back_tile(grad, tokens[i, core].astype(F32), gain1[...])
        pieces[i] = (hidden[pl.ds(pl.multiple_of(i * 256 + core * 128, 128), 128)] + change).astype(BF)
        late[0, 0:1] += by_gain
        late[0, 1:2] += by_shift
    late_copy = net.send(late.at[0], late_land.at[0], net.core)
    leave = row_out(net, pieces, rows_back, grad_out)

    def late_stage(at):
        nonlocal late_copy
        late_copy.wait_recv()
        late[at + 1] = late[at] + late_land[at]
        if at < 4:
            late_copy = net.send(late.at[at + 1], late_land.at[at + 1], (stages[2], stages[3], stages[0], stages[1])[at])

    def split_stage(at):
        nonlocal split_copies
        for copy in split_copies:
            copy.wait_recv()
        if at == 0:
            for s, other in ((0, 0), (1, 2), (2, 1), (3, 3)):
                split_sum[0, s] = split[s] + split_plane[0, other]
            split_copies = [net.send(split_sum.at[0], split_plane.at[1], net.far_plane)]
        elif at == 1:
            split_sum[1] = split_sum[0] + split_plane[1]
            split_copies = [
                net.send(split_sum.at[1, s], split_land.at[s - 1], device)
                for s, device in ((1, net.first), (2, net.second), (3, net.corner))
            ]
        else:
            split_full[core] = split_sum[1, 0] + split_land[0] + split_land[1] + split_land[2]
            split_copies = [net.send(split_full.at[core], split_full.at[core], net.core)]

    late_stage(0)
    split_stage(0)
    late_stage(1)
    each(own_scatters, "q v", "own")
    each(own_lines, "q0 v0 q1 v1", "line0")
    split_stage(1)
    late_stage(2)
    each(own_scatters, "k0 k1", "middle")
    next(leave)
    each(lines, "o0 o1", "line2")
    each(own_lines, "q0", "line1")
    shared_stage(2)
    inner_lines[1].line3()
    each(own_lines, "v0 o0 o1", "line1")
    each(own_scatters, "k0 k1", "own")
    each(own_lines, "k0 k1", "line0")
    each(own_lines, "q1", "line1")
    each(own_lines, "q0", "line2")
    each(own_lines, "v1", "line1")
    each(own_lines, "v0", "line2")
    each(own_lines, "k0 k1", "line1")
    each(own_lines, "q1 v1 o0 o1", "line2")
    each(own_lines, "k0 k1", "line2")
    each(lines, "k0 k1", "line3")
    each(lines, "v0 v1 q0 q1", "line3")
    each(lines, "o0 o1", "line3")
    next(leave)
    shared_stage(3)
    late_stage(3)
    split_stage(2)
    each(own_lines, "q0 v0 q1 v1", "line3")
    late_stage(4)
    each(own_lines, "o0 o1 k0 k1", "line3")
    for line in inner_lines + list(lines.values()) + list(own_lines.values()):
        line.end()
    for _ in leave_mem:
        pass
    for _ in leave:
        pass
    split_copies[0].wait_recv()
    for source, target in ((shared.at[4], shared_out), (late.at[5], late_out), (split_full, split_out)):
        net.move(source, target)
    net.finish()


def last(heads, n2, mem, att2, gh, h1, wc, wo, inner_total, qkv, att1, sums, reach_rows, n1, x, wqkv, shared, split, gain2, gain1):
    length, width = heads.shape[0], n1.shape[-1]
    shape = jax.ShapeDtypeStruct
    quarters = (4, 2, 128, width)
    own = [shape((3, width, 256), BF), shape((256, width), BF)]
    return call_remote(
        last_kernel, 3,
        (
            heads, n2, mem, att2, gh.reshape(length, width), h1, wc, wo, inner_total, qkv, att1, sums, reach_rows, n1, x, wqkv, shared, split,
            gain2[None], gain1[None],
        ),
        [ANY] * 18 + [VM] * 2,
        [shape((2, 2, 128, width), BF)] * 2 + own + own
        + [shape((width, 1024), BF), shape((8, width), F32), shape((8, width), F32), shape((2, 8, 128), F32)],
        [ANY] * 10,
        [
            pltpu.VMEM((length, 1536), BF), pltpu.VMEM((length, width), BF), pltpu.VMEM(quarters, BF),
            pltpu.VMEM((length, 512), BF), pltpu.VMEM((length, width), F32), pltpu.VMEM((length, width), F32),
            pltpu.VMEM((width, 1536), BF), pltpu.VMEM((512, width), BF), pltpu.VMEM(quarters, BF),
            pltpu.VMEM(quarters, BF), pltpu.VMEM(quarters, BF), pltpu.VMEM((4, 128, width), BF),
            pltpu.VMEM((4, 128, width), BF),
        ]
        + [pltpu.VMEM((4, 128, width), BF)] * 4
        + [pltpu.VMEM((width, 1536), BF), pltpu.VMEM((512, width), BF)] * 2
        + [
            pltpu.VMEM((length, 512), BF), pltpu.VMEM((4, 128, 256), F32),
            pltpu.VMEM((4, 8, 128), jnp.int32),
            pltpu.VMEM((8, 4, 256), F32), pltpu.VMEM((width, 512), BF),
        ]
        + [
            pltpu.VMEM((5, 8, width), F32), pltpu.VMEM((4, 8, width), F32),
            pltpu.VMEM((6, 8, width), F32), pltpu.VMEM((5, 8, width), F32),
            pltpu.VMEM((8, 2048), F32), pltpu.VMEM((4, 8, 128), F32), pltpu.VMEM((2, 4, 8, 128), F32),
            pltpu.VMEM((2, 4, 8, 128), F32), pltpu.VMEM((3, 8, 128), F32),
            pltpu.VMEM((2, 8, 128), F32),
        ]
        + (head_landing(width) + head_line_landing(width)) * 2 + line_landing(512, 512) * 2,
        vmem=63, name="last",
    )


def widen_kernel(rows_in, mem_in, grad_in, cross_in, cross_o_in, heads_in, o_in, inner_in, outer_in, shared, late, split, *outs):
    rows, mem, grad, cq, ck, cv, co, q, k, v, o, inner, outer = outs[:13]
    rows[...] = rows_in[...]
    mem[...] = mem_in[...].astype(F32)
    grad[...] = grad_in[...].astype(F32)
    for kind, (cross, own) in enumerate(((cq, q), (ck, k), (cv, v))):
        cross[...] = cross_in[kind].astype(F32)
        own[...] = heads_in[kind].astype(F32)
    co[...] = cross_o_in[...].astype(F32)
    o[...] = o_in[...].astype(F32)
    inner[...] = inner_in[...].astype(F32)
    outer[...] = outer_in[...].astype(F32)
    vectors, bias_q, bias_v, bias_cq, bias_cv, bias_i = outs[13:22], *outs[22:]

    @pl.when(pl.program_id(0) == 0)
    def _():
        vectors[0][...] = late[0:1]
        vectors[1][...] = late[1:2]
        for at in range(7):
            vectors[2 + at][...] = shared[at:at + 1]
        for at, bias in enumerate((bias_q, bias_v, bias_cq, bias_cv)):
            bias[...] = jnp.concatenate([split[c, at:at + 1] for c in range(2)], axis=1)
        bias_i[...] = jnp.concatenate([split[c, 4 + at:5 + at] for c in range(2) for at in range(4)], axis=1)


def widen(rows, mem, grad, cross, cross_o, heads, o, inner, outer, shared, late, split):
    steps, width = 8, rows.shape[-1]
    shape = jax.ShapeDtypeStruct
    flat = lambda a: a.reshape(-1, width)
    block = lambda a: pl.BlockSpec((a.shape[0] // steps, a.shape[1]), lambda i: (i, 0))
    whole = lambda *dims: pl.BlockSpec(dims, lambda i: (0,) * len(dims))
    head = pl.BlockSpec((3, width // steps, 256), lambda i: (0, i, 0))
    ins = [flat(rows), flat(mem), flat(grad), cross, cross_o, heads, o, inner, outer, shared, late, split]
    in_specs = [block(ins[0])] * 3 + [head, block(cross_o), head, block(o), block(inner), block(outer)]
    in_specs += [whole(8, width), whole(8, width), whole(2, 8, 128)]
    wide = lambda a: shape(a.shape, F32)
    columns = shape((width, 256), F32)
    outs = [shape(ins[0].shape, BF), wide(ins[1]), wide(ins[2])] + [columns] * 3 + [wide(cross_o)] + [columns] * 3
    outs += [wide(o), wide(inner), wide(outer)]
    out_specs = [block(a) for a in outs] + [whole(1, width)] * 9 + [whole(1, 256)] * 4 + [whole(1, 1024)]
    outs += [shape((1, width), F32)] * 9 + [shape((1, 256), F32)] * 4 + [shape((1, 1024), F32)]
    return pl.pallas_call(
        widen_kernel,
        grid=(steps,),
        in_specs=in_specs,
        out_specs=out_specs,
        out_shape=outs,
        compiler_params=pltpu.CompilerParams(vmem_limit_bytes=63 << 20),
        name="widen",
    )(*ins)


def solution(mesh):
    if mesh.shape["tensor"] != 4 or mesh.shape["dp"] != 8:
        return general_solution(mesh)

    def local(
        layer_input, memory, grad_out, target_segments, source_segments,
        self_gain, self_shift, query_weight, query_bias, key_weight, value_weight, value_bias,
        attend_weight, attend_bias,
        cross_gain, cross_shift, cross_query, cross_query_bias, cross_key, cross_value, cross_value_bias,
        cross_attend, cross_attend_bias,
        feed_gain, feed_shift, inner_weight, inner_bias, outer_weight, outer_bias,
    ):
        (
            x, mem, top, n1, qkv1, att1, sums1, h1, n2, q2, kv2, att2, sums2, h2, n3, act, slope, g_outer,
            wqkv, wo, wc, wco, wi, wu, spans,
        ) = ahead(
            layer_input, memory, grad_out, (target_segments, source_segments),
            (query_bias, value_bias, cross_query_bias, cross_value_bias, inner_bias),
            (
                query_weight, key_weight, value_weight, attend_weight, cross_query, cross_key, cross_value, cross_attend,
                inner_weight, outer_weight,
            ),
            (self_gain, self_shift, attend_bias, cross_gain, cross_shift, cross_attend_bias, feed_gain, feed_shift),
        )
        block_out, gh2, f_outer, f_inner, heads2, shared, split = turn(
            g_outer, act, slope, n3, h2, top, wi, wu, wco, q2, kv2, att2, sums2, spans, feed_gain, outer_bias
        )
        memory_grad, input_grad, c_heads, c_out, s_heads, s_out, f_inner, shared, late, split = last(
            heads2, n2, mem, att2, gh2, h1, wc, wo, f_inner, qkv1, att1, sums1, spans, n1, x, wqkv, shared, split,
            cross_gain, self_gain,
        )
        (
            block_out, memory_grad, input_grad, g_cq, g_ck, g_cv, g_co, g_q, g_k, g_v, g_o, g_inner, g_outer,
            g_gain1, g_shift1, g_bias_o, g_gain2, g_shift2, g_bias_c, g_gain3, g_shift3, g_bias_u,
            g_bias_q, g_bias_v, g_bias_cq, g_bias_cv, g_bias_i,
        ) = widen(block_out, memory_grad, input_grad, c_heads, c_out, s_heads, s_out, f_inner, f_outer, shared, late, split)
        tokens = layer_input.shape
        vector = lambda v: v.reshape(-1)
        return (
            block_out.reshape(tokens), input_grad.reshape(tokens), memory_grad.reshape(tokens),
            vector(g_gain1), vector(g_shift1),
            g_q, vector(g_bias_q), g_k, g_v, vector(g_bias_v),
            g_o, vector(g_bias_o),
            vector(g_gain2), vector(g_shift2),
            g_cq, vector(g_bias_cq), g_ck, g_cv, vector(g_bias_cv),
            g_co, vector(g_bias_c),
            vector(g_gain3), vector(g_shift3),
            g_inner, vector(g_bias_i), g_outer, vector(g_bias_u),
        )

    row, one, by_column, by_row = P("dp", "tensor", None), P(), P(None, "tensor"), P("tensor", None)
    part, ids = P("tensor"), P("dp", None)
    return jax.shard_map(
        local,
        mesh=mesh,
        in_specs=(
            row, row, row, ids, ids,
            one, one, by_column, part, by_column, by_column, part, by_row, one,
            one, one, by_column, part, by_column, by_column, part, by_row, one,
            one, one, by_column, part, by_row, one,
        ),
        out_specs=(
            row, row, row,
            one, one, by_column, part, by_column, by_column, part, by_row, one,
            one, one, by_column, part, by_column, by_column, part, by_row, one,
            one, one, by_column, part, by_row, one,
        ),
        check_vma=False,
    )


BLOCK_ROWS = 512


def general_norm_forward(values, gain, shift):
    average = jnp.mean(values, axis=-1, keepdims=True)
    center = values - average
    inverse = lax.rsqrt(jnp.mean(center * center, axis=-1, keepdims=True) + EPSILON)
    normed = center * inverse
    return ((normed * gain + shift).astype(jnp.bfloat16), normed, inverse)


def general_norm_backward(grad_in, normed, inverse, gain):
    scaled = grad_in * gain
    first_mean = jnp.mean(scaled, axis=-1, keepdims=True)
    second_mean = jnp.mean(scaled * normed, axis=-1, keepdims=True)
    grad_values = inverse * (scaled - first_mean - normed * second_mean)
    return (grad_values, jnp.sum(grad_in * normed, axis=(0, 1)), jnp.sum(grad_in, axis=(0, 1)))


def gather_rows(values):
    return lax.all_gather(values, "tensor", axis=1, tiled=True)


def gather_grads(values):
    return lax.all_gather(values, "tensor", axis=1, tiled=True)


def reduce_inputs(partial_sum):
    return lax.psum_scatter(partial_sum, "tensor", scatter_dimension=1, tiled=True)


def advance(base, partial_sum, bias):
    return base + lax.psum_scatter(partial_sum, "tensor", scatter_dimension=1, tiled=True) + bias


def next_rows(values, gain, shift):
    return gather_rows(general_norm_forward(values, gain, shift)[0])


def backward_rows(normed_low):
    return gather_rows(normed_low)


def project(rows_in, weight):
    return jnp.einsum("rtd,dc->rtc", rows_in, weight, preferred_element_type=jnp.float32)


def project_back(grads, weight):
    return jnp.einsum("rtc,dc->rtd", grads, weight, preferred_element_type=jnp.float32)


def outer_sum(rows_in, grads):
    return jnp.einsum("rtd,rtc->dc", rows_in, grads, preferred_element_type=jnp.float32)


def bias_sum(grads):
    return jnp.sum(grads.astype(jnp.float32), axis=(0, 1))


def split_heads(values):
    return values.reshape(values.shape[0], values.shape[1], values.shape[2] // HD, HD)


def block_scores(query_block, key_row, query_ids, key_ids, row_start, causal):
    raw_scores = jnp.einsum(
        "qhd,khd->hqk", query_block, key_row, preferred_element_type=jnp.float32
    ) * float(HD) ** (-0.5)
    allowed = query_ids[:, None] == key_ids[None, :]
    if causal:
        query_place = row_start + jnp.arange(query_block.shape[0], dtype=jnp.int32)
        key_place = jnp.arange(key_row.shape[0], dtype=jnp.int32)
        allowed = allowed & (key_place[None, :] <= query_place[:, None])
    return jnp.where(allowed[None], raw_scores, jnp.full(raw_scores.shape, MASKED, jnp.float32))


def block_inputs(
    query_heads, key_heads, value_heads, query_ids, key_ids, position, block_count, block_size
):
    row_index = position // block_count
    row_start = position % block_count * block_size
    query_row = lax.dynamic_index_in_dim(query_heads, row_index, 0, keepdims=False)
    query_block = lax.dynamic_slice_in_dim(query_row, row_start, block_size, 0)
    key_row = lax.dynamic_index_in_dim(key_heads, row_index, 0, keepdims=False)
    value_row = lax.dynamic_index_in_dim(value_heads, row_index, 0, keepdims=False)
    query_seg = lax.dynamic_slice_in_dim(
        lax.dynamic_index_in_dim(query_ids, row_index, 0, keepdims=False), row_start, block_size, 0
    )
    key_seg = lax.dynamic_index_in_dim(key_ids, row_index, 0, keepdims=False)
    return (row_index, row_start, query_block, key_row, value_row, query_seg, key_seg)


def attend_forward(query, keys, values, query_ids, key_ids, causal):
    query_heads = split_heads(query)
    key_heads = split_heads(keys)
    value_heads = split_heads(values)
    block_size = min(BLOCK_ROWS, query.shape[1])
    block_count = query.shape[1] // block_size

    def one_block(position):
        row_index, row_start, query_block, key_row, value_row, query_seg, key_seg = block_inputs(
            query_heads,
            key_heads,
            value_heads,
            query_ids,
            key_ids,
            position,
            block_count,
            block_size,
        )
        scores = block_scores(query_block, key_row, query_seg, key_seg, row_start, causal)
        row_max = jnp.max(scores, axis=-1, keepdims=True)
        expo_scores = jnp.exp(scores - row_max)
        row_total = jnp.sum(expo_scores, axis=-1, keepdims=True)
        softmax_out = expo_scores / row_total
        attended = jnp.einsum(
            "hqk,khd->qhd",
            softmax_out.astype(jnp.bfloat16),
            value_row,
            preferred_element_type=jnp.float32,
        ).astype(jnp.bfloat16)
        return (attended, (row_max + jnp.log(row_total))[..., 0])

    attended_all, log_sums = lax.map(
        one_block, jnp.arange(query.shape[0] * block_count, dtype=jnp.int32)
    )
    return (attended_all.reshape(query.shape), log_sums)


def attend_backward(query, keys, values, grad_att, log_sums, query_ids, key_ids, causal):
    query_heads = split_heads(query)
    key_heads = split_heads(keys)
    value_heads = split_heads(values)
    grad_heads = split_heads(grad_att)
    block_size = min(BLOCK_ROWS, query.shape[1])
    block_count = query.shape[1] // block_size
    score_scale = float(HD) ** (-0.5)

    def one_block(carry, inputs):
        grad_keys, grad_values = carry
        position, log_sum = inputs
        row_index, row_start, query_block, key_row, value_row, query_seg, key_seg = block_inputs(
            query_heads,
            key_heads,
            value_heads,
            query_ids,
            key_ids,
            position,
            block_count,
            block_size,
        )
        grad_row = lax.dynamic_index_in_dim(grad_heads, row_index, 0, keepdims=False)
        grad_block = lax.dynamic_slice_in_dim(grad_row, row_start, block_size, 0)
        scores = block_scores(query_block, key_row, query_seg, key_seg, row_start, causal)
        softmax_out = jnp.exp(scores - log_sum[..., None])
        softmax_low = softmax_out.astype(jnp.bfloat16)
        attended = jnp.einsum(
            "hqk,khd->qhd", softmax_low, value_row, preferred_element_type=jnp.float32
        ).astype(jnp.bfloat16)
        grad_prob = jnp.einsum(
            "qhd,khd->hqk", grad_block, value_row, preferred_element_type=jnp.float32
        )
        correction = jnp.sum(softmax_out * grad_prob, axis=-1, keepdims=True)
        grad_score = (softmax_out * (grad_prob - correction)).astype(jnp.bfloat16)
        grad_query = (
            jnp.einsum("hqk,khd->qhd", grad_score, key_row, preferred_element_type=jnp.float32)
            * score_scale
        ).astype(jnp.bfloat16)
        key_added = (
            jnp.einsum("hqk,qhd->khd", grad_score, query_block, preferred_element_type=jnp.float32)
            * score_scale
        )
        value_added = jnp.einsum(
            "hqk,qhd->khd", softmax_low, grad_block, preferred_element_type=jnp.float32
        )
        grad_keys = grad_keys.at[row_index].add(key_added)
        grad_values = grad_values.at[row_index].add(value_added)
        return ((grad_keys, grad_values), (grad_query, attended))

    empty_grads = jnp.zeros(key_heads.shape, jnp.float32)
    positions = jnp.arange(query.shape[0] * block_count, dtype=jnp.int32)
    (grad_keys, grad_values), (grad_query, attended_all) = lax.scan(
        one_block, (empty_grads, empty_grads), (positions, log_sums)
    )
    return (
        grad_query.reshape(query.shape),
        grad_keys.reshape(keys.shape).astype(jnp.bfloat16),
        grad_values.reshape(values.shape).astype(jnp.bfloat16),
        attended_all.reshape(query.shape),
    )


def general_local(
    layer_input,
    memory,
    grad_out,
    target_segments,
    source_segments,
    self_gain,
    self_shift,
    query_weight,
    query_bias,
    key_weight,
    value_weight,
    value_bias,
    attend_weight,
    attend_bias,
    cross_gain,
    cross_shift,
    cross_query,
    cross_query_bias,
    cross_key,
    cross_value,
    cross_value_bias,
    cross_attend,
    cross_attend_bias,
    feed_gain,
    feed_shift,
    inner_weight,
    inner_bias,
    outer_weight,
    outer_bias,
):
    inputs = layer_input.astype(jnp.float32)
    rows_first = next_rows(inputs, self_gain, self_shift)
    query_first = (project(rows_first, query_weight) + query_bias).astype(jnp.bfloat16)
    keys_first = project(rows_first, key_weight).astype(jnp.bfloat16)
    values_first = (project(rows_first, value_weight) + value_bias).astype(jnp.bfloat16)
    attended_first, sums_first = attend_forward(
        query_first, keys_first, values_first, target_segments, target_segments, True
    )
    base_first = advance(inputs, project(attended_first, attend_weight), attend_bias)
    memory_rows = lax.all_gather(memory, "tensor", axis=1, tiled=True)
    rows_second = next_rows(base_first, cross_gain, cross_shift)
    query_second = (project(rows_second, cross_query) + cross_query_bias).astype(jnp.bfloat16)
    keys_second = project(memory_rows, cross_key).astype(jnp.bfloat16)
    values_second = (project(memory_rows, cross_value) + cross_value_bias).astype(jnp.bfloat16)
    attended_second, sums_second = attend_forward(
        query_second, keys_second, values_second, target_segments, source_segments, False
    )
    base_second = advance(base_first, project(attended_second, cross_attend), cross_attend_bias)
    rows_third = next_rows(base_second, feed_gain, feed_shift)
    pre_active = project(rows_third, inner_weight) + inner_bias
    active = jax.nn.silu(pre_active).astype(jnp.bfloat16)
    base_out = advance(base_second, project(active, outer_weight), outer_bias)
    block_out = base_out.astype(jnp.bfloat16)
    kept_input, kept_first, kept_second, kept_memory, kept_sums_first, kept_sums_second = (
        lax.optimization_barrier(
            (inputs, base_first, base_second, memory_rows, sums_first, sums_second)
        )
    )
    grad_top = grad_out.astype(jnp.float32)
    normed_low3, unit_third, inverse_third = general_norm_forward(kept_second, feed_gain, feed_shift)
    rows_back3 = backward_rows(normed_low3)
    pre_back = project(rows_back3, inner_weight) + inner_bias
    sigmoid_back = jax.nn.sigmoid(pre_back)
    active_back = (pre_back * sigmoid_back).astype(jnp.bfloat16)
    grad_rows3 = gather_grads(grad_top.astype(jnp.bfloat16))
    grad_outer_weight = outer_sum(active_back, grad_rows3)
    grad_outer_bias = jnp.sum(grad_top, axis=(0, 1))
    grad_active = project_back(grad_rows3, outer_weight)
    grad_inner = (grad_active * sigmoid_back * (1.0 + pre_back * (1.0 - sigmoid_back))).astype(
        jnp.bfloat16
    )
    grad_inner_weight = outer_sum(rows_back3, grad_inner)
    grad_inner_bias = bias_sum(grad_inner)
    grad_norm3 = reduce_inputs(project_back(grad_inner, inner_weight))
    grad_from3, grad_feed_gain, grad_feed_shift = general_norm_backward(
        grad_norm3, unit_third, inverse_third, feed_gain
    )
    grad_hidden2 = grad_top + grad_from3
    normed_low2, unit_second, inverse_second = general_norm_forward(kept_first, cross_gain, cross_shift)
    rows_back2 = backward_rows(normed_low2)
    query_back2 = (project(rows_back2, cross_query) + cross_query_bias).astype(jnp.bfloat16)
    keys_back2 = project(kept_memory, cross_key).astype(jnp.bfloat16)
    values_back2 = (project(kept_memory, cross_value) + cross_value_bias).astype(jnp.bfloat16)
    grad_rows2 = gather_grads(grad_hidden2.astype(jnp.bfloat16))
    grad_att2 = project_back(grad_rows2, cross_attend).astype(jnp.bfloat16)
    grad_query2, grad_keys2, grad_values2, attended_back2 = attend_backward(
        query_back2,
        keys_back2,
        values_back2,
        grad_att2,
        kept_sums_second,
        target_segments,
        source_segments,
        False,
    )
    grad_cross_attend = outer_sum(attended_back2, grad_rows2)
    grad_cross_attend_bias = jnp.sum(grad_hidden2, axis=(0, 1))
    grad_cross_query = outer_sum(rows_back2, grad_query2)
    grad_cross_query_bias = bias_sum(grad_query2)
    grad_cross_key = outer_sum(kept_memory, grad_keys2)
    grad_cross_value = outer_sum(kept_memory, grad_values2)
    grad_cross_value_bias = bias_sum(grad_values2)
    memory_grad = lax.psum_scatter(
        (project_back(grad_keys2, cross_key) + project_back(grad_values2, cross_value)).astype(
            jnp.bfloat16
        ),
        "tensor",
        scatter_dimension=1,
        tiled=True,
    ).astype(jnp.float32)
    grad_norm2 = reduce_inputs(project_back(grad_query2, cross_query))
    grad_from2, grad_cross_gain, grad_cross_shift = general_norm_backward(
        grad_norm2, unit_second, inverse_second, cross_gain
    )
    grad_hidden1 = grad_hidden2 + grad_from2
    normed_low1, unit_first, inverse_first = general_norm_forward(kept_input, self_gain, self_shift)
    rows_back1 = backward_rows(normed_low1)
    query_back1 = (project(rows_back1, query_weight) + query_bias).astype(jnp.bfloat16)
    keys_back1 = project(rows_back1, key_weight).astype(jnp.bfloat16)
    values_back1 = (project(rows_back1, value_weight) + value_bias).astype(jnp.bfloat16)
    grad_rows1 = gather_grads(grad_hidden1.astype(jnp.bfloat16))
    grad_att1 = project_back(grad_rows1, attend_weight).astype(jnp.bfloat16)
    grad_query1, grad_keys1, grad_values1, attended_back1 = attend_backward(
        query_back1,
        keys_back1,
        values_back1,
        grad_att1,
        kept_sums_first,
        target_segments,
        target_segments,
        True,
    )
    grad_attend_weight = outer_sum(attended_back1, grad_rows1)
    grad_attend_bias = jnp.sum(grad_hidden1, axis=(0, 1))
    grad_query_weight = outer_sum(rows_back1, grad_query1)
    grad_query_bias = bias_sum(grad_query1)
    grad_key_weight = outer_sum(rows_back1, grad_keys1)
    grad_value_weight = outer_sum(rows_back1, grad_values1)
    grad_value_bias = bias_sum(grad_values1)
    grad_norm1 = reduce_inputs(
        project_back(grad_query1, query_weight)
        + project_back(grad_keys1, key_weight)
        + project_back(grad_values1, value_weight)
    )
    grad_from1, grad_self_gain, grad_self_shift = general_norm_backward(
        grad_norm1, unit_first, inverse_first, self_gain
    )
    input_grad = grad_hidden1 + grad_from1
    (
        grad_query_weight,
        grad_query_bias,
        grad_key_weight,
        grad_value_weight,
        grad_value_bias,
        grad_attend_weight,
        grad_cross_query,
        grad_cross_query_bias,
        grad_cross_key,
        grad_cross_value,
        grad_cross_value_bias,
        grad_cross_attend,
        grad_inner_weight,
        grad_inner_bias,
        grad_outer_weight,
    ) = (
        lax.psum(grad_query_weight.astype(jnp.bfloat16), "dp").astype(jnp.float32),
        lax.psum(grad_query_bias.astype(jnp.bfloat16), "dp").astype(jnp.float32),
        lax.psum(grad_key_weight.astype(jnp.bfloat16), "dp").astype(jnp.float32),
        lax.psum(grad_value_weight.astype(jnp.bfloat16), "dp").astype(jnp.float32),
        lax.psum(grad_value_bias.astype(jnp.bfloat16), "dp").astype(jnp.float32),
        lax.psum(grad_attend_weight.astype(jnp.bfloat16), "dp").astype(jnp.float32),
        lax.psum(grad_cross_query.astype(jnp.bfloat16), "dp").astype(jnp.float32),
        lax.psum(grad_cross_query_bias.astype(jnp.bfloat16), "dp").astype(jnp.float32),
        lax.psum(grad_cross_key.astype(jnp.bfloat16), "dp").astype(jnp.float32),
        lax.psum(grad_cross_value.astype(jnp.bfloat16), "dp").astype(jnp.float32),
        lax.psum(grad_cross_value_bias.astype(jnp.bfloat16), "dp").astype(jnp.float32),
        lax.psum(grad_cross_attend.astype(jnp.bfloat16), "dp").astype(jnp.float32),
        lax.psum(grad_inner_weight.astype(jnp.bfloat16), "dp").astype(jnp.float32),
        lax.psum(grad_inner_bias.astype(jnp.bfloat16), "dp").astype(jnp.float32),
        lax.psum(grad_outer_weight.astype(jnp.bfloat16), "dp").astype(jnp.float32),
    )
    (
        grad_self_gain,
        grad_self_shift,
        grad_attend_bias,
        grad_cross_gain,
        grad_cross_shift,
        grad_cross_attend_bias,
        grad_feed_gain,
        grad_feed_shift,
        grad_outer_bias,
    ) = lax.psum(
        (
            grad_self_gain,
            grad_self_shift,
            grad_attend_bias,
            grad_cross_gain,
            grad_cross_shift,
            grad_cross_attend_bias,
            grad_feed_gain,
            grad_feed_shift,
            grad_outer_bias,
        ),
        ("dp", "tensor"),
    )
    return (
        block_out,
        input_grad,
        memory_grad,
        grad_self_gain,
        grad_self_shift,
        grad_query_weight,
        grad_query_bias,
        grad_key_weight,
        grad_value_weight,
        grad_value_bias,
        grad_attend_weight,
        grad_attend_bias,
        grad_cross_gain,
        grad_cross_shift,
        grad_cross_query,
        grad_cross_query_bias,
        grad_cross_key,
        grad_cross_value,
        grad_cross_value_bias,
        grad_cross_attend,
        grad_cross_attend_bias,
        grad_feed_gain,
        grad_feed_shift,
        grad_inner_weight,
        grad_inner_bias,
        grad_outer_weight,
        grad_outer_bias,
    )


def general_solution(mesh):
    placed = (
        P("dp", "tensor", None),
        P("dp", "tensor", None),
        P("dp", "tensor", None),
        P("dp", None),
        P("dp", None),
        P(),
        P(),
        P(None, "tensor"),
        P("tensor"),
        P(None, "tensor"),
        P(None, "tensor"),
        P("tensor"),
        P("tensor", None),
        P(),
        P(),
        P(),
        P(None, "tensor"),
        P("tensor"),
        P(None, "tensor"),
        P(None, "tensor"),
        P("tensor"),
        P("tensor", None),
        P(),
        P(),
        P(),
        P(None, "tensor"),
        P("tensor"),
        P("tensor", None),
        P(),
    )
    return jax.shard_map(
        general_local,
        mesh=mesh,
        in_specs=placed,
        out_specs=(
            P("dp", "tensor", None),
            P("dp", "tensor", None),
            P("dp", "tensor", None),
            P(),
            P(),
            P(None, "tensor"),
            P("tensor"),
            P(None, "tensor"),
            P(None, "tensor"),
            P("tensor"),
            P("tensor", None),
            P(),
            P(),
            P(),
            P(None, "tensor"),
            P("tensor"),
            P(None, "tensor"),
            P(None, "tensor"),
            P("tensor"),
            P("tensor", None),
            P(),
            P(),
            P(),
            P(None, "tensor"),
            P("tensor"),
            P("tensor", None),
            P(),
        ),
        check_vma=False,
    )
```

```python
import jax
import jax.numpy as jnp
from jax import lax
from jax.experimental import pallas as pl
from jax.experimental.pallas import tpu as pltpu
from jax.sharding import PartitionSpec as P

HD = 64
MASKED = -1000000000.0
QUERIES = 128
KEYS = 256
NT = (((1,), (1,)), ((), ()))
TN = (((0,), (0,)), ((), ()))
NN = (((1,), (0,)), ((), ()))


def dot(a, b, dims):
    return lax.dot_general(a, b, dims, preferred_element_type=jnp.float32)


def both_heads(block):
    first = lax.broadcasted_iota(jnp.int32, block.shape, 1) < HD
    zero = jnp.zeros_like(block)
    return jnp.concatenate([jnp.where(first, block, zero), jnp.where(first, zero, block)], axis=0)


def allowed_keys(least, limit, at):
    key_place = at + lax.broadcasted_iota(jnp.int32, (KEYS, 1), 0)
    seen = (key_place >= least) & (key_place < limit)
    return jnp.concatenate([seen, seen], axis=1)


def attend_step(queries, k_ref, k_at, v_at, rows, seen, acc, top, total):
    pairs = range(len(queries))
    keys = [k_ref[rows, k_at + p * 128:k_at + p * 128 + 128] for p in pairs]
    values = [k_ref[rows, v_at + p * 128:v_at + p * 128 + 128] for p in pairs]
    scores = [jnp.where(seen, dot(keys[p], queries[p], NT), MASKED) for p in pairs]
    before = [top[p:p + 1] for p in pairs]
    now = [jnp.maximum(before[p], jnp.max(scores[p], axis=0, keepdims=True)) for p in pairs]
    weight = [jnp.exp(scores[p] - now[p]) for p in pairs]
    keep = [jnp.exp(before[p] - now[p]) for p in pairs]
    added = [dot(values[p], weight[p].astype(jnp.bfloat16), TN) for p in pairs]
    sums = [jnp.sum(weight[p], axis=0, keepdims=True) for p in pairs]
    for p in pairs:
        top[p:p + 1] = now[p]
        total[p:p + 1] = total[p:p + 1] * keep[p] + sums[p]
        acc[p] = acc[p] * keep[p] + added[p]


def attend_back_step(queries, grads, fixes, sums, k_ref, k_at, v_at, rows, seen, acc, acc_k, acc_v):
    pairs = range(len(queries))
    cuts = [slice(p * 128, (p + 1) * 128) for p in pairs]
    keys = [k_ref[rows, k_at + p * 128:k_at + p * 128 + 128] for p in pairs]
    values = [k_ref[rows, v_at + p * 128:v_at + p * 128 + 128] for p in pairs]
    scores = [dot(keys[p], queries[p], NT) for p in pairs]
    dprob = [dot(values[p], grads[p], NT) for p in pairs]
    prob = [jnp.exp(jnp.where(seen, scores[p] - sums[p], MASKED)) for p in pairs]
    low = [prob[p].astype(jnp.bfloat16) for p in pairs]
    dscore = [(prob[p] * (dprob[p] - fixes[p])).astype(jnp.bfloat16) for p in pairs]
    added_v = [dot(low[p], grads[p], NN) for p in pairs]
    added_k = [dot(dscore[p], queries[p], NN) for p in pairs]
    added_q = [dot(keys[p], dscore[p], TN) for p in pairs]
    for p in pairs:
        acc_v[rows, cuts[p]] += added_v[p]
        acc_k[rows, cuts[p]] += added_k[p]
        acc[p] += added_q[p]


EPSILON = 1e-05
BF = jnp.bfloat16
F32 = jnp.float32


def norm_stats(values):
    average = jnp.mean(values, axis=-1, keepdims=True)
    center = values - average
    inverse = lax.rsqrt(jnp.mean(center * center, axis=-1, keepdims=True) + EPSILON)
    return center * inverse, inverse


def norm_forward(values, gain, shift):
    unit, _ = norm_stats(values)
    return (unit * gain + shift).astype(BF)


class Net:
    def __init__(self, sems, local_sems):
        place = lax.axis_index("dp")
        chip = lax.axis_index("tensor")
        core, plane = place % 2, place // 2
        odd = plane % 2
        beside, over, corner = chip + 1 - 2 * (chip % 2), (chip + 2) % 4, 3 - chip
        self.chip, self.core_index, self.odd, self.plane = chip, core, odd, plane
        self.chips = (beside, over, corner)
        self.core = (plane * 2 + 1 - core, chip)
        self.first = (place, beside + odd * (over - beside))
        self.second = (place, over + odd * (beside - over))
        self.corner = (place, corner)
        self.near_plane = ((plane + 1 - 2 * odd) * 2 + core, chip)
        self.far_plane = ((plane + 2) % 4 * 2 + core, chip)
        self.inside = (plane + 1) // 2 == 1
        self.outside = (plane + 1) // 2 != 1
        self.across = ((3 - plane) * 2 + core, chip)
        self.sems, self.local_sems = sems, local_sems
        self.count = self.local_count = 0
        self.unsent, self.unmoved = [], []

    def meet(self):
        barrier = pltpu.get_barrier_semaphore()
        partners = (
            self.core, self.first, self.second, self.corner, self.near_plane, self.far_plane, self.across,
        )
        for partner in partners:
            pl.semaphore_signal(barrier, inc=1, device_id=partner, device_id_type=pl.DeviceIdType.MESH)
        pl.semaphore_wait(barrier, len(partners))

    def describe(self, source, target, device):
        self.count += 1
        return pltpu.make_async_remote_copy(
            src_ref=source,
            dst_ref=target,
            send_sem=self.sems.at[0, self.count - 1],
            recv_sem=self.sems.at[1, self.count - 1],
            device_id=device,
            device_id_type=pl.DeviceIdType.MESH,
        )

    def describe_move(self, source, target):
        self.local_count += 1
        return pltpu.make_async_copy(source, target, self.local_sems.at[self.local_count - 1])

    def send(self, source, target, device):
        copy = self.describe(source, target, device)
        copy.start()
        self.unsent.append(copy)
        return copy

    def move(self, source, target):
        copy = self.describe_move(source, target)
        copy.start()
        self.unmoved.append(copy)
        return copy

    def moved(self, copy):
        copy.wait()
        self.unmoved = [other for other in self.unmoved if other is not copy]

    def sent(self, copy):
        copy.wait_send()
        self.unsent = [other for other in self.unsent if other is not copy]

    def finish(self):
        for copy in self.unmoved:
            copy.wait()
        for copy in self.unsent:
            copy.wait_send()
        self.unsent, self.unmoved = [], []


def row_in(net, given, rows, row):
    core, chip = net.core_index, net.chip
    mine = pl.ds(2 * core, 2)
    swap = net.send(given.at[:, 1 - core], rows.at[mine], net.core)
    keep = net.move(given.at[:, core], rows.at[mine])
    yield
    net.moved(keep)
    swap.wait_recv()
    own = net.move(rows.at[chip], row.at[chip, core])
    sends = [
        net.send(rows.at[other], row.at[chip, core], (lax.axis_index("dp"), other)) for other in net.chips
    ]
    yield
    net.moved(own)
    shares = [net.send(row.at[chip, core], row.at[chip, core], net.core)]
    for other, copy in zip(net.chips, sends):
        copy.wait_recv()
        shares.append(net.send(row.at[other, core], row.at[other, core], net.core))
    yield
    for copy in shares:
        copy.wait_recv()
        net.sent(copy)


def row_out(net, pieces, rows, result):
    core, chip = net.core_index, net.chip
    own = net.move(pieces.at[chip], rows.at[chip])
    sends = [net.send(pieces.at[other], rows.at[chip], (lax.axis_index("dp"), other)) for other in net.chips]
    yield
    net.moved(own)
    for copy in sends:
        copy.wait_recv()
    keep = net.move(rows.at[pl.ds(2 * core, 2)], result.at[:, core])
    swap = net.send(rows.at[pl.ds(2 * (1 - core), 2)], result.at[:, core], net.core)
    yield
    swap.wait_recv()
    net.moved(keep)


class Gather:
    def __init__(self, net, own, slot, flip=False):
        self.net, self.slot = net, slot
        self.one, self.two = (2, 1) if flip else (1, 2)
        to_one, self.to_two = (net.second, net.first) if flip else (net.first, net.second)
        self.near = net.send(own, slot(self.one), to_one)
        self.own = net.move(own, slot(0))

    def relay(self):
        self.near.wait_recv()
        self.corner = self.net.send(self.slot(self.one), self.slot(3), self.to_two)
        self.other = self.net.send(self.slot(self.one), self.slot(self.two), self.net.near_plane)

    def finish(self):
        self.net.moved(self.own)
        self.corner.wait_recv()
        self.other.wait_recv()


ANY = pl.BlockSpec(memory_space=pl.ANY)
VM = pl.BlockSpec(memory_space=pltpu.VMEM)
SENDS = 224


def half_columns(net, weight, width):
    return weight.at[:, pl.ds(pl.multiple_of(net.core_index * width, width), width)]


def half_rows(net, weight, height):
    return weight.at[pl.ds(pl.multiple_of(net.core_index * height, height), height)]


def tile_rows(i, size=256):
    return pl.ds(pl.multiple_of(i * size, size), size)


def call_remote(kernel, ident, ins, in_specs, outs, out_specs, scratch, vmem=48, name=None):
    return pl.pallas_call(
        kernel,
        in_specs=in_specs,
        out_specs=out_specs,
        out_shape=outs,
        scratch_shapes=list(scratch) + [pltpu.SemaphoreType.DMA((2, SENDS)), pltpu.SemaphoreType.DMA((SENDS,))],
        compiler_params=pltpu.CompilerParams(
            collective_id=ident, has_side_effects=True, vmem_limit_bytes=vmem << 20
        ),
        name=name,
    )(*ins)


def add_up(target, sources):
    step = min(64, target.shape[0])

    def some(i, _):
        cut = pl.ds(pl.multiple_of(i * step, step), step)
        total = sources[0][cut].astype(F32)
        for source in sources[1:]:
            total = total + source[cut].astype(F32)
        target[cut] = total.astype(BF)
        return 0

    lax.fori_loop(0, target.shape[0] // step, some, 0)


class Line:
    def __init__(self, net, total, landing, result):
        self.net, self.total = net, total
        self.one_in, self.two_in = landing
        place = result(net.core_index)
        self.inward = net.describe(total, self.one_in, net.near_plane)
        self.across = net.describe(total, self.two_in, net.across)
        self.outward = net.describe(self.two_in, place, net.near_plane)
        self.keep = net.describe_move(self.two_in, place)
        self.inside_core = net.describe(self.two_in, place, net.core)
        self.outside_core = net.describe(place, place, net.core)

    def line0(self):
        pl.when(self.net.outside)(self.inward.start)

    def line1(self):
        @pl.when(self.net.inside)
        def _():
            self.inward.wait_recv()
            add_up(self.total, [self.total, self.one_in])
            self.across.start()

    def line2(self):
        @pl.when(self.net.inside)
        def _():
            self.across.wait_recv()
            add_up(self.two_in, [self.total, self.two_in])
            self.outward.start()
            self.inside_core.start()
            self.keep.start()

    def line3(self):
        @pl.when(self.net.outside)
        def _():
            self.outward.wait_recv()
            self.outside_core.start()

    def end(self):
        @pl.when(self.net.inside)
        def _():
            self.inside_core.wait_recv()
            for copy in (self.across, self.outward, self.inside_core):
                copy.wait_send()
            self.keep.wait()

        @pl.when(self.net.outside)
        def _():
            self.outside_core.wait_recv()
            for copy in (self.inward, self.outside_core):
                copy.wait_send()


class Scatter:
    def __init__(self, net, part, first, landing, source=None):
        self.net, self.part, self.source = net, part, source or part
        self.near_in, self.pass_in, self.far_in = landing
        self.one, self.two = (1, 2) if first == 1 else (2, 1)
        self.to_one, self.to_two = (net.first, net.second) if first == 1 else (net.second, net.first)

    def start(self):
        self.passed = self.net.send(self.source(3), self.pass_in, self.to_one)
        self.near = self.net.send(self.source(self.one), self.near_in, self.to_one)

    def middle(self):
        self.passed.wait_recv()
        add_up(self.part(self.two), [self.part(self.two), self.pass_in])
        self.far = self.net.send(self.part(self.two), self.far_in, self.to_two)

    def own(self):
        self.near.wait_recv()
        self.far.wait_recv()
        add_up(self.part(0), [self.part(0), self.near_in, self.far_in])


def landing(rows, columns):
    return [pltpu.VMEM((rows, columns), BF)] * 3


def line_landing(rows, columns):
    return [pltpu.VMEM((rows, columns), BF)] * 2


def weight_grad(lhs, rhs, target, start, count, columns=slice(None), size=256):
    def some(i, _):
        cut = pl.ds(pl.multiple_of(start + i * size, size), size)
        target[cut, columns] = dot(lhs(cut), rhs(), TN).astype(BF)
        return 0

    lax.fori_loop(0, count // size, some, 0)


def norm_back_tile(grad_in, values, gain):
    unit, inverse = norm_stats(values)
    scaled = grad_in * gain
    first_mean = jnp.mean(scaled, axis=-1, keepdims=True)
    second_mean = jnp.mean(scaled * unit, axis=-1, keepdims=True)
    grad_values = inverse * (scaled - first_mean - unit * second_mean)
    return grad_values, jnp.sum(grad_in * unit, axis=0, keepdims=True), jnp.sum(grad_in, axis=0, keepdims=True)


def head_scatters(net, g_heads, g_out, lands):
    columns = lambda kind, s: slice(kind * 512 + s * 128, kind * 512 + s * 128 + 128)
    found = {
        "q": Scatter(net, lambda s: g_heads.at[:, columns(0, s)], 1, lands[:3]),
        "v": Scatter(net, lambda s: g_heads.at[:, columns(2, s)], 2, lands[3:6]),
    }
    for half in range(2):
        found["k%d" % half] = Scatter(
            net, lambda s, half=half: g_heads.at[pl.ds(half * 512, 512), columns(1, s)], 1 + half,
            lands[6 + half * 3:9 + half * 3],
        )
        found["o%d" % half] = Scatter(
            net, lambda s, half=half: g_out.at[pl.ds(s * 128 + half * 64, 64)], 1 + half,
            lands[12 + half * 3:15 + half * 3],
        )
    return found


def head_lines(net, g_heads, g_out, full_heads, full_out, lands):
    found = {}
    for kind, name in enumerate("qkv"):
        for half in range(2):
            at = (kind * 2 + half) * 2
            found[name + str(half)] = Line(
                net, g_heads.at[pl.ds(half * 512, 512), kind * 512:kind * 512 + 128], lands[at:at + 2],
                lambda c, kind=kind, half=half: full_heads.at[
                    kind, pl.ds(half * 512, 512), pl.ds(pl.multiple_of(c * 128, 128), 128)
                ],
            )
    for half in range(2):
        found["o%d" % half] = Line(
            net, g_out.at[pl.ds(half * 64, 64)], lands[12 + half * 2:14 + half * 2],
            lambda c, half=half: full_out.at[pl.ds(pl.multiple_of(c * 128 + half * 64, 64), 64)],
        )
    return found


def head_landing(width):
    return landing(1024, 128) * 2 + (landing(512, 128)) * 2 + landing(64, width) * 2


def head_line_landing(width):
    return line_landing(512, 128) * 6 + line_landing(64, width) * 2


def attend_block(i, q_ref, q_at, k_ref, k_at, v_at, low, high, causal, out_ref, sums_ref, acc, top, total):
    pairs = range(4)
    rows = tile_rows(i, QUERIES)
    queries = [
        both_heads(q_ref[rows, q_at + p * 128:q_at + p * 128 + 128] * jnp.bfloat16(HD ** -0.5)) for p in pairs
    ]
    least, limit = low[pl.ds(i, 1)], high[pl.ds(i, 1)]
    acc[...] = jnp.zeros_like(acc)
    total[...] = jnp.zeros_like(total)
    top[...] = jnp.full_like(top, -1e30)

    def step(j, _):
        at = pl.multiple_of(j * KEYS, KEYS)
        seen = allowed_keys(least, limit, at)
        attend_step(queries, k_ref, k_at, v_at, pl.ds(at, KEYS), seen, acc, top, total)
        return 0

    lax.fori_loop(0, i // 2 + 1 if causal else k_ref.shape[0] // KEYS, step, 0)
    for p in pairs:
        sums = total[p:p + 1]
        mixed = acc[p] / sums
        joined = jnp.concatenate([mixed[:HD, :QUERIES], mixed[HD:, QUERIES:]], axis=0)
        out_ref[rows, p * 128:(p + 1) * 128] = joined.T.astype(BF)
        sums_ref[i, p:p + 1] = top[p:p + 1] + jnp.log(sums)


def attend_back_block(
    i, q_ref, q_at, k_ref, k_at, v_at, grad_ref, out_ref, out_at, sums_ref, low, high, causal, dq_ref, dq_at, acc, acc_k, acc_v
):
    pairs = range(4)
    rows = tile_rows(i, QUERIES)
    least, limit = low[pl.ds(i, 1)], high[pl.ds(i, 1)]
    queries, grads, fixes, sums = [], [], [], []
    ones = jnp.ones((8, 128), BF)
    for p in pairs:
        queries.append(both_heads(q_ref[rows, q_at + p * 128:q_at + p * 128 + 128] * jnp.bfloat16(HD ** -0.5)))
        grad = both_heads(grad_ref[rows, p * 128:(p + 1) * 128])
        grads.append(grad)
        out = out_ref[rows, out_at + p * 128:out_at + p * 128 + 128].astype(F32)
        product = grad.astype(F32) * jnp.concatenate([out, out], axis=0)
        coarse = product.astype(BF)
        fine = (product - coarse.astype(F32)).astype(BF)
        fixes.append((dot(ones, coarse, NT) + dot(ones, fine, NT))[:1])
        sums.append(sums_ref[i, p:p + 1])
    acc[...] = jnp.zeros_like(acc)

    def step(j, _):
        at = pl.multiple_of(j * KEYS, KEYS)
        seen = allowed_keys(least, limit, at)
        attend_back_step(queries, grads, fixes, sums, k_ref, k_at, v_at, pl.ds(at, KEYS), seen, acc, acc_k, acc_v)
        return 0

    lax.fori_loop(0, i // 2 + 1 if causal else k_ref.shape[0] // KEYS, step, 0)
    for p in pairs:
        mixed = acc[p] * (HD ** -0.5)
        joined = jnp.concatenate([mixed[:HD, :QUERIES], mixed[HD:, QUERIES:]], axis=0)
        dq_ref[rows, dq_at + p * 128:dq_at + p * 128 + 128] = joined.T.astype(BF)


def reach(query_ids, key_ids):
    low = jnp.zeros(query_ids.shape, F32)
    high = jnp.zeros(query_ids.shape, F32)
    for segment in range(16):
        here = query_ids == segment
        before = jnp.sum((key_ids < segment).astype(F32), axis=(0, 1), keepdims=True)
        upto = jnp.sum((key_ids <= segment).astype(F32), axis=(0, 1), keepdims=True)
        low = low + jnp.where(here, before, 0.0)
        high = high + jnp.where(here, upto, 0.0)
    return low.astype(jnp.int32), high.astype(jnp.int32)


def project_out(net, att, weight, part, part_in):
    swaps = []
    for i in range(4):
        part[i] = dot(att[i * 256:i * 256 + 256], weight[...], NN).astype(BF).reshape(2, 128, -1)
        swaps.append(net.send(part.at[i], part_in.at[i], net.core))
    return swaps


def ahead_kernel(
    x_in, mem_in, top_in, target_ids_in, source_ids_in, bias_q, bias_v, bias_cq, bias_cv, bias_i, wq, wk, wv, wo, wcq, wck, wcv, wco, inner, outer,
    gain1, shift1, bias_o, gain2, shift2, bias_c, gain3, shift3,
    x_out, mem_out, top_out, n1_out, qkv_out, att1_out, sums1_out, h1_out, n2_out, q2_out, kv2_out, att2_out, sums2_out,
    h2_out, n3_out, act_out, slope_out, g_outer_out, wqkv_out, wo_out, wc_out, wco_out, wi_out, wu_out, reach_out,
    rows_x, rows_mem, rows_top, row, mem, weights, weights2, wo_vm, wco_vm, wi, normed, qkv, att, part, part_in, part_in2,
    hidden, queries, keys, act, slope, g_outer, bias, biases, ids, all_ids, spans, sums1, sums2, acc, top, total, sems, local_sems,
):
    net = Net(sems, local_sems)
    core, chip = net.core_index, net.chip
    net.meet()
    enter_x = row_in(net, x_in, rows_x, row)
    next(enter_x)
    mine = pl.ds(2 * core, 2)
    for i in range(2):
        for r in range(8):
            cut = slice(r * 128, r * 128 + 128)
            ids[i, r:r + 1] = target_ids_in[i:i + 1, cut]
            ids[i, 8 + r:9 + r] = source_ids_in[i:i + 1, cut]
    at = 0
    for value in (bias_q, bias_v, bias_cq, bias_cv, bias_i):
        for r in range(value.shape[1] // 128):
            bias[at:at + 1] = value[:, r * 128:r * 128 + 128]
            at += 1
    ids_copies = [net.move(ids, all_ids.at[mine]), net.send(ids, all_ids.at[mine], net.core)]
    bias_own = net.move(bias, biases.at[0])
    bias_copies = [
        net.send(bias, biases.at[1], net.first),
        net.send(bias, biases.at[2], net.second),
        net.send(bias, biases.at[3], net.corner),
    ]

    def gather_columns(weight, target, kind, flip):
        slot = lambda s: target.at[:, kind * 512 + s * 128:kind * 512 + s * 128 + 128]
        return Gather(net, half_columns(net, weight, 128), slot, flip)

    def gather_rows_of(weight, target, flip):
        return Gather(net, half_rows(net, weight, 128), lambda s: target.at[pl.ds(s * 128, 128)], flip)

    def gather_inner(k):
        own = inner.at[pl.ds(k * 256, 256), pl.ds(pl.multiple_of(core * 512, 512), 512)]
        return Gather(net, own, lambda s: wi.at[pl.ds(k * 256, 256), s * 512:s * 512 + 512], k % 2 == 1)

    def gather_outer(k):
        own = outer.at[pl.ds(pl.multiple_of(core * 512 + k * 128, 128), 128)]
        return Gather(net, own, lambda s: wu_out.at[pl.ds(s * 512 + k * 128, 128)], k % 2 == 1)

    gather_q = gather_columns(wq, weights, 0, False)
    gather_k = gather_columns(wk, weights, 1, True)
    next(enter_x)
    gather_v = gather_columns(wv, weights, 2, False)
    gather_o = gather_rows_of(wo, wo_vm, True)
    enter_mem = row_in(net, mem_in, rows_mem, mem)
    next(enter_mem)
    enter_top = row_in(net, top_in, rows_top, top_out)
    next(enter_top)
    gather_q.relay()
    gather_k.relay()
    next(enter_x)
    for _ in enter_x:
        pass
    x_move = net.move(row, x_out)

    def norm_first(i, _):
        normed[tile_rows(i)] = norm_forward(row[i].reshape(256, -1).astype(F32), gain1[...], shift1[...])
        return 0

    lax.fori_loop(0, 4, norm_first, 0)
    n1_move = net.move(normed, n1_out)
    gather_v.relay()
    gather_o.relay()
    next(enter_mem)
    gather_ck = gather_columns(wck, weights2, 1, False)
    gather_cv = gather_columns(wcv, weights2, 2, True)
    net.moved(bias_own)
    for copy in bias_copies:
        copy.wait_recv()

    def project_first(kind):
        cut = slice(kind * 512, kind * 512 + 512)
        bias = None
        if kind != 1:
            bias = jnp.concatenate([biases[s, pl.ds(kind + core, 1)] for s in range(4)], axis=1)

        def some(i, _):
            value = dot(normed[tile_rows(i)], weights[:, cut], NN)
            if kind != 1:
                value = value + bias
            qkv[tile_rows(i), cut] = value.astype(BF)
            return 0

        lax.fori_loop(0, 4, some, 0)

    for kind, gather in enumerate((gather_q, gather_k, gather_v)):
        gather.finish()
        project_first(kind)
    net.move(weights, wqkv_out)
    gather_cq = gather_columns(wcq, weights2, 0, False)
    gather_co = gather_rows_of(wco, wco_vm, True)
    net.move(qkv, qkv_out)
    net.moved(ids_copies[0])
    ids_copies[1].wait_recv()
    target_ids, source_ids = all_ids[chip, :8], all_ids[chip, 8:]
    low, _ = reach(target_ids, target_ids)
    spans[0] = low
    place = lax.broadcasted_iota(jnp.int32, (8, 128), 0) * 128 + lax.broadcasted_iota(jnp.int32, (8, 128), 1)
    spans[1] = place + 1
    low, high = reach(target_ids, source_ids)
    spans[2] = low
    spans[3] = high
    net.move(spans, reach_out)

    def attend_first(i, _):
        attend_block(i, qkv, 0, qkv, 512, 1024, spans.at[0], spans.at[1], True, att, sums1, acc, top, total)
        return 0

    lax.fori_loop(0, 8, attend_first, 0)
    next(enter_mem)
    gather_ck.relay()
    gather_cv.relay()
    gather_cq.relay()
    gather_co.relay()
    att1_move = net.move(att, att1_out)
    net.move(sums1, sums1_out)
    gather_o.finish()
    net.move(wo_vm, wo_out)
    swaps = project_out(net, att, wo_vm, part, part_in)
    inners = [gather_inner(k) for k in range(4)]
    next(enter_top)
    for _ in enter_mem:
        pass
    net.move(mem, mem_out)
    for gather in (gather_ck, gather_cv):
        gather.finish()
    values_bias = jnp.concatenate([biases[s, pl.ds(6 + core, 1)] for s in range(4)], axis=1)
    query_bias = jnp.concatenate([biases[s, pl.ds(4 + core, 1)] for s in range(4)], axis=1)

    def project_memory(i, _):
        tokens = mem[i].reshape(256, -1)
        keys[tile_rows(i), :512] = dot(tokens, weights2[:, 512:1024], NN).astype(BF)
        keys[tile_rows(i), 512:] = (dot(tokens, weights2[:, 1024:], NN) + values_bias).astype(BF)
        return 0

    lax.fori_loop(0, 4, project_memory, 0)
    net.move(keys, kv2_out)
    net.moved(n1_move)
    for i in range(4):
        swaps[i].wait_recv()

    def middle_rows(i, _):
        value = row[i].astype(F32) + part[i].astype(F32) + part_in[i].astype(F32)
        value = value.reshape(256, -1) + bias_o[...]
        hidden[tile_rows(i)] = value
        normed[tile_rows(i)] = norm_forward(value, gain2[...], shift2[...])
        return 0

    lax.fori_loop(0, 4, middle_rows, 0)
    net.moved(x_move)
    h1_move = net.move(hidden, h1_out)
    n2_move = net.move(normed, n2_out)
    gather_cq.finish()
    net.move(weights2, wc_out)

    def project_query(i, _):
        queries[tile_rows(i)] = (dot(normed[tile_rows(i)], weights2[:, :512], NN) + query_bias).astype(BF)
        return 0

    lax.fori_loop(0, 4, project_query, 0)
    net.move(queries, q2_out)
    net.moved(att1_move)

    def attend_second(i, _):
        attend_block(i, queries, 0, keys, 0, 512, spans.at[2], spans.at[3], False, att, sums2, acc, top, total)
        return 0

    lax.fori_loop(0, 3, attend_second, 0)
    for gather in inners:
        gather.relay()
    outers = [gather_outer(k) for k in range(4)]
    lax.fori_loop(3, 8, attend_second, 0)
    net.move(att, att2_out)
    net.move(sums2, sums2_out)
    gather_co.finish()
    net.move(wco_vm, wco_out)
    for copy in swaps:
        net.sent(copy)
    swaps = project_out(net, att, wco_vm, part, part_in2)
    next(enter_top)
    net.moved(h1_move)
    net.moved(n2_move)
    for i in range(4):
        swaps[i].wait_recv()

    def last_rows(i, _):
        value = part[i].astype(F32) + part_in2[i].astype(F32)
        value = hidden[tile_rows(i)] + value.reshape(256, -1) + bias_c[...]
        hidden[tile_rows(i)] = value
        normed[tile_rows(i)] = norm_forward(value, gain3[...], shift3[...])
        return 0

    lax.fori_loop(0, 4, last_rows, 0)
    net.move(hidden, h2_out)
    net.move(normed, n3_out)
    for gather in inners:
        gather.finish()
    net.move(wi, wi_out)

    def feed(i, _):
        tokens = normed[tile_rows(i)]
        for s in range(4):
            cut = slice(s * 512, s * 512 + 512)
            unit_bias = jnp.concatenate([biases[s, pl.ds(8 + core * 4 + k, 1)] for k in range(4)], axis=1)
            pre = dot(tokens, wi[:, cut], NN) + unit_bias
            sigmoid = jax.nn.sigmoid(pre)
            act[tile_rows(i), cut] = (pre * sigmoid).astype(BF)
            slope[tile_rows(i), cut] = (sigmoid * (1.0 + pre * (1.0 - sigmoid))).astype(BF)
        return 0

    lax.fori_loop(0, 1, feed, 0)
    outers[0].relay()
    outers[1].relay()
    lax.fori_loop(1, 2, feed, 0)
    outers[2].relay()
    outers[3].relay()
    for _ in enter_top:
        pass
    top_load = net.move(top_out, row)
    lax.fori_loop(2, 4, feed, 0)
    net.move(act, act_out)
    net.move(slope, slope_out)
    net.moved(top_load)
    weight_grad(lambda cut: act[:, cut], lambda: row[...].reshape(1024, -1), g_outer, 0, 2048, size=512)
    net.move(g_outer, g_outer_out)
    for gather in outers:
        gather.finish()
    net.finish()


def ahead(x, mem, top, ids, biases, weights, vectors):
    length, width = 1024, x.shape[-1]
    shape = jax.ShapeDtypeStruct
    quarters = (4, 2, 128, width)
    rows = lambda columns, kind=BF: shape((length, columns), kind)
    sums = shape((8, 4, 256), F32)
    return call_remote(
        ahead_kernel, 1,
        [a.reshape(2, 2, -1, width) for a in (x, mem, top)] + list(ids) + [v[None] for v in biases] + list(weights)
        + [v[None] for v in vectors],
        [ANY] * 3 + [VM] * 7 + [ANY] * 10 + [VM] * 8,
        [
            shape(quarters, BF), shape(quarters, BF), shape(quarters, BF), rows(width), rows(1536), rows(512), sums,
            rows(width, F32), rows(width), rows(512), rows(1024), rows(512), sums,
            rows(width, F32), rows(width), rows(2048), rows(2048), shape((2048, width), BF),
            shape((width, 1536), BF), shape((512, width), BF), shape((width, 1536), BF), shape((512, width), BF),
            shape((width, 2048), BF), shape((2048, width), BF), shape((4, 8, 128), jnp.int32),
        ],
        [ANY] * 25,
        [pltpu.VMEM((4, 128, width), BF)] * 3 + [pltpu.VMEM(quarters, BF)] * 2 + [pltpu.VMEM((width, 1536), BF)] * 2
        + [pltpu.VMEM((512, width), BF)] * 2
        + [
            pltpu.VMEM((width, 2048), BF), pltpu.VMEM((length, width), BF), pltpu.VMEM((length, 1536), BF),
            pltpu.VMEM((length, 512), BF), pltpu.VMEM(quarters, BF), pltpu.VMEM(quarters, BF), pltpu.VMEM(quarters, BF),
            pltpu.VMEM((length, width), F32), pltpu.VMEM((length, 512), BF), pltpu.VMEM((length, 1024), BF),
            pltpu.VMEM((length, 2048), BF), pltpu.VMEM((length, 2048), BF), pltpu.VMEM((2048, width), BF),
            pltpu.VMEM((16, 128), F32),
            pltpu.VMEM((4, 16, 128), F32), pltpu.VMEM((2, 16, 128), jnp.int32),
            pltpu.VMEM((4, 16, 128), jnp.int32), pltpu.VMEM((4, 8, 128), jnp.int32),
            pltpu.VMEM((8, 4, 256), F32), pltpu.VMEM((8, 4, 256), F32),
            pltpu.VMEM((4, 128, 256), F32), pltpu.VMEM((4, 256), F32), pltpu.VMEM((4, 256), F32),
        ],
        vmem=62, name="ahead",
    )


def turn_kernel(
    g_outer_in, act_in, slope_in, n3_in, h2_in, top_in, wi_in, wu_in, wco_in, q_in, kv_in, att_in, sums_in, reach_in, gain, bias_u,
    block_out, gh_out, outer_out, inner_out, heads_out, vectors_out, split_out,
    act, slope, wu, wi, g_outer, g_inner, hidden, row, normed, wco, part, back_in, out_part, out_in, gatt,
    pieces, result, rows_back, acc_k, acc_v, acc, spans, sums, vectors, split, *rest,
):
    lands, (sems, local_sems) = rest[:-2], rest[-2:]
    net = Net(sems, local_sems)
    core = net.core_index
    loads = [
        net.move(source, target)
        for source, target in (
            (top_in, row), (wu_in, wu), (slope_in, slope), (wi_in, wi), (n3_in, normed), (act_in, act), (g_outer_in, g_outer),
            (h2_in, hidden), (wco_in, wco), (reach_in, spans), (sums_in, sums),
        )
    ]
    net.meet()
    outers = [
        Scatter(
            net, lambda s, k=k: g_outer.at[pl.ds(s * 512 + k * 256, 256)], 1 + k, lands[k * 3:k * 3 + 3],
            lambda s, k=k: g_outer_in.at[pl.ds(s * 512 + k * 256, 256)],
        )
        for k in range(2)
    ]
    outer_lines = [
        Line(
            net, g_outer.at[pl.ds(k * 128, 128)], lands[12 + k * 2:14 + k * 2],
            lambda c, k=k: outer_out.at[pl.ds(pl.multiple_of(c * 512 + k * 128, 128), 128)],
        )
        for k in range(4)
    ]
    inners = [
        Scatter(
            net, lambda s, k=k: g_inner.at[pl.ds(k * 512, 512), s * 512:s * 512 + 512], 1 + k,
            lands[6 + k * 3:9 + k * 3],
        )
        for k in range(2)
    ]

    def inner_grad(k, s):
        cut = slice(s * 512, s * 512 + 512)
        weight_grad(lambda rows: normed[:, rows], lambda: slope[:, cut], g_inner, k * 512, 512, cut)

    for k in range(2):
        outers[k].start()
    for copy in loads[:3]:
        net.moved(copy)
    split[...] = jnp.zeros_like(split)
    vectors[...] = jnp.zeros_like(vectors)

    def feed_back(i, _):
        tokens = row[i].reshape(256, -1)
        for s in range(4):
            cut = slice(s * 512, s * 512 + 512)
            value = (dot(tokens, wu[cut], NT) * slope[tile_rows(i), cut].astype(F32)).astype(BF)
            slope[tile_rows(i), cut] = value
            split[0:1, cut] += jnp.sum(value.astype(F32), axis=0, keepdims=True)
        return 0

    lax.fori_loop(0, 4, feed_back, 0)
    for copy in loads[3:]:
        net.moved(copy)
    swaps = []
    for i in range(4):
        value = dot(slope[i * 256:i * 256 + 256], wi[...], NT)
        part[i] = value.astype(BF).reshape(2, 128, -1)
        swaps.append(net.send(part.at[i], back_in.at[i], net.core))
    outers[0].middle()
    outers[1].middle()
    for k in range(2):
        inner_grad(k, 3)
        inner_grad(k, 1 + k)
        inners[k].start()

    def feed_out(i, _):
        out_part[i] = dot(act[tile_rows(i)], wu[...], NN).astype(BF).reshape(2, 128, -1)
        return 0

    lax.fori_loop(0, 4, feed_out, 0)
    out_swap = net.send(out_part.at[:, 1 - core], out_in, net.core)
    loads = [
        net.move(kv_in, act.at[:, :1024]), net.move(q_in, act.at[:, 1024:1536]), net.move(att_in, act.at[:, 1536:]),
    ]
    for copy in swaps:
        copy.wait_recv()

    def back(i, _):
        grad = (part[i].astype(F32) + back_in[i].astype(F32)).reshape(256, -1)
        before = hidden[i]
        change, by_gain, by_shift = norm_back_tile(grad, before.reshape(256, -1), gain[...])
        top = row[i].reshape(256, -1).astype(F32)
        value = top + change
        pieces[i] = hidden[i, core]
        hidden[i] = value.reshape(2, 128, -1)
        gatt[tile_rows(i)] = dot(value.astype(BF), wco[...], NT).astype(BF)
        vectors[4:5] += by_gain
        vectors[5:6] += by_shift
        vectors[6:7] += jnp.sum(top, axis=0, keepdims=True)
        vectors[3:4] += jnp.sum(value, axis=0, keepdims=True)
        return 0

    lax.fori_loop(0, 4, back, 0)
    net.move(hidden, gh_out)
    net.move(vectors, vectors_out)
    net.move(split, split_out)
    out_swap.wait_recv()
    for i in range(4):
        result[i] = (pieces[i] + out_part[i, core].astype(F32) + out_in[i].astype(F32) + bias_u[...]).astype(BF)
    leave = row_out(net, result, rows_back, block_out)
    next(leave)
    for k in range(2):
        inner_grad(k, 2 - k)
        inner_grad(k, 0)
    for k in range(2):
        outers[k].own()
        outer_lines[2 * k].line0()
        outer_lines[2 * k + 1].line0()
    for copy in loads:
        net.moved(copy)
    acc_k[...] = jnp.zeros_like(acc_k)
    acc_v[...] = jnp.zeros_like(acc_v)

    def attend_back(i, _):
        attend_back_block(
            i, act, 1024, act, 0, 512, gatt, act, 1536, sums, spans.at[2], spans.at[3], False, slope, 0, acc, acc_k, acc_v
        )
        return 0

    lax.fori_loop(0, 3, attend_back, 0)
    inners[0].middle()
    inners[1].middle()
    outer_lines[0].line1()
    outer_lines[1].line1()
    lax.fori_loop(3, 5, attend_back, 0)
    outer_lines[2].line1()
    outer_lines[3].line1()
    outer_lines[0].line2()
    lax.fori_loop(5, 7, attend_back, 0)
    outer_lines[1].line2()
    outer_lines[2].line2()
    lax.fori_loop(7, 8, attend_back, 0)
    outer_lines[3].line2()
    slope[:, 512:1024] = acc_k[...].astype(BF)
    slope[:, 1024:1536] = acc_v[...].astype(BF)
    net.move(slope.at[:, :1536], heads_out)
    inners[0].own()
    net.move(g_inner.at[pl.ds(0, 512), :512], inner_out.at[pl.ds(0, 512)])
    inners[1].own()
    net.move(g_inner.at[pl.ds(512, 512), :512], inner_out.at[pl.ds(512, 512)])
    next(leave)
    for line in outer_lines:
        line.line3()
    for line in outer_lines:
        line.end()
    for _ in leave:
        pass
    net.finish()


def turn(g_outer, act, slope, n3, h2, top, wi, wu, wco, q, kv, att, sums, reach_rows, gain, bias_u):
    length, width = act.shape[0], n3.shape[-1]
    shape = jax.ShapeDtypeStruct
    quarters = (4, 2, 128, width)
    return call_remote(
        turn_kernel, 2,
        (
            g_outer, act, slope, n3, h2.reshape(quarters), top, wi, wu, wco, q, kv, att, sums, reach_rows, gain[None], bias_u[None],
        ),
        [ANY] * 14 + [VM] * 2,
        [
            shape((2, 2, 128, width), BF), shape(quarters, F32), shape((1024, width), BF), shape((width, 512), BF),
            shape((length, 1536), BF), shape((8, width), F32), shape((8, 2048), F32),
        ],
        [ANY] * 7,
        [
            pltpu.VMEM((length, 2048), BF), pltpu.VMEM((length, 2048), BF), pltpu.VMEM((2048, width), BF),
            pltpu.VMEM((width, 2048), BF), pltpu.VMEM((2048, width), BF), pltpu.VMEM((width, 2048), BF),
            pltpu.VMEM(quarters, F32), pltpu.VMEM(quarters, BF), pltpu.VMEM((length, width), BF),
            pltpu.VMEM((512, width), BF), pltpu.VMEM(quarters, BF), pltpu.VMEM(quarters, BF), pltpu.VMEM(quarters, BF),
            pltpu.VMEM((4, 128, width), BF), pltpu.VMEM((length, 512), BF),
            pltpu.VMEM((4, 128, width), F32), pltpu.VMEM((4, 128, width), BF), pltpu.VMEM((4, 128, width), BF),
            pltpu.VMEM((length, 512), F32), pltpu.VMEM((length, 512), F32), pltpu.VMEM((4, 128, 256), F32),
            pltpu.VMEM((4, 8, 128), jnp.int32), pltpu.VMEM((8, 4, 256), F32),
            pltpu.VMEM((8, width), F32), pltpu.VMEM((8, 2048), F32),
        ]
        + landing(256, width) * 2 + landing(512, 512) * 2 + line_landing(128, width) * 4,
        vmem=62, name="turn",
    )


def last_kernel(
    heads_in, n2_in, mem_in, att2_in, gh_in, h1_in, wc_in, wo_in, inner_in, qkv_in, att1_in, sums_in, reach_in, n1_in, x_in,
    wqkv_in, shared_in, split_in, gain2, gain1,
    mem_out, grad_out, cross_out, cross_o_out, heads_out, o_out, inner_out, shared_out, late_out, split_out,
    dqkv, normed, tokens, att, grads, hidden, weights, wo, part, part_in, mem_part, mem_back, grad_in,
    rows_mem, rows_back, g_cross, g_cross_o, g_heads, g_o, gatt, acc, spans, sums,
    inner_total,
    shared, shared_land, late, late_land, split_load, split, split_sum, split_plane, split_land, split_full, *rest,
):
    lands, (sems, local_sems) = rest[:-2], rest[-2:]
    net = Net(sems, local_sems)
    core, chip = net.core_index, net.chip
    place = lax.axis_index("dp")
    loads = [
        net.move(source, target)
        for source, target in (
            (heads_in, dqkv), (wc_in, weights), (inner_in, inner_total), (mem_in, tokens), (n2_in, normed), (att2_in, att),
            (gh_in, grads), (h1_in, hidden), (wo_in, wo), (reach_in, spans), (sums_in, sums), (shared_in, shared.at[0]),
            (split_in, split_load),
        )
    ]
    net.meet()
    inner_lines = [
        Line(
            net, inner_total.at[pl.ds(k * 512, 512)], lands[68 + k * 2:70 + k * 2],
            lambda c, k=k: inner_out.at[pl.ds(k * 512, 512), pl.ds(pl.multiple_of(c * 512, 512), 512)],
        )
        for k in range(2)
    ]
    scatters = head_scatters(net, g_cross, g_cross_o, lands[:18])
    lines = head_lines(net, g_cross, g_cross_o, cross_out, cross_o_out, lands[18:34])
    own_scatters = head_scatters(net, g_heads, g_o, lands[34:52])
    own_lines = head_lines(net, g_heads, g_o, heads_out, o_out, lands[52:68])

    def each(group, names, *steps):
        for step in steps:
            for name in names.split():
                getattr(group[name], step)()

    for copy in loads[:3]:
        net.moved(copy)
    inner_lines[0].line0()
    inner_lines[1].line0()
    swaps = []
    for i in range(4):
        value = dot(dqkv[i * 256:i * 256 + 256, :512], weights[:, :512], NT)
        part[i] = value.astype(BF).reshape(2, 128, -1)
        swaps.append(net.send(part.at[i], part_in.at[i], net.core))
    for copy in loads[3:]:
        net.moved(copy)
    memory = lambda cut: tokens[:, :, :, cut].reshape(1024, -1)
    for kind in (1, 2):
        cut = slice(kind * 512, kind * 512 + 512)
        weight_grad(memory, lambda: dqkv[:, cut], g_cross, 0, 1024, cut)
        each(scatters, "k0 k1" if kind == 1 else "v", "start")
    weight_grad(lambda cut: normed[:, cut], lambda: dqkv[:, :512], g_cross, 0, 1024, slice(0, 512))
    each(scatters, "q", "start")
    load_n1 = net.move(n1_in, normed)
    load_qkv = net.move(qkv_in, g_heads)
    load_x = net.move(x_in, tokens)
    for copy in swaps:
        copy.wait_recv()

    def back(i, _):
        grad = (part[i].astype(F32) + part_in[i].astype(F32)).reshape(256, -1)
        change, by_gain, by_shift = norm_back_tile(grad, hidden[tile_rows(i)], gain2[...])
        value = grads[tile_rows(i)] + change
        mem_part[i] = value.astype(BF).reshape(2, 128, -1)
        gatt[tile_rows(i)] = dot(value.astype(BF), wo[...], NT).astype(BF)
        shared[0, 1:2] += by_gain
        shared[0, 2:3] += by_shift
        shared[0, 0:1] += jnp.sum(value, axis=0, keepdims=True)
        hidden[tile_rows(i)] = value
        return 0

    lax.fori_loop(0, 4, back, 0)
    each(scatters, "k0 k1", "middle")
    inner_lines[0].line1()
    weight_grad(lambda cut: att[:, cut], lambda: grads[...].astype(BF), g_cross_o, 0, 512)
    each(scatters, "o0 o1", "start")
    load_att = net.move(att1_in, att)
    each(scatters, "v q", "middle")
    for s in range(4):
        for k in range(4):
            split[s, 4 + k:5 + k] = split_load[0:1, s * 512 + k * 128:s * 512 + k * 128 + 128]
    for at, kind in ((2, 0), (3, 2)):
        total = jnp.sum(dqkv[:, kind * 512:kind * 512 + 512].astype(F32), axis=0, keepdims=True)
        for s in range(4):
            split[s, at:at + 1] = total[:, s * 128:s * 128 + 128]
    stages = [(place, net.chips[0]), (place, net.chips[1]), net.near_plane, net.far_plane]
    shared_copy = net.send(shared.at[0], shared_land.at[0], stages[0])

    def shared_stage(at):
        nonlocal shared_copy
        shared_copy.wait_recv()
        shared[at + 1] = shared[at] + shared_land[at]
        if at < 3:
            shared_copy = net.send(shared.at[at + 1], shared_land.at[at + 1], stages[at + 1])

    grads[...] = jnp.zeros_like(grads)
    net.moved(load_att)
    weight_grad(lambda cut: att[:, cut], lambda: mem_part[...].reshape(1024, -1), g_o, 0, 512)
    each(own_scatters, "o0 o1", "start")
    net.moved(load_qkv)

    def attend_back(i, _):
        attend_back_block(
            i, g_heads, 0, g_heads, 512, 1024, gatt, att, 0, sums, spans.at[0], spans.at[1], True, dqkv, 0, acc,
            grads.at[:, :512], grads.at[:, 512:],
        )
        return 0

    lax.fori_loop(0, 4, attend_back, 0)
    each(scatters, "k0 k1", "own")
    each(lines, "k0 k1", "line0")
    inner_lines[1].line1()
    each(scatters, "o0 o1", "middle")
    lax.fori_loop(4, 6, attend_back, 0)
    each(scatters, "v q", "own")
    each(lines, "v0 v1 q0 q1", "line0")
    each(lines, "k0 k1", "line1")
    inner_lines[0].line2()
    shared_stage(0)
    lax.fori_loop(6, 8, attend_back, 0)
    for i in range(4):
        part_in[i] = grads[i * 256:i * 256 + 256].astype(BF).reshape(2, 128, -1)
    net.moved(load_n1)

    def head_grad(kind):
        cut = slice(kind * 512, kind * 512 + 512)
        side = slice(kind * 512 - 512, kind * 512)
        rhs = (lambda: part_in[:, :, :, side].reshape(1024, -1)) if kind else (lambda: dqkv[:, :512])
        weight_grad(lambda rows: normed[:, rows], rhs, g_heads, 0, 1024, cut)

    each(own_scatters, "o0 o1", "middle")
    head_grad(0)
    each(own_scatters, "q", "start")
    inner_lines[1].line2()
    each(lines, "v0 v1", "line1")
    each(scatters, "o0 o1", "own")
    each(lines, "o0 o1", "line0")
    each(lines, "q0 q1", "line1")
    head_grad(2)
    each(own_scatters, "v", "start")
    each(lines, "k0 k1", "line2")
    head_grad(1)
    each(own_scatters, "k0 k1", "start")
    inner_lines[0].line3()
    each(lines, "v0 v1", "line2")

    def memory_back(i, _):
        rows = tile_rows(i)
        value = dot(dqkv[rows, 512:1024], weights[:, 512:1024], NT) + dot(dqkv[rows, 1024:], weights[:, 1024:], NT)
        mem_part[i] = value.astype(BF).reshape(2, 128, -1)
        return 0

    lax.fori_loop(0, 4, memory_back, 0)
    mem_swap = net.send(mem_part.at[:, 1 - core], mem_back, net.core)
    load_w = net.move(wqkv_in, weights)
    each(own_scatters, "o0 o1", "own")
    each(own_lines, "o0 o1", "line0")
    each(lines, "o0 o1", "line1")
    each(lines, "q0 q1", "line2")
    each(own_scatters, "q v", "middle")
    net.moved(load_w)
    for copy in swaps:
        net.sent(copy)

    def first_back(i, _):
        rows = tile_rows(i)
        value = dot(dqkv[rows, :512], weights[:, :512], NT)
        value = value + dot(part_in[i].reshape(256, -1), weights[:, 512:], NT)
        part[i] = value.astype(BF).reshape(2, 128, -1)
        return 0

    lax.fori_loop(0, 4, first_back, 0)
    swap = net.send(part.at[:, 1 - core], grad_in, net.core)
    mem_swap.wait_recv()
    for i in range(4):
        mem_back[i] = (mem_part[i, core].astype(F32) + mem_back[i].astype(F32)).astype(BF)
    for at, value in ((0, dqkv[:, :512]), (1, part_in[:, :, :, 512:].reshape(1024, -1))):
        total = jnp.sum(value.astype(F32), axis=0, keepdims=True)
        for s in range(4):
            split[s, at:at + 1] = total[:, s * 128:s * 128 + 128]
    split_copies = [net.send(split, split_plane.at[0], net.near_plane)]
    net.moved(load_x)
    swap.wait_recv()
    each(own_scatters, "k0 k1", "middle")
    leave_mem = row_out(net, mem_back, rows_mem, mem_out)
    next(leave_mem)
    late[0] = jnp.zeros(late.shape[1:], F32)
    for i in range(4):
        grad = part[i, core].astype(F32) + grad_in[i].astype(F32)
        change, by_gain, by_shift = norm_back_tile(grad, tokens[i, core].astype(F32), gain1[...])
        grad_in[i] = (hidden[pl.ds(pl.multiple_of(i * 256 + core * 128, 128), 128)] + change).astype(BF)
        late[0, 0:1] += by_gain
        late[0, 1:2] += by_shift
    late_copy = net.send(late.at[0], late_land.at[0], net.core)
    leave = row_out(net, grad_in, rows_back, grad_out)

    def late_stage(at):
        nonlocal late_copy
        late_copy.wait_recv()
        late[at + 1] = late[at] + late_land[at]
        if at < 4:
            late_copy = net.send(late.at[at + 1], late_land.at[at + 1], (stages[2], stages[3], stages[0], stages[1])[at])

    def split_stage(at):
        nonlocal split_copies
        for copy in split_copies:
            copy.wait_recv()
        if at == 0:
            for s, other in ((0, 0), (1, 2), (2, 1), (3, 3)):
                split_sum[0, s] = split[s] + split_plane[0, other]
            split_copies = [net.send(split_sum.at[0], split_plane.at[1], net.far_plane)]
        elif at == 1:
            split_sum[1] = split_sum[0] + split_plane[1]
            split_copies = [
                net.send(split_sum.at[1, s], split_land.at[s - 1], device)
                for s, device in ((1, net.first), (2, net.second), (3, net.corner))
            ]
        else:
            split_full[core] = split_sum[1, 0] + split_land[0] + split_land[1] + split_land[2]
            split_copies = [net.send(split_full.at[core], split_full.at[core], net.core)]

    late_stage(0)
    each(own_scatters, "q v", "own")
    each(own_lines, "q0 v0 q1 v1", "line0")
    next(leave)
    each(own_scatters, "k0 k1", "own")
    each(own_lines, "k0 k1", "line0")
    shared_stage(1)
    split_stage(0)
    late_stage(1)
    each(own_lines, "q0 v0 o0 o1", "line1")
    each(lines, "o0 o1", "line2")
    each(own_lines, "q1", "line1")
    each(own_lines, "q0", "line2")
    each(own_lines, "v1", "line1")
    each(own_lines, "v0", "line2")
    each(own_lines, "k0 k1", "line1")
    inner_lines[1].line3()
    shared_stage(2)
    split_stage(1)
    late_stage(2)
    each(own_lines, "q1 v1 o0 o1", "line2")
    each(own_lines, "k0 k1", "line2")
    next(leave_mem)
    each(lines, "k0 k1", "line3")
    each(lines, "v0 v1 q0 q1", "line3")
    each(lines, "o0 o1", "line3")
    shared_stage(3)
    late_stage(3)
    split_stage(2)
    each(own_lines, "q0 v0 q1 v1", "line3")
    next(leave)
    late_stage(4)
    each(own_lines, "o0 o1 k0 k1", "line3")
    for line in inner_lines + list(lines.values()) + list(own_lines.values()):
        line.end()
    for _ in leave_mem:
        pass
    for _ in leave:
        pass
    split_copies[0].wait_recv()
    for source, target in ((shared.at[4], shared_out), (late.at[5], late_out), (split_full, split_out)):
        net.move(source, target)
    net.finish()


def last(heads, n2, mem, att2, gh, h1, wc, wo, inner_total, qkv, att1, sums, reach_rows, n1, x, wqkv, shared, split, gain2, gain1):
    length, width = heads.shape[0], n1.shape[-1]
    shape = jax.ShapeDtypeStruct
    quarters = (4, 2, 128, width)
    own = [shape((3, width, 256), BF), shape((256, width), BF)]
    return call_remote(
        last_kernel, 3,
        (
            heads, n2, mem, att2, gh.reshape(length, width), h1, wc, wo, inner_total, qkv, att1, sums, reach_rows, n1, x, wqkv, shared, split,
            gain2[None], gain1[None],
        ),
        [ANY] * 18 + [VM] * 2,
        [shape((2, 2, 128, width), BF)] * 2 + own + own
        + [shape((width, 1024), BF), shape((8, width), F32), shape((8, width), F32), shape((2, 8, 128), F32)],
        [ANY] * 10,
        [
            pltpu.VMEM((length, 1536), BF), pltpu.VMEM((length, width), BF), pltpu.VMEM(quarters, BF),
            pltpu.VMEM((length, 512), BF), pltpu.VMEM((length, width), F32), pltpu.VMEM((length, width), F32),
            pltpu.VMEM((width, 1536), BF), pltpu.VMEM((512, width), BF), pltpu.VMEM(quarters, BF),
            pltpu.VMEM(quarters, BF), pltpu.VMEM(quarters, BF), pltpu.VMEM((4, 128, width), BF),
            pltpu.VMEM((4, 128, width), BF),
        ]
        + [pltpu.VMEM((4, 128, width), BF)] * 2
        + [pltpu.VMEM((width, 1536), BF), pltpu.VMEM((512, width), BF)] * 2
        + [
            pltpu.VMEM((length, 512), BF), pltpu.VMEM((4, 128, 256), F32),
            pltpu.VMEM((4, 8, 128), jnp.int32),
            pltpu.VMEM((8, 4, 256), F32), pltpu.VMEM((width, 512), BF),
        ]
        + [
            pltpu.VMEM((5, 8, width), F32), pltpu.VMEM((4, 8, width), F32),
            pltpu.VMEM((6, 8, width), F32), pltpu.VMEM((5, 8, width), F32),
            pltpu.VMEM((8, 2048), F32), pltpu.VMEM((4, 8, 128), F32), pltpu.VMEM((2, 4, 8, 128), F32),
            pltpu.VMEM((2, 4, 8, 128), F32), pltpu.VMEM((3, 8, 128), F32),
            pltpu.VMEM((2, 8, 128), F32),
        ]
        + (head_landing(width) + head_line_landing(width)) * 2 + line_landing(512, 512) * 2,
        vmem=63, name="last",
    )


def widen_kernel(rows_in, mem_in, grad_in, cross_in, cross_o_in, heads_in, o_in, inner_in, outer_in, shared, late, split, *outs):
    rows, mem, grad, cq, ck, cv, co, q, k, v, o, inner, outer = outs[:13]
    rows[...] = rows_in[...]
    mem[...] = mem_in[...].astype(F32)
    grad[...] = grad_in[...].astype(F32)
    for kind, (cross, own) in enumerate(((cq, q), (ck, k), (cv, v))):
        cross[...] = cross_in[kind].astype(F32)
        own[...] = heads_in[kind].astype(F32)
    co[...] = cross_o_in[...].astype(F32)
    o[...] = o_in[...].astype(F32)
    inner[...] = inner_in[...].astype(F32)
    outer[...] = outer_in[...].astype(F32)
    vectors, bias_q, bias_v, bias_cq, bias_cv, bias_i = outs[13:22], *outs[22:]

    @pl.when(pl.program_id(0) == 0)
    def _():
        vectors[0][...] = late[0:1]
        vectors[1][...] = late[1:2]
        for at in range(7):
            vectors[2 + at][...] = shared[at:at + 1]
        for at, bias in enumerate((bias_q, bias_v, bias_cq, bias_cv)):
            bias[...] = jnp.concatenate([split[c, at:at + 1] for c in range(2)], axis=1)
        bias_i[...] = jnp.concatenate([split[c, 4 + at:5 + at] for c in range(2) for at in range(4)], axis=1)


def widen(rows, mem, grad, cross, cross_o, heads, o, inner, outer, shared, late, split):
    steps, width = 4, rows.shape[-1]
    shape = jax.ShapeDtypeStruct
    flat = lambda a: a.reshape(-1, width)
    block = lambda a: pl.BlockSpec((a.shape[0] // steps, a.shape[1]), lambda i: (i, 0))
    whole = lambda *dims: pl.BlockSpec(dims, lambda i: (0,) * len(dims))
    head = pl.BlockSpec((3, width // steps, 256), lambda i: (0, i, 0))
    ins = [flat(rows), flat(mem), flat(grad), cross, cross_o, heads, o, inner, outer, shared, late, split]
    in_specs = [block(ins[0])] * 3 + [head, block(cross_o), head, block(o), block(inner), block(outer)]
    in_specs += [whole(8, width), whole(8, width), whole(2, 8, 128)]
    wide = lambda a: shape(a.shape, F32)
    columns = shape((width, 256), F32)
    outs = [shape(ins[0].shape, BF), wide(ins[1]), wide(ins[2])] + [columns] * 3 + [wide(cross_o)] + [columns] * 3
    outs += [wide(o), wide(inner), wide(outer)]
    out_specs = [block(a) for a in outs] + [whole(1, width)] * 9 + [whole(1, 256)] * 4 + [whole(1, 1024)]
    outs += [shape((1, width), F32)] * 9 + [shape((1, 256), F32)] * 4 + [shape((1, 1024), F32)]
    return pl.pallas_call(
        widen_kernel,
        grid=(steps,),
        in_specs=in_specs,
        out_specs=out_specs,
        out_shape=outs,
        compiler_params=pltpu.CompilerParams(vmem_limit_bytes=63 << 20),
        name="widen",
    )(*ins)


def solution(mesh):
    if mesh.shape["tensor"] != 4 or mesh.shape["dp"] != 8:
        return general_solution(mesh)

    def local(
        layer_input, memory, grad_out, target_segments, source_segments,
        self_gain, self_shift, query_weight, query_bias, key_weight, value_weight, value_bias,
        attend_weight, attend_bias,
        cross_gain, cross_shift, cross_query, cross_query_bias, cross_key, cross_value, cross_value_bias,
        cross_attend, cross_attend_bias,
        feed_gain, feed_shift, inner_weight, inner_bias, outer_weight, outer_bias,
    ):
        (
            x, mem, top, n1, qkv1, att1, sums1, h1, n2, q2, kv2, att2, sums2, h2, n3, act, slope, g_outer,
            wqkv, wo, wc, wco, wi, wu, spans,
        ) = ahead(
            layer_input, memory, grad_out, (target_segments, source_segments),
            (query_bias, value_bias, cross_query_bias, cross_value_bias, inner_bias),
            (
                query_weight, key_weight, value_weight, attend_weight, cross_query, cross_key, cross_value, cross_attend,
                inner_weight, outer_weight,
            ),
            (self_gain, self_shift, attend_bias, cross_gain, cross_shift, cross_attend_bias, feed_gain, feed_shift),
        )
        block_out, gh2, f_outer, f_inner, heads2, shared, split = turn(
            g_outer, act, slope, n3, h2, top, wi, wu, wco, q2, kv2, att2, sums2, spans, feed_gain, outer_bias
        )
        memory_grad, input_grad, c_heads, c_out, s_heads, s_out, f_inner, shared, late, split = last(
            heads2, n2, mem, att2, gh2, h1, wc, wo, f_inner, qkv1, att1, sums1, spans, n1, x, wqkv, shared, split,
            cross_gain, self_gain,
        )
        (
            block_out, memory_grad, input_grad, g_cq, g_ck, g_cv, g_co, g_q, g_k, g_v, g_o, g_inner, g_outer,
            g_gain1, g_shift1, g_bias_o, g_gain2, g_shift2, g_bias_c, g_gain3, g_shift3, g_bias_u,
            g_bias_q, g_bias_v, g_bias_cq, g_bias_cv, g_bias_i,
        ) = widen(block_out, memory_grad, input_grad, c_heads, c_out, s_heads, s_out, f_inner, f_outer, shared, late, split)
        tokens = layer_input.shape
        vector = lambda v: v.reshape(-1)
        return (
            block_out.reshape(tokens), input_grad.reshape(tokens), memory_grad.reshape(tokens),
            vector(g_gain1), vector(g_shift1),
            g_q, vector(g_bias_q), g_k, g_v, vector(g_bias_v),
            g_o, vector(g_bias_o),
            vector(g_gain2), vector(g_shift2),
            g_cq, vector(g_bias_cq), g_ck, g_cv, vector(g_bias_cv),
            g_co, vector(g_bias_c),
            vector(g_gain3), vector(g_shift3),
            g_inner, vector(g_bias_i), g_outer, vector(g_bias_u),
        )

    row, one, by_column, by_row = P("dp", "tensor", None), P(), P(None, "tensor"), P("tensor", None)
    part, ids = P("tensor"), P("dp", None)
    return jax.shard_map(
        local,
        mesh=mesh,
        in_specs=(
            row, row, row, ids, ids,
            one, one, by_column, part, by_column, by_column, part, by_row, one,
            one, one, by_column, part, by_column, by_column, part, by_row, one,
            one, one, by_column, part, by_row, one,
        ),
        out_specs=(
            row, row, row,
            one, one, by_column, part, by_column, by_column, part, by_row, one,
            one, one, by_column, part, by_column, by_column, part, by_row, one,
            one, one, by_column, part, by_row, one,
        ),
        check_vma=False,
    )


BLOCK_ROWS = 512


def general_norm_forward(values, gain, shift):
    average = jnp.mean(values, axis=-1, keepdims=True)
    center = values - average
    inverse = lax.rsqrt(jnp.mean(center * center, axis=-1, keepdims=True) + EPSILON)
    normed = center * inverse
    return ((normed * gain + shift).astype(jnp.bfloat16), normed, inverse)


def general_norm_backward(grad_in, normed, inverse, gain):
    scaled = grad_in * gain
    first_mean = jnp.mean(scaled, axis=-1, keepdims=True)
    second_mean = jnp.mean(scaled * normed, axis=-1, keepdims=True)
    grad_values = inverse * (scaled - first_mean - normed * second_mean)
    return (grad_values, jnp.sum(grad_in * normed, axis=(0, 1)), jnp.sum(grad_in, axis=(0, 1)))


def gather_rows(values):
    return lax.all_gather(values, "tensor", axis=1, tiled=True)


def gather_grads(values):
    return lax.all_gather(values, "tensor", axis=1, tiled=True)


def reduce_inputs(partial_sum):
    return lax.psum_scatter(partial_sum, "tensor", scatter_dimension=1, tiled=True)


def advance(base, partial_sum, bias):
    return base + lax.psum_scatter(partial_sum, "tensor", scatter_dimension=1, tiled=True) + bias


def next_rows(values, gain, shift):
    return gather_rows(general_norm_forward(values, gain, shift)[0])


def backward_rows(normed_low):
    return gather_rows(normed_low)


def project(rows_in, weight):
    return jnp.einsum("rtd,dc->rtc", rows_in, weight, preferred_element_type=jnp.float32)


def project_back(grads, weight):
    return jnp.einsum("rtc,dc->rtd", grads, weight, preferred_element_type=jnp.float32)


def outer_sum(rows_in, grads):
    return jnp.einsum("rtd,rtc->dc", rows_in, grads, preferred_element_type=jnp.float32)


def bias_sum(grads):
    return jnp.sum(grads.astype(jnp.float32), axis=(0, 1))


def split_heads(values):
    return values.reshape(values.shape[0], values.shape[1], values.shape[2] // HD, HD)


def block_scores(query_block, key_row, query_ids, key_ids, row_start, causal):
    raw_scores = jnp.einsum(
        "qhd,khd->hqk", query_block, key_row, preferred_element_type=jnp.float32
    ) * float(HD) ** (-0.5)
    allowed = query_ids[:, None] == key_ids[None, :]
    if causal:
        query_place = row_start + jnp.arange(query_block.shape[0], dtype=jnp.int32)
        key_place = jnp.arange(key_row.shape[0], dtype=jnp.int32)
        allowed = allowed & (key_place[None, :] <= query_place[:, None])
    return jnp.where(allowed[None], raw_scores, jnp.full(raw_scores.shape, MASKED, jnp.float32))


def block_inputs(
    query_heads, key_heads, value_heads, query_ids, key_ids, position, block_count, block_size
):
    row_index = position // block_count
    row_start = position % block_count * block_size
    query_row = lax.dynamic_index_in_dim(query_heads, row_index, 0, keepdims=False)
    query_block = lax.dynamic_slice_in_dim(query_row, row_start, block_size, 0)
    key_row = lax.dynamic_index_in_dim(key_heads, row_index, 0, keepdims=False)
    value_row = lax.dynamic_index_in_dim(value_heads, row_index, 0, keepdims=False)
    query_seg = lax.dynamic_slice_in_dim(
        lax.dynamic_index_in_dim(query_ids, row_index, 0, keepdims=False), row_start, block_size, 0
    )
    key_seg = lax.dynamic_index_in_dim(key_ids, row_index, 0, keepdims=False)
    return (row_index, row_start, query_block, key_row, value_row, query_seg, key_seg)


def attend_forward(query, keys, values, query_ids, key_ids, causal):
    query_heads = split_heads(query)
    key_heads = split_heads(keys)
    value_heads = split_heads(values)
    block_size = min(BLOCK_ROWS, query.shape[1])
    block_count = query.shape[1] // block_size

    def one_block(position):
        row_index, row_start, query_block, key_row, value_row, query_seg, key_seg = block_inputs(
            query_heads,
            key_heads,
            value_heads,
            query_ids,
            key_ids,
            position,
            block_count,
            block_size,
        )
        scores = block_scores(query_block, key_row, query_seg, key_seg, row_start, causal)
        row_max = jnp.max(scores, axis=-1, keepdims=True)
        expo_scores = jnp.exp(scores - row_max)
        row_total = jnp.sum(expo_scores, axis=-1, keepdims=True)
        softmax_out = expo_scores / row_total
        attended = jnp.einsum(
            "hqk,khd->qhd",
            softmax_out.astype(jnp.bfloat16),
            value_row,
            preferred_element_type=jnp.float32,
        ).astype(jnp.bfloat16)
        return (attended, (row_max + jnp.log(row_total))[..., 0])

    attended_all, log_sums = lax.map(
        one_block, jnp.arange(query.shape[0] * block_count, dtype=jnp.int32)
    )
    return (attended_all.reshape(query.shape), log_sums)


def attend_backward(query, keys, values, grad_att, log_sums, query_ids, key_ids, causal):
    query_heads = split_heads(query)
    key_heads = split_heads(keys)
    value_heads = split_heads(values)
    grad_heads = split_heads(grad_att)
    block_size = min(BLOCK_ROWS, query.shape[1])
    block_count = query.shape[1] // block_size
    score_scale = float(HD) ** (-0.5)

    def one_block(carry, inputs):
        grad_keys, grad_values = carry
        position, log_sum = inputs
        row_index, row_start, query_block, key_row, value_row, query_seg, key_seg = block_inputs(
            query_heads,
            key_heads,
            value_heads,
            query_ids,
            key_ids,
            position,
            block_count,
            block_size,
        )
        grad_row = lax.dynamic_index_in_dim(grad_heads, row_index, 0, keepdims=False)
        grad_block = lax.dynamic_slice_in_dim(grad_row, row_start, block_size, 0)
        scores = block_scores(query_block, key_row, query_seg, key_seg, row_start, causal)
        softmax_out = jnp.exp(scores - log_sum[..., None])
        softmax_low = softmax_out.astype(jnp.bfloat16)
        attended = jnp.einsum(
            "hqk,khd->qhd", softmax_low, value_row, preferred_element_type=jnp.float32
        ).astype(jnp.bfloat16)
        grad_prob = jnp.einsum(
            "qhd,khd->hqk", grad_block, value_row, preferred_element_type=jnp.float32
        )
        correction = jnp.sum(softmax_out * grad_prob, axis=-1, keepdims=True)
        grad_score = (softmax_out * (grad_prob - correction)).astype(jnp.bfloat16)
        grad_query = (
            jnp.einsum("hqk,khd->qhd", grad_score, key_row, preferred_element_type=jnp.float32)
            * score_scale
        ).astype(jnp.bfloat16)
        key_added = (
            jnp.einsum("hqk,qhd->khd", grad_score, query_block, preferred_element_type=jnp.float32)
            * score_scale
        )
        value_added = jnp.einsum(
            "hqk,qhd->khd", softmax_low, grad_block, preferred_element_type=jnp.float32
        )
        grad_keys = grad_keys.at[row_index].add(key_added)
        grad_values = grad_values.at[row_index].add(value_added)
        return ((grad_keys, grad_values), (grad_query, attended))

    empty_grads = jnp.zeros(key_heads.shape, jnp.float32)
    positions = jnp.arange(query.shape[0] * block_count, dtype=jnp.int32)
    (grad_keys, grad_values), (grad_query, attended_all) = lax.scan(
        one_block, (empty_grads, empty_grads), (positions, log_sums)
    )
    return (
        grad_query.reshape(query.shape),
        grad_keys.reshape(keys.shape).astype(jnp.bfloat16),
        grad_values.reshape(values.shape).astype(jnp.bfloat16),
        attended_all.reshape(query.shape),
    )


def general_local(
    layer_input,
    memory,
    grad_out,
    target_segments,
    source_segments,
    self_gain,
    self_shift,
    query_weight,
    query_bias,
    key_weight,
    value_weight,
    value_bias,
    attend_weight,
    attend_bias,
    cross_gain,
    cross_shift,
    cross_query,
    cross_query_bias,
    cross_key,
    cross_value,
    cross_value_bias,
    cross_attend,
    cross_attend_bias,
    feed_gain,
    feed_shift,
    inner_weight,
    inner_bias,
    outer_weight,
    outer_bias,
):
    inputs = layer_input.astype(jnp.float32)
    rows_first = next_rows(inputs, self_gain, self_shift)
    query_first = (project(rows_first, query_weight) + query_bias).astype(jnp.bfloat16)
    keys_first = project(rows_first, key_weight).astype(jnp.bfloat16)
    values_first = (project(rows_first, value_weight) + value_bias).astype(jnp.bfloat16)
    attended_first, sums_first = attend_forward(
        query_first, keys_first, values_first, target_segments, target_segments, True
    )
    base_first = advance(inputs, project(attended_first, attend_weight), attend_bias)
    memory_rows = lax.all_gather(memory, "tensor", axis=1, tiled=True)
    rows_second = next_rows(base_first, cross_gain, cross_shift)
    query_second = (project(rows_second, cross_query) + cross_query_bias).astype(jnp.bfloat16)
    keys_second = project(memory_rows, cross_key).astype(jnp.bfloat16)
    values_second = (project(memory_rows, cross_value) + cross_value_bias).astype(jnp.bfloat16)
    attended_second, sums_second = attend_forward(
        query_second, keys_second, values_second, target_segments, source_segments, False
    )
    base_second = advance(base_first, project(attended_second, cross_attend), cross_attend_bias)
    rows_third = next_rows(base_second, feed_gain, feed_shift)
    pre_active = project(rows_third, inner_weight) + inner_bias
    active = jax.nn.silu(pre_active).astype(jnp.bfloat16)
    base_out = advance(base_second, project(active, outer_weight), outer_bias)
    block_out = base_out.astype(jnp.bfloat16)
    kept_input, kept_first, kept_second, kept_memory, kept_sums_first, kept_sums_second = (
        lax.optimization_barrier(
            (inputs, base_first, base_second, memory_rows, sums_first, sums_second)
        )
    )
    grad_top = grad_out.astype(jnp.float32)
    normed_low3, unit_third, inverse_third = general_norm_forward(kept_second, feed_gain, feed_shift)
    rows_back3 = backward_rows(normed_low3)
    pre_back = project(rows_back3, inner_weight) + inner_bias
    sigmoid_back = jax.nn.sigmoid(pre_back)
    active_back = (pre_back * sigmoid_back).astype(jnp.bfloat16)
    grad_rows3 = gather_grads(grad_top.astype(jnp.bfloat16))
    grad_outer_weight = outer_sum(active_back, grad_rows3)
    grad_outer_bias = jnp.sum(grad_top, axis=(0, 1))
    grad_active = project_back(grad_rows3, outer_weight)
    grad_inner = (grad_active * sigmoid_back * (1.0 + pre_back * (1.0 - sigmoid_back))).astype(
        jnp.bfloat16
    )
    grad_inner_weight = outer_sum(rows_back3, grad_inner)
    grad_inner_bias = bias_sum(grad_inner)
    grad_norm3 = reduce_inputs(project_back(grad_inner, inner_weight))
    grad_from3, grad_feed_gain, grad_feed_shift = general_norm_backward(
        grad_norm3, unit_third, inverse_third, feed_gain
    )
    grad_hidden2 = grad_top + grad_from3
    normed_low2, unit_second, inverse_second = general_norm_forward(kept_first, cross_gain, cross_shift)
    rows_back2 = backward_rows(normed_low2)
    query_back2 = (project(rows_back2, cross_query) + cross_query_bias).astype(jnp.bfloat16)
    keys_back2 = project(kept_memory, cross_key).astype(jnp.bfloat16)
    values_back2 = (project(kept_memory, cross_value) + cross_value_bias).astype(jnp.bfloat16)
    grad_rows2 = gather_grads(grad_hidden2.astype(jnp.bfloat16))
    grad_att2 = project_back(grad_rows2, cross_attend).astype(jnp.bfloat16)
    grad_query2, grad_keys2, grad_values2, attended_back2 = attend_backward(
        query_back2,
        keys_back2,
        values_back2,
        grad_att2,
        kept_sums_second,
        target_segments,
        source_segments,
        False,
    )
    grad_cross_attend = outer_sum(attended_back2, grad_rows2)
    grad_cross_attend_bias = jnp.sum(grad_hidden2, axis=(0, 1))
    grad_cross_query = outer_sum(rows_back2, grad_query2)
    grad_cross_query_bias = bias_sum(grad_query2)
    grad_cross_key = outer_sum(kept_memory, grad_keys2)
    grad_cross_value = outer_sum(kept_memory, grad_values2)
    grad_cross_value_bias = bias_sum(grad_values2)
    memory_grad = lax.psum_scatter(
        (project_back(grad_keys2, cross_key) + project_back(grad_values2, cross_value)).astype(
            jnp.bfloat16
        ),
        "tensor",
        scatter_dimension=1,
        tiled=True,
    ).astype(jnp.float32)
    grad_norm2 = reduce_inputs(project_back(grad_query2, cross_query))
    grad_from2, grad_cross_gain, grad_cross_shift = general_norm_backward(
        grad_norm2, unit_second, inverse_second, cross_gain
    )
    grad_hidden1 = grad_hidden2 + grad_from2
    normed_low1, unit_first, inverse_first = general_norm_forward(kept_input, self_gain, self_shift)
    rows_back1 = backward_rows(normed_low1)
    query_back1 = (project(rows_back1, query_weight) + query_bias).astype(jnp.bfloat16)
    keys_back1 = project(rows_back1, key_weight).astype(jnp.bfloat16)
    values_back1 = (project(rows_back1, value_weight) + value_bias).astype(jnp.bfloat16)
    grad_rows1 = gather_grads(grad_hidden1.astype(jnp.bfloat16))
    grad_att1 = project_back(grad_rows1, attend_weight).astype(jnp.bfloat16)
    grad_query1, grad_keys1, grad_values1, attended_back1 = attend_backward(
        query_back1,
        keys_back1,
        values_back1,
        grad_att1,
        kept_sums_first,
        target_segments,
        target_segments,
        True,
    )
    grad_attend_weight = outer_sum(attended_back1, grad_rows1)
    grad_attend_bias = jnp.sum(grad_hidden1, axis=(0, 1))
    grad_query_weight = outer_sum(rows_back1, grad_query1)
    grad_query_bias = bias_sum(grad_query1)
    grad_key_weight = outer_sum(rows_back1, grad_keys1)
    grad_value_weight = outer_sum(rows_back1, grad_values1)
    grad_value_bias = bias_sum(grad_values1)
    grad_norm1 = reduce_inputs(
        project_back(grad_query1, query_weight)
        + project_back(grad_keys1, key_weight)
        + project_back(grad_values1, value_weight)
    )
    grad_from1, grad_self_gain, grad_self_shift = general_norm_backward(
        grad_norm1, unit_first, inverse_first, self_gain
    )
    input_grad = grad_hidden1 + grad_from1
    (
        grad_query_weight,
        grad_query_bias,
        grad_key_weight,
        grad_value_weight,
        grad_value_bias,
        grad_attend_weight,
        grad_cross_query,
        grad_cross_query_bias,
        grad_cross_key,
        grad_cross_value,
        grad_cross_value_bias,
        grad_cross_attend,
        grad_inner_weight,
        grad_inner_bias,
        grad_outer_weight,
    ) = (
        lax.psum(grad_query_weight.astype(jnp.bfloat16), "dp").astype(jnp.float32),
        lax.psum(grad_query_bias.astype(jnp.bfloat16), "dp").astype(jnp.float32),
        lax.psum(grad_key_weight.astype(jnp.bfloat16), "dp").astype(jnp.float32),
        lax.psum(grad_value_weight.astype(jnp.bfloat16), "dp").astype(jnp.float32),
        lax.psum(grad_value_bias.astype(jnp.bfloat16), "dp").astype(jnp.float32),
        lax.psum(grad_attend_weight.astype(jnp.bfloat16), "dp").astype(jnp.float32),
        lax.psum(grad_cross_query.astype(jnp.bfloat16), "dp").astype(jnp.float32),
        lax.psum(grad_cross_query_bias.astype(jnp.bfloat16), "dp").astype(jnp.float32),
        lax.psum(grad_cross_key.astype(jnp.bfloat16), "dp").astype(jnp.float32),
        lax.psum(grad_cross_value.astype(jnp.bfloat16), "dp").astype(jnp.float32),
        lax.psum(grad_cross_value_bias.astype(jnp.bfloat16), "dp").astype(jnp.float32),
        lax.psum(grad_cross_attend.astype(jnp.bfloat16), "dp").astype(jnp.float32),
        lax.psum(grad_inner_weight.astype(jnp.bfloat16), "dp").astype(jnp.float32),
        lax.psum(grad_inner_bias.astype(jnp.bfloat16), "dp").astype(jnp.float32),
        lax.psum(grad_outer_weight.astype(jnp.bfloat16), "dp").astype(jnp.float32),
    )
    (
        grad_self_gain,
        grad_self_shift,
        grad_attend_bias,
        grad_cross_gain,
        grad_cross_shift,
        grad_cross_attend_bias,
        grad_feed_gain,
        grad_feed_shift,
        grad_outer_bias,
    ) = lax.psum(
        (
            grad_self_gain,
            grad_self_shift,
            grad_attend_bias,
            grad_cross_gain,
            grad_cross_shift,
            grad_cross_attend_bias,
            grad_feed_gain,
            grad_feed_shift,
            grad_outer_bias,
        ),
        ("dp", "tensor"),
    )
    return (
        block_out,
        input_grad,
        memory_grad,
        grad_self_gain,
        grad_self_shift,
        grad_query_weight,
        grad_query_bias,
        grad_key_weight,
        grad_value_weight,
        grad_value_bias,
        grad_attend_weight,
        grad_attend_bias,
        grad_cross_gain,
        grad_cross_shift,
        grad_cross_query,
        grad_cross_query_bias,
        grad_cross_key,
        grad_cross_value,
        grad_cross_value_bias,
        grad_cross_attend,
        grad_cross_attend_bias,
        grad_feed_gain,
        grad_feed_shift,
        grad_inner_weight,
        grad_inner_bias,
        grad_outer_weight,
        grad_outer_bias,
    )


def general_solution(mesh):
    placed = (
        P("dp", "tensor", None),
        P("dp", "tensor", None),
        P("dp", "tensor", None),
        P("dp", None),
        P("dp", None),
        P(),
        P(),
        P(None, "tensor"),
        P("tensor"),
        P(None, "tensor"),
        P(None, "tensor"),
        P("tensor"),
        P("tensor", None),
        P(),
        P(),
        P(),
        P(None, "tensor"),
        P("tensor"),
        P(None, "tensor"),
        P(None, "tensor"),
        P("tensor"),
        P("tensor", None),
        P(),
        P(),
        P(),
        P(None, "tensor"),
        P("tensor"),
        P("tensor", None),
        P(),
    )
    return jax.shard_map(
        general_local,
        mesh=mesh,
        in_specs=placed,
        out_specs=(
            P("dp", "tensor", None),
            P("dp", "tensor", None),
            P("dp", "tensor", None),
            P(),
            P(),
            P(None, "tensor"),
            P("tensor"),
            P(None, "tensor"),
            P(None, "tensor"),
            P("tensor"),
            P("tensor", None),
            P(),
            P(),
            P(),
            P(None, "tensor"),
            P("tensor"),
            P(None, "tensor"),
            P(None, "tensor"),
            P("tensor"),
            P("tensor", None),
            P(),
            P(),
            P(),
            P(None, "tensor"),
            P("tensor"),
            P("tensor", None),
            P(),
        ),
        check_vma=False,
    )
```

```python
import jax
import jax.numpy as jnp
from jax import lax
from jax.experimental import pallas as pl
from jax.experimental.pallas import tpu as pltpu
from jax.sharding import PartitionSpec as P

HD = 64
MASKED = -1000000000.0
QUERIES = 128
KEYS = 256
NT = (((1,), (1,)), ((), ()))
TN = (((0,), (0,)), ((), ()))
NN = (((1,), (0,)), ((), ()))


def dot(a, b, dims):
    return lax.dot_general(a, b, dims, preferred_element_type=jnp.float32)


def both_heads(block):
    first = lax.broadcasted_iota(jnp.int32, block.shape, 1) < HD
    zero = jnp.zeros_like(block)
    return jnp.concatenate([jnp.where(first, block, zero), jnp.where(first, zero, block)], axis=0)


def allowed_keys(least, limit, at):
    key_place = at + lax.broadcasted_iota(jnp.int32, (KEYS, 1), 0)
    seen = (key_place >= least) & (key_place < limit)
    return jnp.concatenate([seen, seen], axis=1)


def attend_step(queries, k_ref, k_at, v_at, rows, seen, acc, top, total):
    pairs = range(len(queries))
    keys = [k_ref[rows, k_at + p * 128:k_at + p * 128 + 128] for p in pairs]
    values = [k_ref[rows, v_at + p * 128:v_at + p * 128 + 128] for p in pairs]
    scores = [jnp.where(seen, dot(keys[p], queries[p], NT), MASKED) for p in pairs]
    before = [top[p:p + 1] for p in pairs]
    now = [jnp.maximum(before[p], jnp.max(scores[p], axis=0, keepdims=True)) for p in pairs]
    weight = [jnp.exp(scores[p] - now[p]) for p in pairs]
    keep = [jnp.exp(before[p] - now[p]) for p in pairs]
    added = [dot(values[p], weight[p].astype(jnp.bfloat16), TN) for p in pairs]
    sums = [jnp.sum(weight[p], axis=0, keepdims=True) for p in pairs]
    for p in pairs:
        top[p:p + 1] = now[p]
        total[p:p + 1] = total[p:p + 1] * keep[p] + sums[p]
        acc[p] = acc[p] * keep[p] + added[p]


def attend_back_step(queries, grads, fixes, sums, k_ref, k_at, v_at, rows, seen, acc, acc_k, acc_v):
    pairs = range(len(queries))
    cuts = [slice(p * 128, (p + 1) * 128) for p in pairs]
    keys = [k_ref[rows, k_at + p * 128:k_at + p * 128 + 128] for p in pairs]
    values = [k_ref[rows, v_at + p * 128:v_at + p * 128 + 128] for p in pairs]
    scores = [dot(keys[p], queries[p], NT) for p in pairs]
    dprob = [dot(values[p], grads[p], NT) for p in pairs]
    prob = [jnp.exp(jnp.where(seen, scores[p] - sums[p], MASKED)) for p in pairs]
    low = [prob[p].astype(jnp.bfloat16) for p in pairs]
    dscore = [(prob[p] * (dprob[p] - fixes[p])).astype(jnp.bfloat16) for p in pairs]
    added_v = [dot(low[p], grads[p], NN) for p in pairs]
    added_k = [dot(dscore[p], queries[p], NN) for p in pairs]
    added_q = [dot(keys[p], dscore[p], TN) for p in pairs]
    for p in pairs:
        acc_v[rows, cuts[p]] += added_v[p]
        acc_k[rows, cuts[p]] += added_k[p]
        acc[p] += added_q[p]


EPSILON = 1e-05
BF = jnp.bfloat16
F32 = jnp.float32


def norm_stats(values):
    average = jnp.mean(values, axis=-1, keepdims=True)
    center = values - average
    inverse = lax.rsqrt(jnp.mean(center * center, axis=-1, keepdims=True) + EPSILON)
    return center * inverse, inverse


def norm_forward(values, gain, shift):
    unit, _ = norm_stats(values)
    return (unit * gain + shift).astype(BF)


class Net:
    def __init__(self, sems, local_sems):
        place = lax.axis_index("dp")
        chip = lax.axis_index("tensor")
        core, plane = place % 2, place // 2
        odd = plane % 2
        beside, over, corner = chip + 1 - 2 * (chip % 2), (chip + 2) % 4, 3 - chip
        self.chip, self.core_index, self.odd, self.plane = chip, core, odd, plane
        self.chips = (beside, over, corner)
        self.core = (plane * 2 + 1 - core, chip)
        self.first = (place, beside + odd * (over - beside))
        self.second = (place, over + odd * (beside - over))
        self.corner = (place, corner)
        self.near_plane = ((plane + 1 - 2 * odd) * 2 + core, chip)
        self.far_plane = ((plane + 2) % 4 * 2 + core, chip)
        self.inside = (plane + 1) // 2 == 1
        self.outside = (plane + 1) // 2 != 1
        self.across = ((3 - plane) * 2 + core, chip)
        self.sems, self.local_sems = sems, local_sems
        self.count = self.local_count = 0
        self.unsent, self.unmoved = [], []

    def meet(self):
        barrier = pltpu.get_barrier_semaphore()
        partners = (
            self.core, self.first, self.second, self.corner, self.near_plane, self.far_plane, self.across,
        )
        for partner in partners:
            pl.semaphore_signal(barrier, inc=1, device_id=partner, device_id_type=pl.DeviceIdType.MESH)
        pl.semaphore_wait(barrier, len(partners))

    def describe(self, source, target, device):
        self.count += 1
        return pltpu.make_async_remote_copy(
            src_ref=source,
            dst_ref=target,
            send_sem=self.sems.at[0, self.count - 1],
            recv_sem=self.sems.at[1, self.count - 1],
            device_id=device,
            device_id_type=pl.DeviceIdType.MESH,
        )

    def describe_move(self, source, target):
        self.local_count += 1
        return pltpu.make_async_copy(source, target, self.local_sems.at[self.local_count - 1])

    def send(self, source, target, device):
        copy = self.describe(source, target, device)
        copy.start()
        self.unsent.append(copy)
        return copy

    def move(self, source, target):
        copy = self.describe_move(source, target)
        copy.start()
        self.unmoved.append(copy)
        return copy

    def moved(self, copy):
        copy.wait()
        self.unmoved = [other for other in self.unmoved if other is not copy]

    def sent(self, copy):
        copy.wait_send()
        self.unsent = [other for other in self.unsent if other is not copy]

    def finish(self):
        for copy in self.unmoved:
            copy.wait()
        for copy in self.unsent:
            copy.wait_send()
        self.unsent, self.unmoved = [], []


def row_in(net, given, rows, row):
    core, chip = net.core_index, net.chip
    mine = pl.ds(2 * core, 2)
    swap = net.send(given.at[:, 1 - core], rows.at[mine], net.core)
    keep = net.move(given.at[:, core], rows.at[mine])
    yield
    net.moved(keep)
    swap.wait_recv()
    own = net.move(rows.at[chip], row.at[chip, core])
    sends = [
        net.send(rows.at[other], row.at[chip, core], (lax.axis_index("dp"), other)) for other in net.chips
    ]
    yield
    net.moved(own)
    shares = [net.send(row.at[chip, core], row.at[chip, core], net.core)]
    for other, copy in zip(net.chips, sends):
        copy.wait_recv()
        shares.append(net.send(row.at[other, core], row.at[other, core], net.core))
    yield
    for copy in shares:
        copy.wait_recv()
        net.sent(copy)


def row_out(net, pieces, rows, result):
    core, chip = net.core_index, net.chip
    own = net.move(pieces.at[chip], rows.at[chip])
    sends = [net.send(pieces.at[other], rows.at[chip], (lax.axis_index("dp"), other)) for other in net.chips]
    yield
    net.moved(own)
    for copy in sends:
        copy.wait_recv()
    keep = net.move(rows.at[pl.ds(2 * core, 2)], result.at[:, core])
    swap = net.send(rows.at[pl.ds(2 * (1 - core), 2)], result.at[:, core], net.core)
    yield
    swap.wait_recv()
    net.moved(keep)


class Gather:
    def __init__(self, net, own, slot, flip=False):
        self.net, self.slot = net, slot
        self.one, self.two = (2, 1) if flip else (1, 2)
        to_one, self.to_two = (net.second, net.first) if flip else (net.first, net.second)
        self.near = net.send(own, slot(self.one), to_one)
        self.own = net.move(own, slot(0))

    def relay(self):
        self.near.wait_recv()
        self.corner = self.net.send(self.slot(self.one), self.slot(3), self.to_two)
        self.other = self.net.send(self.slot(self.one), self.slot(self.two), self.net.near_plane)

    def finish(self):
        self.net.moved(self.own)
        self.corner.wait_recv()
        self.other.wait_recv()


ANY = pl.BlockSpec(memory_space=pl.ANY)
VM = pl.BlockSpec(memory_space=pltpu.VMEM)
SENDS = 224


def half_columns(net, weight, width):
    return weight.at[:, pl.ds(pl.multiple_of(net.core_index * width, width), width)]


def half_rows(net, weight, height):
    return weight.at[pl.ds(pl.multiple_of(net.core_index * height, height), height)]


def tile_rows(i, size=256):
    return pl.ds(pl.multiple_of(i * size, size), size)


def call_remote(kernel, ident, ins, in_specs, outs, out_specs, scratch, vmem=48, name=None):
    return pl.pallas_call(
        kernel,
        in_specs=in_specs,
        out_specs=out_specs,
        out_shape=outs,
        scratch_shapes=list(scratch) + [pltpu.SemaphoreType.DMA((2, SENDS)), pltpu.SemaphoreType.DMA((SENDS,))],
        compiler_params=pltpu.CompilerParams(
            collective_id=ident, has_side_effects=True, vmem_limit_bytes=vmem << 20
        ),
        name=name,
    )(*ins)


def add_up(target, sources):
    step = min(65536 // target.shape[1], target.shape[0])

    def some(i, _):
        cut = pl.ds(pl.multiple_of(i * step, step), step)
        total = sources[0][cut].astype(F32)
        for source in sources[1:]:
            total = total + source[cut].astype(F32)
        target[cut] = total.astype(BF)
        return 0

    lax.fori_loop(0, target.shape[0] // step, some, 0)


class Line:
    def __init__(self, net, total, landing, result):
        self.net, self.total = net, total
        self.one_in, self.two_in = landing
        place = result(net.core_index)
        self.inward = net.describe(total, self.one_in, net.near_plane)
        self.across = net.describe(total, self.two_in, net.across)
        self.outward = net.describe(self.two_in, place, net.near_plane)
        self.keep = net.describe_move(self.two_in, place)
        self.inside_core = net.describe(self.two_in, place, net.core)
        self.outside_core = net.describe(place, place, net.core)

    def line0(self):
        pl.when(self.net.outside)(self.inward.start)

    def line1(self):
        @pl.when(self.net.inside)
        def _():
            self.inward.wait_recv()
            add_up(self.total, [self.total, self.one_in])
            self.across.start()

    def line2(self):
        @pl.when(self.net.inside)
        def _():
            self.across.wait_recv()
            add_up(self.two_in, [self.total, self.two_in])
            self.outward.start()
            self.inside_core.start()
            self.keep.start()

    def line3(self):
        @pl.when(self.net.outside)
        def _():
            self.outward.wait_recv()
            self.outside_core.start()

    def end(self):
        @pl.when(self.net.inside)
        def _():
            self.inside_core.wait_recv()
            for copy in (self.across, self.outward, self.inside_core):
                copy.wait_send()
            self.keep.wait()

        @pl.when(self.net.outside)
        def _():
            self.outside_core.wait_recv()
            for copy in (self.inward, self.outside_core):
                copy.wait_send()


class Scatter:
    def __init__(self, net, part, first, landing, source=None):
        self.net, self.part, self.source = net, part, source or part
        self.near_in, self.pass_in, self.far_in = landing
        self.one, self.two = (1, 2) if first == 1 else (2, 1)
        self.to_one, self.to_two = (net.first, net.second) if first == 1 else (net.second, net.first)

    def start(self):
        self.passed = self.net.send(self.source(3), self.pass_in, self.to_one)
        self.near = self.net.send(self.source(self.one), self.near_in, self.to_one)

    def middle(self):
        self.passed.wait_recv()
        add_up(self.part(self.two), [self.part(self.two), self.pass_in])
        self.far = self.net.send(self.part(self.two), self.far_in, self.to_two)

    def own(self):
        self.near.wait_recv()
        self.far.wait_recv()
        add_up(self.part(0), [self.part(0), self.near_in, self.far_in])


def landing(rows, columns):
    return [pltpu.VMEM((rows, columns), BF)] * 3


def line_landing(rows, columns):
    return [pltpu.VMEM((rows, columns), BF)] * 2


def weight_grad(lhs, rhs, target, start, count, columns=slice(None), size=256):
    def some(i, _):
        cut = pl.ds(pl.multiple_of(start + i * size, size), size)
        target[cut, columns] = dot(lhs(cut), rhs(), TN).astype(BF)
        return 0

    lax.fori_loop(0, count // size, some, 0)


def norm_back_tile(grad_in, values, gain):
    unit, inverse = norm_stats(values)
    scaled = grad_in * gain
    first_mean = jnp.mean(scaled, axis=-1, keepdims=True)
    second_mean = jnp.mean(scaled * unit, axis=-1, keepdims=True)
    grad_values = inverse * (scaled - first_mean - unit * second_mean)
    return grad_values, jnp.sum(grad_in * unit, axis=0, keepdims=True), jnp.sum(grad_in, axis=0, keepdims=True)


def head_scatters(net, g_heads, g_out, lands):
    columns = lambda kind, s: slice(kind * 512 + s * 128, kind * 512 + s * 128 + 128)
    found = {
        "q": Scatter(net, lambda s: g_heads.at[:, columns(0, s)], 1, lands[:3]),
        "v": Scatter(net, lambda s: g_heads.at[:, columns(2, s)], 2, lands[3:6]),
    }
    for half in range(2):
        found["k%d" % half] = Scatter(
            net, lambda s, half=half: g_heads.at[pl.ds(half * 512, 512), columns(1, s)], 1 + half,
            lands[6 + half * 3:9 + half * 3],
        )
        found["o%d" % half] = Scatter(
            net, lambda s, half=half: g_out.at[pl.ds(s * 128 + half * 64, 64)], 1 + half,
            lands[12 + half * 3:15 + half * 3],
        )
    return found


def head_lines(net, g_heads, g_out, full_heads, full_out, lands):
    found = {}
    for kind, name in enumerate("qkv"):
        for half in range(2):
            at = (kind * 2 + half) * 2
            found[name + str(half)] = Line(
                net, g_heads.at[pl.ds(half * 512, 512), kind * 512:kind * 512 + 128], lands[at:at + 2],
                lambda c, kind=kind, half=half: full_heads.at[
                    kind, pl.ds(half * 512, 512), pl.ds(pl.multiple_of(c * 128, 128), 128)
                ],
            )
    for half in range(2):
        found["o%d" % half] = Line(
            net, g_out.at[pl.ds(half * 64, 64)], lands[12 + half * 2:14 + half * 2],
            lambda c, half=half: full_out.at[pl.ds(pl.multiple_of(c * 128 + half * 64, 64), 64)],
        )
    return found


def head_landing(width):
    return landing(1024, 128) * 2 + (landing(512, 128)) * 2 + landing(64, width) * 2


def head_line_landing(width):
    return line_landing(512, 128) * 6 + line_landing(64, width) * 2


def attend_block(i, q_ref, q_at, k_ref, k_at, v_at, low, high, causal, out_ref, sums_ref, acc, top, total):
    pairs = range(4)
    rows = tile_rows(i, QUERIES)
    queries = [
        both_heads(q_ref[rows, q_at + p * 128:q_at + p * 128 + 128] * jnp.bfloat16(HD ** -0.5)) for p in pairs
    ]
    least, limit = low[pl.ds(i, 1)], high[pl.ds(i, 1)]
    acc[...] = jnp.zeros_like(acc)
    total[...] = jnp.zeros_like(total)
    top[...] = jnp.full_like(top, -1e30)

    def step(j, _):
        at = pl.multiple_of(j * KEYS, KEYS)
        seen = allowed_keys(least, limit, at)
        attend_step(queries, k_ref, k_at, v_at, pl.ds(at, KEYS), seen, acc, top, total)
        return 0

    lax.fori_loop(0, i // 2 + 1 if causal else k_ref.shape[0] // KEYS, step, 0)
    for p in pairs:
        sums = total[p:p + 1]
        mixed = acc[p] / sums
        joined = jnp.concatenate([mixed[:HD, :QUERIES], mixed[HD:, QUERIES:]], axis=0)
        out_ref[rows, p * 128:(p + 1) * 128] = joined.T.astype(BF)
        sums_ref[i, p:p + 1] = top[p:p + 1] + jnp.log(sums)


def attend_back_block(
    i, q_ref, q_at, k_ref, k_at, v_at, grad_ref, out_ref, out_at, sums_ref, low, high, causal, dq_ref, dq_at, acc, acc_k, acc_v
):
    pairs = range(4)
    rows = tile_rows(i, QUERIES)
    least, limit = low[pl.ds(i, 1)], high[pl.ds(i, 1)]
    queries, grads, fixes, sums = [], [], [], []
    ones = jnp.ones((8, 128), BF)
    for p in pairs:
        queries.append(both_heads(q_ref[rows, q_at + p * 128:q_at + p * 128 + 128] * jnp.bfloat16(HD ** -0.5)))
        grad = both_heads(grad_ref[rows, p * 128:(p + 1) * 128])
        grads.append(grad)
        out = out_ref[rows, out_at + p * 128:out_at + p * 128 + 128].astype(F32)
        product = grad.astype(F32) * jnp.concatenate([out, out], axis=0)
        coarse = product.astype(BF)
        fine = (product - coarse.astype(F32)).astype(BF)
        fixes.append((dot(ones, coarse, NT) + dot(ones, fine, NT))[:1])
        sums.append(sums_ref[i, p:p + 1])
    acc[...] = jnp.zeros_like(acc)

    def step(j, _):
        at = pl.multiple_of(j * KEYS, KEYS)
        seen = allowed_keys(least, limit, at)
        attend_back_step(queries, grads, fixes, sums, k_ref, k_at, v_at, pl.ds(at, KEYS), seen, acc, acc_k, acc_v)
        return 0

    lax.fori_loop(0, i // 2 + 1 if causal else k_ref.shape[0] // KEYS, step, 0)
    for p in pairs:
        mixed = acc[p] * (HD ** -0.5)
        joined = jnp.concatenate([mixed[:HD, :QUERIES], mixed[HD:, QUERIES:]], axis=0)
        dq_ref[rows, dq_at + p * 128:dq_at + p * 128 + 128] = joined.T.astype(BF)


def reach(query_ids, key_ids):
    low = jnp.zeros(query_ids.shape, F32)
    high = jnp.zeros(query_ids.shape, F32)
    for segment in range(16):
        here = query_ids == segment
        before = jnp.sum((key_ids < segment).astype(F32), axis=(0, 1), keepdims=True)
        upto = jnp.sum((key_ids <= segment).astype(F32), axis=(0, 1), keepdims=True)
        low = low + jnp.where(here, before, 0.0)
        high = high + jnp.where(here, upto, 0.0)
    return low.astype(jnp.int32), high.astype(jnp.int32)


def project_out(net, att, weight, part, part_in):
    swaps = []
    for i in range(4):
        part[i] = dot(att[i * 256:i * 256 + 256], weight[...], NN).astype(BF).reshape(2, 128, -1)
        swaps.append(net.send(part.at[i], part_in.at[i], net.core))
    return swaps


def ahead_kernel(
    x_in, mem_in, top_in, target_ids_in, source_ids_in, bias_q, bias_v, bias_cq, bias_cv, bias_i, wq, wk, wv, wo, wcq, wck, wcv, wco, inner, outer,
    gain1, shift1, bias_o, gain2, shift2, bias_c, gain3, shift3,
    x_out, mem_out, top_out, n1_out, qkv_out, att1_out, sums1_out, h1_out, n2_out, q2_out, kv2_out, att2_out, sums2_out,
    h2_out, n3_out, act_out, slope_out, g_outer_out, wqkv_out, wo_out, wc_out, wco_out, wi_out, wu_out, reach_out,
    rows_x, rows_mem, rows_top, row, mem, weights, weights2, wo_vm, wco_vm, wi, normed, qkv, att, part, part_in, part_in2,
    hidden, queries, keys, act, slope, g_outer, bias, biases, ids, all_ids, spans, sums1, sums2, acc, top, total, sems, local_sems,
):
    net = Net(sems, local_sems)
    core, chip = net.core_index, net.chip
    net.meet()
    enter_x = row_in(net, x_in, rows_x, row)
    next(enter_x)
    mine = pl.ds(2 * core, 2)
    for i in range(2):
        for r in range(8):
            cut = slice(r * 128, r * 128 + 128)
            ids[i, r:r + 1] = target_ids_in[i:i + 1, cut]
            ids[i, 8 + r:9 + r] = source_ids_in[i:i + 1, cut]
    at = 0
    for value in (bias_q, bias_v, bias_cq, bias_cv, bias_i):
        for r in range(value.shape[1] // 128):
            bias[at:at + 1] = value[:, r * 128:r * 128 + 128]
            at += 1
    ids_copies = [net.move(ids, all_ids.at[mine]), net.send(ids, all_ids.at[mine], net.core)]
    bias_own = net.move(bias, biases.at[0])
    bias_copies = [
        net.send(bias, biases.at[1], net.first),
        net.send(bias, biases.at[2], net.second),
        net.send(bias, biases.at[3], net.corner),
    ]

    def gather_columns(weight, target, kind, flip):
        slot = lambda s: target.at[:, kind * 512 + s * 128:kind * 512 + s * 128 + 128]
        return Gather(net, half_columns(net, weight, 128), slot, flip)

    def gather_rows_of(weight, target, flip):
        return Gather(net, half_rows(net, weight, 128), lambda s: target.at[pl.ds(s * 128, 128)], flip)

    def gather_inner(k):
        own = inner.at[pl.ds(k * 256, 256), pl.ds(pl.multiple_of(core * 512, 512), 512)]
        return Gather(net, own, lambda s: wi.at[pl.ds(k * 256, 256), s * 512:s * 512 + 512], k % 2 == 1)

    def gather_outer(k):
        own = outer.at[pl.ds(pl.multiple_of(core * 512 + k * 128, 128), 128)]
        return Gather(net, own, lambda s: wu_out.at[pl.ds(s * 512 + k * 128, 128)], k % 2 == 1)

    gather_q = gather_columns(wq, weights, 0, False)
    gather_k = gather_columns(wk, weights, 1, True)
    next(enter_x)
    gather_v = gather_columns(wv, weights, 2, False)
    gather_o = gather_rows_of(wo, wo_vm, True)
    enter_mem = row_in(net, mem_in, rows_mem, mem)
    next(enter_mem)
    enter_top = row_in(net, top_in, rows_top, top_out)
    next(enter_top)
    gather_q.relay()
    gather_k.relay()
    next(enter_x)
    for _ in enter_x:
        pass
    x_move = net.move(row, x_out)

    def norm_first(i, _):
        normed[tile_rows(i)] = norm_forward(row[i].reshape(256, -1).astype(F32), gain1[...], shift1[...])
        return 0

    lax.fori_loop(0, 4, norm_first, 0)
    n1_move = net.move(normed, n1_out)
    gather_v.relay()
    gather_o.relay()
    next(enter_mem)
    gather_ck = gather_columns(wck, weights2, 1, False)
    gather_cv = gather_columns(wcv, weights2, 2, True)
    net.moved(bias_own)
    for copy in bias_copies:
        copy.wait_recv()

    def project_first(kind):
        cut = slice(kind * 512, kind * 512 + 512)
        bias = None
        if kind != 1:
            bias = jnp.concatenate([biases[s, pl.ds(kind + core, 1)] for s in range(4)], axis=1)

        def some(i, _):
            value = dot(normed[tile_rows(i)], weights[:, cut], NN)
            if kind != 1:
                value = value + bias
            qkv[tile_rows(i), cut] = value.astype(BF)
            return 0

        lax.fori_loop(0, 4, some, 0)

    for kind, gather in enumerate((gather_q, gather_k, gather_v)):
        gather.finish()
        project_first(kind)
    net.move(weights, wqkv_out)
    gather_cq = gather_columns(wcq, weights2, 0, False)
    gather_co = gather_rows_of(wco, wco_vm, True)
    net.move(qkv, qkv_out)
    net.moved(ids_copies[0])
    ids_copies[1].wait_recv()
    target_ids, source_ids = all_ids[chip, :8], all_ids[chip, 8:]
    low, _ = reach(target_ids, target_ids)
    spans[0] = low
    place = lax.broadcasted_iota(jnp.int32, (8, 128), 0) * 128 + lax.broadcasted_iota(jnp.int32, (8, 128), 1)
    spans[1] = place + 1
    low, high = reach(target_ids, source_ids)
    spans[2] = low
    spans[3] = high
    net.move(spans, reach_out)

    def attend_first(i, _):
        attend_block(i, qkv, 0, qkv, 512, 1024, spans.at[0], spans.at[1], True, att, sums1, acc, top, total)
        return 0

    lax.fori_loop(0, 8, attend_first, 0)
    next(enter_mem)
    gather_ck.relay()
    gather_cv.relay()
    gather_cq.relay()
    gather_co.relay()
    att1_move = net.move(att, att1_out)
    net.move(sums1, sums1_out)
    gather_o.finish()
    net.move(wo_vm, wo_out)
    swaps = project_out(net, att, wo_vm, part, part_in)
    inners = [gather_inner(k) for k in range(4)]
    next(enter_top)
    for _ in enter_mem:
        pass
    net.move(mem, mem_out)
    for gather in (gather_ck, gather_cv):
        gather.finish()
    values_bias = jnp.concatenate([biases[s, pl.ds(6 + core, 1)] for s in range(4)], axis=1)
    query_bias = jnp.concatenate([biases[s, pl.ds(4 + core, 1)] for s in range(4)], axis=1)

    def project_memory(i, _):
        tokens = mem[i].reshape(256, -1)
        keys[tile_rows(i), :512] = dot(tokens, weights2[:, 512:1024], NN).astype(BF)
        keys[tile_rows(i), 512:] = (dot(tokens, weights2[:, 1024:], NN) + values_bias).astype(BF)
        return 0

    lax.fori_loop(0, 4, project_memory, 0)
    net.move(keys, kv2_out)
    net.moved(n1_move)
    for i in range(4):
        swaps[i].wait_recv()

    def middle_rows(i, _):
        value = row[i].astype(F32) + part[i].astype(F32) + part_in[i].astype(F32)
        value = value.reshape(256, -1) + bias_o[...]
        hidden[tile_rows(i)] = value
        normed[tile_rows(i)] = norm_forward(value, gain2[...], shift2[...])
        return 0

    lax.fori_loop(0, 4, middle_rows, 0)
    net.moved(x_move)
    h1_move = net.move(hidden, h1_out)
    n2_move = net.move(normed, n2_out)
    gather_cq.finish()
    net.move(weights2, wc_out)

    def project_query(i, _):
        queries[tile_rows(i)] = (dot(normed[tile_rows(i)], weights2[:, :512], NN) + query_bias).astype(BF)
        return 0

    lax.fori_loop(0, 4, project_query, 0)
    net.move(queries, q2_out)
    net.moved(att1_move)

    def attend_second(i, _):
        attend_block(i, queries, 0, keys, 0, 512, spans.at[2], spans.at[3], False, att, sums2, acc, top, total)
        return 0

    lax.fori_loop(0, 3, attend_second, 0)
    for gather in inners:
        gather.relay()
    outers = [gather_outer(k) for k in range(4)]
    lax.fori_loop(3, 8, attend_second, 0)
    net.move(att, att2_out)
    net.move(sums2, sums2_out)
    gather_co.finish()
    net.move(wco_vm, wco_out)
    for copy in swaps:
        net.sent(copy)
    swaps = project_out(net, att, wco_vm, part, part_in2)
    next(enter_top)
    net.moved(h1_move)
    net.moved(n2_move)
    for i in range(4):
        swaps[i].wait_recv()

    def last_rows(i, _):
        value = part[i].astype(F32) + part_in2[i].astype(F32)
        value = hidden[tile_rows(i)] + value.reshape(256, -1) + bias_c[...]
        hidden[tile_rows(i)] = value
        normed[tile_rows(i)] = norm_forward(value, gain3[...], shift3[...])
        return 0

    lax.fori_loop(0, 4, last_rows, 0)
    net.move(hidden, h2_out)
    net.move(normed, n3_out)
    for gather in inners:
        gather.finish()
    net.move(wi, wi_out)

    def feed(i, _):
        tokens = normed[tile_rows(i)]
        for s in range(4):
            cut = slice(s * 512, s * 512 + 512)
            unit_bias = jnp.concatenate([biases[s, pl.ds(8 + core * 4 + k, 1)] for k in range(4)], axis=1)
            pre = dot(tokens, wi[:, cut], NN) + unit_bias
            sigmoid = jax.nn.sigmoid(pre)
            act[tile_rows(i), cut] = (pre * sigmoid).astype(BF)
            slope[tile_rows(i), cut] = (sigmoid * (1.0 + pre * (1.0 - sigmoid))).astype(BF)
        return 0

    lax.fori_loop(0, 1, feed, 0)
    outers[0].relay()
    outers[1].relay()
    lax.fori_loop(1, 2, feed, 0)
    outers[2].relay()
    outers[3].relay()
    for _ in enter_top:
        pass
    top_load = net.move(top_out, row)
    lax.fori_loop(2, 4, feed, 0)
    net.move(act, act_out)
    net.move(slope, slope_out)
    net.moved(top_load)
    weight_grad(lambda cut: act[:, cut], lambda: row[...].reshape(1024, -1), g_outer, 0, 2048, size=512)
    net.move(g_outer, g_outer_out)
    for gather in outers:
        gather.finish()
    net.finish()


def ahead(x, mem, top, ids, biases, weights, vectors):
    length, width = 1024, x.shape[-1]
    shape = jax.ShapeDtypeStruct
    quarters = (4, 2, 128, width)
    rows = lambda columns, kind=BF: shape((length, columns), kind)
    sums = shape((8, 4, 256), F32)
    return call_remote(
        ahead_kernel, 1,
        [a.reshape(2, 2, -1, width) for a in (x, mem, top)] + list(ids) + [v[None] for v in biases] + list(weights)
        + [v[None] for v in vectors],
        [ANY] * 3 + [VM] * 7 + [ANY] * 10 + [VM] * 8,
        [
            shape(quarters, BF), shape(quarters, BF), shape(quarters, BF), rows(width), rows(1536), rows(512), sums,
            rows(width, F32), rows(width), rows(512), rows(1024), rows(512), sums,
            rows(width, F32), rows(width), rows(2048), rows(2048), shape((2048, width), BF),
            shape((width, 1536), BF), shape((512, width), BF), shape((width, 1536), BF), shape((512, width), BF),
            shape((width, 2048), BF), shape((2048, width), BF), shape((4, 8, 128), jnp.int32),
        ],
        [ANY] * 25,
        [pltpu.VMEM((4, 128, width), BF)] * 3 + [pltpu.VMEM(quarters, BF)] * 2 + [pltpu.VMEM((width, 1536), BF)] * 2
        + [pltpu.VMEM((512, width), BF)] * 2
        + [
            pltpu.VMEM((width, 2048), BF), pltpu.VMEM((length, width), BF), pltpu.VMEM((length, 1536), BF),
            pltpu.VMEM((length, 512), BF), pltpu.VMEM(quarters, BF), pltpu.VMEM(quarters, BF), pltpu.VMEM(quarters, BF),
            pltpu.VMEM((length, width), F32), pltpu.VMEM((length, 512), BF), pltpu.VMEM((length, 1024), BF),
            pltpu.VMEM((length, 2048), BF), pltpu.VMEM((length, 2048), BF), pltpu.VMEM((2048, width), BF),
            pltpu.VMEM((16, 128), F32),
            pltpu.VMEM((4, 16, 128), F32), pltpu.VMEM((2, 16, 128), jnp.int32),
            pltpu.VMEM((4, 16, 128), jnp.int32), pltpu.VMEM((4, 8, 128), jnp.int32),
            pltpu.VMEM((8, 4, 256), F32), pltpu.VMEM((8, 4, 256), F32),
            pltpu.VMEM((4, 128, 256), F32), pltpu.VMEM((4, 256), F32), pltpu.VMEM((4, 256), F32),
        ],
        vmem=62, name="ahead",
    )


def turn_kernel(
    g_outer_in, act_in, slope_in, n3_in, h2_in, top_in, wi_in, wu_in, wco_in, q_in, kv_in, att_in, sums_in, reach_in, gain, bias_u,
    block_out, gh_out, outer_out, inner_out, heads_out, vectors_out, split_out,
    act, slope, wu, wi, g_outer, g_inner, hidden, row, normed, wco, part, back_in, out_part, out_in, gatt,
    pieces, result, rows_back, acc_k, acc_v, acc, spans, sums, vectors, split, *rest,
):
    lands, (sems, local_sems) = rest[:-2], rest[-2:]
    net = Net(sems, local_sems)
    core = net.core_index
    loads = [
        net.move(source, target)
        for source, target in (
            (top_in, row), (wu_in, wu), (slope_in, slope), (wi_in, wi), (n3_in, normed), (act_in, act), (g_outer_in, g_outer),
            (h2_in, hidden), (wco_in, wco), (reach_in, spans), (sums_in, sums),
        )
    ]
    net.meet()
    outers = [
        Scatter(
            net, lambda s, k=k: g_outer.at[pl.ds(s * 512 + k * 256, 256)], 1 + k, lands[k * 3:k * 3 + 3],
            lambda s, k=k: g_outer_in.at[pl.ds(s * 512 + k * 256, 256)],
        )
        for k in range(2)
    ]
    outer_lines = [
        Line(
            net, g_outer.at[pl.ds(k * 128, 128)], lands[12 + k * 2:14 + k * 2],
            lambda c, k=k: outer_out.at[pl.ds(pl.multiple_of(c * 512 + k * 128, 128), 128)],
        )
        for k in range(4)
    ]
    inners = [
        Scatter(
            net, lambda s, k=k: g_inner.at[pl.ds(k * 512, 512), s * 512:s * 512 + 512], 1 + k,
            lands[6 + k * 3:9 + k * 3],
        )
        for k in range(2)
    ]

    def inner_grad(k, s):
        cut = slice(s * 512, s * 512 + 512)
        weight_grad(lambda rows: normed[:, rows], lambda: slope[:, cut], g_inner, k * 512, 512, cut)

    for k in range(2):
        outers[k].start()
    for copy in loads[:3]:
        net.moved(copy)
    split[...] = jnp.zeros_like(split)
    vectors[...] = jnp.zeros_like(vectors)

    def feed_back(i, _):
        tokens = row[i].reshape(256, -1)
        for s in range(4):
            cut = slice(s * 512, s * 512 + 512)
            value = (dot(tokens, wu[cut], NT) * slope[tile_rows(i), cut].astype(F32)).astype(BF)
            slope[tile_rows(i), cut] = value
            split[0:1, cut] += jnp.sum(value.astype(F32), axis=0, keepdims=True)
        return 0

    lax.fori_loop(0, 4, feed_back, 0)
    for copy in loads[3:]:
        net.moved(copy)
    swaps = []
    for i in range(4):
        value = dot(slope[i * 256:i * 256 + 256], wi[...], NT)
        part[i] = value.astype(BF).reshape(2, 128, -1)
        swaps.append(net.send(part.at[i], back_in.at[i], net.core))
    outers[0].middle()
    outers[1].middle()
    for k in range(2):
        inner_grad(k, 3)
        inner_grad(k, 1 + k)
        inners[k].start()

    def feed_out(i, _):
        out_part[i] = dot(act[tile_rows(i)], wu[...], NN).astype(BF).reshape(2, 128, -1)
        return 0

    lax.fori_loop(0, 4, feed_out, 0)
    out_swap = net.send(out_part.at[:, 1 - core], out_in, net.core)
    loads = [
        net.move(kv_in, act.at[:, :1024]), net.move(q_in, act.at[:, 1024:1536]), net.move(att_in, act.at[:, 1536:]),
    ]
    for copy in swaps:
        copy.wait_recv()

    def back(i, _):
        grad = (part[i].astype(F32) + back_in[i].astype(F32)).reshape(256, -1)
        before = hidden[i]
        change, by_gain, by_shift = norm_back_tile(grad, before.reshape(256, -1), gain[...])
        top = row[i].reshape(256, -1).astype(F32)
        value = top + change
        pieces[i] = hidden[i, core]
        hidden[i] = value.reshape(2, 128, -1)
        gatt[tile_rows(i)] = dot(value.astype(BF), wco[...], NT).astype(BF)
        vectors[4:5] += by_gain
        vectors[5:6] += by_shift
        vectors[6:7] += jnp.sum(top, axis=0, keepdims=True)
        vectors[3:4] += jnp.sum(value, axis=0, keepdims=True)
        return 0

    lax.fori_loop(0, 4, back, 0)
    net.move(hidden, gh_out)
    net.move(vectors, vectors_out)
    net.move(split, split_out)
    out_swap.wait_recv()
    for i in range(4):
        result[i] = (pieces[i] + out_part[i, core].astype(F32) + out_in[i].astype(F32) + bias_u[...]).astype(BF)
    leave = row_out(net, result, rows_back, block_out)
    next(leave)
    for k in range(2):
        inner_grad(k, 2 - k)
        inner_grad(k, 0)
    for k in range(2):
        outers[k].own()
        outer_lines[2 * k].line0()
        outer_lines[2 * k + 1].line0()
    for copy in loads:
        net.moved(copy)
    acc_k[...] = jnp.zeros_like(acc_k)
    acc_v[...] = jnp.zeros_like(acc_v)

    def attend_back(i, _):
        attend_back_block(
            i, act, 1024, act, 0, 512, gatt, act, 1536, sums, spans.at[2], spans.at[3], False, slope, 0, acc, acc_k, acc_v
        )
        return 0

    lax.fori_loop(0, 3, attend_back, 0)
    inners[0].middle()
    inners[1].middle()
    outer_lines[0].line1()
    outer_lines[1].line1()
    lax.fori_loop(3, 5, attend_back, 0)
    outer_lines[2].line1()
    outer_lines[3].line1()
    outer_lines[0].line2()
    lax.fori_loop(5, 7, attend_back, 0)
    outer_lines[1].line2()
    outer_lines[2].line2()
    lax.fori_loop(7, 8, attend_back, 0)
    outer_lines[3].line2()
    slope[:, 512:1024] = acc_k[...].astype(BF)
    slope[:, 1024:1536] = acc_v[...].astype(BF)
    net.move(slope.at[:, :1536], heads_out)
    inners[0].own()
    net.move(g_inner.at[pl.ds(0, 512), :512], inner_out.at[pl.ds(0, 512)])
    inners[1].own()
    net.move(g_inner.at[pl.ds(512, 512), :512], inner_out.at[pl.ds(512, 512)])
    next(leave)
    for line in outer_lines:
        line.line3()
    for line in outer_lines:
        line.end()
    for _ in leave:
        pass
    net.finish()


def turn(g_outer, act, slope, n3, h2, top, wi, wu, wco, q, kv, att, sums, reach_rows, gain, bias_u):
    length, width = act.shape[0], n3.shape[-1]
    shape = jax.ShapeDtypeStruct
    quarters = (4, 2, 128, width)
    return call_remote(
        turn_kernel, 2,
        (
            g_outer, act, slope, n3, h2.reshape(quarters), top, wi, wu, wco, q, kv, att, sums, reach_rows, gain[None], bias_u[None],
        ),
        [ANY] * 14 + [VM] * 2,
        [
            shape((2, 2, 128, width), BF), shape(quarters, F32), shape((1024, width), BF), shape((width, 512), BF),
            shape((length, 1536), BF), shape((8, width), F32), shape((8, 2048), F32),
        ],
        [ANY] * 7,
        [
            pltpu.VMEM((length, 2048), BF), pltpu.VMEM((length, 2048), BF), pltpu.VMEM((2048, width), BF),
            pltpu.VMEM((width, 2048), BF), pltpu.VMEM((2048, width), BF), pltpu.VMEM((width, 2048), BF),
            pltpu.VMEM(quarters, F32), pltpu.VMEM(quarters, BF), pltpu.VMEM((length, width), BF),
            pltpu.VMEM((512, width), BF), pltpu.VMEM(quarters, BF), pltpu.VMEM(quarters, BF), pltpu.VMEM(quarters, BF),
            pltpu.VMEM((4, 128, width), BF), pltpu.VMEM((length, 512), BF),
            pltpu.VMEM((4, 128, width), F32), pltpu.VMEM((4, 128, width), BF), pltpu.VMEM((4, 128, width), BF),
            pltpu.VMEM((length, 512), F32), pltpu.VMEM((length, 512), F32), pltpu.VMEM((4, 128, 256), F32),
            pltpu.VMEM((4, 8, 128), jnp.int32), pltpu.VMEM((8, 4, 256), F32),
            pltpu.VMEM((8, width), F32), pltpu.VMEM((8, 2048), F32),
        ]
        + landing(256, width) * 2 + landing(512, 512) * 2 + line_landing(128, width) * 4,
        vmem=62, name="turn",
    )


def last_kernel(
    heads_in, n2_in, mem_in, att2_in, gh_in, h1_in, wc_in, wo_in, inner_in, qkv_in, att1_in, sums_in, reach_in, n1_in, x_in,
    wqkv_in, shared_in, split_in, gain2, gain1,
    mem_out, grad_out, cross_out, cross_o_out, heads_out, o_out, inner_out, shared_out, late_out, split_out,
    dqkv, normed, tokens, att, grads, hidden, weights, wo, part, part_in, mem_part, mem_back, grad_in,
    rows_mem, rows_back, g_cross, g_cross_o, g_heads, g_o, gatt, acc, spans, sums,
    inner_total,
    shared, shared_land, late, late_land, split_load, split, split_sum, split_plane, split_land, split_full, *rest,
):
    lands, (sems, local_sems) = rest[:-2], rest[-2:]
    net = Net(sems, local_sems)
    core, chip = net.core_index, net.chip
    place = lax.axis_index("dp")
    loads = [
        net.move(source, target)
        for source, target in (
            (heads_in, dqkv), (wc_in, weights), (inner_in, inner_total), (mem_in, tokens), (n2_in, normed), (att2_in, att),
            (gh_in, grads), (h1_in, hidden), (wo_in, wo), (reach_in, spans), (sums_in, sums), (shared_in, shared.at[0]),
            (split_in, split_load),
        )
    ]
    net.meet()
    inner_lines = [
        Line(
            net, inner_total.at[pl.ds(k * 512, 512)], lands[68 + k * 2:70 + k * 2],
            lambda c, k=k: inner_out.at[pl.ds(k * 512, 512), pl.ds(pl.multiple_of(c * 512, 512), 512)],
        )
        for k in range(2)
    ]
    scatters = head_scatters(net, g_cross, g_cross_o, lands[:18])
    lines = head_lines(net, g_cross, g_cross_o, cross_out, cross_o_out, lands[18:34])
    own_scatters = head_scatters(net, g_heads, g_o, lands[34:52])
    own_lines = head_lines(net, g_heads, g_o, heads_out, o_out, lands[52:68])

    def each(group, names, *steps):
        for step in steps:
            for name in names.split():
                getattr(group[name], step)()

    for copy in loads[:4]:
        net.moved(copy)
    inner_lines[0].line0()
    inner_lines[1].line0()
    memory = lambda cut: tokens[:, :, :, cut].reshape(1024, -1)

    def cross_grad(kind, names):
        cut = slice(kind * 512, kind * 512 + 512)
        weight_grad(memory, lambda: dqkv[:, cut], g_cross, 0, 1024, cut)
        each(scatters, names, "start")

    cross_grad(1, "k0 k1")
    swaps = []
    for i in range(4):
        value = dot(dqkv[i * 256:i * 256 + 256, :512], weights[:, :512], NT)
        part[i] = value.astype(BF).reshape(2, 128, -1)
        swaps.append(net.send(part.at[i], part_in.at[i], net.core))
    for copy in loads[4:]:
        net.moved(copy)
    cross_grad(2, "v")
    weight_grad(lambda cut: normed[:, cut], lambda: dqkv[:, :512], g_cross, 0, 1024, slice(0, 512))
    each(scatters, "q", "start")
    load_n1 = net.move(n1_in, normed)
    load_qkv = net.move(qkv_in, g_heads)
    load_x = net.move(x_in, tokens)
    for copy in swaps:
        copy.wait_recv()

    def back(i, _):
        grad = (part[i].astype(F32) + part_in[i].astype(F32)).reshape(256, -1)
        change, by_gain, by_shift = norm_back_tile(grad, hidden[tile_rows(i)], gain2[...])
        value = grads[tile_rows(i)] + change
        mem_part[i] = value.astype(BF).reshape(2, 128, -1)
        gatt[tile_rows(i)] = dot(value.astype(BF), wo[...], NT).astype(BF)
        shared[0, 1:2] += by_gain
        shared[0, 2:3] += by_shift
        shared[0, 0:1] += jnp.sum(value, axis=0, keepdims=True)
        hidden[tile_rows(i)] = value
        return 0

    lax.fori_loop(0, 4, back, 0)
    each(scatters, "k0 k1", "middle")
    inner_lines[0].line1()
    weight_grad(lambda cut: att[:, cut], lambda: grads[...].astype(BF), g_cross_o, 0, 512)
    each(scatters, "o0 o1", "start")
    load_att = net.move(att1_in, att)
    each(scatters, "v q", "middle")
    for s in range(4):
        for k in range(4):
            split[s, 4 + k:5 + k] = split_load[0:1, s * 512 + k * 128:s * 512 + k * 128 + 128]
    for at, kind in ((2, 0), (3, 2)):
        total = jnp.sum(dqkv[:, kind * 512:kind * 512 + 512].astype(F32), axis=0, keepdims=True)
        for s in range(4):
            split[s, at:at + 1] = total[:, s * 128:s * 128 + 128]
    stages = [(place, net.chips[0]), (place, net.chips[1]), net.near_plane, net.far_plane]
    shared_copy = net.send(shared.at[0], shared_land.at[0], stages[0])

    def shared_stage(at):
        nonlocal shared_copy
        shared_copy.wait_recv()
        shared[at + 1] = shared[at] + shared_land[at]
        if at < 3:
            shared_copy = net.send(shared.at[at + 1], shared_land.at[at + 1], stages[at + 1])

    grads[...] = jnp.zeros_like(grads)
    net.moved(load_att)
    weight_grad(lambda cut: att[:, cut], lambda: mem_part[...].reshape(1024, -1), g_o, 0, 512)
    each(own_scatters, "o0 o1", "start")
    net.moved(load_qkv)

    def attend_back(i, _):
        attend_back_block(
            i, g_heads, 0, g_heads, 512, 1024, gatt, att, 0, sums, spans.at[0], spans.at[1], True, dqkv, 0, acc,
            grads.at[:, :512], grads.at[:, 512:],
        )
        return 0

    lax.fori_loop(0, 4, attend_back, 0)
    each(scatters, "k0 k1", "own")
    each(lines, "k0 k1", "line0")
    inner_lines[1].line1()
    each(scatters, "o0 o1", "middle")
    lax.fori_loop(4, 6, attend_back, 0)
    each(scatters, "v q", "own")
    each(lines, "v0 v1 q0 q1", "line0")
    each(lines, "k0 k1", "line1")
    inner_lines[0].line2()
    shared_stage(0)
    lax.fori_loop(6, 8, attend_back, 0)
    for i in range(4):
        part_in[i] = grads[i * 256:i * 256 + 256].astype(BF).reshape(2, 128, -1)
    net.moved(load_n1)

    def head_grad(kind):
        cut = slice(kind * 512, kind * 512 + 512)
        side = slice(kind * 512 - 512, kind * 512)
        rhs = (lambda: part_in[:, :, :, side].reshape(1024, -1)) if kind else (lambda: dqkv[:, :512])
        weight_grad(lambda rows: normed[:, rows], rhs, g_heads, 0, 1024, cut)

    each(own_scatters, "o0 o1", "middle")
    head_grad(0)
    each(own_scatters, "q", "start")
    inner_lines[1].line2()
    each(lines, "v0 v1", "line1")
    each(scatters, "o0 o1", "own")
    each(lines, "o0 o1", "line0")
    each(lines, "q0 q1", "line1")
    head_grad(2)
    each(own_scatters, "v", "start")
    each(lines, "k0 k1", "line2")
    head_grad(1)
    each(own_scatters, "k0 k1", "start")
    inner_lines[0].line3()
    each(lines, "v0 v1", "line2")

    def memory_back(i, _):
        rows = tile_rows(i)
        value = dot(dqkv[rows, 512:1024], weights[:, 512:1024], NT) + dot(dqkv[rows, 1024:], weights[:, 1024:], NT)
        mem_part[i] = value.astype(BF).reshape(2, 128, -1)
        return 0

    lax.fori_loop(0, 4, memory_back, 0)
    mem_swap = net.send(mem_part.at[:, 1 - core], mem_back, net.core)
    load_w = net.move(wqkv_in, weights)
    each(own_scatters, "o0 o1", "own")
    each(own_lines, "o0 o1", "line0")
    each(lines, "o0 o1", "line1")
    each(lines, "q0 q1", "line2")
    each(own_scatters, "q v", "middle")
    net.moved(load_w)
    for copy in swaps:
        net.sent(copy)

    def first_back(i, _):
        rows = tile_rows(i)
        value = dot(dqkv[rows, :512], weights[:, :512], NT)
        value = value + dot(part_in[i].reshape(256, -1), weights[:, 512:], NT)
        part[i] = value.astype(BF).reshape(2, 128, -1)
        return 0

    lax.fori_loop(0, 4, first_back, 0)
    swap = net.send(part.at[:, 1 - core], grad_in, net.core)
    mem_swap.wait_recv()
    for i in range(4):
        mem_back[i] = (mem_part[i, core].astype(F32) + mem_back[i].astype(F32)).astype(BF)
    for at, value in ((0, dqkv[:, :512]), (1, part_in[:, :, :, 512:].reshape(1024, -1))):
        total = jnp.sum(value.astype(F32), axis=0, keepdims=True)
        for s in range(4):
            split[s, at:at + 1] = total[:, s * 128:s * 128 + 128]
    split_copies = [net.send(split, split_plane.at[0], net.near_plane)]
    net.moved(load_x)
    swap.wait_recv()
    each(own_scatters, "k0 k1", "middle")
    leave_mem = row_out(net, mem_back, rows_mem, mem_out)
    next(leave_mem)
    late[0] = jnp.zeros(late.shape[1:], F32)
    for i in range(4):
        grad = part[i, core].astype(F32) + grad_in[i].astype(F32)
        change, by_gain, by_shift = norm_back_tile(grad, tokens[i, core].astype(F32), gain1[...])
        grad_in[i] = (hidden[pl.ds(pl.multiple_of(i * 256 + core * 128, 128), 128)] + change).astype(BF)
        late[0, 0:1] += by_gain
        late[0, 1:2] += by_shift
    late_copy = net.send(late.at[0], late_land.at[0], net.core)
    leave = row_out(net, grad_in, rows_back, grad_out)

    def late_stage(at):
        nonlocal late_copy
        late_copy.wait_recv()
        late[at + 1] = late[at] + late_land[at]
        if at < 4:
            late_copy = net.send(late.at[at + 1], late_land.at[at + 1], (stages[2], stages[3], stages[0], stages[1])[at])

    def split_stage(at):
        nonlocal split_copies
        for copy in split_copies:
            copy.wait_recv()
        if at == 0:
            for s, other in ((0, 0), (1, 2), (2, 1), (3, 3)):
                split_sum[0, s] = split[s] + split_plane[0, other]
            split_copies = [net.send(split_sum.at[0], split_plane.at[1], net.far_plane)]
        elif at == 1:
            split_sum[1] = split_sum[0] + split_plane[1]
            split_copies = [
                net.send(split_sum.at[1, s], split_land.at[s - 1], device)
                for s, device in ((1, net.first), (2, net.second), (3, net.corner))
            ]
        else:
            split_full[core] = split_sum[1, 0] + split_land[0] + split_land[1] + split_land[2]
            split_copies = [net.send(split_full.at[core], split_full.at[core], net.core)]

    late_stage(0)
    each(own_scatters, "q v", "own")
    each(own_lines, "q0 v0 q1 v1", "line0")
    next(leave)
    each(own_scatters, "k0 k1", "own")
    each(own_lines, "k0 k1", "line0")
    shared_stage(1)
    split_stage(0)
    late_stage(1)
    each(own_lines, "q0 v0 o0 o1", "line1")
    each(lines, "o0 o1", "line2")
    each(own_lines, "q1", "line1")
    each(own_lines, "q0", "line2")
    each(own_lines, "v1", "line1")
    each(own_lines, "v0", "line2")
    each(own_lines, "k0 k1", "line1")
    inner_lines[1].line3()
    shared_stage(2)
    split_stage(1)
    late_stage(2)
    each(own_lines, "q1 v1 o0 o1", "line2")
    each(own_lines, "k0 k1", "line2")
    next(leave_mem)
    each(lines, "k0 k1", "line3")
    each(lines, "v0 v1 q0 q1", "line3")
    each(lines, "o0 o1", "line3")
    shared_stage(3)
    late_stage(3)
    split_stage(2)
    each(own_lines, "q0 v0 q1 v1", "line3")
    next(leave)
    late_stage(4)
    each(own_lines, "o0 o1 k0 k1", "line3")
    for line in inner_lines + list(lines.values()) + list(own_lines.values()):
        line.end()
    for _ in leave_mem:
        pass
    for _ in leave:
        pass
    split_copies[0].wait_recv()
    for source, target in ((shared.at[4], shared_out), (late.at[5], late_out), (split_full, split_out)):
        net.move(source, target)
    net.finish()


def last(heads, n2, mem, att2, gh, h1, wc, wo, inner_total, qkv, att1, sums, reach_rows, n1, x, wqkv, shared, split, gain2, gain1):
    length, width = heads.shape[0], n1.shape[-1]
    shape = jax.ShapeDtypeStruct
    quarters = (4, 2, 128, width)
    own = [shape((3, width, 256), BF), shape((256, width), BF)]
    return call_remote(
        last_kernel, 3,
        (
            heads, n2, mem, att2, gh.reshape(length, width), h1, wc, wo, inner_total, qkv, att1, sums, reach_rows, n1, x, wqkv, shared, split,
            gain2[None], gain1[None],
        ),
        [ANY] * 18 + [VM] * 2,
        [shape((2, 2, 128, width), BF)] * 2 + own + own
        + [shape((width, 1024), BF), shape((8, width), F32), shape((8, width), F32), shape((2, 8, 128), F32)],
        [ANY] * 10,
        [
            pltpu.VMEM((length, 1536), BF), pltpu.VMEM((length, width), BF), pltpu.VMEM(quarters, BF),
            pltpu.VMEM((length, 512), BF), pltpu.VMEM((length, width), F32), pltpu.VMEM((length, width), F32),
            pltpu.VMEM((width, 1536), BF), pltpu.VMEM((512, width), BF), pltpu.VMEM(quarters, BF),
            pltpu.VMEM(quarters, BF), pltpu.VMEM(quarters, BF), pltpu.VMEM((4, 128, width), BF),
            pltpu.VMEM((4, 128, width), BF),
        ]
        + [pltpu.VMEM((4, 128, width), BF)] * 2
        + [pltpu.VMEM((width, 1536), BF), pltpu.VMEM((512, width), BF)] * 2
        + [
            pltpu.VMEM((length, 512), BF), pltpu.VMEM((4, 128, 256), F32),
            pltpu.VMEM((4, 8, 128), jnp.int32),
            pltpu.VMEM((8, 4, 256), F32), pltpu.VMEM((width, 512), BF),
        ]
        + [
            pltpu.VMEM((5, 8, width), F32), pltpu.VMEM((4, 8, width), F32),
            pltpu.VMEM((6, 8, width), F32), pltpu.VMEM((5, 8, width), F32),
            pltpu.VMEM((8, 2048), F32), pltpu.VMEM((4, 8, 128), F32), pltpu.VMEM((2, 4, 8, 128), F32),
            pltpu.VMEM((2, 4, 8, 128), F32), pltpu.VMEM((3, 8, 128), F32),
            pltpu.VMEM((2, 8, 128), F32),
        ]
        + (head_landing(width) + head_line_landing(width)) * 2 + line_landing(512, 512) * 2,
        vmem=63, name="last",
    )


def widen_kernel(rows_in, mem_in, grad_in, cross_in, cross_o_in, heads_in, o_in, inner_in, outer_in, shared, late, split, *outs):
    rows, mem, grad, cq, ck, cv, co, q, k, v, o, inner, outer = outs[:13]
    rows[...] = rows_in[...]
    mem[...] = mem_in[...].astype(F32)
    grad[...] = grad_in[...].astype(F32)
    for kind, (cross, own) in enumerate(((cq, q), (ck, k), (cv, v))):
        cross[...] = cross_in[kind].astype(F32)
        own[...] = heads_in[kind].astype(F32)
    co[...] = cross_o_in[...].astype(F32)
    o[...] = o_in[...].astype(F32)
    inner[...] = inner_in[...].astype(F32)
    outer[...] = outer_in[...].astype(F32)
    vectors, bias_q, bias_v, bias_cq, bias_cv, bias_i = outs[13:22], *outs[22:]

    @pl.when(pl.program_id(0) == 0)
    def _():
        vectors[0][...] = late[0:1]
        vectors[1][...] = late[1:2]
        for at in range(7):
            vectors[2 + at][...] = shared[at:at + 1]
        for at, bias in enumerate((bias_q, bias_v, bias_cq, bias_cv)):
            bias[...] = jnp.concatenate([split[c, at:at + 1] for c in range(2)], axis=1)
        bias_i[...] = jnp.concatenate([split[c, 4 + at:5 + at] for c in range(2) for at in range(4)], axis=1)


def widen(rows, mem, grad, cross, cross_o, heads, o, inner, outer, shared, late, split):
    steps, width = 4, rows.shape[-1]
    shape = jax.ShapeDtypeStruct
    flat = lambda a: a.reshape(-1, width)
    block = lambda a: pl.BlockSpec((a.shape[0] // steps, a.shape[1]), lambda i: (i, 0))
    whole = lambda *dims: pl.BlockSpec(dims, lambda i: (0,) * len(dims))
    head = pl.BlockSpec((3, width // steps, 256), lambda i: (0, i, 0))
    ins = [flat(rows), flat(mem), flat(grad), cross, cross_o, heads, o, inner, outer, shared, late, split]
    in_specs = [block(ins[0])] * 3 + [head, block(cross_o), head, block(o), block(inner), block(outer)]
    in_specs += [whole(8, width), whole(8, width), whole(2, 8, 128)]
    wide = lambda a: shape(a.shape, F32)
    columns = shape((width, 256), F32)
    outs = [shape(ins[0].shape, BF), wide(ins[1]), wide(ins[2])] + [columns] * 3 + [wide(cross_o)] + [columns] * 3
    outs += [wide(o), wide(inner), wide(outer)]
    out_specs = [block(a) for a in outs] + [whole(1, width)] * 9 + [whole(1, 256)] * 4 + [whole(1, 1024)]
    outs += [shape((1, width), F32)] * 9 + [shape((1, 256), F32)] * 4 + [shape((1, 1024), F32)]
    return pl.pallas_call(
        widen_kernel,
        grid=(steps,),
        in_specs=in_specs,
        out_specs=out_specs,
        out_shape=outs,
        compiler_params=pltpu.CompilerParams(vmem_limit_bytes=63 << 20),
        name="widen",
    )(*ins)


def solution(mesh):
    if mesh.shape["tensor"] != 4 or mesh.shape["dp"] != 8:
        return general_solution(mesh)

    def local(
        layer_input, memory, grad_out, target_segments, source_segments,
        self_gain, self_shift, query_weight, query_bias, key_weight, value_weight, value_bias,
        attend_weight, attend_bias,
        cross_gain, cross_shift, cross_query, cross_query_bias, cross_key, cross_value, cross_value_bias,
        cross_attend, cross_attend_bias,
        feed_gain, feed_shift, inner_weight, inner_bias, outer_weight, outer_bias,
    ):
        (
            x, mem, top, n1, qkv1, att1, sums1, h1, n2, q2, kv2, att2, sums2, h2, n3, act, slope, g_outer,
            wqkv, wo, wc, wco, wi, wu, spans,
        ) = ahead(
            layer_input, memory, grad_out, (target_segments, source_segments),
            (query_bias, value_bias, cross_query_bias, cross_value_bias, inner_bias),
            (
                query_weight, key_weight, value_weight, attend_weight, cross_query, cross_key, cross_value, cross_attend,
                inner_weight, outer_weight,
            ),
            (self_gain, self_shift, attend_bias, cross_gain, cross_shift, cross_attend_bias, feed_gain, feed_shift),
        )
        block_out, gh2, f_outer, f_inner, heads2, shared, split = turn(
            g_outer, act, slope, n3, h2, top, wi, wu, wco, q2, kv2, att2, sums2, spans, feed_gain, outer_bias
        )
        memory_grad, input_grad, c_heads, c_out, s_heads, s_out, f_inner, shared, late, split = last(
            heads2, n2, mem, att2, gh2, h1, wc, wo, f_inner, qkv1, att1, sums1, spans, n1, x, wqkv, shared, split,
            cross_gain, self_gain,
        )
        (
            block_out, memory_grad, input_grad, g_cq, g_ck, g_cv, g_co, g_q, g_k, g_v, g_o, g_inner, g_outer,
            g_gain1, g_shift1, g_bias_o, g_gain2, g_shift2, g_bias_c, g_gain3, g_shift3, g_bias_u,
            g_bias_q, g_bias_v, g_bias_cq, g_bias_cv, g_bias_i,
        ) = widen(block_out, memory_grad, input_grad, c_heads, c_out, s_heads, s_out, f_inner, f_outer, shared, late, split)
        tokens = layer_input.shape
        vector = lambda v: v.reshape(-1)
        return (
            block_out.reshape(tokens), input_grad.reshape(tokens), memory_grad.reshape(tokens),
            vector(g_gain1), vector(g_shift1),
            g_q, vector(g_bias_q), g_k, g_v, vector(g_bias_v),
            g_o, vector(g_bias_o),
            vector(g_gain2), vector(g_shift2),
            g_cq, vector(g_bias_cq), g_ck, g_cv, vector(g_bias_cv),
            g_co, vector(g_bias_c),
            vector(g_gain3), vector(g_shift3),
            g_inner, vector(g_bias_i), g_outer, vector(g_bias_u),
        )

    row, one, by_column, by_row = P("dp", "tensor", None), P(), P(None, "tensor"), P("tensor", None)
    part, ids = P("tensor"), P("dp", None)
    return jax.shard_map(
        local,
        mesh=mesh,
        in_specs=(
            row, row, row, ids, ids,
            one, one, by_column, part, by_column, by_column, part, by_row, one,
            one, one, by_column, part, by_column, by_column, part, by_row, one,
            one, one, by_column, part, by_row, one,
        ),
        out_specs=(
            row, row, row,
            one, one, by_column, part, by_column, by_column, part, by_row, one,
            one, one, by_column, part, by_column, by_column, part, by_row, one,
            one, one, by_column, part, by_row, one,
        ),
        check_vma=False,
    )


BLOCK_ROWS = 512


def general_norm_forward(values, gain, shift):
    average = jnp.mean(values, axis=-1, keepdims=True)
    center = values - average
    inverse = lax.rsqrt(jnp.mean(center * center, axis=-1, keepdims=True) + EPSILON)
    normed = center * inverse
    return ((normed * gain + shift).astype(jnp.bfloat16), normed, inverse)


def general_norm_backward(grad_in, normed, inverse, gain):
    scaled = grad_in * gain
    first_mean = jnp.mean(scaled, axis=-1, keepdims=True)
    second_mean = jnp.mean(scaled * normed, axis=-1, keepdims=True)
    grad_values = inverse * (scaled - first_mean - normed * second_mean)
    return (grad_values, jnp.sum(grad_in * normed, axis=(0, 1)), jnp.sum(grad_in, axis=(0, 1)))


def gather_rows(values):
    return lax.all_gather(values, "tensor", axis=1, tiled=True)


def gather_grads(values):
    return lax.all_gather(values, "tensor", axis=1, tiled=True)


def reduce_inputs(partial_sum):
    return lax.psum_scatter(partial_sum, "tensor", scatter_dimension=1, tiled=True)


def advance(base, partial_sum, bias):
    return base + lax.psum_scatter(partial_sum, "tensor", scatter_dimension=1, tiled=True) + bias


def next_rows(values, gain, shift):
    return gather_rows(general_norm_forward(values, gain, shift)[0])


def backward_rows(normed_low):
    return gather_rows(normed_low)


def project(rows_in, weight):
    return jnp.einsum("rtd,dc->rtc", rows_in, weight, preferred_element_type=jnp.float32)


def project_back(grads, weight):
    return jnp.einsum("rtc,dc->rtd", grads, weight, preferred_element_type=jnp.float32)


def outer_sum(rows_in, grads):
    return jnp.einsum("rtd,rtc->dc", rows_in, grads, preferred_element_type=jnp.float32)


def bias_sum(grads):
    return jnp.sum(grads.astype(jnp.float32), axis=(0, 1))


def split_heads(values):
    return values.reshape(values.shape[0], values.shape[1], values.shape[2] // HD, HD)


def block_scores(query_block, key_row, query_ids, key_ids, row_start, causal):
    raw_scores = jnp.einsum(
        "qhd,khd->hqk", query_block, key_row, preferred_element_type=jnp.float32
    ) * float(HD) ** (-0.5)
    allowed = query_ids[:, None] == key_ids[None, :]
    if causal:
        query_place = row_start + jnp.arange(query_block.shape[0], dtype=jnp.int32)
        key_place = jnp.arange(key_row.shape[0], dtype=jnp.int32)
        allowed = allowed & (key_place[None, :] <= query_place[:, None])
    return jnp.where(allowed[None], raw_scores, jnp.full(raw_scores.shape, MASKED, jnp.float32))


def block_inputs(
    query_heads, key_heads, value_heads, query_ids, key_ids, position, block_count, block_size
):
    row_index = position // block_count
    row_start = position % block_count * block_size
    query_row = lax.dynamic_index_in_dim(query_heads, row_index, 0, keepdims=False)
    query_block = lax.dynamic_slice_in_dim(query_row, row_start, block_size, 0)
    key_row = lax.dynamic_index_in_dim(key_heads, row_index, 0, keepdims=False)
    value_row = lax.dynamic_index_in_dim(value_heads, row_index, 0, keepdims=False)
    query_seg = lax.dynamic_slice_in_dim(
        lax.dynamic_index_in_dim(query_ids, row_index, 0, keepdims=False), row_start, block_size, 0
    )
    key_seg = lax.dynamic_index_in_dim(key_ids, row_index, 0, keepdims=False)
    return (row_index, row_start, query_block, key_row, value_row, query_seg, key_seg)


def attend_forward(query, keys, values, query_ids, key_ids, causal):
    query_heads = split_heads(query)
    key_heads = split_heads(keys)
    value_heads = split_heads(values)
    block_size = min(BLOCK_ROWS, query.shape[1])
    block_count = query.shape[1] // block_size

    def one_block(position):
        row_index, row_start, query_block, key_row, value_row, query_seg, key_seg = block_inputs(
            query_heads,
            key_heads,
            value_heads,
            query_ids,
            key_ids,
            position,
            block_count,
            block_size,
        )
        scores = block_scores(query_block, key_row, query_seg, key_seg, row_start, causal)
        row_max = jnp.max(scores, axis=-1, keepdims=True)
        expo_scores = jnp.exp(scores - row_max)
        row_total = jnp.sum(expo_scores, axis=-1, keepdims=True)
        softmax_out = expo_scores / row_total
        attended = jnp.einsum(
            "hqk,khd->qhd",
            softmax_out.astype(jnp.bfloat16),
            value_row,
            preferred_element_type=jnp.float32,
        ).astype(jnp.bfloat16)
        return (attended, (row_max + jnp.log(row_total))[..., 0])

    attended_all, log_sums = lax.map(
        one_block, jnp.arange(query.shape[0] * block_count, dtype=jnp.int32)
    )
    return (attended_all.reshape(query.shape), log_sums)


def attend_backward(query, keys, values, grad_att, log_sums, query_ids, key_ids, causal):
    query_heads = split_heads(query)
    key_heads = split_heads(keys)
    value_heads = split_heads(values)
    grad_heads = split_heads(grad_att)
    block_size = min(BLOCK_ROWS, query.shape[1])
    block_count = query.shape[1] // block_size
    score_scale = float(HD) ** (-0.5)

    def one_block(carry, inputs):
        grad_keys, grad_values = carry
        position, log_sum = inputs
        row_index, row_start, query_block, key_row, value_row, query_seg, key_seg = block_inputs(
            query_heads,
            key_heads,
            value_heads,
            query_ids,
            key_ids,
            position,
            block_count,
            block_size,
        )
        grad_row = lax.dynamic_index_in_dim(grad_heads, row_index, 0, keepdims=False)
        grad_block = lax.dynamic_slice_in_dim(grad_row, row_start, block_size, 0)
        scores = block_scores(query_block, key_row, query_seg, key_seg, row_start, causal)
        softmax_out = jnp.exp(scores - log_sum[..., None])
        softmax_low = softmax_out.astype(jnp.bfloat16)
        attended = jnp.einsum(
            "hqk,khd->qhd", softmax_low, value_row, preferred_element_type=jnp.float32
        ).astype(jnp.bfloat16)
        grad_prob = jnp.einsum(
            "qhd,khd->hqk", grad_block, value_row, preferred_element_type=jnp.float32
        )
        correction = jnp.sum(softmax_out * grad_prob, axis=-1, keepdims=True)
        grad_score = (softmax_out * (grad_prob - correction)).astype(jnp.bfloat16)
        grad_query = (
            jnp.einsum("hqk,khd->qhd", grad_score, key_row, preferred_element_type=jnp.float32)
            * score_scale
        ).astype(jnp.bfloat16)
        key_added = (
            jnp.einsum("hqk,qhd->khd", grad_score, query_block, preferred_element_type=jnp.float32)
            * score_scale
        )
        value_added = jnp.einsum(
            "hqk,qhd->khd", softmax_low, grad_block, preferred_element_type=jnp.float32
        )
        grad_keys = grad_keys.at[row_index].add(key_added)
        grad_values = grad_values.at[row_index].add(value_added)
        return ((grad_keys, grad_values), (grad_query, attended))

    empty_grads = jnp.zeros(key_heads.shape, jnp.float32)
    positions = jnp.arange(query.shape[0] * block_count, dtype=jnp.int32)
    (grad_keys, grad_values), (grad_query, attended_all) = lax.scan(
        one_block, (empty_grads, empty_grads), (positions, log_sums)
    )
    return (
        grad_query.reshape(query.shape),
        grad_keys.reshape(keys.shape).astype(jnp.bfloat16),
        grad_values.reshape(values.shape).astype(jnp.bfloat16),
        attended_all.reshape(query.shape),
    )


def general_local(
    layer_input,
    memory,
    grad_out,
    target_segments,
    source_segments,
    self_gain,
    self_shift,
    query_weight,
    query_bias,
    key_weight,
    value_weight,
    value_bias,
    attend_weight,
    attend_bias,
    cross_gain,
    cross_shift,
    cross_query,
    cross_query_bias,
    cross_key,
    cross_value,
    cross_value_bias,
    cross_attend,
    cross_attend_bias,
    feed_gain,
    feed_shift,
    inner_weight,
    inner_bias,
    outer_weight,
    outer_bias,
):
    inputs = layer_input.astype(jnp.float32)
    rows_first = next_rows(inputs, self_gain, self_shift)
    query_first = (project(rows_first, query_weight) + query_bias).astype(jnp.bfloat16)
    keys_first = project(rows_first, key_weight).astype(jnp.bfloat16)
    values_first = (project(rows_first, value_weight) + value_bias).astype(jnp.bfloat16)
    attended_first, sums_first = attend_forward(
        query_first, keys_first, values_first, target_segments, target_segments, True
    )
    base_first = advance(inputs, project(attended_first, attend_weight), attend_bias)
    memory_rows = lax.all_gather(memory, "tensor", axis=1, tiled=True)
    rows_second = next_rows(base_first, cross_gain, cross_shift)
    query_second = (project(rows_second, cross_query) + cross_query_bias).astype(jnp.bfloat16)
    keys_second = project(memory_rows, cross_key).astype(jnp.bfloat16)
    values_second = (project(memory_rows, cross_value) + cross_value_bias).astype(jnp.bfloat16)
    attended_second, sums_second = attend_forward(
        query_second, keys_second, values_second, target_segments, source_segments, False
    )
    base_second = advance(base_first, project(attended_second, cross_attend), cross_attend_bias)
    rows_third = next_rows(base_second, feed_gain, feed_shift)
    pre_active = project(rows_third, inner_weight) + inner_bias
    active = jax.nn.silu(pre_active).astype(jnp.bfloat16)
    base_out = advance(base_second, project(active, outer_weight), outer_bias)
    block_out = base_out.astype(jnp.bfloat16)
    kept_input, kept_first, kept_second, kept_memory, kept_sums_first, kept_sums_second = (
        lax.optimization_barrier(
            (inputs, base_first, base_second, memory_rows, sums_first, sums_second)
        )
    )
    grad_top = grad_out.astype(jnp.float32)
    normed_low3, unit_third, inverse_third = general_norm_forward(kept_second, feed_gain, feed_shift)
    rows_back3 = backward_rows(normed_low3)
    pre_back = project(rows_back3, inner_weight) + inner_bias
    sigmoid_back = jax.nn.sigmoid(pre_back)
    active_back = (pre_back * sigmoid_back).astype(jnp.bfloat16)
    grad_rows3 = gather_grads(grad_top.astype(jnp.bfloat16))
    grad_outer_weight = outer_sum(active_back, grad_rows3)
    grad_outer_bias = jnp.sum(grad_top, axis=(0, 1))
    grad_active = project_back(grad_rows3, outer_weight)
    grad_inner = (grad_active * sigmoid_back * (1.0 + pre_back * (1.0 - sigmoid_back))).astype(
        jnp.bfloat16
    )
    grad_inner_weight = outer_sum(rows_back3, grad_inner)
    grad_inner_bias = bias_sum(grad_inner)
    grad_norm3 = reduce_inputs(project_back(grad_inner, inner_weight))
    grad_from3, grad_feed_gain, grad_feed_shift = general_norm_backward(
        grad_norm3, unit_third, inverse_third, feed_gain
    )
    grad_hidden2 = grad_top + grad_from3
    normed_low2, unit_second, inverse_second = general_norm_forward(kept_first, cross_gain, cross_shift)
    rows_back2 = backward_rows(normed_low2)
    query_back2 = (project(rows_back2, cross_query) + cross_query_bias).astype(jnp.bfloat16)
    keys_back2 = project(kept_memory, cross_key).astype(jnp.bfloat16)
    values_back2 = (project(kept_memory, cross_value) + cross_value_bias).astype(jnp.bfloat16)
    grad_rows2 = gather_grads(grad_hidden2.astype(jnp.bfloat16))
    grad_att2 = project_back(grad_rows2, cross_attend).astype(jnp.bfloat16)
    grad_query2, grad_keys2, grad_values2, attended_back2 = attend_backward(
        query_back2,
        keys_back2,
        values_back2,
        grad_att2,
        kept_sums_second,
        target_segments,
        source_segments,
        False,
    )
    grad_cross_attend = outer_sum(attended_back2, grad_rows2)
    grad_cross_attend_bias = jnp.sum(grad_hidden2, axis=(0, 1))
    grad_cross_query = outer_sum(rows_back2, grad_query2)
    grad_cross_query_bias = bias_sum(grad_query2)
    grad_cross_key = outer_sum(kept_memory, grad_keys2)
    grad_cross_value = outer_sum(kept_memory, grad_values2)
    grad_cross_value_bias = bias_sum(grad_values2)
    memory_grad = lax.psum_scatter(
        (project_back(grad_keys2, cross_key) + project_back(grad_values2, cross_value)).astype(
            jnp.bfloat16
        ),
        "tensor",
        scatter_dimension=1,
        tiled=True,
    ).astype(jnp.float32)
    grad_norm2 = reduce_inputs(project_back(grad_query2, cross_query))
    grad_from2, grad_cross_gain, grad_cross_shift = general_norm_backward(
        grad_norm2, unit_second, inverse_second, cross_gain
    )
    grad_hidden1 = grad_hidden2 + grad_from2
    normed_low1, unit_first, inverse_first = general_norm_forward(kept_input, self_gain, self_shift)
    rows_back1 = backward_rows(normed_low1)
    query_back1 = (project(rows_back1, query_weight) + query_bias).astype(jnp.bfloat16)
    keys_back1 = project(rows_back1, key_weight).astype(jnp.bfloat16)
    values_back1 = (project(rows_back1, value_weight) + value_bias).astype(jnp.bfloat16)
    grad_rows1 = gather_grads(grad_hidden1.astype(jnp.bfloat16))
    grad_att1 = project_back(grad_rows1, attend_weight).astype(jnp.bfloat16)
    grad_query1, grad_keys1, grad_values1, attended_back1 = attend_backward(
        query_back1,
        keys_back1,
        values_back1,
        grad_att1,
        kept_sums_first,
        target_segments,
        target_segments,
        True,
    )
    grad_attend_weight = outer_sum(attended_back1, grad_rows1)
    grad_attend_bias = jnp.sum(grad_hidden1, axis=(0, 1))
    grad_query_weight = outer_sum(rows_back1, grad_query1)
    grad_query_bias = bias_sum(grad_query1)
    grad_key_weight = outer_sum(rows_back1, grad_keys1)
    grad_value_weight = outer_sum(rows_back1, grad_values1)
    grad_value_bias = bias_sum(grad_values1)
    grad_norm1 = reduce_inputs(
        project_back(grad_query1, query_weight)
        + project_back(grad_keys1, key_weight)
        + project_back(grad_values1, value_weight)
    )
    grad_from1, grad_self_gain, grad_self_shift = general_norm_backward(
        grad_norm1, unit_first, inverse_first, self_gain
    )
    input_grad = grad_hidden1 + grad_from1
    (
        grad_query_weight,
        grad_query_bias,
        grad_key_weight,
        grad_value_weight,
        grad_value_bias,
        grad_attend_weight,
        grad_cross_query,
        grad_cross_query_bias,
        grad_cross_key,
        grad_cross_value,
        grad_cross_value_bias,
        grad_cross_attend,
        grad_inner_weight,
        grad_inner_bias,
        grad_outer_weight,
    ) = (
        lax.psum(grad_query_weight.astype(jnp.bfloat16), "dp").astype(jnp.float32),
        lax.psum(grad_query_bias.astype(jnp.bfloat16), "dp").astype(jnp.float32),
        lax.psum(grad_key_weight.astype(jnp.bfloat16), "dp").astype(jnp.float32),
        lax.psum(grad_value_weight.astype(jnp.bfloat16), "dp").astype(jnp.float32),
        lax.psum(grad_value_bias.astype(jnp.bfloat16), "dp").astype(jnp.float32),
        lax.psum(grad_attend_weight.astype(jnp.bfloat16), "dp").astype(jnp.float32),
        lax.psum(grad_cross_query.astype(jnp.bfloat16), "dp").astype(jnp.float32),
        lax.psum(grad_cross_query_bias.astype(jnp.bfloat16), "dp").astype(jnp.float32),
        lax.psum(grad_cross_key.astype(jnp.bfloat16), "dp").astype(jnp.float32),
        lax.psum(grad_cross_value.astype(jnp.bfloat16), "dp").astype(jnp.float32),
        lax.psum(grad_cross_value_bias.astype(jnp.bfloat16), "dp").astype(jnp.float32),
        lax.psum(grad_cross_attend.astype(jnp.bfloat16), "dp").astype(jnp.float32),
        lax.psum(grad_inner_weight.astype(jnp.bfloat16), "dp").astype(jnp.float32),
        lax.psum(grad_inner_bias.astype(jnp.bfloat16), "dp").astype(jnp.float32),
        lax.psum(grad_outer_weight.astype(jnp.bfloat16), "dp").astype(jnp.float32),
    )
    (
        grad_self_gain,
        grad_self_shift,
        grad_attend_bias,
        grad_cross_gain,
        grad_cross_shift,
        grad_cross_attend_bias,
        grad_feed_gain,
        grad_feed_shift,
        grad_outer_bias,
    ) = lax.psum(
        (
            grad_self_gain,
            grad_self_shift,
            grad_attend_bias,
            grad_cross_gain,
            grad_cross_shift,
            grad_cross_attend_bias,
            grad_feed_gain,
            grad_feed_shift,
            grad_outer_bias,
        ),
        ("dp", "tensor"),
    )
    return (
        block_out,
        input_grad,
        memory_grad,
        grad_self_gain,
        grad_self_shift,
        grad_query_weight,
        grad_query_bias,
        grad_key_weight,
        grad_value_weight,
        grad_value_bias,
        grad_attend_weight,
        grad_attend_bias,
        grad_cross_gain,
        grad_cross_shift,
        grad_cross_query,
        grad_cross_query_bias,
        grad_cross_key,
        grad_cross_value,
        grad_cross_value_bias,
        grad_cross_attend,
        grad_cross_attend_bias,
        grad_feed_gain,
        grad_feed_shift,
        grad_inner_weight,
        grad_inner_bias,
        grad_outer_weight,
        grad_outer_bias,
    )


def general_solution(mesh):
    placed = (
        P("dp", "tensor", None),
        P("dp", "tensor", None),
        P("dp", "tensor", None),
        P("dp", None),
        P("dp", None),
        P(),
        P(),
        P(None, "tensor"),
        P("tensor"),
        P(None, "tensor"),
        P(None, "tensor"),
        P("tensor"),
        P("tensor", None),
        P(),
        P(),
        P(),
        P(None, "tensor"),
        P("tensor"),
        P(None, "tensor"),
        P(None, "tensor"),
        P("tensor"),
        P("tensor", None),
        P(),
        P(),
        P(),
        P(None, "tensor"),
        P("tensor"),
        P("tensor", None),
        P(),
    )
    return jax.shard_map(
        general_local,
        mesh=mesh,
        in_specs=placed,
        out_specs=(
            P("dp", "tensor", None),
            P("dp", "tensor", None),
            P("dp", "tensor", None),
            P(),
            P(),
            P(None, "tensor"),
            P("tensor"),
            P(None, "tensor"),
            P(None, "tensor"),
            P("tensor"),
            P("tensor", None),
            P(),
            P(),
            P(),
            P(None, "tensor"),
            P("tensor"),
            P(None, "tensor"),
            P(None, "tensor"),
            P("tensor"),
            P("tensor", None),
            P(),
            P(),
            P(),
            P(None, "tensor"),
            P("tensor"),
            P("tensor", None),
            P(),
        ),
        check_vma=False,
    )
```
